32 devices in a mesh: section: 2 (over y), dp: 4 (over x, core), tensor: 4 (over z).
Axes of the slice: x: 2, y: 2, z: 4, core: 2. Of those that a mesh axis runs over, the one named last changes fastest.
Arguments:
- inputs: bfloat16 [2, 4, 512, 1536], P(None, 'dp'), may hold values from -6 to 6
- cotangent: bfloat16 [2, 4, 512, 1536], P(None, 'dp'), may hold values from -6 to 6
- lengths: int32 [2, 4], P(None, 'dp'), may hold values from 1 to 512, 1280 in all within a row
- norm_attn: float32 [2, 1536], P('section'), may hold values from 0.1 to 1.9
- w_query: bfloat16 [2, 1536, 1536], P('section', None, 'tensor'), may hold values from -0.15625 to 0.15625
- w_key: bfloat16 [2, 1536, 768], P('section', None, 'tensor'), may hold values from -0.15625 to 0.15625
- w_value: bfloat16 [2, 1536, 768], P('section', None, 'tensor'), may hold values from -0.15625 to 0.15625
- w_out: bfloat16 [2, 1536, 1536], P('section', 'tensor'), may hold values from -0.625 to 0.625
- norm_ffn: float32 [2, 1536], P('section'), may hold values from 0.1 to 1.9
- w_gate: bfloat16 [2, 1536, 4096], P('section', None, 'tensor'), may hold values from -0.15625 to 0.15625
- w_up: bfloat16 [2, 1536, 4096], P('section', None, 'tensor'), may hold values from -0.15625 to 0.15625
- w_down: bfloat16 [2, 4096, 1536], P('section', 'tensor'), may hold values from -0.09375 to 0.09375
Outputs:
- activations: bfloat16 [2, 2, 4, 512, 1536], P('section', None, 'dp')
- input_grads: bfloat16 [2, 2, 4, 512, 1536], P('section', None, 'dp')
- grad_norm_attn: float32 [2, 1536], P('section', 'dp')
- grad_query: float32 [2, 1536, 1536], P('section', 'dp', 'tensor')
- grad_key: float32 [2, 1536, 768], P('section', 'dp', 'tensor')
- grad_value: float32 [2, 1536, 768], P('section', 'dp', 'tensor')
- grad_out: float32 [2, 1536, 1536], P('section', 'tensor', 'dp')
- grad_norm_ffn: float32 [2, 1536], P('section', 'dp')
- grad_gate: float32 [2, 1536, 4096], P('section', 'dp', 'tensor')
- grad_up: float32 [2, 1536, 4096], P('section', 'dp', 'tensor')
- grad_down: float32 [2, 4096, 1536], P('section', 'tensor', 'dp')
The draws below stay inside these ranges and needn't reach their ends.
Inputs may be any that keep to these rules, and one draw needn't show every extreme that they name: In each micro-batch the lengths sum to 1280 and the longest is exactly 512.
All inputs are finite; a program needn't handle non-finite values.
Results may differ from the reference program's by a relative error of at most 0.035.
Values may be sent and summed in bfloat16 or wider, within the bound.
A program may use at most 192 MiB of HBM per device.

```python
import math
import jax
import jax.numpy as jnp
import numpy as np
from jax import lax

D = 1536
HQ = 16
HK = 8
HD = 96
FF = 4096
SEQ = 512
MICRO = 2
GROUPS = 4


def shard_levels(own_key, extent, pieces, smallest, largest):
    def one(dim, parts):
        heights = jax.random.uniform(jax.random.fold_in(jax.random.fold_in(own_key, 6), dim), (parts,), jnp.float32, smallest / len(pieces), largest / len(pieces))
        return jnp.repeat(jnp.exp(heights), extent[dim] // parts).reshape((-1,) + (1,) * (len(extent) - dim - 1))

    gain = one(*pieces[0])
    for cut in pieces[1:]:
        gain = gain * one(*cut)
    return gain


def length_profile(count, total, limit, skew):
    portions = [(1 << 20) // math.isqrt(grade ** skew) + 1 for grade in range(2, count + 1)]
    spare, given = total - limit - (count - 1), [1] * (count - 1)
    while spare > 0:
        free = [i for i in range(count - 1) if given[i] < limit]
        pool, left = sum([portions[i] for i in free]), spare
        for i in free:
            extra = min(limit - given[i], max(1, left * portions[i] // pool), spare)
            given[i] = given[i] + extra
            spare = spare - extra
    return np.array([limit] + given)


def ragged_sizes(key, amount, total, most, slope):
    if amount == 2:
        one = jax.random.randint(key, (), max(1, total - most), min(most, total - 1) + 1)
        return jnp.stack([one, total - one])
    tallies = jnp.asarray(length_profile(amount, total, most, slope), jnp.int32)
    pairs = (amount - 1) // 2
    giver, sink = tallies[1:1 + 2 * pairs:2], tallies[2:2 + 2 * pairs:2]
    room = jnp.minimum(giver - 1, most - sink)
    moved = jax.random.randint(jax.random.fold_in(key, 1), (pairs,), 0, 1 << 20) % (room + 1)
    tallies = tallies.at[1:1 + 2 * pairs:2].set(giver - moved).at[2:2 + 2 * pairs:2].set(sink + moved)
    return tallies[jax.random.permutation(jax.random.fold_in(key, 2), amount)]


def noise(rng, dims, width, most, shards=(), kind=jnp.bfloat16):
    drawn = jax.random.normal(rng, dims, jnp.float32) * width
    if len(shards) > 0:
        drawn = shard_levels(rng, dims, shards, -0.22, 0.18) * drawn
    return jnp.clip(drawn, min=-most, max=most).astype(kind)


def setup_inputs(seed: int = 0) -> dict:
    keys = jax.random.split(jax.random.key(seed), 13)
    inputs = noise(keys[0], (MICRO, GROUPS, SEQ, D), 1.0, 6.0, ((1, 4),))
    cotangent = noise(keys[1], (MICRO, GROUPS, SEQ, D), 1.0, 6.0, ((1, 4),))
    lengths = jax.vmap(lambda own: ragged_sizes(own, GROUPS, GROUPS * SEQ * 5 // 8, SEQ, 2))(jax.random.split(keys[2], MICRO)).reshape((MICRO, GROUPS)).astype(jnp.int32)
    norm_attn = jnp.clip(1.0 + 0.18 * jax.random.normal(keys[3], (2, D), jnp.float32), 0.1, 1.9)
    w_query = noise(keys[4], (2, D, HQ * HD), D ** -0.5, 0.15625, ((0, 2), (2, 4)))
    w_key = noise(keys[5], (2, D, HK * HD), D ** -0.5, 0.15625, ((0, 2), (2, 4)))
    w_value = noise(keys[6], (2, D, HK * HD), D ** -0.5, 0.15625, ((0, 2), (2, 4)))
    w_out = noise(keys[7], (2, HQ * HD, D), (HQ * HD // 16) ** -0.5, 0.625, ((0, 2), (1, 4)))
    norm_ffn = jnp.clip(1.0 + 0.18 * jax.random.normal(keys[8], (2, D), jnp.float32), 0.1, 1.9)
    w_gate = noise(keys[9], (2, D, FF), D ** -0.5, 0.15625, ((0, 2), (2, 4)))
    w_up = noise(keys[10], (2, D, FF), D ** -0.5, 0.15625, ((0, 2), (2, 4)))
    w_down = noise(keys[11], (2, FF, D), FF ** -0.5, 0.09375, ((0, 2), (1, 4)))
    return {"inputs": inputs, "cotangent": cotangent, "lengths": lengths, "norm_attn": norm_attn, "w_query": w_query, "w_key": w_key, "w_value": w_value, "w_out": w_out, "norm_ffn": norm_ffn, "w_gate": w_gate, "w_up": w_up, "w_down": w_down}


epsilon = 1e-05
rope_base = 100000.0
negative = -1e+30

@jax.custom_vjp
def low(v):
    return lax.optimization_barrier(v.astype(jnp.bfloat16)).astype(jnp.float32)

@jax.custom_vjp
def low_back(v):
    return v

def low_keep(v):
    return (low(v), None)

def low_pass(kept, grad):
    return (grad,)

def back_keep(v):
    return (v, None)

def back_low(kept, grad):
    return (low(grad),)
low.defvjp(low_keep, low_pass)
low_back.defvjp(back_keep, back_low)

def tables(seq_len, head_width):
    half_width = head_width // 2
    inverse = rope_base ** (-(jnp.arange(half_width, dtype=jnp.float32) * 2.0 / head_width))
    angle = jnp.arange(seq_len, dtype=jnp.float32)[:, None] * inverse[None, :]
    cosine = jnp.concatenate([jnp.cos(angle), jnp.cos(angle)], axis=-1)
    sine = jnp.concatenate([jnp.sin(angle), jnp.sin(angle)], axis=-1)
    return (cosine[:, None, :], sine[:, None, :])

def rotate(value_in, cosine, sine):
    half_width = value_in.shape[-1] // 2
    turned = jnp.concatenate([-value_in[..., half_width:], value_in[..., :half_width]], axis=-1)
    return value_in * cosine + turned * sine

def normalize(stream):
    return stream * lax.rsqrt(lax.optimization_barrier(jnp.mean(stream * stream, axis=-1, keepdims=True)) + epsilon)

def matmul(left, right):
    return jnp.dot(left, right, precision=lax.Precision.HIGHEST)

def attention(triple):
    queries, key_rows, value_rows = triple
    seq_len = queries.shape[0]
    grouped = queries.reshape(seq_len, HK, HQ // HK, HD)
    scores = low_back(jnp.einsum('qgrd,kgd->grqk', grouped, key_rows, precision=lax.Precision.HIGHEST) * HD ** (-0.5))
    position = jnp.arange(seq_len)
    scores = jnp.where(position[None, :] <= position[:, None], scores, negative)
    row_max = lax.optimization_barrier(jnp.max(scores, axis=-1, keepdims=True))
    expo = jnp.exp(scores - row_max)
    attn_prob = expo / lax.optimization_barrier(jnp.sum(expo, axis=-1, keepdims=True))
    mixed = jnp.einsum('grqk,kgd->qgrd', low(attn_prob), value_rows, precision=lax.Precision.HIGHEST)
    return low(low_back(mixed.reshape(seq_len, HQ * HD)))

def layer(stream, live_rows, weights):
    norm_one, query_w, key_w, value_w, out_w, norm_two, gate_w, up_w, down_w = weights
    row_count, seq_len = (stream.shape[0], stream.shape[1])
    cosine, sine = tables(seq_len, HD)
    normed_one = low(normalize(stream) * norm_one).reshape(-1, D)
    query_pre = low_back(matmul(normed_one, query_w)).reshape(row_count, seq_len, HQ, HD)
    key_pre = low_back(matmul(normed_one, key_w)).reshape(row_count, seq_len, HK, HD)
    value_pre = low_back(matmul(normed_one, value_w)).reshape(row_count, seq_len, HK, HD)
    queries = low(rotate(query_pre, cosine, sine))
    key_rows = low(rotate(key_pre, cosine, sine))
    value_rows = low(value_pre)
    mixed = lax.map(jax.checkpoint(attention), (queries, key_rows, value_rows))
    attn_sum = low_back(matmul(mixed.reshape(-1, HQ * HD), out_w)).reshape(row_count, seq_len, D)
    resid = stream + live_rows * attn_sum
    normed_two = low(normalize(resid) * norm_two).reshape(-1, D)
    gate_pre = low_back(matmul(normed_two, gate_w))
    up_pre = low_back(matmul(normed_two, up_w))
    activated = low(gate_pre * jax.nn.sigmoid(gate_pre) * up_pre)
    ffn_sum = low_back(matmul(activated, down_w)).reshape(row_count, seq_len, D)
    return resid + live_rows * ffn_sum

def reference(inputs, cotangent, lengths, norm_attn, w_query, w_key, w_value, w_out, norm_ffn, w_gate, w_up, w_down):
    stream = inputs.astype(jnp.float32).reshape(MICRO * GROUPS, SEQ, D)
    position = jnp.arange(SEQ, dtype=jnp.int32)
    live_rows = (position[None, :] < lengths.reshape(-1)[:, None]).astype(jnp.float32)[..., None]
    params = tuple((item.astype(jnp.float32) for item in (norm_attn, w_query, w_key, w_value, w_out, norm_ffn, w_gate, w_up, w_down)))
    zero_in = jnp.zeros_like(stream)

    def whole(stream, zero_in, params):
        first_w = tuple((item[0] for item in params))
        second_w = tuple((item[1] for item in params))
        first_out = layer(stream, live_rows, first_w)
        middle = low(low_back(first_out)) + zero_in
        second_out = layer(middle, live_rows, second_w)
        return (second_out, first_out)
    second_out, vjp_fn, first_out = jax.vjp(whole, stream, zero_in, params, has_aux=True)
    d_stream, d_middle, grads = vjp_fn(cotangent.astype(jnp.float32).reshape(MICRO * GROUPS, SEQ, D))
    shape_out = (2, MICRO, GROUPS, SEQ, D)
    acts_out = jnp.stack([first_out, second_out]).reshape(shape_out).astype(jnp.bfloat16)
    back_out = jnp.stack([d_stream, d_middle]).reshape(shape_out).astype(jnp.bfloat16)
    return (acts_out, back_out, grads[0], grads[1], grads[2], grads[3], grads[4], grads[5], grads[6], grads[7], grads[8])
```

```python
import functools

import jax
import jax.numpy as jnp
from jax import lax
from jax.experimental import pallas as pl
from jax.experimental.pallas import tpu as pltpu
from jax.sharding import PartitionSpec as P

HD = 96

epsilon = 1e-05
rope_base = 100000.0
negative = -1e30
MESH = pl.DeviceIdType.MESH
F32 = jnp.float32
BF16 = jnp.bfloat16


def line_kernel(half, pieces, lag_b, lag_c, normed, shift, *refs):
    if normed:
        part, base, xrow, gain, out, gsum = refs[:6]
        rest = refs[6:]
    else:
        part, base, out = refs[:3]
        rest = refs[3:]
    if shift:
        arrived, rest = rest[0], rest[1:]
    (rin, smid, rmid, s_up, r_up, s_mid, r_mid, s_b1, s_b2, r_b, s_c, r_c) = rest[:12]
    if shift:
        s_s, r_s = rest[12:]
    step_rows = half // pieces
    t = lax.axis_index("tensor")
    section = lax.axis_index("section")
    mid = jnp.logical_or(t == 1, t == 2)
    bar = pltpu.get_barrier_semaphore()

    @pl.when(t > 0)
    def _():
        pl.semaphore_signal(bar, inc=1, device_id={"tensor": jnp.maximum(t - 1, 0)}, device_id_type=MESH)

    @pl.when(t < 3)
    def _():
        pl.semaphore_signal(bar, inc=1, device_id={"tensor": jnp.minimum(t + 1, 3)}, device_id_type=MESH)

    if shift:
        pl.semaphore_signal(bar, inc=1, device_id={"section": 1 - section}, device_id_type=MESH)
    more = 1 if shift else 0

    @pl.when(mid)
    def _():
        pl.semaphore_wait(bar, 2 + more)

    @pl.when(jnp.logical_not(mid))
    def _():
        pl.semaphore_wait(bar, 1 + more)

    sends = section == (0 if shift > 0 else 1)

    def rows(start, p):
        return pl.ds(pl.multiple_of(start + p * step_rows, step_rows), step_rows)

    def remote(src, dst, s_sem, r_sem, where):
        return pltpu.make_async_remote_copy(
            src_ref=src, dst_ref=dst, send_sem=s_sem, recv_sem=r_sem, device_id=where, device_id_type=MESH
        )

    def moved(start, p):
        side = start // half
        return remote(
            out.at[rows(start, p)], arrived.at[rows(start, p)], s_s.at[side, p], r_s.at[side, p], {"section": 1 - section}
        )

    def pass_on(start, p):
        if shift:

            @pl.when(sends)
            def _():
                moved(start, p).start()

    def outcome(src, s_sem, r_sem, where, start, p):
        return remote(out.at[rows(start, p)], out.at[rows(start, p)], s_sem.at[p], r_sem.at[p], where)

    @pl.when(jnp.logical_not(mid))
    def _():
        nbr = {"tensor": jnp.where(t == 0, 1, 2)}
        far = jnp.where(t == 0, half, 0)
        near = half - far
        if normed:
            gsum[...] = jnp.zeros_like(gsum)

        def up(start, p, k):
            return remote(part.at[rows(start, p)], rin.at[rows(start, p)], s_up.at[k, p], r_up.at[k, p], nbr)

        def begin(p, c):
            up(far, p, 0).start()
            up(near, p, 1).start()
            return c

        lax.fori_loop(0, pieces, begin, 0)

        def finish(p, c):
            outcome(None, s_b2, r_b, nbr, near, p).wait_recv()
            pass_on(near, p)
            outcome(None, s_c, r_c, nbr, far, p).wait_recv()
            pass_on(far, p)
            up(far, p, 0).wait_send()
            up(near, p, 1).wait_send()
            return c

        lax.fori_loop(0, pieces, finish, 0)

    @pl.when(mid)
    def _():
        outer = {"tensor": jnp.where(t == 1, 0, 3)}
        other = {"tensor": 3 - t}
        near = (t - 1) * half
        far = half - near
        if normed:
            gsum[...] = jnp.zeros_like(gsum)

        def up(start, p, k):
            return remote(part.at[rows(start, p)], rin.at[rows(start, p)], s_up.at[k, p], r_up.at[k, p], outer)

        def cross(p):
            return remote(smid.at[rows(0, p)], rmid.at[rows(0, p)], s_mid.at[p], r_mid.at[p], other)

        def step(i, c):
            @pl.when(i < pieces)
            def _():
                up(far, i, 0).wait_recv()
                smid[rows(0, i)] = (part[rows(far, i)].astype(F32) + rin[rows(far, i)].astype(F32)).astype(BF16)
                cross(i).start()

            j = i - lag_b

            @pl.when(jnp.logical_and(j >= 0, j < pieces))
            def _():
                up(near, j, 1).wait_recv()
                cross(j).wait_recv()
                here = rows(near, j)
                total = part[here].astype(F32) + rin[here].astype(F32) + rmid[rows(0, j)].astype(F32)
                start_val = base[here].astype(F32)
                if normed:
                    x = xrow[here].astype(F32)
                    scale = lax.rsqrt(jnp.mean(x * x, axis=-1, keepdims=True) + epsilon)
                    unit = x * scale
                    gsum[...] += jnp.sum(total * unit, axis=0, keepdims=True)
                    inner = total * gain[...]
                    total = scale * (inner - unit * jnp.mean(inner * unit, axis=-1, keepdims=True))
                out[here] = (start_val + total).astype(BF16)
                outcome(None, s_b1, r_b, other, near, j).start()
                outcome(None, s_b2, r_b, outer, near, j).start()
                pass_on(near, j)

            k = i - lag_c

            @pl.when(k >= 0)
            def _():
                outcome(None, s_b1, r_b, other, far, k).wait_recv()
                outcome(None, s_c, r_c, outer, far, k).start()
                pass_on(far, k)

            return c

        lax.fori_loop(0, pieces + lag_c, step, 0)

        def finish(p, c):
            cross(p).wait_send()
            outcome(None, s_b1, r_b, other, near, p).wait_send()
            outcome(None, s_b2, r_b, outer, near, p).wait_send()
            outcome(None, s_c, r_c, outer, far, p).wait_send()
            return c

        lax.fori_loop(0, pieces, finish, 0)

    if shift:

        def close(p, c):
            @pl.when(sends)
            def _():
                moved(0, p).wait_send()
                moved(half, p).wait_send()

            @pl.when(jnp.logical_not(sends))
            def _():
                moved(0, p).wait_recv()
                moved(half, p).wait_recv()

            return c

        lax.fori_loop(0, pieces, close, 0)


def line_sum(part, base, cid, xrow=None, gain=None, shift=0, pieces=10):
    count, width = part.shape
    half = count // 2
    normed = xrow is not None
    whole = jax.ShapeDtypeStruct((count, width), BF16)
    outs = [whole]
    args = [part, base]
    if normed:
        outs.append(jax.ShapeDtypeStruct((1, width), F32))
        args += [xrow, gain[None]]
    if shift:
        outs.append(whole)
    dma = pltpu.SemaphoreType.DMA
    scratch = [
        pltpu.VMEM((count, width), BF16),
        pltpu.VMEM((half, width), BF16),
        pltpu.VMEM((half, width), BF16),
        dma((2, pieces)),
        dma((2, pieces)),
    ] + [dma((pieces,))] * 7
    if shift:
        scratch += [dma((2, pieces))] * 2
    vmem = pl.BlockSpec(memory_space=pltpu.VMEM)
    return pl.pallas_call(
        functools.partial(line_kernel, half, pieces, 2, 4, normed, shift),
        out_shape=outs,
        in_specs=[vmem] * len(args),
        out_specs=[vmem] * len(outs),
        scratch_shapes=scratch,
        compiler_params=pltpu.CompilerParams(
            collective_id=cid, has_side_effects=True, vmem_limit_bytes=32 * 2**20
        ),
        name="line_sum_%d" % cid,
    )(*args)


def rope_tables(pos):
    half_width = HD // 2
    inverse = rope_base ** (-(jnp.arange(half_width, dtype=F32) * 2.0 / HD))
    angle = pos.astype(F32)[:, None] * inverse[None, :]
    cosine = jnp.concatenate([jnp.cos(angle), jnp.cos(angle)], axis=-1)
    sine = jnp.concatenate([jnp.sin(angle), jnp.sin(angle)], axis=-1)
    return (cosine[:, None, :], sine[:, None, :])


def rotate(value_in, cosine, sine):
    half_width = value_in.shape[-1] // 2
    turned = jnp.concatenate([-value_in[..., half_width:], value_in[..., :half_width]], axis=-1)
    return value_in * cosine + turned * sine


def unrotate(grad_in, cosine, sine):
    half_width = grad_in.shape[-1] // 2
    scaled = grad_in * sine
    turned = jnp.concatenate([scaled[..., half_width:], -scaled[..., :half_width]], axis=-1)
    return grad_in * cosine + turned


def with_transpose(left, right):
    return lax.dot_general(left, right, (((1,), (1,)), ((), ())), preferred_element_type=F32)


def rows_contract(left, right):
    return lax.dot_general(left, right, (((0,), (0,)), ((), ())), preferred_element_type=F32)


def normalize(rows, gain):
    rows = rows.astype(F32)
    scale = lax.rsqrt(jnp.mean(rows * rows, axis=-1, keepdims=True) + epsilon)
    return (rows * scale * gain).astype(BF16)


def slots_of(lens, count):
    groups = lens.shape[0]
    kept = jnp.minimum(lens, count)
    free, extra = count - kept, lens - kept
    free_off = jnp.cumsum(free) - free
    extra_end = jnp.cumsum(extra)
    slot = jnp.arange(count)
    own = slot[None, :] < kept[:, None]
    index = free_off[:, None] + slot[None, :] - kept[:, None]
    source = jnp.sum(index[:, :, None] >= extra_end[None, None, :], axis=-1)
    begins = jnp.sum(jnp.where(index[:, :, None] >= extra_end[None, None, :], extra[None, None, :], 0), axis=-1)
    seq = jnp.where(own, jnp.arange(groups)[:, None], source)
    pos = jnp.where(own, slot[None, :], count + index - begins)
    return seq, pos, own


def forward(stream, spots, weights, first_id):
    norm_one, query_w, key_w, value_w, out_w, norm_two, gate_w, up_w, down_w = weights
    cosine, sine, allowed = spots
    count = stream.shape[0]
    normed_one = normalize(stream, norm_one)
    query_pre = jnp.dot(normed_one, query_w, preferred_element_type=F32)
    key_pre = jnp.dot(normed_one, key_w, preferred_element_type=F32)
    value_pre = jnp.dot(normed_one, value_w, preferred_element_type=F32)
    queries = rotate(query_pre.reshape(count, -1, HD), cosine, sine).astype(BF16)
    key_rows = rotate(key_pre.reshape(count, -1, HD), cosine, sine).astype(BF16)
    own_keys = jnp.concatenate([key_rows.reshape(count, -1), value_pre.astype(BF16)], axis=1)
    every = lax.all_gather(own_keys, "dp", axis=0, tiled=True)
    width = key_w.shape[1]
    keys_all = every[:, :width].reshape(every.shape[0], -1, HD)
    values_all = every[:, width:].reshape(every.shape[0], -1, HD)
    groups = keys_all.shape[1]
    q = queries.reshape(count, groups, -1, HD)
    scores = jnp.einsum("qgrd,kgd->grqk", q, keys_all, preferred_element_type=F32) * HD ** (-0.5)
    scores = jnp.where(allowed, scores, negative)
    row_max = jnp.max(scores, axis=-1, keepdims=True)
    expo = jnp.exp(scores - row_max)
    row_total = jnp.sum(expo, axis=-1, keepdims=True)
    prob = (expo / row_total).astype(BF16)
    mixed = jnp.einsum("grqk,kgd->qgrd", prob, values_all, preferred_element_type=F32)
    mixed = mixed.astype(BF16).reshape(count, -1)
    logsum = (row_max + jnp.log(row_total))[..., 0]
    attn_part = jnp.dot(mixed, out_w, preferred_element_type=F32)
    resid = line_sum(attn_part.astype(BF16), stream, first_id)[0]
    normed_two = normalize(resid, norm_two)
    gate_pre = jnp.dot(normed_two, gate_w, preferred_element_type=F32)
    up_pre = jnp.dot(normed_two, up_w, preferred_element_type=F32)
    activated = (gate_pre * jax.nn.sigmoid(gate_pre) * up_pre).astype(BF16)
    ffn_part = jnp.dot(activated, down_w, preferred_element_type=F32)
    result, arrived = line_sum(ffn_part.astype(BF16), resid, first_id + 1, shift=1)
    kept = (stream, normed_one, q, keys_all, values_all, logsum, mixed, resid, normed_two, gate_pre, up_pre, activated)
    return result, arrived, kept


def backward(incoming, kept, spots, weights, first_id):
    norm_one, query_w, key_w, value_w, out_w, norm_two, gate_w, up_w, down_w = weights
    stream, normed_one, q, keys_all, values_all, logsum, mixed, resid, normed_two, gate_pre, up_pre, activated = kept
    cosine, sine, allowed = spots
    count = stream.shape[0]
    d_act = with_transpose(incoming, down_w)
    sigma = jax.nn.sigmoid(gate_pre)
    d_up = (d_act * gate_pre * sigma).astype(BF16)
    d_gate = (d_act * up_pre * sigma * (1.0 + gate_pre * (1.0 - sigma))).astype(BF16)
    grad_down = rows_contract(activated, incoming)
    grad_gate = rows_contract(normed_two, d_gate)
    grad_up = rows_contract(normed_two, d_up)
    partial_two = with_transpose(d_gate, gate_w) + with_transpose(d_up, up_w)
    d_resid, grad_norm_two = line_sum(partial_two.astype(BF16), incoming, first_id, xrow=resid, gain=norm_two)
    d_mixed = with_transpose(d_resid, out_w).astype(BF16)
    grad_out = rows_contract(mixed, d_resid)
    dm = d_mixed.reshape(q.shape)
    score_scale = HD ** (-0.5)
    scores = jnp.einsum("qgrd,kgd->grqk", q, keys_all, preferred_element_type=F32) * score_scale
    prob = jnp.exp(jnp.where(allowed, scores, negative) - logsum[..., None])
    d_prob = jnp.einsum("qgrd,kgd->grqk", dm, values_all, preferred_element_type=F32)
    row_dot = jnp.sum(prob * d_prob, axis=-1, keepdims=True)
    d_scores = (prob * (d_prob - row_dot)).astype(BF16)
    d_query = jnp.einsum("grqk,kgd->qgrd", d_scores, keys_all, preferred_element_type=F32) * score_scale
    d_keys = jnp.einsum("grqk,qgrd->kgd", d_scores, q, preferred_element_type=F32) * score_scale
    d_values = jnp.einsum("grqk,qgrd->kgd", prob.astype(BF16), dm, preferred_element_type=F32)
    every = jnp.concatenate([d_keys.reshape(keys_all.shape[0], -1), d_values.reshape(keys_all.shape[0], -1)], axis=1)
    own = lax.psum_scatter(every.astype(BF16), "dp", scatter_dimension=0, tiled=True).astype(F32)
    width = key_w.shape[1]
    d_query_pre = unrotate(d_query.reshape(count, -1, HD), cosine, sine).reshape(count, -1).astype(BF16)
    d_key_pre = unrotate(own[:, :width].reshape(count, -1, HD), cosine, sine).reshape(count, -1).astype(BF16)
    d_value_pre = own[:, width:].astype(BF16)
    grad_query = rows_contract(normed_one, d_query_pre)
    grad_key = rows_contract(normed_one, d_key_pre)
    grad_value = rows_contract(normed_one, d_value_pre)
    partial_one = (
        with_transpose(d_query_pre, query_w)
        + with_transpose(d_key_pre, key_w)
        + with_transpose(d_value_pre, value_w)
    )
    d_stream, grad_norm_one, arrived = line_sum(
        partial_one.astype(BF16), d_resid, first_id + 1, xrow=stream, gain=norm_one, shift=-1
    )
    return (
        d_stream,
        arrived,
        (
            grad_norm_one[0],
            grad_query,
            grad_key,
            grad_value,
            grad_out,
            grad_norm_two[0],
            grad_gate,
            grad_up,
            grad_down,
        ),
    )


def on_device(
    inputs,
    cotangent,
    lengths,
    norm_attn,
    w_query,
    w_key,
    w_value,
    w_out,
    norm_ffn,
    w_gate,
    w_up,
    w_down,
):
    first = lax.axis_index("section") == 0
    me = lax.axis_index("dp")
    groups = lax.axis_size("dp")
    micro, seq_len, width = inputs.shape[0], inputs.shape[2], inputs.shape[3]
    count = seq_len * 5 // 8
    spare = seq_len - count
    weights = tuple(
        item[0] for item in (norm_attn, w_query, w_key, w_value, w_out, norm_ffn, w_gate, w_up, w_down)
    )
    lens = lax.all_gather(lengths[:, 0], "dp", axis=1)

    source = jnp.where(first, inputs[:, 0], cotangent[:, 0])
    packed, slots = [], []
    for b in range(micro):
        seq, pos, own = slots_of(lens[b], count)
        slots.append((seq, pos))
        extra = lax.all_gather(source[b, count:], "dp", axis=0, tiled=True)
        wanted = seq[me] * spare + pos[me] - count
        chosen = jnp.logical_and(jnp.arange(groups * spare)[None, :] == wanted[:, None], ~own[me][:, None])
        brought = jnp.dot(chosen.astype(BF16), extra, preferred_element_type=F32).astype(BF16)
        packed.append(jnp.where(own[me][:, None], source[b, :count], brought))

    def spots_of(b):
        seq, pos = slots[b]
        same = seq[me][:, None] == seq.reshape(-1)[None, :]
        allowed = jnp.logical_and(same, pos.reshape(-1)[None, :] <= pos[me][:, None])
        return rope_tables(pos[me]) + (allowed,)

    spots = [spots_of(b) for b in range(micro)]

    def spots_at(tick):
        early, late = spots[min(tick, micro - 1)], spots[max(tick - 1, 0)]
        return tuple(jnp.where(first, a, b) for a, b in zip(early, late))

    empty = jnp.zeros((count, width), BF16)
    arriving = empty
    results, saved = [], []
    for tick in range(micro + 1):
        stream = jnp.where(first, packed[tick] if tick < micro else empty, arriving)
        result, arriving, kept = forward(stream, spots_at(tick), weights, 0)
        results.append(result)
        saved.append(kept)
    arriving = empty
    grads_in, totals = [], None
    for tick in range(micro + 1):
        incoming = jnp.where(first, arriving, packed[micro - 1 - tick] if tick < micro else empty)
        d_stream, arriving, grads = backward(incoming, saved[micro - tick], spots_at(micro - tick), weights, 2)
        grads_in.append(d_stream)
        totals = grads if totals is None else tuple(a + b for a, b in zip(totals, grads))

    def scattered(value, dim):
        return lax.psum_scatter(value.astype(BF16), "dp", scatter_dimension=dim, tiled=True).astype(F32)

    gains = lax.psum(jnp.stack([totals[0], totals[5]]), ("tensor", "dp"))
    part = width // groups
    gains = lax.dynamic_slice_in_dim(gains, me * part, part, axis=1)
    final = (
        gains[0],
        scattered(totals[1], 0),
        scattered(totals[2], 0),
        scattered(totals[3], 0),
        scattered(totals[4], 1),
        gains[1],
        scattered(totals[6], 0),
        scattered(totals[7], 0),
        scattered(totals[8], 1),
    )

    def unpack(rows, b, through):
        seq, pos = slots[b]
        everything = lax.all_gather(rows, "dp", axis=0, tiled=True)
        wanted = count + jnp.arange(spare)
        chosen = jnp.logical_and(seq.reshape(-1)[None, :] == me, pos.reshape(-1)[None, :] == wanted[:, None])
        back = jnp.dot(chosen.astype(BF16), everything, preferred_element_type=F32).astype(BF16)
        live = (jnp.arange(seq_len) < lens[b, me])[:, None]
        return jnp.where(live, jnp.concatenate([rows, back], axis=0), through)

    acts = jnp.stack(
        [unpack(jnp.where(first, results[b], results[b + 1]), b, inputs[b, 0]) for b in range(micro)]
    )
    back = jnp.stack(
        [
            unpack(jnp.where(first, grads_in[micro - b], grads_in[micro - 1 - b]), b, cotangent[b, 0])
            for b in range(micro)
        ]
    )
    return (acts[None, :, None], back[None, :, None]) + tuple(item[None] for item in final)


def solution(mesh):
    placed = (
        P(None, "dp", None, None),
        P(None, "dp", None, None),
        P(None, "dp"),
        P("section", None),
        P("section", None, "tensor"),
        P("section", None, "tensor"),
        P("section", None, "tensor"),
        P("section", "tensor", None),
        P("section", None),
        P("section", None, "tensor"),
        P("section", None, "tensor"),
        P("section", "tensor", None),
    )
    return jax.shard_map(
        on_device,
        mesh=mesh,
        in_specs=placed,
        out_specs=(
            P("section", None, "dp", None, None),
            P("section", None, "dp", None, None),
            P("section", "dp"),
            P("section", "dp", "tensor"),
            P("section", "dp", "tensor"),
            P("section", "dp", "tensor"),
            P("section", "tensor", "dp"),
            P("section", "dp"),
            P("section", "dp", "tensor"),
            P("section", "dp", "tensor"),
            P("section", "tensor", "dp"),
        ),
        check_vma=False,
    )
```

```python
import functools

import jax
import jax.numpy as jnp
from jax import lax
from jax.experimental import pallas as pl
from jax.experimental.pallas import tpu as pltpu
from jax.sharding import PartitionSpec as P

HD = 96

epsilon = 1e-05
rope_base = 100000.0
negative = -1e30
MESH = pl.DeviceIdType.MESH
F32 = jnp.float32
BF16 = jnp.bfloat16


def remote(src, dst, s_sem, r_sem, where):
    return pltpu.make_async_remote_copy(
        src_ref=src, dst_ref=dst, send_sem=s_sem, recv_sem=r_sem, device_id=where, device_id_type=MESH
    )


def greet(where):
    pl.semaphore_signal(pltpu.get_barrier_semaphore(), inc=1, device_id=where, device_id_type=MESH)


def dp_bits(groups):
    return groups.bit_length() - 1


def dp_partner(level):
    me = lax.axis_index("dp")
    bit = lax.rem(me // (1 << level), 2)
    return {"dp": me + (1 - 2 * bit) * (1 << level)}, bit


class Scatter:
    def __init__(self, groups, rows, chunks, refs):
        self.levels = dp_bits(groups)
        self.groups, self.rows, self.chunks, self.size = groups, rows, chunks, rows // chunks
        self.value, self.out = refs[0], refs[1]
        m = self.levels
        self.arrive = refs[2 : 2 + m]
        self.held = refs[2 + m : 1 + 2 * m]
        self.s_sem = refs[1 + 2 * m : 1 + 3 * m]
        self.r_sem = refs[1 + 3 * m : 1 + 4 * m]
        self.links = [dp_partner(k) for k in range(m)]

    @staticmethod
    def scratch(groups, rows, width, chunks, dtype):
        m = dp_bits(groups)
        sizes = [groups >> (k + 1) for k in range(m)]
        return (
            [pltpu.VMEM((size * rows, width), dtype) for size in sizes]
            + [pltpu.VMEM((size * rows, width), dtype) for size in sizes[:-1]]
            + [pltpu.SemaphoreType.DMA((size, chunks)) for size in sizes] * 2
        )

    def at(self, block, c):
        return pl.ds(pl.multiple_of(block * self.rows + c * self.size, self.size), self.size)

    def copy(self, level, slot, c):
        where, bit = self.links[level]
        source = self.value if level == 0 else self.held[level - 1]
        return remote(
            source.at[self.at(2 * slot + 1 - bit, c)],
            self.arrive[level].at[self.at(slot, c)],
            self.s_sem[level].at[slot, c],
            self.r_sem[level].at[slot, c],
            where,
        )

    def order(self, level):
        count = self.groups >> (level + 1)
        if count == 1:
            return [(0, False)]
        bit = self.links[level + 1][1]
        return [(2 * i + 1 - bit, True) for i in range(count // 2)] + [(2 * i + bit, False) for i in range(count // 2)]

    def start(self):
        def one(c, carry):
            for slot, _ in self.order(0):
                self.copy(0, slot, c).start()
            return carry

        lax.fori_loop(0, self.chunks, one, 0)

    def step(self, i, lag):
        for level in range(self.levels):
            c = i - level * lag

            @pl.when(jnp.logical_and(c >= 0, c < self.chunks))
            def _():
                bit = self.links[level][1]
                source = self.value if level == 0 else self.held[level - 1]
                for slot, goes in self.order(level):
                    self.copy(level, slot, c).wait_recv()
                    here = self.at(slot, c)
                    total = source[self.at(2 * slot + bit, c)].astype(F32) + self.arrive[level][here].astype(F32)
                    if level == self.levels - 1:
                        self.out[here] = total.astype(self.out.dtype)
                    else:
                        self.held[level][here] = total.astype(self.held[level].dtype)
                        if goes:
                            self.copy(level + 1, slot // 2, c).start()

    def steps(self, lag):
        return self.chunks + (self.levels - 1) * lag

    def finish(self):
        def one(c, carry):
            for level in range(self.levels):
                for slot in range(self.groups >> (level + 1)):
                    self.copy(level, slot, c).wait_send()
            return carry

        lax.fori_loop(0, self.chunks, one, 0)


def return_kernel(groups, rows, chunks, plans, *refs):
    refs = list(refs)

    def take(count):
        taken = refs[:count]
        del refs[:count]
        return taken

    m = dp_bits(groups)
    count = 4 * m - 1
    value, gains = take(2)
    grads = take(len(plans))
    out, gains_out = take(2)
    totals = take(len(plans))
    gains_all, gains_sum, g_s, g_r = take(4)
    task = Scatter(groups, rows, chunks, [value, out] + take(count))
    small = Scatter(groups, 8, 1, [gains_sum, gains_out] + take(count))
    large = [
        Scatter(groups, block, parts, [grad, total] + take(count))
        for (block, parts), grad, total in zip(plans, grads, totals)
    ]
    t = lax.axis_index("tensor")
    for where, _ in task.links:
        greet(where)
    for k in range(1, 4):
        greet({"tensor": lax.rem(t + k, 4)})
    pl.semaphore_wait(pltpu.get_barrier_semaphore(), m + 3)

    def spread(k):
        return remote(gains, gains_all.at[k - 1], g_s.at[k - 1], g_r.at[k - 1], {"tensor": lax.rem(t + k, 4)})

    for k in range(1, 4):
        spread(k).start()
    task.start()
    for item in large:
        item.start()
    for k in range(1, 4):
        spread(k).wait()
    gains_sum[...] = gains[...] + gains_all[0] + gains_all[1] + gains_all[2]
    small.start()

    def body(i, c):
        small.step(i, 1)
        task.step(i, 2)
        for item in large:
            item.step(i, 4)
        return c

    lax.fori_loop(0, max([task.steps(2), small.steps(1)] + [item.steps(4) for item in large]), body, 0)
    small.finish()
    task.finish()
    for item in large:
        item.finish()


def return_rows(value, gains, grads, groups, cid, chunks):
    rows, width = value.shape[0] // groups, value.shape[1]
    vmem = pl.BlockSpec(memory_space=pltpu.VMEM)
    part = gains.shape[1]
    plans, outs = [], [jax.ShapeDtypeStruct((rows, width), BF16), jax.ShapeDtypeStruct((8, part), F32)]
    scratch = [
        pltpu.VMEM((3,) + gains.shape, F32),
        pltpu.VMEM(gains.shape, F32),
        pltpu.SemaphoreType.DMA((3,)),
        pltpu.SemaphoreType.DMA((3,)),
    ]
    scratch += Scatter.scratch(groups, rows, width, chunks, BF16) + Scatter.scratch(groups, 8, part, 1, F32)
    for grad in grads:
        block = grad.shape[0] // groups
        plans.append((block, max(1, block // 48)))
        outs.append(jax.ShapeDtypeStruct((block, grad.shape[1]), F32))
        scratch += Scatter.scratch(groups, block, grad.shape[1], plans[-1][1], BF16)
    return pl.pallas_call(
        functools.partial(return_kernel, groups, rows, chunks, plans),
        out_shape=outs,
        in_specs=[vmem] * (2 + len(grads)),
        out_specs=[vmem] * len(outs),
        scratch_shapes=scratch,
        compiler_params=pltpu.CompilerParams(
            collective_id=cid, has_side_effects=True, vmem_limit_bytes=VMEM_LIMIT
        ),
        name="return_%d" % cid,
    )(value, gains, *grads)


def gather_kernel(groups, count, *refs):
    values, outs = refs[:count], refs[count : 2 * count]
    s_sem, r_sem, own = refs[2 * count :]
    m = dp_bits(groups)
    me = lax.axis_index("dp")
    links = [dp_partner(k) for k in range(m)]
    for where, _ in links:
        greet(where)
    pl.semaphore_wait(pltpu.get_barrier_semaphore(), m)

    def place(a, block):
        rows = values[a].shape[0]
        return outs[a].at[pl.ds(pl.multiple_of(block * rows, rows), rows)]

    def copy(a, level, i, mine):
        where, bit = links[level]
        low = lax.rem(me, 1 << (level + 1))
        if not mine:
            low = low + (1 - 2 * bit) * (1 << level)
        block = i * (1 << (level + 1)) + low
        return remote(place(a, block), place(a, block), s_sem.at[a, level, i], r_sem.at[a, level, i], where)

    locals_ = [pltpu.make_async_copy(values[a], place(a, me), own.at[a]) for a in range(count)]
    for item in locals_:
        item.start()
    for item in locals_:
        item.wait()
    for level in reversed(range(m)):
        for i in range(groups >> (level + 1)):
            for a in range(count):
                copy(a, level, i, True).start()
        for i in range(groups >> (level + 1)):
            for a in range(count):
                copy(a, level, i, False).wait_recv()
    for level in range(m):
        for i in range(groups >> (level + 1)):
            for a in range(count):
                copy(a, level, i, True).wait_send()


def gather_rows(values, groups, cid):
    vmem = pl.BlockSpec(memory_space=pltpu.VMEM)
    m, count = dp_bits(groups), len(values)
    dma = pltpu.SemaphoreType.DMA
    return pl.pallas_call(
        functools.partial(gather_kernel, groups, count),
        out_shape=[jax.ShapeDtypeStruct((groups * v.shape[0], v.shape[1]), v.dtype) for v in values],
        in_specs=[vmem] * count,
        out_specs=[vmem] * count,
        scratch_shapes=[dma((count, m, groups // 2)), dma((count, m, groups // 2)), dma((count,))],
        compiler_params=pltpu.CompilerParams(
            collective_id=cid, has_side_effects=True, vmem_limit_bytes=48 * 2**20
        ),
        name="gather_%d" % cid,
    )(*values)


class Line:
    lag_b, lag_c, lag_o = 2, 4, 6

    def __init__(self, first, half, pieces, part, base, out, scratch, norm=None, moved=None):
        self.first, self.half, self.pieces, self.size = first, half, pieces, half // pieces
        self.part, self.base, self.out = part, base, out
        (self.rin, self.smid, self.rmid) = scratch[:3]
        (self.s_up, self.r_up, self.s_mid, self.r_mid, self.s_b1, self.s_b2, self.r_b, self.s_c, self.r_c) = scratch[3:12]
        self.norm, self.moved = norm, moved
        if moved:
            self.arrived, self.shift = moved
            self.s_s, self.r_s = scratch[12:14]
            section = lax.axis_index("section")
            self.sends = section == (0 if self.shift > 0 else 1)
            self.partner = {"section": 1 - section}
        t = lax.axis_index("tensor")
        self.mid = jnp.logical_or(t == 1, t == 2)
        self.outside = jnp.logical_not(self.mid)
        self.outer = {"tensor": jnp.where(t == 1, 0, 3)}
        self.other = {"tensor": jnp.where(t == 1, 2, 1)}
        self.nbr = {"tensor": jnp.where(t == 0, 1, 2)}
        self.near = jnp.where(t < 2, 0, half)
        self.far = half - self.near

    @staticmethod
    def scratch(half, pieces, width, moved):
        dma = pltpu.SemaphoreType.DMA
        kinds = [
            pltpu.VMEM((2 * half, width), BF16),
            pltpu.VMEM((half, width), BF16),
            pltpu.VMEM((half, width), BF16),
            dma((2, pieces)),
            dma((2, pieces)),
        ] + [dma((pieces,))] * 7
        return kinds + ([dma((2, pieces))] * 2 if moved else [])

    @staticmethod
    def greet():
        t = lax.axis_index("tensor")

        @pl.when(t > 0)
        def _():
            greet({"tensor": jnp.maximum(t - 1, 0)})

        @pl.when(t < 3)
        def _():
            greet({"tensor": jnp.minimum(t + 1, 3)})

    def greet_sender(self):
        if self.moved:

            @pl.when(jnp.logical_not(self.sends))
            def _():
                greet(self.partner)

    def enter(self, others):
        bar = pltpu.get_barrier_semaphore()
        count = jnp.where(self.mid, 2, 1) + others
        if self.moved:
            count = count + jnp.where(self.sends, 1, 0)
        pl.semaphore_wait(bar, count)

    def local(self, start, p):
        return pl.ds(pl.multiple_of(start + p * self.size, self.size), self.size)

    def rows(self, start, p):
        return pl.ds(pl.multiple_of(self.first + start + p * self.size, self.size), self.size)

    def shifted(self, start, p):
        side = start // self.half
        here = self.rows(start, p)
        return remote(self.out.at[here], self.arrived.at[here], self.s_s.at[side, p], self.r_s.at[side, p], self.partner)

    def pass_on(self, start, p):
        if self.moved:

            @pl.when(self.sends)
            def _():
                self.shifted(start, p).start()

    def outcome(self, s_sem, r_sem, where, start, p):
        here = self.rows(start, p)
        return remote(self.out.at[here], self.out.at[here], s_sem.at[p], r_sem.at[p], where)

    def up(self, start, p, k, where):
        return remote(
            self.part.at[self.rows(start, p)], self.rin.at[self.local(start, p)], self.s_up.at[k, p], self.r_up.at[k, p], where
        )

    def cross(self, p):
        return remote(
            self.smid.at[self.local(0, p)], self.rmid.at[self.local(0, p)], self.s_mid.at[p], self.r_mid.at[p], self.other
        )

    def start(self):
        @pl.when(self.outside)
        def _():
            def begin(p, c):
                self.up(self.far, p, 0, self.nbr).start()
                self.up(self.near, p, 1, self.nbr).start()
                return c

            lax.fori_loop(0, self.pieces, begin, 0)

    def outer_step(self, i):
        p = i - self.lag_o

        @pl.when(jnp.logical_and(p >= 0, p < self.pieces))
        def _():
            self.outcome(self.s_b2, self.r_b, self.nbr, self.near, p).wait_recv()
            self.pass_on(self.near, p)
            self.outcome(self.s_c, self.r_c, self.nbr, self.far, p).wait_recv()
            self.pass_on(self.far, p)

    def mid_step(self, i):
        @pl.when(jnp.logical_and(i >= 0, i < self.pieces))
        def _():
            self.up(self.far, i, 0, self.outer).wait_recv()
            total = self.part[self.rows(self.far, i)].astype(F32) + self.rin[self.local(self.far, i)].astype(F32)
            self.smid[self.local(0, i)] = total.astype(BF16)
            self.cross(i).start()

        j = i - self.lag_b

        @pl.when(jnp.logical_and(j >= 0, j < self.pieces))
        def _():
            self.up(self.near, j, 1, self.outer).wait_recv()
            self.cross(j).wait_recv()
            here = self.rows(self.near, j)
            total = self.part[here].astype(F32) + self.rin[self.local(self.near, j)].astype(F32)
            total = total + self.rmid[self.local(0, j)].astype(F32)
            if self.norm:
                xrow, gain, gsum = self.norm
                x = xrow[here].astype(F32)
                scale = lax.rsqrt(jnp.mean(x * x, axis=-1, keepdims=True) + epsilon)
                unit = x * scale
                gsum[...] += jnp.sum(total * unit, axis=0, keepdims=True)
                inner = total * gain[...]
                total = scale * (inner - unit * jnp.mean(inner * unit, axis=-1, keepdims=True))
            self.out[here] = (self.base[here].astype(F32) + total).astype(BF16)
            self.outcome(self.s_b1, self.r_b, self.other, self.near, j).start()
            self.outcome(self.s_b2, self.r_b, self.outer, self.near, j).start()
            self.pass_on(self.near, j)

        k = i - self.lag_c

        @pl.when(jnp.logical_and(k >= 0, k < self.pieces))
        def _():
            self.outcome(self.s_b1, self.r_b, self.other, self.far, k).wait_recv()
            self.outcome(self.s_c, self.r_c, self.outer, self.far, k).start()
            self.pass_on(self.far, k)

    @property
    def steps(self):
        return self.pieces + self.lag_o

    def step(self, i):
        @pl.when(self.mid)
        def _():
            self.mid_step(i)

        @pl.when(self.outside)
        def _():
            self.outer_step(i)

    def finish(self):
        @pl.when(self.mid)
        def _():
            def one(p, c):
                self.cross(p).wait_send()
                self.outcome(self.s_b1, self.r_b, self.other, self.near, p).wait_send()
                self.outcome(self.s_b2, self.r_b, self.outer, self.near, p).wait_send()
                self.outcome(self.s_c, self.r_c, self.outer, self.far, p).wait_send()
                return c

            lax.fori_loop(0, self.pieces, one, 0)

        @pl.when(self.outside)
        def _():
            def one(p, c):
                self.up(self.far, p, 0, self.nbr).wait_send()
                self.up(self.near, p, 1, self.nbr).wait_send()
                return c

            lax.fori_loop(0, self.pieces, one, 0)

        if self.moved:

            def close(p, c):
                @pl.when(self.sends)
                def _():
                    self.shifted(0, p).wait_send()
                    self.shifted(self.half, p).wait_send()

                @pl.when(jnp.logical_not(self.sends))
                def _():
                    self.shifted(0, p).wait_recv()
                    self.shifted(self.half, p).wait_recv()

                return c

            lax.fori_loop(0, self.pieces, close, 0)


def run_steps(begin, end, *planned):
    def body(i, c):
        for step, offset in planned:
            step(i - offset)
        return c

    lax.fori_loop(begin, end, body, 0)


class Gather:
    def __init__(self, groups, rows, out, s_sem, r_sem):
        self.groups, self.rows, self.out, self.s_sem, self.r_sem = groups, rows, out, s_sem, r_sem
        self.levels = dp_bits(groups)
        self.links = [dp_partner(k) for k in range(self.levels)]
        self.me = lax.axis_index("dp")

    @staticmethod
    def scratch(groups):
        return [pltpu.SemaphoreType.DMA((dp_bits(groups), groups // 2))] * 2

    def copy(self, level, i, mine):
        where, bit = self.links[level]
        low = lax.rem(self.me, 1 << (level + 1))
        if not mine:
            low = low + (1 - 2 * bit) * (1 << level)
        block = i * (1 << (level + 1)) + low
        place = self.out.at[pl.ds(pl.multiple_of(block * self.rows, self.rows), self.rows)]
        return remote(place, place, self.s_sem.at[level, i], self.r_sem.at[level, i], where)

    def start(self, level):
        for i in range(self.groups >> (level + 1)):
            self.copy(level, i, True).start()

    def arrive(self, level):
        for i in range(self.groups >> (level + 1)):
            self.copy(level, i, False).wait_recv()

    def finish(self):
        for level in range(self.levels):
            for i in range(self.groups >> (level + 1)):
                self.copy(level, i, True).wait_send()


def with_transpose(left, right):
    return lax.dot_general(left, right, (((1,), (1,)), ((), ())), preferred_element_type=F32)


def rows_contract(left, right):
    return lax.dot_general(left, right, (((0,), (0,)), ((), ())), preferred_element_type=F32)


def times(left, right):
    return jnp.dot(left, right, preferred_element_type=F32)


LANES = 128
TILE = 256


def lanes(i, size=LANES):
    return pl.ds(pl.multiple_of(i * size, size), size)


def normalize(rows, gain):
    rows = rows.astype(F32)
    scale = lax.rsqrt(jnp.mean(rows * rows, axis=-1, keepdims=True) + epsilon)
    return (rows * scale * gain).astype(BF16)


def normalize_into(target, source, gain, first, count, block=32):
    def one(i, c):
        here = pl.ds(pl.multiple_of(first + i * block, block), block)
        target[here] = normalize(source[here], gain[...])
        return c

    lax.fori_loop(0, count // block, one, 0)


def rolled(value, cosine, sine):
    return value * cosine + pltpu.roll(value, LANES // 2, 1) * sine


def block_rows(keys):
    for rows in (160, 80, 32):
        if rows * keys <= 160 * 1280:
            return rows
    return 16


def score_rows(q, kv, h, g, here, qcode, qstart, kcode):
    scores = with_transpose(q[here, lanes(h)], kv[:, lanes(g)]) * HD ** (-0.5)
    code = kcode[...]
    return scores, jnp.logical_and(code <= qcode[here], code >= qstart[here])


def load_all(pairs, sems):
    copies = [pltpu.make_async_copy(src, dst, sems.at[i]) for i, (src, dst) in enumerate(pairs)]
    for item in copies:
        item.start()
    return copies


def forward_kernel(groups, q_heads, k_heads, pieces, *refs):
    refs = list(refs)

    def take(count):
        taken = refs[:count]
        del refs[:count]
        return taken

    x, cosine, sine, qcode, qstart, kcode, gain_one, gain_two = take(8)
    far_weights = take(5)
    q, kv, lse, mixed, resid, gate, up, act, y, arrived = take(10)
    near_weights = take(5)
    wqkv, wout, wgate, wup, wdown = near_weights
    part_one, part_two, n1, n2, w_sem = take(5)
    gather = Gather(groups, x.shape[0], kv, *take(2))
    count, width = x.shape
    quarter = count // 4
    lines = []
    for k in range(4):
        first = (k % 2) * 2 * quarter
        source = (part_one, x, resid) if k < 2 else (part_two, resid, y)
        lines.append(
            Line(first, quarter, pieces, *source, take(12 if k < 2 else 14), moved=None if k < 2 else (arrived, 1))
        )
    one_a, one_b, two_a, two_b = lines

    loads = load_all(list(zip(far_weights, near_weights)), w_sem)
    Line.greet()
    two_a.greet_sender()
    for where, _ in gather.links:
        greet(where)
    normalize_into(n1, x, gain_one, 0, count)
    loads[0].wait()

    mine = pl.ds(pl.multiple_of(lax.axis_index("dp") * count, count), count)
    for g in range(k_heads):
        column = (q_heads + g) * LANES
        value = times(n1[...], wqkv[:, column : column + LANES])
        kv[mine, g * LANES : (g + 1) * LANES] = rolled(value, cosine[...], sine[...]).astype(BF16)
        column += k_heads * LANES
        kv[mine, (k_heads + g) * LANES : (k_heads + g + 1) * LANES] = times(
            n1[...], wqkv[:, column : column + LANES]
        ).astype(BF16)

    two_a.enter(gather.levels)

    top = gather.levels - 1
    gather.start(top)

    def queries(h, c):
        value = times(n1[...], wqkv[:, lanes(h)])
        q[:, lanes(h)] = rolled(value, cosine[...], sine[...]).astype(BF16)
        return c

    lax.fori_loop(0, q_heads, queries, 0)
    for level in range(top, -1, -1):
        gather.arrive(level)
        if level:
            gather.start(level - 1)

    rows = block_rows(kv.shape[0])
    blocks = count // rows

    def attend(i, c):
        h, b = i // blocks, lax.rem(i, blocks)
        g = h // (q_heads // k_heads)
        here = pl.ds(pl.multiple_of(b * rows, rows), rows)
        scores, allowed = score_rows(q, kv, h, g, here, qcode, qstart, kcode)
        scores = jnp.where(allowed, scores, negative)
        row_max = jnp.max(scores, axis=-1, keepdims=True)
        expo = jnp.exp(scores - row_max)
        row_total = jnp.sum(expo, axis=-1, keepdims=True)
        prob = (expo / row_total).astype(BF16)
        mixed[here, lanes(h)] = times(prob, kv[:, lanes(k_heads + g)]).astype(BF16)
        there = pl.ds(pl.multiple_of(h * count + b * rows, rows), rows)
        lse[there] = jnp.broadcast_to(row_max + jnp.log(row_total), (rows, LANES))
        return c

    lax.fori_loop(0, q_heads * blocks, attend, 0)
    loads[1].wait()

    def projected(target, left, right, first, each=None):
        here = pl.ds(first, 2 * quarter)

        def one(i, c):
            target[here, lanes(i, TILE)] = times(left[here], right[:, lanes(i, TILE)]).astype(BF16)
            if each:
                each(i)
            return c

        lax.fori_loop(0, width // TILE, one, 0)

    projected(part_one, mixed, wout, 0)
    one_a.start()
    projected(part_one, mixed, wout, 2 * quarter)
    one_b.start()
    run_steps(0, one_a.steps, (one_a.step, 0), (one_b.step, pieces))
    loads[2].wait()
    loads[3].wait()
    loads[4].wait()

    def hidden(first, each):
        here = pl.ds(first, 2 * quarter)
        normalize_into(n2, resid, gain_two, first, 2 * quarter)

        def one(i, c):
            columns = lanes(i, TILE)
            gate_pre = times(n2[here], wgate[:, columns])
            up_pre = times(n2[here], wup[:, columns])
            gate[here, columns] = gate_pre.astype(BF16)
            up[here, columns] = up_pre.astype(BF16)
            act[here, columns] = (gate_pre * jax.nn.sigmoid(gate_pre) * up_pre).astype(BF16)
            each(i)
            return c

        lax.fori_loop(0, gate.shape[1] // TILE, one, 0)

    tiles = gate.shape[1] // TILE
    done = one_a.steps - pieces
    hidden(0, lambda i: one_b.step(done + i))
    projected(part_two, act, wdown, 0)
    two_a.start()
    run_steps(done + tiles, one_b.steps, (one_b.step, 0))
    hidden(2 * quarter, lambda i: two_a.step(i))
    projected(part_two, act, wdown, 2 * quarter)
    two_b.start()
    run_steps(tiles, two_b.steps + tiles, (two_a.step, 0), (two_b.step, tiles))
    gather.finish()
    for line in lines:
        line.finish()


VMEM_LIMIT = 58 * 2**20


def forward_tick(x, spots, weights, groups, q_heads, k_heads, cid):
    norm_one, wqkv, wout, norm_two, wgate, wup, wdown = weights
    count, width = x.shape
    hidden = wgate.shape[1]
    pieces = 5
    vmem = pl.BlockSpec(memory_space=pltpu.VMEM)
    far = pl.BlockSpec(memory_space=pl.ANY)

    def shape(*dims, dtype=BF16):
        return jax.ShapeDtypeStruct(dims, dtype)

    outs = [
        shape(count, q_heads * LANES),
        shape(groups * count, 2 * k_heads * LANES),
        shape(q_heads * count, LANES, dtype=F32),
        shape(count, q_heads * LANES),
        shape(count, width),
        shape(count, hidden),
        shape(count, hidden),
        shape(count, hidden),
        shape(count, width),
        shape(count, width),
    ]
    far_weights = [wqkv, wout, wgate, wup, wdown]
    scratch = [pltpu.VMEM(item.shape, BF16) for item in far_weights]
    scratch += [pltpu.VMEM((count, width), BF16)] * 4 + [pltpu.SemaphoreType.DMA((5,))]
    scratch += Gather.scratch(groups)
    for k in range(4):
        scratch += Line.scratch(count // 4, pieces, width, k >= 2)
    q, kv, lse, mixed, resid, gate, up, act, y, arrived = pl.pallas_call(
        functools.partial(forward_kernel, groups, q_heads, k_heads, pieces),
        out_shape=outs,
        in_specs=[vmem] * 8 + [far] * 5,
        out_specs=[vmem] * len(outs),
        scratch_shapes=scratch,
        compiler_params=pltpu.CompilerParams(
            collective_id=cid, has_side_effects=True, vmem_limit_bytes=VMEM_LIMIT
        ),
        name="forward_tick",
    )(x, *spots, norm_one[None], norm_two[None], *far_weights)
    return y, arrived, (x, q, kv, lse, mixed, resid, gate, up, act)


def back_ffn_kernel(pieces, *refs):
    dy, gate, up, resid, gain = refs[:5]
    far_weights = refs[5:8]
    dresid, gsum, dgate, dup = refs[8:12]
    wdown, wgate, wup = near_weights = refs[12:15]
    part, w_sem = refs[15:17]
    count, width = dy.shape
    quarter = count // 4
    a, b = [
        Line(k * 2 * quarter, quarter, pieces, part, dy, dresid, refs[17 + 12 * k : 29 + 12 * k], norm=(resid, gain, gsum))
        for k in range(2)
    ]
    loads = load_all(list(zip(far_weights, near_weights)), w_sem)
    Line.greet()
    gsum[...] = jnp.zeros_like(gsum)

    def hidden(first, each=None):
        here = pl.ds(first, 2 * quarter)

        def one(i, c):
            columns = lanes(i, TILE)
            d_act = with_transpose(dy[here], wdown[columns, :])
            gate_pre, up_pre = gate[here, columns].astype(F32), up[here, columns].astype(F32)
            sigma = jax.nn.sigmoid(gate_pre)
            d_silu = d_act * sigma
            dup[here, columns] = (d_silu * gate_pre).astype(BF16)
            dgate[here, columns] = (d_silu * up_pre * (1.0 + gate_pre * (1.0 - sigma))).astype(BF16)
            if each:
                each(i)
            return c

        lax.fori_loop(0, gate.shape[1] // TILE, one, 0)

    def back(first):
        here = pl.ds(first, 2 * quarter)

        def one(i, c):
            columns = lanes(i, TILE)
            total = with_transpose(dgate[here], wgate[columns, :]) + with_transpose(dup[here], wup[columns, :])
            part[here, columns] = total.astype(BF16)
            return c

        lax.fori_loop(0, width // TILE, one, 0)

    loads[0].wait()
    hidden(0)
    loads[1].wait()
    loads[2].wait()
    back(0)
    a.enter(0)
    a.start()
    tiles = gate.shape[1] // TILE
    hidden(2 * quarter, lambda i: a.step(i))
    back(2 * quarter)
    b.start()
    run_steps(tiles, b.steps + tiles, (a.step, 0), (b.step, tiles))
    a.finish()
    b.finish()


def back_ffn(dy, kept, weights, cid):
    norm_one, wqkv, wout, norm_two, wgate, wup, wdown = weights
    x, q, kv, lse, mixed, resid, gate, up, act = kept
    count, width = dy.shape
    pieces = 5
    vmem = pl.BlockSpec(memory_space=pltpu.VMEM)
    far = pl.BlockSpec(memory_space=pl.ANY)
    far_weights = [wdown, wgate, wup]
    scratch = [pltpu.VMEM(item.shape, BF16) for item in far_weights]
    scratch += [pltpu.VMEM((count, width), BF16), pltpu.SemaphoreType.DMA((3,))]
    scratch += Line.scratch(count // 4, pieces, width, False) * 2
    return pl.pallas_call(
        functools.partial(back_ffn_kernel, pieces),
        out_shape=[
            jax.ShapeDtypeStruct((count, width), BF16),
            jax.ShapeDtypeStruct((1, width), F32),
            jax.ShapeDtypeStruct(gate.shape, BF16),
            jax.ShapeDtypeStruct(gate.shape, BF16),
        ],
        in_specs=[vmem] * 5 + [far] * 3,
        out_specs=[vmem] * 4,
        scratch_shapes=scratch,
        compiler_params=pltpu.CompilerParams(
            collective_id=cid, has_side_effects=True, vmem_limit_bytes=VMEM_LIMIT
        ),
        name="back_ffn",
    )(dy, gate, up, resid, norm_two[None], *far_weights)


def back_attn_kernel(groups, q_heads, k_heads, pieces, shift, plans, *refs):
    refs = list(refs)

    def take(count):
        taken = refs[:count]
        del refs[:count]
        return taken

    dresid, x, q, kv, lse, cosine, sine, qcode, qstart, kcode, gain = take(11)
    far_weights = take(2)
    values = take(len(plans))
    dx, gsum, dqkv = take(3)
    (arrived,) = take(1) if shift else (None,)
    totals = take(len(plans))
    wout, wqkv = near_weights = take(2)
    part, dmixed, dkv, w_sem = take(4)
    levels = dp_bits(groups)
    count, width = x.shape
    quarter = count // 4
    keys = kv.shape[0]
    shares, owns, scatters = [], [], []
    for g in range(k_heads):
        share, own = take(2)
        shares.append(share)
        owns.append(own)
        scatters.append(Scatter(groups, count, 5, [share, own] + take(4 * levels - 1)))
    tasks = [
        Scatter(groups, rows, chunks, [value, total] + take(4 * levels - 1))
        for (rows, chunks), value, total in zip(plans, values, totals)
    ]
    moved = (arrived, shift) if shift else None
    a, b = [
        Line(
            k * 2 * quarter,
            quarter,
            pieces,
            part,
            dresid,
            dx,
            take(14 if shift else 12),
            norm=(x, gain, gsum),
            moved=moved,
        )
        for k in range(2)
    ]
    loads = load_all(list(zip(far_weights, near_weights)), w_sem)
    Line.greet()
    for where, _ in scatters[0].links:
        greet(where)
    a.greet_sender()
    gsum[...] = jnp.zeros_like(gsum)
    dkv[...] = jnp.zeros_like(dkv)
    a.enter(levels)
    for task in tasks:
        task.start()
    loads[0].wait()

    def mix(h, c):
        dmixed[:, lanes(h)] = with_transpose(dresid[...], wout[lanes(h), :]).astype(BF16)
        return c

    lax.fori_loop(0, q_heads, mix, 0)
    rows = block_rows(keys)
    blocks = count // rows
    repeat = q_heads // k_heads
    lag = 4
    scale = HD ** (-0.5)

    for g in range(k_heads):

        def one(i, c):
            h, n = g * repeat + i // blocks, lax.rem(i, blocks)
            here = pl.ds(pl.multiple_of(n * rows, rows), rows)
            there = pl.ds(pl.multiple_of(h * count + n * rows, rows), rows)
            scores, allowed = score_rows(q, kv, h, g, here, qcode, qstart, kcode)
            prob = jnp.where(allowed, jnp.exp(scores - lse[there][:, :1]), 0.0)
            dm = dmixed[here, lanes(h)]
            d_prob = with_transpose(dm, kv[:, lanes(k_heads + g)])
            row_dot = jnp.sum(prob * d_prob, axis=-1, keepdims=True)
            d_scores = (prob * (d_prob - row_dot)).astype(BF16)
            d_query = times(d_scores, kv[:, lanes(g)]) * scale
            dqkv[here, lanes(h)] = rolled(d_query, cosine[here], -sine[here]).astype(BF16)
            dkv[:, lanes(g)] += rows_contract(d_scores, q[here, lanes(h)]) * scale
            dkv[:, lanes(k_heads + g)] += rows_contract(prob.astype(BF16), dm)
            for task in tasks:
                task.step(g * repeat * blocks + i, lag)
            return c

        lax.fori_loop(0, repeat * blocks, one, 0)

        def narrow(i, c):
            here = pl.ds(pl.multiple_of(i * LANES, LANES), LANES)
            shares[g][here, :LANES] = dkv[here, lanes(g)].astype(BF16)
            shares[g][here, LANES:] = dkv[here, lanes(k_heads + g)].astype(BF16)
            return c

        lax.fori_loop(0, keys // LANES, narrow, 0)
        scatters[g].start()
    run_steps(0, scatters[0].steps(1), *[(functools.partial(lambda s, i: s.step(i, 1), s), 0) for s in scatters])
    for g in range(k_heads):
        dqkv[:, lanes(q_heads + g)] = rolled(owns[g][:, :LANES], cosine[...], -sine[...]).astype(BF16)
        dqkv[:, lanes(q_heads + k_heads + g)] = owns[g][:, LANES:].astype(BF16)
    loads[1].wait()

    def back(first, each=None):
        here = pl.ds(first, 2 * quarter)

        def one(i, c):
            columns = lanes(i, TILE)
            part[here, columns] = with_transpose(dqkv[here], wqkv[columns, :]).astype(BF16)
            if each:
                each(i)
            return c

        lax.fori_loop(0, width // TILE, one, 0)

    back(0)
    a.start()
    back(2 * quarter)
    b.start()
    begun = q_heads * blocks
    more = [(functools.partial(lambda s, i: s.step(i + begun, lag), s), 0) for s in tasks]
    last = max([b.steps + pieces] + [s.steps(lag) - begun for s in tasks])
    run_steps(0, last, (a.step, 0), (b.step, pieces), *more)
    a.finish()
    b.finish()
    for item in scatters + tasks:
        item.finish()


def back_attn(dresid, kept, spots, weights, groups, q_heads, k_heads, cid, shift, sums=()):
    norm_one, wqkv, wout, norm_two, wgate, wup, wdown = weights
    x, q, kv, lse, mixed, resid, gate, up, act = kept
    count, width = x.shape
    keys = kv.shape[0]
    pieces = 5
    vmem = pl.BlockSpec(memory_space=pltpu.VMEM)
    far = pl.BlockSpec(memory_space=pl.ANY)
    outs = [
        jax.ShapeDtypeStruct((count, width), BF16),
        jax.ShapeDtypeStruct((1, width), F32),
        jax.ShapeDtypeStruct((count, wqkv.shape[1]), BF16),
    ]
    if shift:
        outs.append(jax.ShapeDtypeStruct((count, width), BF16))
    scratch = [
        pltpu.VMEM(wout.shape, BF16),
        pltpu.VMEM(wqkv.shape, BF16),
        pltpu.VMEM((count, width), BF16),
        pltpu.VMEM(q.shape, BF16),
        pltpu.VMEM(kv.shape, F32),
        pltpu.SemaphoreType.DMA((2,)),
    ]
    for _ in range(k_heads):
        scratch += [pltpu.VMEM((keys, 2 * LANES), BF16), pltpu.VMEM((count, 2 * LANES), F32)]
        scratch += Scatter.scratch(groups, count, 2 * LANES, 5, BF16)
    plans = []
    for value in sums:
        rows = value.shape[0] // groups
        parts = max(1, min(8, rows // 16))
        while rows % (parts * 16):
            parts -= 1
        plans.append((rows, parts))
        outs.append(jax.ShapeDtypeStruct((rows, value.shape[1]), F32))
        scratch += Scatter.scratch(groups, rows, value.shape[1], parts, BF16)
    scratch += Line.scratch(count // 4, pieces, width, bool(shift)) * 2
    return pl.pallas_call(
        functools.partial(back_attn_kernel, groups, q_heads, k_heads, pieces, shift, plans),
        out_shape=outs,
        in_specs=[vmem] * 11 + [far] * 2 + [vmem] * len(sums),
        out_specs=[vmem] * len(outs),
        scratch_shapes=scratch,
        compiler_params=pltpu.CompilerParams(
            collective_id=cid, has_side_effects=True, vmem_limit_bytes=VMEM_LIMIT
        ),
        name="back_attn_%d" % cid,
    )(dresid, x, q, kv, lse, *spots, norm_one[None], wout, wqkv, *sums)


def rope_tables(pos):
    half_width = HD // 2
    inverse = rope_base ** (-(jnp.arange(half_width, dtype=F32) * 2.0 / HD))
    angle = pos.astype(F32)[:, None] * inverse[None, :]
    blank = jnp.zeros((pos.shape[0], LANES // 2 - half_width), F32)
    cosine, sine = jnp.cos(angle), jnp.sin(angle)
    return (
        jnp.concatenate([cosine, blank, cosine, blank], axis=1),
        jnp.concatenate([-sine, blank, sine, blank], axis=1),
    )


def spreader(heads, turned):
    feature = jnp.arange(HD)
    place = jnp.where(feature < HD // 2, feature, feature - HD // 2 + LANES // 2) if turned else feature
    lane = (jnp.arange(heads)[:, None] * LANES + place[None, :]).reshape(-1)
    return (lane[:, None] == jnp.arange(heads * LANES)[None, :]).astype(BF16)


def slots_of(lens, count):
    groups = lens.shape[0]
    kept = jnp.minimum(lens, count)
    free, extra = count - kept, lens - kept
    free_off = jnp.cumsum(free) - free
    extra_end = jnp.cumsum(extra)
    slot = jnp.arange(count)
    own = slot[None, :] < kept[:, None]
    index = free_off[:, None] + slot[None, :] - kept[:, None]
    source = jnp.sum(index[:, :, None] >= extra_end[None, None, :], axis=-1)
    begins = jnp.sum(jnp.where(index[:, :, None] >= extra_end[None, None, :], extra[None, None, :], 0), axis=-1)
    seq = jnp.where(own, jnp.arange(groups)[:, None], source)
    pos = jnp.where(own, slot[None, :], count + index - begins)
    return seq, pos, own


def on_device(
    inputs,
    cotangent,
    lengths,
    norm_attn,
    w_query,
    w_key,
    w_value,
    w_out,
    norm_ffn,
    w_gate,
    w_up,
    w_down,
):
    first = lax.axis_index("section") == 0
    me = lax.axis_index("dp")
    groups = lax.axis_size("dp")
    micro, seq_len, width = inputs.shape[0], inputs.shape[2], inputs.shape[3]
    count = seq_len * 5 // 8
    spare = seq_len - count
    q_heads, k_heads = w_query.shape[2] // HD, w_key.shape[2] // HD
    spread_q, spread_k = spreader(q_heads, True), spreader(k_heads, True)
    spread_v, spread_o = spreader(k_heads, False), spreader(q_heads, False)
    wqkv = jnp.concatenate(
        [times(w_query[0], spread_q), times(w_key[0], spread_k), times(w_value[0], spread_v)], axis=1
    ).astype(BF16)
    wout = rows_contract(spread_o, w_out[0]).astype(BF16)
    weights = (norm_attn[0], wqkv, wout, norm_ffn[0], w_gate[0], w_up[0], w_down[0])

    source = jnp.where(first, inputs[:, 0], cotangent[:, 0])
    length_rows = jnp.broadcast_to(lengths[:, 0].astype(F32)[:, None], (micro, 128))
    length_rows = jnp.concatenate([length_rows, jnp.zeros((8 - micro, 128), F32)], axis=0)
    first_extra, length_all = gather_rows([source[0, count:], length_rows], groups, 4)
    lens = length_all.reshape(groups, 8, 128)[:, :micro, 0].T.astype(jnp.int32)
    packed, slots = [], []
    for b in range(micro):
        seq, pos, own = slots_of(lens[b], count)
        slots.append((seq, pos))
        extra = first_extra if b == 0 else lax.all_gather(source[b, count:], "dp", axis=0, tiled=True)
        wanted = seq[me] * spare + pos[me] - count
        chosen = jnp.logical_and(jnp.arange(groups * spare)[None, :] == wanted[:, None], ~own[me][:, None])
        brought = jnp.dot(chosen.astype(BF16), extra, preferred_element_type=F32).astype(BF16)
        packed.append(jnp.where(own[me][:, None], source[b, :count], brought))

    def spots_of(b):
        seq, pos = slots[b]
        code = seq * seq_len + pos
        return rope_tables(pos[me]) + (code[me][:, None], (seq[me] * seq_len)[:, None], code.reshape(1, -1))

    spots = [spots_of(b) for b in range(micro)]

    def spots_at(tick):
        early, late = spots[min(tick, micro - 1)], spots[max(tick - 1, 0)]
        return tuple(jnp.where(first, a, b) for a, b in zip(early, late))

    empty = jnp.zeros((count, width), BF16)
    arriving = empty
    results, saved = [], []
    for tick in range(micro + 1):
        stream = jnp.where(first, packed[tick] if tick < micro else empty, arriving)
        result, arriving, kept = forward_tick(stream, spots_at(tick), weights, groups, q_heads, k_heads, 0)
        results.append(result)
        saved.append(kept)
    norm_one, norm_two = weights[0], weights[3]
    arriving = empty
    grads_in, before, gain_sums = [], [], []

    def all_rows(now, index):
        old = [item[index] for item in before]
        return jnp.concatenate([jnp.where(first, now, old[0])] + old[1:], axis=0)

    for tick in range(micro + 1):
        kept = saved[micro - tick]
        x, mixed, resid, act = kept[0], kept[4], kept[5], kept[8]
        incoming = jnp.where(first, arriving, packed[micro - 1 - tick] if tick < micro else empty)
        d_resid, gain_two, d_gate, d_up = back_ffn(incoming, kept, weights, 1)
        place = spots_at(micro - tick)
        if tick < micro:
            d_stream, gain_one, d_qkv, arriving = back_attn(
                d_resid, kept, place, weights, groups, q_heads, k_heads, 2, -1
            )
            before.append((resid, d_gate, d_up, incoming, act, x, d_qkv, d_resid, mixed))
        else:
            n2 = normalize(all_rows(resid, 0), norm_two)
            grad_gate = rows_contract(n2, all_rows(d_gate, 1)).astype(BF16)
            grad_up = rows_contract(n2, all_rows(d_up, 2)).astype(BF16)
            grad_down = rows_contract(all_rows(incoming, 3), all_rows(act, 4)).astype(BF16)
            ffn_grads = (grad_gate, grad_up, grad_down)
            beside = len(ffn_grads) if groups * count <= 2048 else 1
            d_stream, gain_one, d_qkv, *ffn_sums = back_attn(
                d_resid,
                kept,
                place,
                weights,
                groups,
                q_heads,
                k_heads,
                3,
                0,
                sums=ffn_grads[:beside],
            )
            n1 = normalize(all_rows(x, 5), norm_one)
            back_spread = [(spread_q, 0, q_heads), (spread_k, q_heads, k_heads), (spread_v, q_heads + k_heads, k_heads)]
            dqkv = all_rows(d_qkv, 6)
            dqkv = jnp.concatenate(
                [with_transpose(dqkv[:, i * LANES : (i + n) * LANES], item) for item, i, n in back_spread], axis=1
            ).astype(BF16)
            mix = with_transpose(all_rows(mixed, 8), spread_o).astype(BF16)
            grad_attn = jnp.concatenate(
                [rows_contract(n1, dqkv).astype(BF16), rows_contract(all_rows(d_resid, 7), mix).astype(BF16)], axis=1
            )
        grads_in.append(d_stream)
        gain_sums.append(jnp.concatenate([gain_one, gain_two], axis=0))

    gains = sum(gain_sums[1:], gain_sums[0])
    gains = jnp.concatenate([gains, jnp.zeros((6, width), F32)], axis=0)
    gains = gains.reshape(8, groups, -1).transpose(1, 0, 2).reshape(groups * 8, -1)

    def holder(b):
        seq, pos = slots[b]
        row = jnp.arange(groups * spare)[:, None]
        return jnp.logical_and(row == seq[me][None, :] * spare + pos[me][None, :] - count, pos[me][None, :] >= count)

    def spread(rows, b):
        return jnp.dot(holder(b).astype(BF16), rows, preferred_element_type=F32).astype(BF16)

    def unpack(rows, back, b, through):
        live = (jnp.arange(seq_len) < lens[b, me])[:, None]
        return jnp.where(live, jnp.concatenate([rows, back], axis=0), through)

    def come_back(rows, b):
        return lax.psum_scatter(spread(rows, b), "dp", scatter_dimension=0, tiled=True)

    acts = []
    for b in range(micro):
        rows = jnp.where(first, results[b], results[b + 1])
        acts.append(unpack(rows, come_back(rows, b), b, inputs[b, 0]))
    backs = []
    for b in range(micro):
        rows = jnp.where(first, grads_in[micro - b], grads_in[micro - 1 - b])
        if b == 0:
            back, gains, grad_attn, *rest = return_rows(
                spread(rows, b), gains, (grad_attn,) + ffn_grads[beside:], groups, 5, spare // 16
            )
            grad_gate, grad_up, grad_down = ffn_sums + rest
        else:
            back = come_back(rows, b)
        backs.append(unpack(rows, back, b, cotangent[b, 0]))
    acts, backs = jnp.stack(acts), jnp.stack(backs)
    ends = [0]
    for item in (w_query, w_key, w_value, w_query):
        ends.append(ends[-1] + item.shape[2])
    grad_query, grad_key, grad_value, grad_out = (grad_attn[:, a:b] for a, b in zip(ends, ends[1:]))
    final = (
        gains[0],
        grad_query,
        grad_key,
        grad_value,
        grad_out.T,
        gains[1],
        grad_gate,
        grad_up,
        grad_down.T,
    )
    return (acts[None, :, None], backs[None, :, None]) + tuple(item[None] for item in final)


def solution(mesh):
    placed = (
        P(None, "dp", None, None),
        P(None, "dp", None, None),
        P(None, "dp"),
        P("section", None),
        P("section", None, "tensor"),
        P("section", None, "tensor"),
        P("section", None, "tensor"),
        P("section", "tensor", None),
        P("section", None),
        P("section", None, "tensor"),
        P("section", None, "tensor"),
        P("section", "tensor", None),
    )
    return jax.shard_map(
        on_device,
        mesh=mesh,
        in_specs=placed,
        out_specs=(
            P("section", None, "dp", None, None),
            P("section", None, "dp", None, None),
            P("section", "dp"),
            P("section", "dp", "tensor"),
            P("section", "dp", "tensor"),
            P("section", "dp", "tensor"),
            P("section", "tensor", "dp"),
            P("section", "dp"),
            P("section", "dp", "tensor"),
            P("section", "dp", "tensor"),
            P("section", "tensor", "dp"),
        ),
        check_vma=False,
    )
```

```python
import functools

import jax
import jax.numpy as jnp
from jax import lax
from jax.experimental import pallas as pl
from jax.experimental.pallas import tpu as pltpu
from jax.sharding import PartitionSpec as P

HD = 96

epsilon = 1e-05
rope_base = 100000.0
negative = -1e30
MESH = pl.DeviceIdType.MESH
F32 = jnp.float32
BF16 = jnp.bfloat16


def remote(src, dst, s_sem, r_sem, where):
    return pltpu.make_async_remote_copy(
        src_ref=src, dst_ref=dst, send_sem=s_sem, recv_sem=r_sem, device_id=where, device_id_type=MESH
    )


def greet(where):
    pl.semaphore_signal(pltpu.get_barrier_semaphore(), inc=1, device_id=where, device_id_type=MESH)


def dp_bits(groups):
    return groups.bit_length() - 1


def dp_partner(level):
    me = lax.axis_index("dp")
    bit = lax.rem(me // (1 << level), 2)
    return {"dp": me + (1 - 2 * bit) * (1 << level)}, bit


class Scatter:
    def __init__(self, groups, rows, chunks, refs):
        self.levels = dp_bits(groups)
        self.groups, self.rows, self.chunks, self.size = groups, rows, chunks, rows // chunks
        self.value, self.out = refs[0], refs[1]
        m = self.levels
        self.arrive = refs[2 : 2 + m]
        self.held = refs[2 + m : 1 + 2 * m]
        self.s_sem = refs[1 + 2 * m : 1 + 3 * m]
        self.r_sem = refs[1 + 3 * m : 1 + 4 * m]
        self.links = [dp_partner(k) for k in range(m)]

    @staticmethod
    def scratch(groups, rows, width, chunks, dtype):
        m = dp_bits(groups)
        sizes = [groups >> (k + 1) for k in range(m)]
        return (
            [pltpu.VMEM((size * rows, width), dtype) for size in sizes]
            + [pltpu.VMEM((size * rows, width), dtype) for size in sizes[:-1]]
            + [pltpu.SemaphoreType.DMA((size, chunks)) for size in sizes] * 2
        )

    def at(self, block, c):
        return pl.ds(pl.multiple_of(block * self.rows + c * self.size, self.size), self.size)

    def copy(self, level, slot, c):
        where, bit = self.links[level]
        source = self.value if level == 0 else self.held[level - 1]
        return remote(
            source.at[self.at(2 * slot + 1 - bit, c)],
            self.arrive[level].at[self.at(slot, c)],
            self.s_sem[level].at[slot, c],
            self.r_sem[level].at[slot, c],
            where,
        )

    def order(self, level):
        count = self.groups >> (level + 1)
        if count == 1:
            return [(0, False)]
        bit = self.links[level + 1][1]
        return [(2 * i + 1 - bit, True) for i in range(count // 2)] + [(2 * i + bit, False) for i in range(count // 2)]

    def start(self):
        def one(c, carry):
            for slot, _ in self.order(0):
                self.copy(0, slot, c).start()
            return carry

        lax.fori_loop(0, self.chunks, one, 0)

    def step(self, i, lag):
        for level in range(self.levels):
            c = i - level * lag

            @pl.when(jnp.logical_and(c >= 0, c < self.chunks))
            def _():
                bit = self.links[level][1]
                source = self.value if level == 0 else self.held[level - 1]
                for slot, goes in self.order(level):
                    self.copy(level, slot, c).wait_recv()
                    here = self.at(slot, c)
                    total = source[self.at(2 * slot + bit, c)].astype(F32) + self.arrive[level][here].astype(F32)
                    if level == self.levels - 1:
                        self.out[here] = total.astype(self.out.dtype)
                    else:
                        self.held[level][here] = total.astype(self.held[level].dtype)
                        if goes:
                            self.copy(level + 1, slot // 2, c).start()

    def steps(self, lag):
        return self.chunks + (self.levels - 1) * lag

    def finish(self):
        def one(c, carry):
            for level in range(self.levels):
                for slot in range(self.groups >> (level + 1)):
                    self.copy(level, slot, c).wait_send()
            return carry

        lax.fori_loop(0, self.chunks, one, 0)


def return_kernel(groups, rows, chunks, plans, *refs):
    refs = list(refs)

    def take(count):
        taken = refs[:count]
        del refs[:count]
        return taken

    m = dp_bits(groups)
    count = 4 * m - 1
    value, gains = take(2)
    grads = take(len(plans))
    out, gains_out = take(2)
    totals = take(len(plans))
    gains_all, gains_sum, g_s, g_r = take(4)
    task = Scatter(groups, rows, chunks, [value, out] + take(count))
    small = Scatter(groups, 8, 1, [gains_sum, gains_out] + take(count))
    large = [
        Scatter(groups, block, parts, [grad, total] + take(count))
        for (block, parts), grad, total in zip(plans, grads, totals)
    ]
    t = lax.axis_index("tensor")
    for where, _ in task.links:
        greet(where)
    for k in range(1, 4):
        greet({"tensor": lax.rem(t + k, 4)})
    pl.semaphore_wait(pltpu.get_barrier_semaphore(), m + 3)

    def spread(k):
        return remote(gains, gains_all.at[k - 1], g_s.at[k - 1], g_r.at[k - 1], {"tensor": lax.rem(t + k, 4)})

    for k in range(1, 4):
        spread(k).start()
    task.start()
    for item in large:
        item.start()
    for k in range(1, 4):
        spread(k).wait()
    gains_sum[...] = gains[...] + gains_all[0] + gains_all[1] + gains_all[2]
    small.start()

    def body(i, c):
        small.step(i, 1)
        task.step(i, 2)
        for item in large:
            item.step(i, 4)
        return c

    lax.fori_loop(0, max([task.steps(2), small.steps(1)] + [item.steps(4) for item in large]), body, 0)
    small.finish()
    task.finish()
    for item in large:
        item.finish()


def return_rows(value, gains, grads, groups, cid, chunks):
    rows, width = value.shape[0] // groups, value.shape[1]
    vmem = pl.BlockSpec(memory_space=pltpu.VMEM)
    part = gains.shape[1]
    plans, outs = [], [jax.ShapeDtypeStruct((rows, width), BF16), jax.ShapeDtypeStruct((8, part), F32)]
    scratch = [
        pltpu.VMEM((3,) + gains.shape, F32),
        pltpu.VMEM(gains.shape, F32),
        pltpu.SemaphoreType.DMA((3,)),
        pltpu.SemaphoreType.DMA((3,)),
    ]
    scratch += Scatter.scratch(groups, rows, width, chunks, BF16) + Scatter.scratch(groups, 8, part, 1, F32)
    for grad in grads:
        block = grad.shape[0] // groups
        plans.append((block, max(1, block // 48)))
        outs.append(jax.ShapeDtypeStruct((block, grad.shape[1]), F32))
        scratch += Scatter.scratch(groups, block, grad.shape[1], plans[-1][1], BF16)
    return pl.pallas_call(
        functools.partial(return_kernel, groups, rows, chunks, plans),
        out_shape=outs,
        in_specs=[vmem] * (2 + len(grads)),
        out_specs=[vmem] * len(outs),
        scratch_shapes=scratch,
        compiler_params=pltpu.CompilerParams(
            collective_id=cid, has_side_effects=True, vmem_limit_bytes=VMEM_LIMIT
        ),
        name="return_%d" % cid,
    )(value, gains, *grads)


def gather_kernel(groups, count, *refs):
    values, outs = refs[:count], refs[count : 2 * count]
    s_sem, r_sem, own = refs[2 * count :]
    m = dp_bits(groups)
    me = lax.axis_index("dp")
    links = [dp_partner(k) for k in range(m)]
    for where, _ in links:
        greet(where)
    pl.semaphore_wait(pltpu.get_barrier_semaphore(), m)

    def place(a, block):
        rows = values[a].shape[0]
        return outs[a].at[pl.ds(pl.multiple_of(block * rows, rows), rows)]

    def copy(a, level, i, mine):
        where, bit = links[level]
        low = lax.rem(me, 1 << (level + 1))
        if not mine:
            low = low + (1 - 2 * bit) * (1 << level)
        block = i * (1 << (level + 1)) + low
        return remote(place(a, block), place(a, block), s_sem.at[a, level, i], r_sem.at[a, level, i], where)

    locals_ = [pltpu.make_async_copy(values[a], place(a, me), own.at[a]) for a in range(count)]
    for item in locals_:
        item.start()
    for item in locals_:
        item.wait()
    for level in reversed(range(m)):
        for i in range(groups >> (level + 1)):
            for a in range(count):
                copy(a, level, i, True).start()
        for i in range(groups >> (level + 1)):
            for a in range(count):
                copy(a, level, i, False).wait_recv()
    for level in range(m):
        for i in range(groups >> (level + 1)):
            for a in range(count):
                copy(a, level, i, True).wait_send()


def gather_rows(values, groups, cid):
    vmem = pl.BlockSpec(memory_space=pltpu.VMEM)
    m, count = dp_bits(groups), len(values)
    dma = pltpu.SemaphoreType.DMA
    return pl.pallas_call(
        functools.partial(gather_kernel, groups, count),
        out_shape=[jax.ShapeDtypeStruct((groups * v.shape[0], v.shape[1]), v.dtype) for v in values],
        in_specs=[vmem] * count,
        out_specs=[vmem] * count,
        scratch_shapes=[dma((count, m, groups // 2)), dma((count, m, groups // 2)), dma((count,))],
        compiler_params=pltpu.CompilerParams(
            collective_id=cid, has_side_effects=True, vmem_limit_bytes=48 * 2**20
        ),
        name="gather_%d" % cid,
    )(*values)


class OwnScatter(Scatter):
    def __init__(self, groups, rows, chunks, refs):
        m = dp_bits(groups)
        super().__init__(groups, rows, chunks, list(refs[: 2 + m]) + [None] * (m - 1) + list(refs[2 + m :]))
        self.me = lax.axis_index("dp")

    @staticmethod
    def scratch(groups, rows, width, chunks, dtype):
        m = dp_bits(groups)
        kinds = Scatter.scratch(groups, rows, width, chunks, dtype)
        return kinds[:m] + kinds[2 * m - 1 :]

    @staticmethod
    def refs(groups):
        return 3 * dp_bits(groups)

    def whole(self, level, slot, c):
        return self.at(slot * (1 << level) + lax.rem(self.me, 1 << level), c)

    def copy(self, level, slot, c):
        where, bit = self.links[level]
        return remote(
            self.value.at[self.whole(level, 2 * slot + 1 - bit, c)],
            self.arrive[level].at[self.at(slot, c)],
            self.s_sem[level].at[slot, c],
            self.r_sem[level].at[slot, c],
            where,
        )

    def step(self, i, lag):
        for level in range(self.levels):
            c = i - level * lag

            @pl.when(jnp.logical_and(c >= 0, c < self.chunks))
            def _():
                bit = self.links[level][1]
                for slot, goes in self.order(level):
                    self.copy(level, slot, c).wait_recv()
                    here = self.whole(level, 2 * slot + bit, c)
                    total = self.value[here].astype(F32) + self.arrive[level][self.at(slot, c)].astype(F32)
                    if level == self.levels - 1:
                        self.out[self.at(0, c)] = total.astype(self.out.dtype)
                    else:
                        self.value[here] = total.astype(self.value.dtype)
                        if goes:
                            self.copy(level + 1, slot // 2, c).start()


class Line:
    lag_b, lag_c, lag_o = 2, 4, 5

    def __init__(self, first, half, pieces, part, base, out, scratch, norm=None, moved=None, at=(0, 0, 0), turns=1):
        self.first, self.half, self.size = first, half, half // pieces
        self.each, self.pieces = pieces, pieces * turns
        self.base_at, self.out_at, self.moved_at = at
        self.part, self.base, self.out = part, base, out
        (self.rin, self.smid, self.rmid) = scratch[:3]
        (self.s_up, self.r_up, self.s_mid, self.r_mid, self.s_b1, self.s_b2, self.r_b, self.s_c, self.r_c) = scratch[3:12]
        self.norm, self.moved = norm, moved
        if moved:
            self.arrived, self.shift = moved
            self.s_s, self.r_s = scratch[12:14]
            section = lax.axis_index("section")
            self.sends = section == (0 if self.shift > 0 else 1)
            self.partner = {"section": 1 - section}
        t = lax.axis_index("tensor")
        self.mid = jnp.logical_or(t == 1, t == 2)
        self.outside = jnp.logical_not(self.mid)
        self.outer = {"tensor": jnp.where(t == 1, 0, 3)}
        self.other = {"tensor": jnp.where(t == 1, 2, 1)}
        self.nbr = {"tensor": jnp.where(t == 0, 1, 2)}
        self.near = jnp.where(t < 2, 0, half)
        self.far = half - self.near

    @staticmethod
    def scratch(half, pieces, width, moved, turns=1):
        dma = pltpu.SemaphoreType.DMA
        half, pieces = half * turns, pieces * turns
        kinds = [
            pltpu.VMEM((2 * half, width), BF16),
            pltpu.VMEM((half, width), BF16),
            pltpu.VMEM((half, width), BF16),
            dma((2, pieces)),
            dma((2, pieces)),
        ] + [dma((pieces,))] * 7
        return kinds + ([dma((2, pieces))] * 2 if moved else [])

    @staticmethod
    def greet():
        t = lax.axis_index("tensor")

        @pl.when(t > 0)
        def _():
            greet({"tensor": jnp.maximum(t - 1, 0)})

        @pl.when(t < 3)
        def _():
            greet({"tensor": jnp.minimum(t + 1, 3)})

    def greet_sender(self):
        if self.moved:

            @pl.when(jnp.logical_not(self.sends))
            def _():
                greet(self.partner)

    def enter(self, others):
        bar = pltpu.get_barrier_semaphore()
        count = jnp.where(self.mid, 2, 1) + others
        if self.moved:
            count = count + jnp.where(self.sends, 1, 0)
        pl.semaphore_wait(bar, count)

    def local(self, start, p):
        if self.each < self.pieces:
            start, p = start + (p // self.each) * (2 * self.half), lax.rem(p, self.each)
        return pl.ds(pl.multiple_of(start + p * self.size, self.size), self.size)

    def own(self, p):
        return pl.ds(pl.multiple_of(p * self.size, self.size), self.size)

    def rows(self, start, p, at=0):
        return self.local(self.first + at + start, p)

    def shifted(self, start, p):
        side = start // self.half
        here, there = self.rows(start, p, self.out_at), self.rows(start, p, self.moved_at)
        return remote(self.out.at[here], self.arrived.at[there], self.s_s.at[side, p], self.r_s.at[side, p], self.partner)

    def pass_on(self, start, p):
        if self.moved:

            @pl.when(self.sends)
            def _():
                self.shifted(start, p).start()

    def outcome(self, s_sem, r_sem, where, start, p):
        here = self.rows(start, p, self.out_at)
        return remote(self.out.at[here], self.out.at[here], s_sem.at[p], r_sem.at[p], where)

    def up(self, start, p, k, where):
        return remote(
            self.part.at[self.rows(start, p)], self.rin.at[self.local(start, p)], self.s_up.at[k, p], self.r_up.at[k, p], where
        )

    def cross(self, p):
        return remote(
            self.smid.at[self.own(p)], self.rmid.at[self.own(p)], self.s_mid.at[p], self.r_mid.at[p], self.other
        )

    def start(self, turn=0):
        @pl.when(self.outside)
        def _():
            def begin(p, c):
                self.up(self.far, p, 0, self.nbr).start()
                self.up(self.near, p, 1, self.nbr).start()
                return c

            lax.fori_loop(turn * self.each, (turn + 1) * self.each, begin, 0)

    def outer_step(self, i):
        p = i - self.lag_o

        @pl.when(jnp.logical_and(p >= 0, p < self.pieces))
        def _():
            self.outcome(self.s_b2, self.r_b, self.nbr, self.near, p).wait_recv()
            self.pass_on(self.near, p)
            self.outcome(self.s_c, self.r_c, self.nbr, self.far, p).wait_recv()
            self.pass_on(self.far, p)

    def mid_step(self, i):
        @pl.when(jnp.logical_and(i >= 0, i < self.pieces))
        def _():
            self.up(self.far, i, 0, self.outer).wait_recv()
            total = self.part[self.rows(self.far, i)].astype(F32) + self.rin[self.local(self.far, i)].astype(F32)
            self.smid[self.own(i)] = total.astype(BF16)
            self.cross(i).start()

        j = i - self.lag_b

        @pl.when(jnp.logical_and(j >= 0, j < self.pieces))
        def _():
            self.up(self.near, j, 1, self.outer).wait_recv()
            self.cross(j).wait_recv()
            here = self.rows(self.near, j, self.base_at)
            total = self.part[self.rows(self.near, j)].astype(F32) + self.rin[self.local(self.near, j)].astype(F32)
            total = total + self.rmid[self.own(j)].astype(F32)
            if self.norm:
                xrow, gain, gsum = self.norm
                x = xrow[here].astype(F32)
                scale = lax.rsqrt(jnp.mean(x * x, axis=-1, keepdims=True) + epsilon)
                unit = x * scale
                gsum[...] += jnp.sum(total * unit, axis=0, keepdims=True)
                inner = total * gain[...]
                total = scale * (inner - unit * jnp.mean(inner * unit, axis=-1, keepdims=True))
            total = self.base[here].astype(F32) + total
            self.out[self.rows(self.near, j, self.out_at)] = total.astype(BF16)
            self.outcome(self.s_b1, self.r_b, self.other, self.near, j).start()
            self.outcome(self.s_b2, self.r_b, self.outer, self.near, j).start()
            self.pass_on(self.near, j)

        k = i - self.lag_c

        @pl.when(jnp.logical_and(k >= 0, k < self.pieces))
        def _():
            self.outcome(self.s_b1, self.r_b, self.other, self.far, k).wait_recv()
            self.outcome(self.s_c, self.r_c, self.outer, self.far, k).start()
            self.pass_on(self.far, k)

    @property
    def steps(self):
        return self.pieces + self.lag_o

    def step(self, i):
        @pl.when(self.mid)
        def _():
            self.mid_step(i)

        @pl.when(self.outside)
        def _():
            self.outer_step(i)

    def finish(self):
        @pl.when(self.mid)
        def _():
            def one(p, c):
                self.cross(p).wait_send()
                self.outcome(self.s_b1, self.r_b, self.other, self.near, p).wait_send()
                self.outcome(self.s_b2, self.r_b, self.outer, self.near, p).wait_send()
                self.outcome(self.s_c, self.r_c, self.outer, self.far, p).wait_send()
                return c

            lax.fori_loop(0, self.pieces, one, 0)

        @pl.when(self.outside)
        def _():
            def one(p, c):
                self.up(self.far, p, 0, self.nbr).wait_send()
                self.up(self.near, p, 1, self.nbr).wait_send()
                return c

            lax.fori_loop(0, self.pieces, one, 0)

        if self.moved:

            @pl.when(self.sends)
            def _():
                def close(p, c):
                    self.shifted(0, p).wait_send()
                    self.shifted(self.half, p).wait_send()
                    return c

                lax.fori_loop(0, self.pieces, close, 0)

    def receive(self):
        @pl.when(jnp.logical_not(self.sends))
        def _():
            def close(p, c):
                self.shifted(0, p).wait_recv()
                self.shifted(self.half, p).wait_recv()
                return c

            lax.fori_loop(0, self.pieces, close, 0)


def run_steps(begin, end, *planned):
    def body(i, c):
        for step, offset in planned:
            step(i - offset)
        return c

    lax.fori_loop(begin, end, body, 0)


class Gather:
    def __init__(self, groups, rows, out, s_sem, r_sem):
        self.groups, self.rows, self.out, self.s_sem, self.r_sem = groups, rows, out, s_sem, r_sem
        self.levels = dp_bits(groups)
        self.links = [dp_partner(k) for k in range(self.levels)]
        self.me = lax.axis_index("dp")

    @staticmethod
    def scratch(groups):
        return [pltpu.SemaphoreType.DMA((dp_bits(groups), groups // 2))] * 2

    def copy(self, level, i, mine):
        where, bit = self.links[level]
        low = lax.rem(self.me, 1 << (level + 1))
        if not mine:
            low = low + (1 - 2 * bit) * (1 << level)
        block = i * (1 << (level + 1)) + low
        place = self.out.at[pl.ds(pl.multiple_of(block * self.rows, self.rows), self.rows)]
        return remote(place, place, self.s_sem.at[level, i], self.r_sem.at[level, i], where)

    def start(self, level):
        for i in range(self.groups >> (level + 1)):
            self.copy(level, i, True).start()

    def arrive(self, level):
        for i in range(self.groups >> (level + 1)):
            self.copy(level, i, False).wait_recv()

    def finish(self):
        for level in range(self.levels):
            for i in range(self.groups >> (level + 1)):
                self.copy(level, i, True).wait_send()


def with_transpose(left, right):
    return lax.dot_general(left, right, (((1,), (1,)), ((), ())), preferred_element_type=F32)


def rows_contract(left, right):
    return lax.dot_general(left, right, (((0,), (0,)), ((), ())), preferred_element_type=F32)


def times(left, right):
    return jnp.dot(left, right, preferred_element_type=F32)


LANES = 128
TILE = 256
WIDE = 512


def lanes(i, size=LANES):
    return pl.ds(pl.multiple_of(i * size, size), size)


def normalize(rows, gain):
    rows = rows.astype(F32)
    scale = lax.rsqrt(jnp.mean(rows * rows, axis=-1, keepdims=True) + epsilon)
    return (rows * scale * gain).astype(BF16)


def normalize_into(target, source, gain, first, count, block=32, source_at=0):
    def one(i, c):
        here = pl.ds(pl.multiple_of(first + i * block, block), block)
        there = pl.ds(pl.multiple_of(source_at + first + i * block, block), block)
        target[here] = normalize(source[there], gain[...])
        return c

    lax.fori_loop(0, count // block, one, 0)


def rolled(value, cosine, sine):
    return value * cosine + pltpu.roll(value, LANES // 2, 1) * sine


def block_rows(keys):
    for rows in (160, 80, 32):
        if rows * keys <= 160 * 1280:
            return rows
    return 16


def score_rows(q, kv, h, g, here, qcode, qstart, kcode):
    scores = with_transpose(q[here, lanes(h)], kv[:, lanes(g)]) * HD ** (-0.5)
    code = kcode[...]
    return scores, jnp.logical_and(code <= qcode[here], code >= qstart[here])


def load_all(pairs, sems):
    copies = [pltpu.make_async_copy(src, dst, sems.at[i]) for i, (src, dst) in enumerate(pairs)]
    for item in copies:
        item.start()
    return copies


def forward_kernel(groups, q_heads, k_heads, pieces, *refs):
    refs = list(refs)

    def take(count):
        taken = refs[:count]
        del refs[:count]
        return taken

    x, cosine, sine, qcode, qstart, kcode, gain_one, gain_two = take(8)
    far_weights = take(5)
    q, kv, lse, mixed, resid, gate, up, act, y, arrived = take(10)
    near_weights = take(5)
    wqkv, wout, wgate, wup, wdown = near_weights
    part_one, part_two, n1, n2, w_sem = take(5)
    gather = Gather(groups, x.shape[0], kv, *take(2))
    count, width = x.shape
    quarter = count // 4
    lines = []
    for k in range(4):
        first = (k % 2) * 2 * quarter
        source = (part_one, x, resid) if k < 2 else (part_two, resid, y)
        lines.append(
            Line(first, quarter, pieces, *source, take(12 if k < 2 else 14), moved=None if k < 2 else (arrived, 1))
        )
    one_a, one_b, two_a, two_b = lines

    loads = load_all(list(zip(far_weights, near_weights)), w_sem)
    Line.greet()
    two_a.greet_sender()
    for where, _ in gather.links:
        greet(where)
    normalize_into(n1, x, gain_one, 0, count)
    loads[0].wait()

    mine = pl.ds(pl.multiple_of(lax.axis_index("dp") * count, count), count)
    for g in range(k_heads):
        column = (q_heads + g) * LANES
        value = times(n1[...], wqkv[:, column : column + LANES])
        kv[mine, g * LANES : (g + 1) * LANES] = rolled(value, cosine[...], sine[...]).astype(BF16)
        column += k_heads * LANES
        kv[mine, (k_heads + g) * LANES : (k_heads + g + 1) * LANES] = times(
            n1[...], wqkv[:, column : column + LANES]
        ).astype(BF16)

    two_a.enter(gather.levels)

    top = gather.levels - 1
    gather.start(top)

    def queries(h, c):
        value = times(n1[...], wqkv[:, lanes(h)])
        q[:, lanes(h)] = rolled(value, cosine[...], sine[...]).astype(BF16)
        return c

    lax.fori_loop(0, q_heads, queries, 0)
    for level in range(top, -1, -1):
        gather.arrive(level)
        if level:
            gather.start(level - 1)

    rows = block_rows(kv.shape[0])
    blocks = count // rows

    def attend(i, c):
        h, b = i // blocks, lax.rem(i, blocks)
        g = h // (q_heads // k_heads)
        here = pl.ds(pl.multiple_of(b * rows, rows), rows)
        scores, allowed = score_rows(q, kv, h, g, here, qcode, qstart, kcode)
        scores = jnp.where(allowed, scores, negative)
        row_max = jnp.max(scores, axis=-1, keepdims=True)
        expo = jnp.exp(scores - row_max)
        row_total = jnp.sum(expo, axis=-1, keepdims=True)
        prob = (expo * (1.0 / row_total)).astype(BF16)
        mixed[here, lanes(h)] = times(prob, kv[:, lanes(k_heads + g)]).astype(BF16)
        there = pl.ds(pl.multiple_of(h * count + b * rows, rows), rows)
        lse[there] = jnp.broadcast_to(row_max + jnp.log(row_total), (rows, LANES))
        return c

    lax.fori_loop(0, q_heads * blocks, attend, 0)
    loads[1].wait()

    def projected(target, left, right, first, each=None):
        here = pl.ds(first, 2 * quarter)

        def one(i, c):
            target[here, lanes(i, TILE)] = times(left[here], right[:, lanes(i, TILE)]).astype(BF16)
            if each:
                each(i)
            return c

        lax.fori_loop(0, width // TILE, one, 0)

    projected(part_one, mixed, wout, 0)
    one_a.start()
    projected(part_one, mixed, wout, 2 * quarter)
    one_b.start()
    run_steps(0, one_a.steps, (one_a.step, 0), (one_b.step, pieces))
    loads[2].wait()
    loads[3].wait()
    loads[4].wait()

    def hidden(first, each):
        here = pl.ds(first, 2 * quarter)
        normalize_into(n2, resid, gain_two, first, 2 * quarter)

        def one(i, c):
            columns = lanes(i, TILE)
            gate_pre = times(n2[here], wgate[:, columns])
            up_pre = times(n2[here], wup[:, columns])
            gate[here, columns] = gate_pre.astype(BF16)
            up[here, columns] = up_pre.astype(BF16)
            act[here, columns] = (gate_pre * jax.nn.sigmoid(gate_pre) * up_pre).astype(BF16)
            each(i)
            return c

        lax.fori_loop(0, gate.shape[1] // TILE, one, 0)

    tiles = gate.shape[1] // TILE
    done = one_a.steps - pieces
    hidden(0, lambda i: one_b.step(done + i))
    projected(part_two, act, wdown, 0)
    two_a.start()
    run_steps(done + tiles, one_b.steps, (one_b.step, 0))
    hidden(2 * quarter, lambda i: two_a.step(i))
    projected(part_two, act, wdown, 2 * quarter)
    two_b.start()
    run_steps(tiles, two_b.steps + tiles, (two_a.step, 0), (two_b.step, tiles))
    gather.finish()
    for line in lines:
        line.finish()
    two_a.receive()
    two_b.receive()


VMEM_LIMIT = 58 * 2**20


def forward_tick(x, spots, weights, groups, q_heads, k_heads, cid):
    norm_one, wqkv, wout, norm_two, wgate, wup, wdown = weights
    count, width = x.shape
    hidden = wgate.shape[1]
    pieces = 5
    vmem = pl.BlockSpec(memory_space=pltpu.VMEM)
    far = pl.BlockSpec(memory_space=pl.ANY)

    def shape(*dims, dtype=BF16):
        return jax.ShapeDtypeStruct(dims, dtype)

    outs = [
        shape(count, q_heads * LANES),
        shape(groups * count, 2 * k_heads * LANES),
        shape(q_heads * count, LANES, dtype=F32),
        shape(count, q_heads * LANES),
        shape(count, width),
        shape(count, hidden),
        shape(count, hidden),
        shape(count, hidden),
        shape(count, width),
        shape(count, width),
    ]
    far_weights = [wqkv, wout, wgate, wup, wdown]
    scratch = [pltpu.VMEM(item.shape, BF16) for item in far_weights]
    scratch += [pltpu.VMEM((count, width), BF16)] * 4 + [pltpu.SemaphoreType.DMA((5,))]
    scratch += Gather.scratch(groups)
    for k in range(4):
        scratch += Line.scratch(count // 4, pieces, width, k >= 2)
    q, kv, lse, mixed, resid, gate, up, act, y, arrived = pl.pallas_call(
        functools.partial(forward_kernel, groups, q_heads, k_heads, pieces),
        out_shape=outs,
        in_specs=[vmem] * 8 + [far] * 5,
        out_specs=[vmem] * len(outs),
        scratch_shapes=scratch,
        compiler_params=pltpu.CompilerParams(
            collective_id=cid, has_side_effects=True, vmem_limit_bytes=VMEM_LIMIT
        ),
        name="forward_tick",
    )(x, *spots, norm_one[None], norm_two[None], *far_weights)
    return y, arrived, (x, q, kv, lse, mixed, resid, gate, up, act)


def back_ffn_kernel(pieces, *refs):
    dy, gate, up, resid, gain = refs[:5]
    far_weights = refs[5:8]
    dresid, gsum, dgate, dup = refs[8:12]
    wdown, wgate, wup = near_weights = refs[12:15]
    part, w_sem = refs[15:17]
    count, width = dy.shape
    quarter = count // 4
    a, b = [
        Line(k * 2 * quarter, quarter, pieces, part, dy, dresid, refs[17 + 12 * k : 29 + 12 * k], norm=(resid, gain, gsum))
        for k in range(2)
    ]
    loads = load_all(list(zip(far_weights, near_weights)), w_sem)
    Line.greet()
    gsum[...] = jnp.zeros_like(gsum)

    def hidden(first, each=None):
        here = pl.ds(first, 2 * quarter)

        def one(i, c):
            columns = lanes(i, TILE)
            d_act = with_transpose(dy[here], wdown[columns, :])
            gate_pre, up_pre = gate[here, columns].astype(F32), up[here, columns].astype(F32)
            sigma = jax.nn.sigmoid(gate_pre)
            d_silu = d_act * sigma
            dup[here, columns] = (d_silu * gate_pre).astype(BF16)
            dgate[here, columns] = (d_silu * up_pre * (1.0 + gate_pre * (1.0 - sigma))).astype(BF16)
            if each:
                each(i)
            return c

        lax.fori_loop(0, gate.shape[1] // TILE, one, 0)

    def back(first):
        here = pl.ds(first, 2 * quarter)

        def one(i, c):
            columns = lanes(i, TILE)
            total = with_transpose(dgate[here], wgate[columns, :]) + with_transpose(dup[here], wup[columns, :])
            part[here, columns] = total.astype(BF16)
            return c

        lax.fori_loop(0, width // TILE, one, 0)

    loads[0].wait()
    hidden(0)
    loads[1].wait()
    loads[2].wait()
    back(0)
    a.enter(0)
    a.start()
    tiles = gate.shape[1] // TILE
    hidden(2 * quarter, lambda i: a.step(i))
    back(2 * quarter)
    b.start()
    run_steps(tiles, b.steps + tiles, (a.step, 0), (b.step, tiles))
    a.finish()
    b.finish()


def back_ffn(dy, kept, weights, cid):
    norm_one, wqkv, wout, norm_two, wgate, wup, wdown = weights
    x, q, kv, lse, mixed, resid, gate, up, act = kept
    count, width = dy.shape
    pieces = 5
    vmem = pl.BlockSpec(memory_space=pltpu.VMEM)
    far = pl.BlockSpec(memory_space=pl.ANY)
    far_weights = [wdown, wgate, wup]
    scratch = [pltpu.VMEM(item.shape, BF16) for item in far_weights]
    scratch += [pltpu.VMEM((count, width), BF16), pltpu.SemaphoreType.DMA((3,))]
    scratch += Line.scratch(count // 4, pieces, width, False) * 2
    return pl.pallas_call(
        functools.partial(back_ffn_kernel, pieces),
        out_shape=[
            jax.ShapeDtypeStruct((count, width), BF16),
            jax.ShapeDtypeStruct((1, width), F32),
            jax.ShapeDtypeStruct(gate.shape, BF16),
            jax.ShapeDtypeStruct(gate.shape, BF16),
        ],
        in_specs=[vmem] * 5 + [far] * 3,
        out_specs=[vmem] * 4,
        scratch_shapes=scratch,
        compiler_params=pltpu.CompilerParams(
            collective_id=cid, has_side_effects=True, vmem_limit_bytes=VMEM_LIMIT
        ),
        name="back_ffn",
    )(dy, gate, up, resid, norm_two[None], *far_weights)


def back_attn_kernel(groups, q_heads, k_heads, pieces, shift, plans, *refs):
    refs = list(refs)

    def take(count):
        taken = refs[:count]
        del refs[:count]
        return taken

    dresid, x, q, kv, lse, cosine, sine, qcode, qstart, kcode, gain = take(11)
    far_weights = take(2)
    values = take(len(plans))
    dx, gsum, dqkv = take(3)
    (arrived,) = take(1) if shift else (None,)
    totals = take(len(plans))
    wout, wqkv = near_weights = take(2)
    part, dmixed, dkv, w_sem = take(4)
    levels = dp_bits(groups)
    count, width = x.shape
    quarter = count // 4
    keys = kv.shape[0]
    shares, owns, scatters = [], [], []
    for g in range(k_heads):
        share, own = take(2)
        shares.append(share)
        owns.append(own)
        scatters.append(Scatter(groups, count, 5, [share, own] + take(4 * levels - 1)))
    tasks = [
        Scatter(groups, rows, chunks, [value, total] + take(4 * levels - 1))
        for (rows, chunks), value, total in zip(plans, values, totals)
    ]
    moved = (arrived, shift) if shift else None
    a, b = [
        Line(
            k * 2 * quarter,
            quarter,
            pieces,
            part,
            dresid,
            dx,
            take(14 if shift else 12),
            norm=(x, gain, gsum),
            moved=moved,
        )
        for k in range(2)
    ]
    loads = load_all(list(zip(far_weights, near_weights)), w_sem)
    Line.greet()
    for where, _ in scatters[0].links:
        greet(where)
    a.greet_sender()
    gsum[...] = jnp.zeros_like(gsum)
    dkv[...] = jnp.zeros_like(dkv)
    a.enter(levels)
    for task in tasks:
        task.start()
    loads[0].wait()

    def mix(h, c):
        dmixed[:, lanes(h)] = with_transpose(dresid[...], wout[lanes(h), :]).astype(BF16)
        return c

    lax.fori_loop(0, q_heads, mix, 0)
    rows = block_rows(keys)
    blocks = count // rows
    repeat = q_heads // k_heads
    lag = 4
    scale = HD ** (-0.5)

    for g in range(k_heads):

        def one(i, c):
            h, n = g * repeat + i // blocks, lax.rem(i, blocks)
            here = pl.ds(pl.multiple_of(n * rows, rows), rows)
            there = pl.ds(pl.multiple_of(h * count + n * rows, rows), rows)
            scores, allowed = score_rows(q, kv, h, g, here, qcode, qstart, kcode)
            prob = jnp.where(allowed, jnp.exp(scores - lse[there][:, :1]), 0.0)
            dm = dmixed[here, lanes(h)]
            d_prob = with_transpose(dm, kv[:, lanes(k_heads + g)])
            row_dot = jnp.sum(prob * d_prob, axis=-1, keepdims=True)
            d_scores = (prob * (d_prob - row_dot)).astype(BF16)
            d_query = times(d_scores, kv[:, lanes(g)]) * scale
            dqkv[here, lanes(h)] = rolled(d_query, cosine[here], -sine[here]).astype(BF16)
            dkv[:, lanes(g)] += rows_contract(d_scores, q[here, lanes(h)]) * scale
            dkv[:, lanes(k_heads + g)] += rows_contract(prob.astype(BF16), dm)
            for task in tasks:
                task.step(g * repeat * blocks + i, lag)
            return c

        lax.fori_loop(0, repeat * blocks, one, 0)

        def narrow(i, c):
            here = pl.ds(pl.multiple_of(i * LANES, LANES), LANES)
            shares[g][here, :LANES] = dkv[here, lanes(g)].astype(BF16)
            shares[g][here, LANES:] = dkv[here, lanes(k_heads + g)].astype(BF16)
            return c

        lax.fori_loop(0, keys // LANES, narrow, 0)
        scatters[g].start()
    run_steps(0, scatters[0].steps(1), *[(functools.partial(lambda s, i: s.step(i, 1), s), 0) for s in scatters])
    for g in range(k_heads):
        dqkv[:, lanes(q_heads + g)] = rolled(owns[g][:, :LANES], cosine[...], -sine[...]).astype(BF16)
        dqkv[:, lanes(q_heads + k_heads + g)] = owns[g][:, LANES:].astype(BF16)
    loads[1].wait()

    def back(first, each=None):
        here = pl.ds(first, 2 * quarter)

        def one(i, c):
            columns = lanes(i, TILE)
            part[here, columns] = with_transpose(dqkv[here], wqkv[columns, :]).astype(BF16)
            if each:
                each(i)
            return c

        lax.fori_loop(0, width // TILE, one, 0)

    back(0)
    a.start()
    back(2 * quarter)
    b.start()
    begun = q_heads * blocks
    more = [(functools.partial(lambda s, i: s.step(i + begun, lag), s), 0) for s in tasks]
    last = max([b.steps + pieces] + [s.steps(lag) - begun for s in tasks])
    run_steps(0, last, (a.step, 0), (b.step, pieces), *more)
    a.finish()
    b.finish()
    if shift:
        a.receive()
        b.receive()
    for item in scatters + tasks:
        item.finish()


def back_attn(dresid, kept, spots, weights, groups, q_heads, k_heads, cid, shift, sums=()):
    norm_one, wqkv, wout, norm_two, wgate, wup, wdown = weights
    x, q, kv, lse, mixed, resid, gate, up, act = kept
    count, width = x.shape
    keys = kv.shape[0]
    pieces = 5
    vmem = pl.BlockSpec(memory_space=pltpu.VMEM)
    far = pl.BlockSpec(memory_space=pl.ANY)
    outs = [
        jax.ShapeDtypeStruct((count, width), BF16),
        jax.ShapeDtypeStruct((1, width), F32),
        jax.ShapeDtypeStruct((count, wqkv.shape[1]), BF16),
    ]
    if shift:
        outs.append(jax.ShapeDtypeStruct((count, width), BF16))
    scratch = [
        pltpu.VMEM(wout.shape, BF16),
        pltpu.VMEM(wqkv.shape, BF16),
        pltpu.VMEM((count, width), BF16),
        pltpu.VMEM(q.shape, BF16),
        pltpu.VMEM(kv.shape, F32),
        pltpu.SemaphoreType.DMA((2,)),
    ]
    for _ in range(k_heads):
        scratch += [pltpu.VMEM((keys, 2 * LANES), BF16), pltpu.VMEM((count, 2 * LANES), F32)]
        scratch += Scatter.scratch(groups, count, 2 * LANES, 5, BF16)
    plans = []
    for value in sums:
        rows = value.shape[0] // groups
        parts = max(1, min(8, rows // 16))
        while rows % (parts * 16):
            parts -= 1
        plans.append((rows, parts))
        outs.append(jax.ShapeDtypeStruct((rows, value.shape[1]), F32))
        scratch += Scatter.scratch(groups, rows, value.shape[1], parts, BF16)
    scratch += Line.scratch(count // 4, pieces, width, bool(shift)) * 2
    return pl.pallas_call(
        functools.partial(back_attn_kernel, groups, q_heads, k_heads, pieces, shift, plans),
        out_shape=outs,
        in_specs=[vmem] * 11 + [far] * 2 + [vmem] * len(sums),
        out_specs=[vmem] * len(outs),
        scratch_shapes=scratch,
        compiler_params=pltpu.CompilerParams(
            collective_id=cid, has_side_effects=True, vmem_limit_bytes=VMEM_LIMIT
        ),
        name="back_attn_%d" % cid,
    )(dresid, x, q, kv, lse, *spots, norm_one[None], wout, wqkv, *sums)


def announce(sems, neighbours):
    for here, where, k in neighbours:

        @pl.when(here)
        def _():
            pl.semaphore_signal(sems.at[k], inc=1, device_id=where, device_id_type=MESH)


def heard(sems, neighbours):
    for k, (here, _, _) in enumerate(neighbours):

        @pl.when(here)
        def _():
            pl.semaphore_wait(sems.at[k], 1)


def main_kernel(groups, q_heads, k_heads, pieces, *refs):
    refs = list(refs)

    def take(count):
        taken = refs[:count]
        del refs[:count]
        return taken

    packed, cosine, sine, qcode, qstart, kcode, gain_one, gain_two, holder = take(9)
    far_weights = take(5)
    y_out, dx_out, back_out, xs, q, kv, lse, mixed, resid, gate, up, act, dys, dresid, dgate, dup, dqkv, gsum_one, gsum_two = take(19)
    wqkv, wout, wgate, wup, wdown = near_weights = take(5)
    part_one, part_two, normed, y, dmixed, dkv, w_sem, io_sem, meet_sem = take(9)
    levels = dp_bits(groups)
    gather_sems = take(2)
    line_scratch = [take(12) for _ in range(4)]
    forth_s, forth_r, back_s, back_r = take(4)
    spares, returned = take(2)
    spare = returned.shape[0]
    give_lag = Line.lag_o + pieces
    give = OwnScatter(groups, spare, spare // 32, [spares, returned] + take(OwnScatter.refs(groups)))
    count, width = part_one.shape
    keys = groups * count
    quarter = count // 4
    half = 2 * quarter
    shares, owns, scatters = [], [], []
    for g in range(k_heads):
        share, own = take(2)
        shares.append(share)
        owns.append(own)
        scatters.append(Scatter(groups, count, 5, [share, own] + take(4 * levels - 1)))
    section = lax.axis_index("section")
    t = lax.axis_index("tensor")
    tiles, wide = gate.shape[1] // WIDE, width // WIDE
    repeat = q_heads // k_heads
    rows = block_rows(keys)
    blocks = half // rows
    scale = HD ** (-0.5)

    def span(first, size):
        return pl.ds(pl.multiple_of(first, 32), size)

    neighbours = [
        (t > 0, {"tensor": jnp.maximum(t - 1, 0)}, 1),
        (t < 3, {"tensor": jnp.minimum(t + 1, 3)}, 0),
    ]
    for k in range(levels):
        neighbours.append((t >= 0, dp_partner(k)[0], 2 + k))

    for _, where, _ in neighbours[2:]:
        greet(where)
    Line.greet()
    greet({"section": 1 - section})

    loads = load_all(list(zip(far_weights, near_weights)), w_sem)

    def fetch(slot, target):
        place = span(slot * count, count)
        return pltpu.make_async_copy(packed.at[place], target.at[place], io_sem.at[slot])

    for slot in range(2):

        @pl.when(section == 0)
        def _():
            fetch(slot, xs).start()

        @pl.when(section == 1)
        def _():
            fetch(slot, dys).start()

    pl.semaphore_wait(pltpu.get_barrier_semaphore(), jnp.where(jnp.logical_or(t == 1, t == 2), 2, 1) + levels + 1)
    announce(meet_sem, neighbours)
    gsum_one[...] = jnp.zeros_like(gsum_one)
    gsum_two[...] = jnp.zeros_like(gsum_two)
    for slot in range(2):

        @pl.when(section == 0)
        def _():
            fetch(slot, xs).wait()

        @pl.when(section == 1)
        def _():
            fetch(slot, dys).wait()

    def projected(target, left, right, first, left_at, each=None):
        here, there = span(first, half), span(first + left_at, half)

        def one(i, c):
            target[here, lanes(i, WIDE)] = times(left[there], right[:, lanes(i, WIDE)]).astype(BF16)
            if each:
                each(i)
            return c

        lax.fori_loop(0, wide, one, 0)

    def give_back(slot, now, line):
        @pl.when(now)
        def _():
            spares[...] = times(holder[span(slot * groups * spare, groups * spare)], y[...]).astype(BF16)
            give.start()

        def one(i, c):
            line.step(i)

            @pl.when(now)
            def _():
                give.step(i, give_lag)

            return c

        lax.fori_loop(0, line.steps, one, 0)

    def give_rest(now, line, begun):
        def one(i, c):
            line.step(i)

            @pl.when(now)
            def _():
                give.step(i - begun + give_lag, give_lag)

            return c

        lax.fori_loop(begun, max(line.steps, begun + give.steps(give_lag) - give_lag), one, 0)

    def given(slot, now):
        @pl.when(now)
        def _():
            give.finish()
            pltpu.make_async_copy(returned, back_out.at[span(slot * spare, spare)], io_sem.at[1]).start()
            pltpu.make_async_copy(returned, back_out.at[span(slot * spare, spare)], io_sem.at[1]).wait()

    def forward(slot, carry):
        base = slot * count
        whole = span(base, count)
        moved = (xs, 1)
        lines = []
        for k in range(4):
            first = (k % 2) * half
            scratch = list(line_scratch[k])
            if k < 2:
                lines.append(Line(first, quarter, pieces, part_one, xs, resid, scratch, at=(base, base, 0)))
            else:
                scratch += [forth_s.at[k - 2], forth_r.at[2 * slot + k - 2]]
                lines.append(
                    Line(first, quarter, pieces, part_two, resid, y, scratch, moved=moved, at=(base, 0, base))
                )
        one_a, one_b, two_a, two_b = lines
        gather = Gather(groups, count, kv.at[span(slot * keys, keys)], *gather_sems)
        two_a.receive()
        two_b.receive()
        normalize_into(normed, xs, gain_one, 0, count, source_at=base)

        @pl.when(slot == 0)
        def _():
            loads[0].wait()

        mine = span(slot * keys + lax.axis_index("dp") * count, count)
        middle = (q_heads + k_heads) * LANES
        value = times(normed[...], wqkv[:, q_heads * LANES : middle])
        for g in range(k_heads):
            here = slice(g * LANES, (g + 1) * LANES)
            kv[mine, here] = rolled(value[:, here], cosine[whole], sine[whole]).astype(BF16)
        kv[mine, k_heads * LANES :] = times(normed[...], wqkv[:, middle:]).astype(BF16)
        heard(meet_sem, neighbours)
        gather.start(levels - 1)
        for first in range(0, q_heads, 2):
            value = times(normed[...], wqkv[:, first * LANES : (first + 2) * LANES])
            for h in range(2):
                here = slice((first + h) * LANES, (first + h + 1) * LANES)
                q[whole, here] = rolled(
                    value[:, h * LANES : (h + 1) * LANES], cosine[whole], sine[whole]
                ).astype(BF16)
        for level in range(levels - 1, -1, -1):
            gather.arrive(level)
            if level:
                gather.start(level - 1)

        def attend(first, each=None):
            def one(i, c):
                h, b = i // blocks, lax.rem(i, blocks)
                g = h // repeat
                here = span(base + first + b * rows, rows)
                scores = with_transpose(q[here, lanes(h)], kv[span(slot * keys, keys), lanes(g)]) * scale
                code = kcode[slot]
                allowed = jnp.logical_and(code <= qcode[here], code >= qstart[here])
                scores = jnp.where(allowed, scores, negative)
                row_max = jnp.max(scores, axis=-1, keepdims=True)
                expo = jnp.exp(scores - row_max)
                row_total = jnp.sum(expo, axis=-1, keepdims=True)
                prob = (expo * (1.0 / row_total)).astype(BF16)
                mixed[here, lanes(h)] = times(prob, kv[span(slot * keys, keys), lanes(k_heads + g)]).astype(BF16)
                lse[span((slot * q_heads + h) * count + first + b * rows, rows)] = jnp.broadcast_to(
                    row_max + jnp.log(row_total), (rows, LANES)
                )
                if each:
                    each(i)
                return c

            lax.fori_loop(0, q_heads * blocks, one, 0)

        attend(0)

        @pl.when(slot == 0)
        def _():
            loads[1].wait()

        projected(part_one, mixed, wout, 0, base)
        one_a.start()
        attend(half)
        projected(part_one, mixed, wout, half, base)
        one_b.start()
        give_back(0, slot == 1, one_a)

        @pl.when(slot == 0)
        def _():
            for item in loads[2:]:
                item.wait()

        def hidden(first, each):
            here, there = span(first, half), span(base + first, half)
            normalize_into(normed, resid, gain_two, first, half, source_at=base)

            def one(i, c):
                columns = lanes(i, WIDE)
                gate_pre = times(normed[here], wgate[:, columns])
                up_pre = times(normed[here], wup[:, columns])
                gate[there, columns] = gate_pre.astype(BF16)
                up[there, columns] = up_pre.astype(BF16)
                act[there, columns] = (gate_pre * jax.nn.sigmoid(gate_pre) * up_pre).astype(BF16)
                each(i)
                return c

            lax.fori_loop(0, tiles, one, 0)

        hidden(0, one_b.step)
        projected(part_two, act, wdown, 0, base)
        two_a.start()
        give_rest(slot == 1, one_b, tiles)
        hidden(half, two_a.step)
        projected(part_two, act, wdown, half, base)
        two_b.start()
        run_steps(tiles, two_a.steps, (two_a.step, 0))
        run_steps(0, two_b.steps, (two_b.step, 0))
        out = pltpu.make_async_copy(y, y_out.at[whole], io_sem.at[0])
        out.start()
        gather.finish()
        for line in lines:
            line.finish()
        given(0, slot == 1)
        out.wait()
        announce(meet_sem, neighbours)
        return carry

    lax.fori_loop(0, 2, forward, 0)

    def backward(tick, carry):
        slot = 1 - tick
        base = slot * count
        whole = span(base, count)
        lines = []
        for k in range(4):
            first = (k % 2) * half
            scratch = list(line_scratch[k])
            if k < 2:
                norm = (resid, gain_two, gsum_two)
                lines.append(Line(first, quarter, pieces, part_one, dys, dresid, scratch, norm=norm, at=(base, base, 0)))
            else:
                scratch += [back_s.at[k - 2], back_r.at[2 * slot + k - 2]]
                norm = (xs, gain_one, gsum_one)
                lines.append(
                    Line(
                        first, quarter, pieces, part_two, dresid, y, scratch, norm=norm, moved=(dys, -1), at=(base, 0, base)
                    )
                )
        one_a, one_b, two_a, two_b = lines
        two_a.receive()
        two_b.receive()
        dkv[...] = jnp.zeros_like(dkv)
        heard(meet_sem, neighbours)

        def hidden(first, each=None):
            here = span(base + first, half)

            def one(i, c):
                columns = lanes(i, WIDE)
                d_act = with_transpose(dys[here], wdown[columns, :])
                gate_pre, up_pre = gate[here, columns].astype(F32), up[here, columns].astype(F32)
                sigma = jax.nn.sigmoid(gate_pre)
                d_silu = d_act * sigma
                dup[here, columns] = (d_silu * gate_pre).astype(BF16)
                dgate[here, columns] = (d_silu * up_pre * (1.0 + gate_pre * (1.0 - sigma))).astype(BF16)
                if each:
                    each(i)
                return c

            lax.fori_loop(0, tiles, one, 0)

        def back_hidden(first):
            here, there = span(first, half), span(base + first, half)

            def one(i, c):
                columns = lanes(i, WIDE)
                total = with_transpose(dgate[there], wgate[columns, :]) + with_transpose(dup[there], wup[columns, :])
                part_one[here, columns] = total.astype(BF16)
                return c

            lax.fori_loop(0, wide, one, 0)

        hidden(0)
        back_hidden(0)
        one_a.start()
        hidden(half)
        back_hidden(half)
        one_b.start()
        give_back(1, tick == 0, one_a)

        def attend(first, g, each=None):
            def one(i, c):
                h, n = g * repeat + i // blocks, lax.rem(i, blocks)
                here = span(base + first + n * rows, rows)
                near = span(first + n * rows, rows)
                k_rows = kv[span(slot * keys, keys), lanes(g)]
                scores = with_transpose(q[here, lanes(h)], k_rows) * scale
                code = kcode[slot]
                allowed = jnp.logical_and(code <= qcode[here], code >= qstart[here])
                known = lse[span((slot * q_heads + h) * count + first + n * rows, rows)][:, :1]
                prob = jnp.where(allowed, jnp.exp(scores - known), 0.0)
                dm = dmixed[near, lanes(h)]
                d_prob = with_transpose(dm, kv[span(slot * keys, keys), lanes(k_heads + g)])
                row_dot = jnp.sum(prob * d_prob, axis=-1, keepdims=True)
                d_scores = (prob * (d_prob - row_dot)).astype(BF16)
                d_query = times(d_scores, k_rows) * scale
                dqkv[here, lanes(h)] = rolled(d_query, cosine[here], -sine[here]).astype(BF16)
                dkv[lanes(g), :] += rows_contract(q[here, lanes(h)], d_scores) * scale
                dkv[lanes(k_heads + g), :] += rows_contract(dm, prob.astype(BF16))
                if each:
                    each(i)
                return c

            lax.fori_loop(0, repeat * blocks, one, 0)

        def mix(first):
            here, there = span(first, half), span(base + first, half)

            def one(h, c):
                dmixed[here, lanes(h)] = with_transpose(dresid[there], wout[lanes(h), :]).astype(BF16)
                return c

            lax.fori_loop(0, q_heads, one, 0)

        mix(0)
        turns = repeat * blocks
        for g in range(k_heads):
            attend(0, g, lambda i: one_b.step(g * turns + i))
        give_rest(tick == 0, one_b, k_heads * turns)
        mix(half)
        for g in range(k_heads):
            attend(half, g)

            shares[g][:, :LANES] = jnp.transpose(dkv[lanes(g), :]).astype(BF16)
            shares[g][:, LANES:] = jnp.transpose(dkv[lanes(k_heads + g), :]).astype(BF16)
            scatters[g].start()
        run_steps(0, scatters[0].steps(1), *[(functools.partial(lambda s, i: s.step(i, 1), s), 0) for s in scatters])
        for g in range(k_heads):
            dqkv[whole, lanes(q_heads + g)] = rolled(owns[g][:, :LANES], cosine[whole], -sine[whole]).astype(BF16)
            dqkv[whole, lanes(q_heads + k_heads + g)] = owns[g][:, LANES:].astype(BF16)

        def back(first, each=None):
            here, there = span(first, half), span(base + first, half)

            def one(i, c):
                columns = lanes(i, WIDE)
                part_two[here, columns] = with_transpose(dqkv[there], wqkv[columns, :]).astype(BF16)
                if each:
                    each(i)
                return c

            lax.fori_loop(0, wide, one, 0)

        back(0)
        two_a.start()
        back(half)
        two_b.start()
        run_steps(0, two_a.steps, (two_a.step, 0))
        run_steps(0, two_b.steps, (two_b.step, 0))
        out = pltpu.make_async_copy(y, dx_out.at[whole], io_sem.at[0])
        out.start()
        for line in lines:
            line.finish()
        for item in scatters:
            item.finish()
        given(1, tick == 0)
        out.wait()
        announce(meet_sem, neighbours)
        return carry

    lax.fori_loop(0, 1 + section, backward, 0)
    heard(meet_sem, neighbours)
    for k in range(2):
        Line(
            k * half,
            quarter,
            pieces,
            part_two,
            dresid,
            y,
            list(line_scratch[2 + k]) + [back_s.at[k], back_r.at[k]],
            moved=(dys, -1),
        ).receive()


def main_ticks(packed, spots, holder, weights, groups, q_heads, k_heads, cid):
    norm_one, wqkv, wout, norm_two, wgate, wup, wdown = weights
    count, width = packed.shape[0] // 2, packed.shape[1]
    hidden, keys = wgate.shape[1], groups * count
    pieces = 5
    vmem = pl.BlockSpec(memory_space=pltpu.VMEM)
    far = pl.BlockSpec(memory_space=pl.ANY)
    dma = pltpu.SemaphoreType.DMA

    def shape(columns, rows=2 * count, dtype=BF16):
        return jax.ShapeDtypeStruct((rows, columns), dtype)

    heads, both = q_heads * LANES, (q_heads + 2 * k_heads) * LANES
    spare = holder.shape[0] // (2 * groups)
    outs = [
        shape(width),
        shape(width),
        shape(width, 2 * spare),
        shape(width),
        shape(heads),
        shape(2 * k_heads * LANES, 2 * keys),
        shape(LANES, 2 * q_heads * count, F32),
        shape(heads),
        shape(width),
        shape(hidden),
        shape(hidden),
        shape(hidden),
        shape(width),
        shape(width),
        shape(hidden),
        shape(hidden),
        shape(both),
        shape(width, 1, F32),
        shape(width, 1, F32),
    ]
    far_weights = [wqkv, wout, wgate, wup, wdown]
    scratch = [pltpu.VMEM(item.shape, BF16) for item in far_weights]
    scratch += [pltpu.VMEM((count, width), BF16)] * 4 + [
        pltpu.VMEM((count, heads), BF16),
        pltpu.VMEM((2 * k_heads * LANES, keys), F32),
        dma((5,)),
        dma((2,)),
        pltpu.SemaphoreType.REGULAR((2 + dp_bits(groups),)),
    ]
    scratch += Gather.scratch(groups)
    for k in range(4):
        scratch += Line.scratch(quarter_rows(count), pieces, width, False)
    scratch += [dma((2, 2, pieces)), dma((4, 2, pieces))] * 2
    scratch += [pltpu.VMEM((groups * spare, width), BF16), pltpu.VMEM((spare, width), BF16)]
    scratch += OwnScatter.scratch(groups, spare, width, spare // 32, BF16)
    for _ in range(k_heads):
        scratch += [pltpu.VMEM((keys, 2 * LANES), BF16), pltpu.VMEM((count, 2 * LANES), F32)]
        scratch += Scatter.scratch(groups, count, 2 * LANES, 5, BF16)
    return pl.pallas_call(
        functools.partial(main_kernel, groups, q_heads, k_heads, pieces),
        out_shape=outs,
        in_specs=[far] + [vmem] * 8 + [far] * 5,
        out_specs=[far] * 3 + [vmem] * (len(outs) - 3),
        scratch_shapes=scratch,
        compiler_params=pltpu.CompilerParams(
            collective_id=cid, has_side_effects=True, vmem_limit_bytes=VMEM_LIMIT
        ),
        name="main_ticks",
    )(packed, *spots, norm_one[None], norm_two[None], holder, *far_weights)


def quarter_rows(count):
    return count // 4


def weight_job(target, left, right, i, block=256):
    here = lanes(i, block)
    target[here, :] = rows_contract(left[:, here], right[...]).astype(BF16)


def last_ffn_kernel(groups, pieces, chunks, *refs):
    refs = list(refs)

    def take(count):
        taken = refs[:count]
        del refs[:count]
        return taken

    gain, holder = take(2)
    sources = take(12)
    first_dresid, gsum, g_up, down_sum, gate_sum, returned = take(6)
    wdown, wgate, wup, dys, act, gate, up, dgate, dup, resid = kept = take(10)
    n2, part, g_down, g_gate, spares, dx, w_sem = take(7)
    (scratch,) = (take(12),)
    count, width = part.shape
    half = count // 2
    line_a, line_b = [
        Line(k * half, half // 2, pieces, part, dys, first_dresid, item, norm=(resid, gain, gsum))
        for k, item in enumerate((scratch, take(12)))
    ]
    down = OwnScatter(groups, width // groups, chunks, [g_down, down_sum] + take(OwnScatter.refs(groups)))
    gated = OwnScatter(groups, width // groups, chunks, [g_gate, gate_sum] + take(OwnScatter.refs(groups)))
    spare = returned.shape[0]
    give = OwnScatter(groups, spare, spare // 32, [spares, returned] + take(OwnScatter.refs(groups)))
    section = lax.axis_index("section")
    mine = section == 0
    tiles, wide, blocks = act.shape[1] // WIDE, width // WIDE, width // TILE

    def load(k):
        if k in (7, 8):
            return pltpu.make_async_copy(sources[k].at[count:], kept[k].at[count:], w_sem.at[k])
        return pltpu.make_async_copy(sources[k], kept[k], w_sem.at[k])

    lacks = [
        pltpu.make_async_copy(sources[7].at[:count], kept[7].at[:count], w_sem.at[10]),
        pltpu.make_async_copy(sources[8].at[:count], kept[8].at[:count], w_sem.at[11]),
        pltpu.make_async_copy(sources[10].at[:count], first_dresid, w_sem.at[12]),
    ]
    last_dx = pltpu.make_async_copy(sources[11].at[count:], dx, w_sem.at[13])
    loads = [load(k) for k in range(10)]
    for k in (3, 0, 5, 6, 1, 2):
        loads[k].start()
    last_dx.start()
    for k in (4, 9, 7, 8):
        loads[k].start()

    @pl.when(section > 0)
    def _():
        for item in lacks:
            item.start()

    Line.greet()
    for where, _ in down.links:
        greet(where)
    gsum[...] = jnp.zeros_like(gsum)
    line_a.enter(down.levels)
    for k in (3, 0, 5, 6):
        loads[k].wait()

    def hidden(first):
        here = pl.ds(first, half)

        def one(i, c):
            columns = lanes(i, WIDE)
            d_act = with_transpose(dys[here], wdown[columns, :])
            gate_pre, up_pre = gate[here, columns].astype(F32), up[here, columns].astype(F32)
            sigma = jax.nn.sigmoid(gate_pre)
            d_silu = d_act * sigma
            dup[here, columns] = (d_silu * gate_pre).astype(BF16)
            dgate[here, columns] = (d_silu * up_pre * (1.0 + gate_pre * (1.0 - sigma))).astype(BF16)
            return c

        lax.fori_loop(0, tiles, one, 0)

    def back(first):
        here = pl.ds(first, half)

        def one(i, c):
            columns = lanes(i, WIDE)
            total = with_transpose(dgate[here], wgate[columns, :]) + with_transpose(dup[here], wup[columns, :])
            part[here, columns] = total.astype(BF16)
            return c

        lax.fori_loop(0, wide, one, 0)

    @pl.when(mine)
    def _():
        hidden(0)

    loads[1].wait()
    loads[2].wait()

    @pl.when(mine)
    def _():
        back(0)
        line_a.start()

    last_dx.wait()
    spares[...] = times(holder[...], dx[...]).astype(BF16)
    give.start()

    @pl.when(mine)
    def _():
        hidden(half)
        back(half)
        line_b.start()

    for k in (4, 9, 7, 8):
        loads[k].wait()

    kinds = ((g_down, dys, act), (g_gate, n2, dgate), (g_up, n2, dup))

    def job(k):
        for which, (target, left, right) in enumerate(kinds):

            @pl.when(k // blocks == which)
            def _():
                weight_job(target, left, right, lax.rem(k, blocks))

    normalize_into(n2, resid, gain, 0, 2 * count)
    for k in range(2):
        job(k)

    @pl.when(section > 0)
    def _():
        lacks[0].wait()
        lacks[1].wait()

    lag = 4
    first_part = blocks - 2
    begin_down, begin_gate = first_part, first_part + blocks

    def step(i, c):
        @pl.when(mine)
        def _():
            line_a.step(i)
            line_b.step(i - line_a.steps)

        @pl.when(i + 2 < 3 * blocks)
        def _():
            job(i + 2)

        @pl.when(i == begin_down - 1)
        def _():
            down.start()

        @pl.when(i == begin_gate - 1)
        def _():
            gated.start()

        give.step(i, 6)
        down.step(i - begin_down, lag)
        gated.step(i - begin_gate, lag)
        return c

    ending = max(
        line_a.steps + line_b.steps, 3 * blocks - 2, begin_down + down.steps(lag), begin_gate + gated.steps(lag), give.steps(6)
    )
    lax.fori_loop(0, ending, step, 0)

    @pl.when(mine)
    def _():
        line_a.finish()
        line_b.finish()

    @pl.when(section > 0)
    def _():
        lacks[2].wait()

    give.finish()
    down.finish()
    gated.finish()


def last_ffn(known, holder, weights, groups, cid):
    norm_one, wqkv, wout, norm_two, wgate, wup, wdown = weights
    dys, act, gate, up, dgate, dup, resid, dresid, dx = known
    spare = holder.shape[0] // groups
    count, width = dys.shape[0] // 2, dys.shape[1]
    hidden = act.shape[1]
    pieces, chunks = 5, 8
    vmem = pl.BlockSpec(memory_space=pltpu.VMEM)
    far = pl.BlockSpec(memory_space=pl.ANY)
    sources = [wdown, wgate, wup, dys, act, gate, up, dgate, dup, resid]
    scratch = [pltpu.VMEM(item.shape, BF16) for item in sources]
    scratch += [
        pltpu.VMEM((2 * count, width), BF16),
        pltpu.VMEM((count, width), BF16),
        pltpu.VMEM((width, hidden), BF16),
        pltpu.VMEM((width, hidden), BF16),
        pltpu.VMEM((groups * spare, width), BF16),
        pltpu.VMEM((count, width), BF16),
        pltpu.SemaphoreType.DMA((14,)),
    ]
    scratch += Line.scratch(count // 4, pieces, width, False) * 2
    scratch += OwnScatter.scratch(groups, width // groups, hidden, chunks, BF16) * 2
    scratch += OwnScatter.scratch(groups, spare, width, spare // 32, BF16)
    return pl.pallas_call(
        functools.partial(last_ffn_kernel, groups, pieces, chunks),
        out_shape=[
            jax.ShapeDtypeStruct((count, width), BF16),
            jax.ShapeDtypeStruct((1, width), F32),
            jax.ShapeDtypeStruct((width, hidden), BF16),
            jax.ShapeDtypeStruct((width // groups, hidden), F32),
            jax.ShapeDtypeStruct((width // groups, hidden), F32),
            jax.ShapeDtypeStruct((spare, width), BF16),
        ],
        in_specs=[vmem] * 2 + [far] * 12,
        out_specs=[vmem] * 6,
        scratch_shapes=scratch,
        compiler_params=pltpu.CompilerParams(
            collective_id=cid, has_side_effects=True, vmem_limit_bytes=VMEM_LIMIT
        ),
        name="last_ffn",
    )(norm_two[None], holder, *sources, dresid, dx)


def last_attn_kernel(groups, q_heads, k_heads, pieces, chunks, spare_chunks, *refs):
    refs = list(refs)

    def take(count):
        taken = refs[:count]
        del refs[:count]
        return taken

    cosine, sine, qcode, qstart, kcode, gain, dresid, holder, gains, spread_q, spread_k, spread_v, spread_o = take(13)
    sources = take(10)
    (dx_known,) = take(1)
    dx, returned, gains_out, up_sum, attn_sum = take(5)
    wout, wqkv, x, q, kv, lse, mixed, dqkv, other_dresid, g_up = kept = take(10)
    part, dmixed, dkv, n1, g_attn, spares, gsum, gains_own, gains_all, gains_sum, w_sem, g_s, g_r = take(13)
    levels = dp_bits(groups)
    count, width = part.shape
    half = count // 2
    keys = kv.shape[0]
    shares, owns, scatters = [], [], []
    for g in range(k_heads):
        share, own = take(2)
        shares.append(share)
        owns.append(own)
        scatters.append(OwnScatter(groups, count, 5, [share, own] + take(OwnScatter.refs(groups))))
    block = width // groups
    up_task, attn_task = [
        OwnScatter(groups, block, chunks, [value, total] + take(OwnScatter.refs(groups)))
        for value, total in ((g_up, up_sum), (g_attn, attn_sum))
    ]
    spare = spares.shape[0] // groups
    back_task = OwnScatter(groups, spare, spare_chunks, [spares, returned] + take(OwnScatter.refs(groups)))
    small = OwnScatter(groups, 8, 1, [gains_sum, gains_out] + take(OwnScatter.refs(groups)))
    line_a, line_b = [
        Line(k * half, half // 2, pieces, part, dresid, dx, take(12), norm=(x, gain, gsum)) for k in range(2)
    ]
    section, t = lax.axis_index("section"), lax.axis_index("tensor")
    mine = section == 0
    order = [9, 0, 3, 4, 5, 1, 2, 6, 7, 8]
    loads = [pltpu.make_async_copy(sources[k], kept[k], w_sem.at[k]) for k in range(10)]
    for k in order:
        loads[k].start()
    known = pltpu.make_async_copy(dx_known.at[:count], dx, w_sem.at[11])

    @pl.when(section > 0)
    def _():
        known.start()

    for k in range(1, 4):
        greet({"tensor": lax.rem(t + k, 4)})
    for where, _ in up_task.links:
        greet(where)
    gsum[...] = jnp.zeros_like(gsum)
    dkv[...] = jnp.zeros_like(dkv)
    pl.semaphore_wait(pltpu.get_barrier_semaphore(), 3 + levels)
    loads[9].wait()
    up_task.start()
    for k in order[1:]:
        loads[k].wait()

    wide, jobs = width // WIDE, width // TILE
    repeat = q_heads // k_heads
    rows = block_rows(keys)
    blocks = half // rows
    turns = repeat * blocks
    scale = HD ** (-0.5)
    lag = 6

    begun = k_heads * turns

    def early(i):
        @pl.when(lax.rem(i, 2) == 0)
        def _():
            up_task.step(i // 2, lag)

    def sums(i):
        up_task.step(i, lag)

    def mix(first):
        here = pl.ds(first, half)

        def one(h, c):
            dmixed[here, lanes(h)] = with_transpose(dresid[here], wout[lanes(h), :]).astype(BF16)
            return c

        lax.fori_loop(0, q_heads, one, 0)

    def attend(first, g, each):
        def one(i, c):
            h, n = g * repeat + i // blocks, lax.rem(i, blocks)
            here = pl.ds(pl.multiple_of(first + n * rows, rows), rows)
            scores, allowed = score_rows(q, kv, h, g, here, qcode, qstart, kcode)
            there = pl.ds(pl.multiple_of(h * count + first + n * rows, rows), rows)
            prob = jnp.where(allowed, jnp.exp(scores - lse[there][:, :1]), 0.0)
            dm = dmixed[here, lanes(h)]
            d_prob = with_transpose(dm, kv[:, lanes(k_heads + g)])
            row_dot = jnp.sum(prob * d_prob, axis=-1, keepdims=True)
            d_scores = (prob * (d_prob - row_dot)).astype(BF16)
            d_query = times(d_scores, kv[:, lanes(g)]) * scale
            dqkv[here, lanes(h)] = rolled(d_query, cosine[here], -sine[here]).astype(BF16)
            dkv[lanes(g), :] += rows_contract(q[here, lanes(h)], d_scores) * scale
            dkv[lanes(k_heads + g), :] += rows_contract(dm, prob.astype(BF16))
            each(i)
            return c

        lax.fori_loop(0, turns, one, 0)

    def back(first):
        here = pl.ds(first, half)

        def one(i, c):
            columns = lanes(i, WIDE)
            part[here, columns] = with_transpose(dqkv[here], wqkv[columns, :]).astype(BF16)
            return c

        lax.fori_loop(0, wide, one, 0)

    @pl.when(mine)
    def _():
        mix(0)
        mix(half)
        for g in range(k_heads):
            for first in (0, half):
                at = 2 * g * turns + (turns if first else 0)
                attend(first, g, lambda i: early(at + i))

            shares[g][:, :LANES] = jnp.transpose(dkv[lanes(g), :]).astype(BF16)
            shares[g][:, LANES:] = jnp.transpose(dkv[lanes(k_heads + g), :]).astype(BF16)
            scatters[g].start()
        run_steps(0, scatters[0].steps(1), *[(functools.partial(lambda s, i: s.step(i, 1), s), 0) for s in scatters])
        for g in range(k_heads):
            dqkv[:count, lanes(q_heads + g)] = rolled(owns[g][:, :LANES], cosine[...], -sine[...]).astype(BF16)
            dqkv[:count, lanes(q_heads + k_heads + g)] = owns[g][:, LANES:].astype(BF16)
        back(0)
        line_a.start()
        back(half)
        line_b.start()

    @pl.when(section > 0)
    def _():
        run_steps(0, begun, (sums, 0))
        known.wait()

    normalize_into(n1, x, gain, 0, 2 * count)
    ends = [0]
    for item in (spread_q, spread_k, spread_v, spread_o):
        ends.append(ends[-1] + item.shape[0])
    starts = [0, q_heads, q_heads + k_heads, q_heads + 2 * k_heads]
    plain = [
        with_transpose(dqkv[:, a * LANES : b * LANES], item[...]).astype(BF16)
        for a, b, item in zip(starts, starts[1:], (spread_q, spread_k, spread_v))
    ]
    plain = jnp.concatenate(plain, axis=1)
    plain_mixed = with_transpose(mixed[...], spread_o[...]).astype(BF16)
    other_dresid[:count] = dresid[...]

    def job(i, c):
        here = lanes(i, TILE)
        g_attn[here, : ends[3]] = rows_contract(n1[:, here], plain).astype(BF16)
        g_attn[here, ends[3] :] = rows_contract(other_dresid[:, here], plain_mixed).astype(BF16)
        return c

    lax.fori_loop(0, jobs, job, 0)
    attn_task.start()

    def spread(k):
        return remote(gains_own, gains_all.at[k - 1], g_s.at[k - 1], g_r.at[k - 1], {"tensor": lax.rem(t + k, 4)})

    def steps(line, at):
        def one(i, c):
            @pl.when(mine)
            def _():
                line.step(i)

            sums(begun + at + i)
            attn_task.step(at + i - 2, lag)
            return c

        lax.fori_loop(0, line.steps, one, 0)

    steps(line_a, 0)
    steps(line_b, line_a.steps)
    past = line_a.steps + line_b.steps
    spares[...] = times(holder[...], dx[...]).astype(BF16)
    back_task.start()
    section_one = jnp.where(mine, 1.0, 0.0)
    gains_own[...] = gains[...]
    gains_own[:1] = gains[:1] + gsum[...] * section_one
    for k in range(1, 4):
        spread(k).start()
    for k in range(1, 4):
        spread(k).wait()
    total = gains_own[...] + gains_all[0] + gains_all[1] + gains_all[2]
    part_width = width // groups
    for d in range(groups):
        gains_sum[8 * d : 8 * d + 8, :] = total[:, d * part_width : (d + 1) * part_width]
    small.start()
    ending = max(
        up_task.steps(lag) - begun - past,
        attn_task.steps(lag) + 2 - past,
        back_task.steps(2),
        small.steps(1),
    )

    def close(i, c):
        sums(begun + past + i)
        attn_task.step(past + i - 2, lag)
        small.step(i, 1)
        back_task.step(i, 2)
        return c

    lax.fori_loop(0, ending, close, 0)

    @pl.when(mine)
    def _():
        line_a.finish()
        line_b.finish()
        for item in scatters:
            item.finish()

    for item in (up_task, attn_task, back_task, small):
        item.finish()


def last_attn(known, spots, dresid, dx, holder, gains, spreads, grads, weights, groups, q_heads, k_heads, cid):
    norm_one, wqkv, wout, norm_two, wgate, wup, wdown = weights
    x, q, kv, lse, mixed, dqkv, other_dresid = known
    count, width = dresid.shape
    keys = kv.shape[0]
    spare = holder.shape[0] // groups
    pieces, chunks, spare_chunks = 5, 8, spare // 32
    vmem = pl.BlockSpec(memory_space=pltpu.VMEM)
    far = pl.BlockSpec(memory_space=pl.ANY)
    dma = pltpu.SemaphoreType.DMA
    sources = [wout, wqkv, x, q, kv, lse, mixed, dqkv, other_dresid, *grads]
    attn_width = sum(item.shape[0] for item in spreads)
    block = width // groups
    scratch = [pltpu.VMEM(item.shape, item.dtype) for item in sources]
    scratch += [
        pltpu.VMEM((count, width), BF16),
        pltpu.VMEM(q.shape, BF16),
        pltpu.VMEM((kv.shape[1], keys), F32),
        pltpu.VMEM((2 * count, width), BF16),
        pltpu.VMEM((width, attn_width), BF16),
        pltpu.VMEM((groups * spare, width), BF16),
        pltpu.VMEM((1, width), F32),
        pltpu.VMEM(gains.shape, F32),
        pltpu.VMEM((3,) + gains.shape, F32),
        pltpu.VMEM((groups * 8, block), F32),
        dma((12,)),
        dma((3,)),
        dma((3,)),
    ]
    for _ in range(k_heads):
        scratch += [pltpu.VMEM((keys, 2 * LANES), BF16), pltpu.VMEM((count, 2 * LANES), F32)]
        scratch += OwnScatter.scratch(groups, count, 2 * LANES, 5, BF16)
    for columns in (grads[0].shape[1], attn_width):
        scratch += OwnScatter.scratch(groups, block, columns, chunks, BF16)
    scratch += OwnScatter.scratch(groups, spare, width, spare_chunks, BF16)
    scratch += OwnScatter.scratch(groups, 8, block, 1, F32)
    scratch += Line.scratch(count // 4, pieces, width, False) * 2
    return pl.pallas_call(
        functools.partial(last_attn_kernel, groups, q_heads, k_heads, pieces, chunks, spare_chunks),
        out_shape=[
            jax.ShapeDtypeStruct((count, width), BF16),
            jax.ShapeDtypeStruct((spare, width), BF16),
            jax.ShapeDtypeStruct((8, block), F32),
            jax.ShapeDtypeStruct((block, grads[0].shape[1]), F32),
            jax.ShapeDtypeStruct((block, attn_width), F32),
        ],
        in_specs=[vmem] * 13 + [far] * 11,
        out_specs=[vmem] * 5,
        scratch_shapes=scratch,
        compiler_params=pltpu.CompilerParams(
            collective_id=cid, has_side_effects=True, vmem_limit_bytes=VMEM_LIMIT
        ),
        name="last_attn",
    )(*spots, norm_one[None], dresid, holder, gains, *spreads, *sources, dx)


def rope_tables(pos):
    half_width = HD // 2
    inverse = rope_base ** (-(jnp.arange(half_width, dtype=F32) * 2.0 / HD))
    angle = pos.astype(F32)[:, None] * inverse[None, :]
    blank = jnp.zeros((pos.shape[0], LANES // 2 - half_width), F32)
    cosine, sine = jnp.cos(angle), jnp.sin(angle)
    return (
        jnp.concatenate([cosine, blank, cosine, blank], axis=1),
        jnp.concatenate([-sine, blank, sine, blank], axis=1),
    )


def spreader(heads, turned):
    feature = jnp.arange(HD)
    place = jnp.where(feature < HD // 2, feature, feature - HD // 2 + LANES // 2) if turned else feature
    lane = (jnp.arange(heads)[:, None] * LANES + place[None, :]).reshape(-1)
    return (lane[:, None] == jnp.arange(heads * LANES)[None, :]).astype(BF16)


def slots_of(lens, count):
    groups = lens.shape[0]
    kept = jnp.minimum(lens, count)
    free, extra = count - kept, lens - kept
    free_off = jnp.cumsum(free) - free
    extra_end = jnp.cumsum(extra)
    slot = jnp.arange(count)
    own = slot[None, :] < kept[:, None]
    index = free_off[:, None] + slot[None, :] - kept[:, None]
    source = jnp.sum(index[:, :, None] >= extra_end[None, None, :], axis=-1)
    begins = jnp.sum(jnp.where(index[:, :, None] >= extra_end[None, None, :], extra[None, None, :], 0), axis=-1)
    seq = jnp.where(own, jnp.arange(groups)[:, None], source)
    pos = jnp.where(own, slot[None, :], count + index - begins)
    return seq, pos, own


def on_device(
    inputs,
    cotangent,
    lengths,
    norm_attn,
    w_query,
    w_key,
    w_value,
    w_out,
    norm_ffn,
    w_gate,
    w_up,
    w_down,
):
    first = lax.axis_index("section") == 0
    me = lax.axis_index("dp")
    groups = lax.axis_size("dp")
    micro, seq_len, width = inputs.shape[0], inputs.shape[2], inputs.shape[3]
    count = seq_len * 5 // 8
    spare = seq_len - count
    q_heads, k_heads = w_query.shape[2] // HD, w_key.shape[2] // HD
    spread_q, spread_k = spreader(q_heads, True), spreader(k_heads, True)
    spread_v, spread_o = spreader(k_heads, False), spreader(q_heads, False)
    wqkv = jnp.concatenate(
        [times(w_query[0], spread_q), times(w_key[0], spread_k), times(w_value[0], spread_v)], axis=1
    ).astype(BF16)
    wout = rows_contract(spread_o, w_out[0]).astype(BF16)
    weights = (norm_attn[0], wqkv, wout, norm_ffn[0], w_gate[0], w_up[0], w_down[0])

    source = jnp.where(first, inputs[:, 0], cotangent[:, 0])
    length_rows = jnp.broadcast_to(lengths[:, 0].astype(F32)[:, None], (micro, 128))
    length_rows = jnp.concatenate([length_rows, jnp.zeros((8 - micro, 128), F32)], axis=0)
    first_extra, length_all = gather_rows([source[0, count:], length_rows], groups, 4)
    lens = length_all.reshape(groups, 8, 128)[:, :micro, 0].T.astype(jnp.int32)
    packed, slots = [], []
    for b in range(micro):
        seq, pos, own = slots_of(lens[b], count)
        slots.append((seq, pos))
        extra = first_extra if b == 0 else lax.all_gather(source[b, count:], "dp", axis=0, tiled=True)
        wanted = seq[me] * spare + pos[me] - count
        chosen = jnp.logical_and(jnp.arange(groups * spare)[None, :] == wanted[:, None], ~own[me][:, None])
        brought = jnp.dot(chosen.astype(BF16), extra, preferred_element_type=F32).astype(BF16)
        packed.append(jnp.where(own[me][:, None], source[b, :count], brought))

    def spots_of(b):
        seq, pos = slots[b]
        code = seq * seq_len + pos
        return rope_tables(pos[me]) + (code[me][:, None], (seq[me] * seq_len)[:, None], code.reshape(1, -1))

    spots = [spots_of(b) for b in range(micro)]

    def holder(b):
        seq, pos = slots[b]
        row = jnp.arange(groups * spare)[:, None]
        return jnp.logical_and(row == seq[me][None, :] * spare + pos[me][None, :] - count, pos[me][None, :] >= count)

    def spread(rows, b):
        return jnp.dot(holder(b).astype(BF16), rows, preferred_element_type=F32).astype(BF16)

    def unpack(rows, back, b, through):
        live = (jnp.arange(seq_len) < lens[b, me])[:, None]
        return jnp.where(live, jnp.concatenate([rows, back], axis=0), through)

    def come_back(rows, b):
        return lax.psum_scatter(spread(rows, b), "dp", scatter_dimension=0, tiled=True)

    norm_one, norm_two = weights[0], weights[3]
    all_in_one = micro == 2 and groups * count <= 2048
    empty = jnp.zeros((count, width), BF16)

    def spots_at(tick):
        early, late = spots[min(tick, micro - 1)], spots[max(tick - 1, 0)]
        return tuple(jnp.where(first, a, b) for a, b in zip(early, late))

    grads_in, before, gain_sums = [], [], []
    if all_in_one:
        joined = [jnp.concatenate(items, axis=0) for items in zip(*spots)]
        joined[4] = joined[4][:, None]
        held = jnp.concatenate([holder(b) for b in range(micro)], axis=0).astype(BF16)
        y, dx, y_back, x, q, kv, lse, mixed, resid, gate, up, act, dy, d_resid, d_gate, d_up, d_qkv, gain_one, gain_two = main_ticks(
            jnp.concatenate(packed, axis=0), joined, held, weights, groups, q_heads, k_heads, 0
        )
        results = [y[:count], y[count:]]
        first_dresid, gain_last, grad_up, grad_down, grad_gate, back_last = last_ffn(
            (dy, act, gate, up, d_gate, d_up, resid, d_resid, dx), held[groups * spare :], weights, groups, 1
        )
        gain_last = jnp.where(first, gain_last, jnp.zeros_like(gain_last))
        gains = jnp.concatenate([gain_one, gain_two + gain_last, jnp.zeros((6, width), F32)], axis=0)
        last_dx, back_first, gains, grad_up, grad_attn = last_attn(
            (x, q[:count], kv[: groups * count], lse[: q_heads * count], mixed, d_qkv, d_resid),
            spots[0],
            first_dresid,
            dx,
            held[: groups * spare],
            gains,
            (spread_q, spread_k, spread_v, spread_o),
            (grad_up,),
            weights,
            groups,
            q_heads,
            k_heads,
            2,
        )
        grads_at = [last_dx, dx[count:]]

    else:
        arriving = empty
        results, saved = [], []
        for tick in range(micro + 1):
            stream = jnp.where(first, packed[tick] if tick < micro else empty, arriving)
            result, arriving, kept = forward_tick(stream, spots_at(tick), weights, groups, q_heads, k_heads, 0)
            results.append(result)
            saved.append(kept)
        results = [jnp.where(first, results[b], results[b + 1]) for b in range(micro)]
        arriving = empty
        for tick in range(micro):
            kept = saved[micro - tick]
            incoming = jnp.where(first, arriving, packed[micro - 1 - tick])
            d_resid, gain_two, d_gate, d_up = back_ffn(incoming, kept, weights, 1)
            d_stream, gain_one, d_qkv, arriving = back_attn(
                d_resid, kept, spots_at(micro - tick), weights, groups, q_heads, k_heads, 2, -1
            )
            before.append((kept[5], d_gate, d_up, incoming, kept[8], kept[0], d_qkv, d_resid, kept[4]))
            grads_in.append(d_stream)
            gain_sums.append(jnp.concatenate([gain_one, gain_two], axis=0))
        kept_last = saved[0]
        last_in, last_spots = jnp.where(first, arriving, empty), spots_at(0)
        grads_at = [grads_in[micro - 1 - b] if b == 0 else jnp.where(first, grads_in[micro - b], grads_in[micro - 1 - b]) for b in range(micro)]

        def all_rows(now, index):
            old = [item[index] for item in before]
            return jnp.concatenate([jnp.where(first, now, old[0])] + old[1:], axis=0)

        x, mixed, resid, act = kept_last[0], kept_last[4], kept_last[5], kept_last[8]
        d_resid, gain_two, d_gate, d_up = back_ffn(last_in, kept_last, weights, 1)
        n2 = normalize(all_rows(resid, 0), norm_two)
        grad_gate = rows_contract(n2, all_rows(d_gate, 1)).astype(BF16)
        grad_up = rows_contract(n2, all_rows(d_up, 2)).astype(BF16)
        grad_down = rows_contract(all_rows(last_in, 3), all_rows(act, 4)).astype(BF16)
        ffn_grads = (grad_gate, grad_up, grad_down)
        beside = len(ffn_grads) if groups * count <= 2048 else 1
        d_stream, gain_one, d_qkv, *ffn_sums = back_attn(
            d_resid, kept_last, last_spots, weights, groups, q_heads, k_heads, 3, 0, sums=ffn_grads[:beside]
        )
        n1 = normalize(all_rows(x, 5), norm_one)
        back_spread = [(spread_q, 0, q_heads), (spread_k, q_heads, k_heads), (spread_v, q_heads + k_heads, k_heads)]
        dqkv = all_rows(d_qkv, 6)
        dqkv = jnp.concatenate(
            [with_transpose(dqkv[:, i * LANES : (i + n) * LANES], item) for item, i, n in back_spread], axis=1
        ).astype(BF16)
        mix = with_transpose(all_rows(mixed, 8), spread_o).astype(BF16)
        grad_attn = jnp.concatenate(
            [rows_contract(n1, dqkv).astype(BF16), rows_contract(all_rows(d_resid, 7), mix).astype(BF16)], axis=1
        )
        grads_at[0] = jnp.where(first, d_stream, grads_at[0])
        last_gains = jnp.concatenate([gain_one, gain_two], axis=0)
        gain_sums.append(jnp.where(first, last_gains, jnp.zeros_like(last_gains)))

        gains = sum(gain_sums[1:], gain_sums[0])
        gains = jnp.concatenate([gains, jnp.zeros((6, width), F32)], axis=0)
        gains = gains.reshape(8, groups, -1).transpose(1, 0, 2).reshape(groups * 8, -1)

    acts = []
    for b in range(micro):
        rows = results[b]
        back = y_back[b * spare : (b + 1) * spare] if all_in_one else come_back(rows, b)
        acts.append(unpack(rows, back, b, inputs[b, 0]))
    backs = []
    for b in range(micro):
        rows = grads_at[b]
        if all_in_one:
            back = back_first if b == 0 else back_last
        elif b == 0:
            back, gains, grad_attn, *rest = return_rows(
                spread(rows, b), gains, (grad_attn,) + ffn_grads[beside:], groups, 5, spare // 16
            )
            grad_gate, grad_up, grad_down = ffn_sums + rest
        else:
            back = come_back(rows, b)
        backs.append(unpack(rows, back, b, cotangent[b, 0]))
    acts, backs = jnp.stack(acts), jnp.stack(backs)
    ends = [0]
    for item in (w_query, w_key, w_value, w_query):
        ends.append(ends[-1] + item.shape[2])
    grad_query, grad_key, grad_value, grad_out = (grad_attn[:, a:b] for a, b in zip(ends, ends[1:]))
    final = (
        gains[0],
        grad_query,
        grad_key,
        grad_value,
        grad_out.T,
        gains[1],
        grad_gate,
        grad_up,
        grad_down.T,
    )
    return (acts[None, :, None], backs[None, :, None]) + tuple(item[None] for item in final)


def solution(mesh):
    placed = (
        P(None, "dp", None, None),
        P(None, "dp", None, None),
        P(None, "dp"),
        P("section", None),
        P("section", None, "tensor"),
        P("section", None, "tensor"),
        P("section", None, "tensor"),
        P("section", "tensor", None),
        P("section", None),
        P("section", None, "tensor"),
        P("section", None, "tensor"),
        P("section", "tensor", None),
    )
    return jax.shard_map(
        on_device,
        mesh=mesh,
        in_specs=placed,
        out_specs=(
            P("section", None, "dp", None, None),
            P("section", None, "dp", None, None),
            P("section", "dp"),
            P("section", "dp", "tensor"),
            P("section", "dp", "tensor"),
            P("section", "dp", "tensor"),
            P("section", "tensor", "dp"),
            P("section", "dp"),
            P("section", "dp", "tensor"),
            P("section", "dp", "tensor"),
            P("section", "tensor", "dp"),
        ),
        check_vma=False,
    )
```

```python
import functools

import jax
import jax.numpy as jnp
from jax import lax
from jax.experimental import pallas as pl
from jax.experimental.pallas import tpu as pltpu
from jax.sharding import PartitionSpec as P

HD = 96

epsilon = 1e-05
rope_base = 100000.0
negative = -1e30
MESH = pl.DeviceIdType.MESH
F32 = jnp.float32
BF16 = jnp.bfloat16


def remote(src, dst, s_sem, r_sem, where):
    return pltpu.make_async_remote_copy(
        src_ref=src, dst_ref=dst, send_sem=s_sem, recv_sem=r_sem, device_id=where, device_id_type=MESH
    )


def greet(where):
    pl.semaphore_signal(pltpu.get_barrier_semaphore(), inc=1, device_id=where, device_id_type=MESH)


def dp_bits(groups):
    return groups.bit_length() - 1


def dp_partner(level):
    me = lax.axis_index("dp")
    bit = lax.rem(me // (1 << level), 2)
    return {"dp": me + (1 - 2 * bit) * (1 << level)}, bit


class Scatter:
    def __init__(self, groups, rows, chunks, refs):
        self.levels = dp_bits(groups)
        self.groups, self.rows, self.chunks, self.size = groups, rows, chunks, rows // chunks
        self.value, self.out = refs[0], refs[1]
        m = self.levels
        self.arrive = refs[2 : 2 + m]
        self.held = refs[2 + m : 1 + 2 * m]
        self.s_sem = refs[1 + 2 * m : 1 + 3 * m]
        self.r_sem = refs[1 + 3 * m : 1 + 4 * m]
        self.links = [dp_partner(k) for k in range(m)]

    @staticmethod
    def scratch(groups, rows, width, chunks, dtype):
        m = dp_bits(groups)
        sizes = [groups >> (k + 1) for k in range(m)]
        return (
            [pltpu.VMEM((size * rows, width), dtype) for size in sizes]
            + [pltpu.VMEM((size * rows, width), dtype) for size in sizes[:-1]]
            + [pltpu.SemaphoreType.DMA((size, chunks)) for size in sizes] * 2
        )

    def at(self, block, c):
        return pl.ds(pl.multiple_of(block * self.rows + c * self.size, self.size), self.size)

    def copy(self, level, slot, c):
        where, bit = self.links[level]
        source = self.value if level == 0 else self.held[level - 1]
        return remote(
            source.at[self.at(2 * slot + 1 - bit, c)],
            self.arrive[level].at[self.at(slot, c)],
            self.s_sem[level].at[slot, c],
            self.r_sem[level].at[slot, c],
            where,
        )

    def order(self, level):
        count = self.groups >> (level + 1)
        if count == 1:
            return [(0, False)]
        bit = self.links[level + 1][1]
        return [(2 * i + 1 - bit, True) for i in range(count // 2)] + [(2 * i + bit, False) for i in range(count // 2)]

    def start(self):
        def one(c, carry):
            for slot, _ in self.order(0):
                self.copy(0, slot, c).start()
            return carry

        lax.fori_loop(0, self.chunks, one, 0)

    def step(self, i, lag):
        for level in range(self.levels):
            c = i - level * lag

            @pl.when(jnp.logical_and(c >= 0, c < self.chunks))
            def _():
                bit = self.links[level][1]
                source = self.value if level == 0 else self.held[level - 1]
                for slot, goes in self.order(level):
                    self.copy(level, slot, c).wait_recv()
                    here = self.at(slot, c)
                    total = source[self.at(2 * slot + bit, c)].astype(F32) + self.arrive[level][here].astype(F32)
                    if level == self.levels - 1:
                        self.out[here] = total.astype(self.out.dtype)
                    else:
                        self.held[level][here] = total.astype(self.held[level].dtype)
                        if goes:
                            self.copy(level + 1, slot // 2, c).start()

    def steps(self, lag):
        return self.chunks + (self.levels - 1) * lag

    def finish(self):
        def one(c, carry):
            for level in range(self.levels):
                for slot in range(self.groups >> (level + 1)):
                    self.copy(level, slot, c).wait_send()
            return carry

        lax.fori_loop(0, self.chunks, one, 0)


def return_kernel(groups, rows, chunks, plans, *refs):
    refs = list(refs)

    def take(count):
        taken = refs[:count]
        del refs[:count]
        return taken

    m = dp_bits(groups)
    count = 4 * m - 1
    value, gains = take(2)
    grads = take(len(plans))
    out, gains_out = take(2)
    totals = take(len(plans))
    gains_all, gains_sum, g_s, g_r = take(4)
    task = Scatter(groups, rows, chunks, [value, out] + take(count))
    small = Scatter(groups, 8, 1, [gains_sum, gains_out] + take(count))
    large = [
        Scatter(groups, block, parts, [grad, total] + take(count))
        for (block, parts), grad, total in zip(plans, grads, totals)
    ]
    t = lax.axis_index("tensor")
    for where, _ in task.links:
        greet(where)
    for k in range(1, 4):
        greet({"tensor": lax.rem(t + k, 4)})
    pl.semaphore_wait(pltpu.get_barrier_semaphore(), m + 3)

    def spread(k):
        return remote(gains, gains_all.at[k - 1], g_s.at[k - 1], g_r.at[k - 1], {"tensor": lax.rem(t + k, 4)})

    for k in range(1, 4):
        spread(k).start()
    task.start()
    for item in large:
        item.start()
    for k in range(1, 4):
        spread(k).wait()
    gains_sum[...] = gains[...] + gains_all[0] + gains_all[1] + gains_all[2]
    small.start()

    def body(i, c):
        small.step(i, 1)
        task.step(i, 2)
        for item in large:
            item.step(i, 4)
        return c

    lax.fori_loop(0, max([task.steps(2), small.steps(1)] + [item.steps(4) for item in large]), body, 0)
    small.finish()
    task.finish()
    for item in large:
        item.finish()


def return_rows(value, gains, grads, groups, cid, chunks):
    rows, width = value.shape[0] // groups, value.shape[1]
    vmem = pl.BlockSpec(memory_space=pltpu.VMEM)
    part = gains.shape[1]
    plans, outs = [], [jax.ShapeDtypeStruct((rows, width), BF16), jax.ShapeDtypeStruct((8, part), F32)]
    scratch = [
        pltpu.VMEM((3,) + gains.shape, F32),
        pltpu.VMEM(gains.shape, F32),
        pltpu.SemaphoreType.DMA((3,)),
        pltpu.SemaphoreType.DMA((3,)),
    ]
    scratch += Scatter.scratch(groups, rows, width, chunks, BF16) + Scatter.scratch(groups, 8, part, 1, F32)
    for grad in grads:
        block = grad.shape[0] // groups
        plans.append((block, max(1, block // 48)))
        outs.append(jax.ShapeDtypeStruct((block, grad.shape[1]), F32))
        scratch += Scatter.scratch(groups, block, grad.shape[1], plans[-1][1], BF16)
    return pl.pallas_call(
        functools.partial(return_kernel, groups, rows, chunks, plans),
        out_shape=outs,
        in_specs=[vmem] * (2 + len(grads)),
        out_specs=[vmem] * len(outs),
        scratch_shapes=scratch,
        compiler_params=pltpu.CompilerParams(
            collective_id=cid, has_side_effects=True, vmem_limit_bytes=VMEM_LIMIT
        ),
        name="return_%d" % cid,
    )(value, gains, *grads)


def gather_kernel(groups, count, *refs):
    values, outs = refs[:count], refs[count : 2 * count]
    s_sem, r_sem, own = refs[2 * count :]
    m = dp_bits(groups)
    me = lax.axis_index("dp")
    links = [dp_partner(k) for k in range(m)]
    for where, _ in links:
        greet(where)
    pl.semaphore_wait(pltpu.get_barrier_semaphore(), m)

    def place(a, block):
        rows = values[a].shape[0]
        return outs[a].at[pl.ds(pl.multiple_of(block * rows, rows), rows)]

    def copy(a, level, i, mine):
        where, bit = links[level]
        low = lax.rem(me, 1 << (level + 1))
        if not mine:
            low = low + (1 - 2 * bit) * (1 << level)
        block = i * (1 << (level + 1)) + low
        return remote(place(a, block), place(a, block), s_sem.at[a, level, i], r_sem.at[a, level, i], where)

    locals_ = [pltpu.make_async_copy(values[a], place(a, me), own.at[a]) for a in range(count)]
    for item in locals_:
        item.start()
    for item in locals_:
        item.wait()
    for level in reversed(range(m)):
        for i in range(groups >> (level + 1)):
            for a in range(count):
                copy(a, level, i, True).start()
        for i in range(groups >> (level + 1)):
            for a in range(count):
                copy(a, level, i, False).wait_recv()
    for level in range(m):
        for i in range(groups >> (level + 1)):
            for a in range(count):
                copy(a, level, i, True).wait_send()


def gather_rows(values, groups, cid):
    vmem = pl.BlockSpec(memory_space=pltpu.VMEM)
    m, count = dp_bits(groups), len(values)
    dma = pltpu.SemaphoreType.DMA
    return pl.pallas_call(
        functools.partial(gather_kernel, groups, count),
        out_shape=[jax.ShapeDtypeStruct((groups * v.shape[0], v.shape[1]), v.dtype) for v in values],
        in_specs=[vmem] * count,
        out_specs=[vmem] * count,
        scratch_shapes=[dma((count, m, groups // 2)), dma((count, m, groups // 2)), dma((count,))],
        compiler_params=pltpu.CompilerParams(
            collective_id=cid, has_side_effects=True, vmem_limit_bytes=48 * 2**20
        ),
        name="gather_%d" % cid,
    )(*values)


class OwnScatter(Scatter):
    def __init__(self, groups, rows, chunks, refs):
        m = dp_bits(groups)
        super().__init__(groups, rows, chunks, list(refs[: 2 + m]) + [None] * (m - 1) + list(refs[2 + m :]))
        self.me = lax.axis_index("dp")

    @staticmethod
    def scratch(groups, rows, width, chunks, dtype):
        m = dp_bits(groups)
        kinds = Scatter.scratch(groups, rows, width, chunks, dtype)
        return kinds[:m] + kinds[2 * m - 1 :]

    @staticmethod
    def refs(groups):
        return 3 * dp_bits(groups)

    def whole(self, level, slot, c):
        return self.at(slot * (1 << level) + lax.rem(self.me, 1 << level), c)

    def copy(self, level, slot, c):
        where, bit = self.links[level]
        return remote(
            self.value.at[self.whole(level, 2 * slot + 1 - bit, c)],
            self.arrive[level].at[self.at(slot, c)],
            self.s_sem[level].at[slot, c],
            self.r_sem[level].at[slot, c],
            where,
        )

    def step(self, i, lag):
        for level in range(self.levels):
            c = i - level * lag

            @pl.when(jnp.logical_and(c >= 0, c < self.chunks))
            def _():
                bit = self.links[level][1]
                for slot, goes in self.order(level):
                    self.copy(level, slot, c).wait_recv()
                    here, there = self.whole(level, 2 * slot + bit, c), self.at(slot, c)
                    if level == self.levels - 1:
                        total = self.value[here].astype(F32) + self.arrive[level][there].astype(F32)
                        self.out[self.at(0, c)] = total.astype(self.out.dtype)
                    else:
                        self.value[here] = self.value[here] + self.arrive[level][there]
                        if goes:
                            self.copy(level + 1, slot // 2, c).start()


class Line:
    lag_b, lag_c, lag_o = 2, 4, 5

    def __init__(self, first, half, pieces, part, base, out, scratch, norm=None, moved=None, at=(0, 0, 0), turns=1):
        self.first, self.half, self.size = first, half, half // pieces
        self.each, self.pieces = pieces, pieces * turns
        self.base_at, self.out_at, self.moved_at = at
        self.part, self.base, self.out = part, base, out
        (self.rin, self.smid, self.rmid) = scratch[:3]
        (self.s_up, self.r_up, self.s_mid, self.r_mid, self.s_b1, self.s_b2, self.r_b, self.s_c, self.r_c) = scratch[3:12]
        self.norm, self.moved = norm, moved
        if moved:
            self.arrived, self.shift = moved
            self.s_s, self.r_s = scratch[12:14]
            section = lax.axis_index("section")
            self.sends = section == (0 if self.shift > 0 else 1)
            self.partner = {"section": 1 - section}
        t = lax.axis_index("tensor")
        self.mid = jnp.logical_or(t == 1, t == 2)
        self.outside = jnp.logical_not(self.mid)
        self.outer = {"tensor": jnp.where(t == 1, 0, 3)}
        self.other = {"tensor": jnp.where(t == 1, 2, 1)}
        self.nbr = {"tensor": jnp.where(t == 0, 1, 2)}
        self.near = jnp.where(t < 2, 0, half)
        self.far = half - self.near

    @staticmethod
    def scratch(half, pieces, width, moved, turns=1):
        dma = pltpu.SemaphoreType.DMA
        half, pieces = half * turns, pieces * turns
        kinds = [
            pltpu.VMEM((2 * half, width), BF16),
            pltpu.VMEM((half, width), BF16),
            pltpu.VMEM((half, width), BF16),
            dma((2, pieces)),
            dma((2, pieces)),
        ] + [dma((pieces,))] * 7
        return kinds + ([dma((2, pieces))] * 2 if moved else [])

    @staticmethod
    def greet():
        t = lax.axis_index("tensor")

        @pl.when(t > 0)
        def _():
            greet({"tensor": jnp.maximum(t - 1, 0)})

        @pl.when(t < 3)
        def _():
            greet({"tensor": jnp.minimum(t + 1, 3)})

    def greet_sender(self):
        if self.moved:

            @pl.when(jnp.logical_not(self.sends))
            def _():
                greet(self.partner)

    def enter(self, others):
        bar = pltpu.get_barrier_semaphore()
        count = jnp.where(self.mid, 2, 1) + others
        if self.moved:
            count = count + jnp.where(self.sends, 1, 0)
        pl.semaphore_wait(bar, count)

    def local(self, start, p):
        if self.each < self.pieces:
            start, p = start + (p // self.each) * (2 * self.half), lax.rem(p, self.each)
        return pl.ds(pl.multiple_of(start + p * self.size, self.size), self.size)

    def own(self, p):
        return pl.ds(pl.multiple_of(p * self.size, self.size), self.size)

    def rows(self, start, p, at=0):
        return self.local(self.first + at + start, p)

    def shifted(self, start, p):
        side = start // self.half
        here, there = self.rows(start, p, self.out_at), self.rows(start, p, self.moved_at)
        return remote(self.out.at[here], self.arrived.at[there], self.s_s.at[side, p], self.r_s.at[side, p], self.partner)

    def pass_on(self, start, p):
        if self.moved:

            @pl.when(self.sends)
            def _():
                self.shifted(start, p).start()

    def outcome(self, s_sem, r_sem, where, start, p):
        here = self.rows(start, p, self.out_at)
        return remote(self.out.at[here], self.out.at[here], s_sem.at[p], r_sem.at[p], where)

    def up(self, start, p, k, where):
        return remote(
            self.part.at[self.rows(start, p)], self.rin.at[self.local(start, p)], self.s_up.at[k, p], self.r_up.at[k, p], where
        )

    def cross(self, p):
        return remote(
            self.smid.at[self.own(p)], self.rmid.at[self.own(p)], self.s_mid.at[p], self.r_mid.at[p], self.other
        )

    def start(self, turn=0):
        @pl.when(self.outside)
        def _():
            def begin(p, c):
                self.up(self.far, p, 0, self.nbr).start()
                self.up(self.near, p, 1, self.nbr).start()
                return c

            lax.fori_loop(turn * self.each, (turn + 1) * self.each, begin, 0)

    def outer_step(self, i):
        p = i - self.lag_o

        @pl.when(jnp.logical_and(p >= 0, p < self.pieces))
        def _():
            self.outcome(self.s_b2, self.r_b, self.nbr, self.near, p).wait_recv()
            self.pass_on(self.near, p)
            self.outcome(self.s_c, self.r_c, self.nbr, self.far, p).wait_recv()
            self.pass_on(self.far, p)

    def mid_step(self, i):
        @pl.when(jnp.logical_and(i >= 0, i < self.pieces))
        def _():
            self.up(self.far, i, 0, self.outer).wait_recv()
            total = self.part[self.rows(self.far, i)].astype(F32) + self.rin[self.local(self.far, i)].astype(F32)
            self.smid[self.own(i)] = total.astype(BF16)
            self.cross(i).start()

        j = i - self.lag_b

        @pl.when(jnp.logical_and(j >= 0, j < self.pieces))
        def _():
            self.up(self.near, j, 1, self.outer).wait_recv()
            self.cross(j).wait_recv()
            here = self.rows(self.near, j, self.base_at)
            total = self.part[self.rows(self.near, j)].astype(F32) + self.rin[self.local(self.near, j)].astype(F32)
            total = total + self.rmid[self.own(j)].astype(F32)
            if self.norm:
                xrow, gain, gsum = self.norm
                x = xrow[here].astype(F32)
                scale = lax.rsqrt(jnp.mean(x * x, axis=-1, keepdims=True) + epsilon)
                unit = x * scale
                gsum[...] += jnp.sum(total * unit, axis=0, keepdims=True)
                inner = total * gain[...]
                total = scale * (inner - unit * jnp.mean(inner * unit, axis=-1, keepdims=True))
            total = self.base[here].astype(F32) + total
            self.out[self.rows(self.near, j, self.out_at)] = total.astype(BF16)
            self.outcome(self.s_b1, self.r_b, self.other, self.near, j).start()
            self.outcome(self.s_b2, self.r_b, self.outer, self.near, j).start()
            self.pass_on(self.near, j)

        k = i - self.lag_c

        @pl.when(jnp.logical_and(k >= 0, k < self.pieces))
        def _():
            self.outcome(self.s_b1, self.r_b, self.other, self.far, k).wait_recv()
            self.outcome(self.s_c, self.r_c, self.outer, self.far, k).start()
            self.pass_on(self.far, k)

    @property
    def steps(self):
        return self.pieces + self.lag_o

    def step(self, i):
        @pl.when(self.mid)
        def _():
            self.mid_step(i)

        @pl.when(self.outside)
        def _():
            self.outer_step(i)

    def finish(self):
        @pl.when(self.mid)
        def _():
            def one(p, c):
                self.cross(p).wait_send()
                self.outcome(self.s_b1, self.r_b, self.other, self.near, p).wait_send()
                self.outcome(self.s_b2, self.r_b, self.outer, self.near, p).wait_send()
                self.outcome(self.s_c, self.r_c, self.outer, self.far, p).wait_send()
                return c

            lax.fori_loop(0, self.pieces, one, 0)

        @pl.when(self.outside)
        def _():
            def one(p, c):
                self.up(self.far, p, 0, self.nbr).wait_send()
                self.up(self.near, p, 1, self.nbr).wait_send()
                return c

            lax.fori_loop(0, self.pieces, one, 0)

        if self.moved:

            @pl.when(self.sends)
            def _():
                def close(p, c):
                    self.shifted(0, p).wait_send()
                    self.shifted(self.half, p).wait_send()
                    return c

                lax.fori_loop(0, self.pieces, close, 0)

    def receive(self):
        @pl.when(jnp.logical_not(self.sends))
        def _():
            def close(p, c):
                self.shifted(0, p).wait_recv()
                self.shifted(self.half, p).wait_recv()
                return c

            lax.fori_loop(0, self.pieces, close, 0)


def run_steps(begin, end, *planned):
    def body(i, c):
        for step, offset in planned:
            step(i - offset)
        return c

    lax.fori_loop(begin, end, body, 0)


class Gather:
    def __init__(self, groups, rows, out, s_sem, r_sem):
        self.groups, self.rows, self.out, self.s_sem, self.r_sem = groups, rows, out, s_sem, r_sem
        self.levels = dp_bits(groups)
        self.links = [dp_partner(k) for k in range(self.levels)]
        self.me = lax.axis_index("dp")

    @staticmethod
    def scratch(groups):
        return [pltpu.SemaphoreType.DMA((dp_bits(groups), groups // 2))] * 2

    def copy(self, level, i, mine):
        where, bit = self.links[level]
        low = lax.rem(self.me, 1 << (level + 1))
        if not mine:
            low = low + (1 - 2 * bit) * (1 << level)
        block = i * (1 << (level + 1)) + low
        place = self.out.at[pl.ds(pl.multiple_of(block * self.rows, self.rows), self.rows)]
        return remote(place, place, self.s_sem.at[level, i], self.r_sem.at[level, i], where)

    def start(self, level):
        for i in range(self.groups >> (level + 1)):
            self.copy(level, i, True).start()

    def arrive(self, level):
        for i in range(self.groups >> (level + 1)):
            self.copy(level, i, False).wait_recv()

    def finish(self):
        for level in range(self.levels):
            for i in range(self.groups >> (level + 1)):
                self.copy(level, i, True).wait_send()


def with_transpose(left, right):
    return lax.dot_general(left, right, (((1,), (1,)), ((), ())), preferred_element_type=F32)


def rows_contract(left, right):
    return lax.dot_general(left, right, (((0,), (0,)), ((), ())), preferred_element_type=F32)


def times(left, right):
    return jnp.dot(left, right, preferred_element_type=F32)


LANES = 128
TILE = 256
WIDE = 512


def lanes(i, size=LANES):
    return pl.ds(pl.multiple_of(i * size, size), size)


def normalize(rows, gain):
    rows = rows.astype(F32)
    scale = lax.rsqrt(jnp.mean(rows * rows, axis=-1, keepdims=True) + epsilon)
    return (rows * scale * gain).astype(BF16)


def normalize_into(target, source, gain, first, count, block=32, source_at=0):
    def one(i, c):
        here = pl.ds(pl.multiple_of(first + i * block, block), block)
        there = pl.ds(pl.multiple_of(source_at + first + i * block, block), block)
        target[here] = normalize(source[there], gain[...])
        return c

    lax.fori_loop(0, count // block, one, 0)


def rolled(value, cosine, sine):
    return value * cosine + pltpu.roll(value, LANES // 2, 1) * sine


def block_rows(keys):
    for rows in (160, 80, 32):
        if rows * keys <= 160 * 1280:
            return rows
    return 16


def score_rows(q, kv, h, g, here, qcode, qstart, kcode):
    scores = with_transpose(q[here, lanes(h)], kv[:, lanes(g)]) * HD ** (-0.5)
    code = kcode[...]
    return scores, jnp.logical_and(code <= qcode[here], code >= qstart[here])


def load_all(pairs, sems):
    copies = [pltpu.make_async_copy(src, dst, sems.at[i]) for i, (src, dst) in enumerate(pairs)]
    for item in copies:
        item.start()
    return copies


def forward_kernel(groups, q_heads, k_heads, pieces, *refs):
    refs = list(refs)

    def take(count):
        taken = refs[:count]
        del refs[:count]
        return taken

    x, cosine, sine, qcode, qstart, kcode, gain_one, gain_two = take(8)
    far_weights = take(5)
    q, kv, lse, mixed, resid, gate, up, act, y, arrived = take(10)
    near_weights = take(5)
    wqkv, wout, wgate, wup, wdown = near_weights
    part_one, part_two, n1, n2, w_sem = take(5)
    gather = Gather(groups, x.shape[0], kv, *take(2))
    count, width = x.shape
    quarter = count // 4
    lines = []
    for k in range(4):
        first = (k % 2) * 2 * quarter
        source = (part_one, x, resid) if k < 2 else (part_two, resid, y)
        lines.append(
            Line(first, quarter, pieces, *source, take(12 if k < 2 else 14), moved=None if k < 2 else (arrived, 1))
        )
    one_a, one_b, two_a, two_b = lines

    loads = load_all(list(zip(far_weights, near_weights)), w_sem)
    Line.greet()
    two_a.greet_sender()
    for where, _ in gather.links:
        greet(where)
    normalize_into(n1, x, gain_one, 0, count)
    loads[0].wait()

    mine = pl.ds(pl.multiple_of(lax.axis_index("dp") * count, count), count)
    for g in range(k_heads):
        column = (q_heads + g) * LANES
        value = times(n1[...], wqkv[:, column : column + LANES])
        kv[mine, g * LANES : (g + 1) * LANES] = rolled(value, cosine[...], sine[...]).astype(BF16)
        column += k_heads * LANES
        kv[mine, (k_heads + g) * LANES : (k_heads + g + 1) * LANES] = times(
            n1[...], wqkv[:, column : column + LANES]
        ).astype(BF16)

    two_a.enter(gather.levels)

    top = gather.levels - 1
    gather.start(top)

    def queries(h, c):
        value = times(n1[...], wqkv[:, lanes(h)])
        q[:, lanes(h)] = rolled(value, cosine[...], sine[...]).astype(BF16)
        return c

    lax.fori_loop(0, q_heads, queries, 0)
    for level in range(top, -1, -1):
        gather.arrive(level)
        if level:
            gather.start(level - 1)

    rows = block_rows(kv.shape[0])
    blocks = count // rows

    def attend(i, c):
        h, b = i // blocks, lax.rem(i, blocks)
        g = h // (q_heads // k_heads)
        here = pl.ds(pl.multiple_of(b * rows, rows), rows)
        scores, allowed = score_rows(q, kv, h, g, here, qcode, qstart, kcode)
        scores = jnp.where(allowed, scores, negative)
        row_max = jnp.max(scores, axis=-1, keepdims=True)
        expo = jnp.exp(scores - row_max)
        row_total = jnp.sum(expo, axis=-1, keepdims=True)
        prob = (expo * (1.0 / row_total)).astype(BF16)
        mixed[here, lanes(h)] = times(prob, kv[:, lanes(k_heads + g)]).astype(BF16)
        there = pl.ds(pl.multiple_of(h * count + b * rows, rows), rows)
        lse[there] = jnp.broadcast_to(row_max + jnp.log(row_total), (rows, LANES))
        return c

    lax.fori_loop(0, q_heads * blocks, attend, 0)
    loads[1].wait()

    def projected(target, left, right, first, each=None):
        here = pl.ds(first, 2 * quarter)

        def one(i, c):
            target[here, lanes(i, TILE)] = times(left[here], right[:, lanes(i, TILE)]).astype(BF16)
            if each:
                each(i)
            return c

        lax.fori_loop(0, width // TILE, one, 0)

    projected(part_one, mixed, wout, 0)
    one_a.start()
    projected(part_one, mixed, wout, 2 * quarter)
    one_b.start()
    run_steps(0, one_a.steps, (one_a.step, 0), (one_b.step, pieces))
    loads[2].wait()
    loads[3].wait()
    loads[4].wait()

    def hidden(first, each):
        here = pl.ds(first, 2 * quarter)
        normalize_into(n2, resid, gain_two, first, 2 * quarter)

        def one(i, c):
            columns = lanes(i, TILE)
            gate_pre = times(n2[here], wgate[:, columns])
            up_pre = times(n2[here], wup[:, columns])
            gate[here, columns] = gate_pre.astype(BF16)
            up[here, columns] = up_pre.astype(BF16)
            act[here, columns] = (gate_pre * jax.nn.sigmoid(gate_pre) * up_pre).astype(BF16)
            each(i)
            return c

        lax.fori_loop(0, gate.shape[1] // TILE, one, 0)

    tiles = gate.shape[1] // TILE
    done = one_a.steps - pieces
    hidden(0, lambda i: one_b.step(done + i))
    projected(part_two, act, wdown, 0)
    two_a.start()
    run_steps(done + tiles, one_b.steps, (one_b.step, 0))
    hidden(2 * quarter, lambda i: two_a.step(i))
    projected(part_two, act, wdown, 2 * quarter)
    two_b.start()
    run_steps(tiles, two_b.steps + tiles, (two_a.step, 0), (two_b.step, tiles))
    gather.finish()
    for line in lines:
        line.finish()
    two_a.receive()
    two_b.receive()


VMEM_LIMIT = 58 * 2**20


def forward_tick(x, spots, weights, groups, q_heads, k_heads, cid):
    norm_one, wqkv, wout, norm_two, wgate, wup, wdown = weights
    count, width = x.shape
    hidden = wgate.shape[1]
    pieces = 5
    vmem = pl.BlockSpec(memory_space=pltpu.VMEM)
    far = pl.BlockSpec(memory_space=pl.ANY)

    def shape(*dims, dtype=BF16):
        return jax.ShapeDtypeStruct(dims, dtype)

    outs = [
        shape(count, q_heads * LANES),
        shape(groups * count, 2 * k_heads * LANES),
        shape(q_heads * count, LANES, dtype=F32),
        shape(count, q_heads * LANES),
        shape(count, width),
        shape(count, hidden),
        shape(count, hidden),
        shape(count, hidden),
        shape(count, width),
        shape(count, width),
    ]
    far_weights = [wqkv, wout, wgate, wup, wdown]
    scratch = [pltpu.VMEM(item.shape, BF16) for item in far_weights]
    scratch += [pltpu.VMEM((count, width), BF16)] * 4 + [pltpu.SemaphoreType.DMA((5,))]
    scratch += Gather.scratch(groups)
    for k in range(4):
        scratch += Line.scratch(count // 4, pieces, width, k >= 2)
    q, kv, lse, mixed, resid, gate, up, act, y, arrived = pl.pallas_call(
        functools.partial(forward_kernel, groups, q_heads, k_heads, pieces),
        out_shape=outs,
        in_specs=[vmem] * 8 + [far] * 5,
        out_specs=[vmem] * len(outs),
        scratch_shapes=scratch,
        compiler_params=pltpu.CompilerParams(
            collective_id=cid, has_side_effects=True, vmem_limit_bytes=VMEM_LIMIT
        ),
        name="forward_tick",
    )(x, *spots, norm_one[None], norm_two[None], *far_weights)
    return y, arrived, (x, q, kv, lse, mixed, resid, gate, up, act)


def back_ffn_kernel(pieces, *refs):
    dy, gate, up, resid, gain = refs[:5]
    far_weights = refs[5:8]
    dresid, gsum, dgate, dup = refs[8:12]
    wdown, wgate, wup = near_weights = refs[12:15]
    part, w_sem = refs[15:17]
    count, width = dy.shape
    quarter = count // 4
    a, b = [
        Line(k * 2 * quarter, quarter, pieces, part, dy, dresid, refs[17 + 12 * k : 29 + 12 * k], norm=(resid, gain, gsum))
        for k in range(2)
    ]
    loads = load_all(list(zip(far_weights, near_weights)), w_sem)
    Line.greet()
    gsum[...] = jnp.zeros_like(gsum)

    def hidden(first, each=None):
        here = pl.ds(first, 2 * quarter)

        def one(i, c):
            columns = lanes(i, TILE)
            d_act = with_transpose(dy[here], wdown[columns, :])
            gate_pre, up_pre = gate[here, columns].astype(F32), up[here, columns].astype(F32)
            sigma = jax.nn.sigmoid(gate_pre)
            d_silu = d_act * sigma
            dup[here, columns] = (d_silu * gate_pre).astype(BF16)
            dgate[here, columns] = (d_silu * up_pre * (1.0 + gate_pre * (1.0 - sigma))).astype(BF16)
            if each:
                each(i)
            return c

        lax.fori_loop(0, gate.shape[1] // TILE, one, 0)

    def back(first):
        here = pl.ds(first, 2 * quarter)

        def one(i, c):
            columns = lanes(i, TILE)
            total = with_transpose(dgate[here], wgate[columns, :]) + with_transpose(dup[here], wup[columns, :])
            part[here, columns] = total.astype(BF16)
            return c

        lax.fori_loop(0, width // TILE, one, 0)

    loads[0].wait()
    hidden(0)
    loads[1].wait()
    loads[2].wait()
    back(0)
    a.enter(0)
    a.start()
    tiles = gate.shape[1] // TILE
    hidden(2 * quarter, lambda i: a.step(i))
    back(2 * quarter)
    b.start()
    run_steps(tiles, b.steps + tiles, (a.step, 0), (b.step, tiles))
    a.finish()
    b.finish()


def back_ffn(dy, kept, weights, cid):
    norm_one, wqkv, wout, norm_two, wgate, wup, wdown = weights
    x, q, kv, lse, mixed, resid, gate, up, act = kept
    count, width = dy.shape
    pieces = 5
    vmem = pl.BlockSpec(memory_space=pltpu.VMEM)
    far = pl.BlockSpec(memory_space=pl.ANY)
    far_weights = [wdown, wgate, wup]
    scratch = [pltpu.VMEM(item.shape, BF16) for item in far_weights]
    scratch += [pltpu.VMEM((count, width), BF16), pltpu.SemaphoreType.DMA((3,))]
    scratch += Line.scratch(count // 4, pieces, width, False) * 2
    return pl.pallas_call(
        functools.partial(back_ffn_kernel, pieces),
        out_shape=[
            jax.ShapeDtypeStruct((count, width), BF16),
            jax.ShapeDtypeStruct((1, width), F32),
            jax.ShapeDtypeStruct(gate.shape, BF16),
            jax.ShapeDtypeStruct(gate.shape, BF16),
        ],
        in_specs=[vmem] * 5 + [far] * 3,
        out_specs=[vmem] * 4,
        scratch_shapes=scratch,
        compiler_params=pltpu.CompilerParams(
            collective_id=cid, has_side_effects=True, vmem_limit_bytes=VMEM_LIMIT
        ),
        name="back_ffn",
    )(dy, gate, up, resid, norm_two[None], *far_weights)


def back_attn_kernel(groups, q_heads, k_heads, pieces, shift, plans, *refs):
    refs = list(refs)

    def take(count):
        taken = refs[:count]
        del refs[:count]
        return taken

    dresid, x, q, kv, lse, cosine, sine, qcode, qstart, kcode, gain = take(11)
    far_weights = take(2)
    values = take(len(plans))
    dx, gsum, dqkv = take(3)
    (arrived,) = take(1) if shift else (None,)
    totals = take(len(plans))
    wout, wqkv = near_weights = take(2)
    part, dmixed, dkv, w_sem = take(4)
    levels = dp_bits(groups)
    count, width = x.shape
    quarter = count // 4
    keys = kv.shape[0]
    shares, owns, scatters = [], [], []
    for g in range(k_heads):
        share, own = take(2)
        shares.append(share)
        owns.append(own)
        scatters.append(Scatter(groups, count, 5, [share, own] + take(4 * levels - 1)))
    tasks = [
        Scatter(groups, rows, chunks, [value, total] + take(4 * levels - 1))
        for (rows, chunks), value, total in zip(plans, values, totals)
    ]
    moved = (arrived, shift) if shift else None
    a, b = [
        Line(
            k * 2 * quarter,
            quarter,
            pieces,
            part,
            dresid,
            dx,
            take(14 if shift else 12),
            norm=(x, gain, gsum),
            moved=moved,
        )
        for k in range(2)
    ]
    loads = load_all(list(zip(far_weights, near_weights)), w_sem)
    Line.greet()
    for where, _ in scatters[0].links:
        greet(where)
    a.greet_sender()
    gsum[...] = jnp.zeros_like(gsum)
    dkv[...] = jnp.zeros_like(dkv)
    a.enter(levels)
    for task in tasks:
        task.start()
    loads[0].wait()

    def mix(h, c):
        dmixed[:, lanes(h)] = with_transpose(dresid[...], wout[lanes(h), :]).astype(BF16)
        return c

    lax.fori_loop(0, q_heads, mix, 0)
    rows = block_rows(keys)
    blocks = count // rows
    repeat = q_heads // k_heads
    lag = 4
    scale = HD ** (-0.5)

    for g in range(k_heads):

        def one(i, c):
            h, n = g * repeat + i // blocks, lax.rem(i, blocks)
            here = pl.ds(pl.multiple_of(n * rows, rows), rows)
            there = pl.ds(pl.multiple_of(h * count + n * rows, rows), rows)
            scores, allowed = score_rows(q, kv, h, g, here, qcode, qstart, kcode)
            prob = jnp.where(allowed, jnp.exp(scores - lse[there][:, :1]), 0.0)
            dm = dmixed[here, lanes(h)]
            d_prob = with_transpose(dm, kv[:, lanes(k_heads + g)])
            row_dot = jnp.sum(prob * d_prob, axis=-1, keepdims=True)
            d_scores = (prob * (d_prob - row_dot)).astype(BF16)
            d_query = times(d_scores, kv[:, lanes(g)]) * scale
            dqkv[here, lanes(h)] = rolled(d_query, cosine[here], -sine[here]).astype(BF16)
            dkv[:, lanes(g)] += rows_contract(d_scores, q[here, lanes(h)]) * scale
            dkv[:, lanes(k_heads + g)] += rows_contract(prob.astype(BF16), dm)
            for task in tasks:
                task.step(g * repeat * blocks + i, lag)
            return c

        lax.fori_loop(0, repeat * blocks, one, 0)

        def narrow(i, c):
            here = pl.ds(pl.multiple_of(i * LANES, LANES), LANES)
            shares[g][here, :LANES] = dkv[here, lanes(g)].astype(BF16)
            shares[g][here, LANES:] = dkv[here, lanes(k_heads + g)].astype(BF16)
            return c

        lax.fori_loop(0, keys // LANES, narrow, 0)
        scatters[g].start()
    run_steps(0, scatters[0].steps(1), *[(functools.partial(lambda s, i: s.step(i, 1), s), 0) for s in scatters])
    for g in range(k_heads):
        dqkv[:, lanes(q_heads + g)] = rolled(owns[g][:, :LANES], cosine[...], -sine[...]).astype(BF16)
        dqkv[:, lanes(q_heads + k_heads + g)] = owns[g][:, LANES:].astype(BF16)
    loads[1].wait()

    def back(first, each=None):
        here = pl.ds(first, 2 * quarter)

        def one(i, c):
            columns = lanes(i, TILE)
            part[here, columns] = with_transpose(dqkv[here], wqkv[columns, :]).astype(BF16)
            if each:
                each(i)
            return c

        lax.fori_loop(0, width // TILE, one, 0)

    back(0)
    a.start()
    back(2 * quarter)
    b.start()
    begun = q_heads * blocks
    more = [(functools.partial(lambda s, i: s.step(i + begun, lag), s), 0) for s in tasks]
    last = max([b.steps + pieces] + [s.steps(lag) - begun for s in tasks])
    run_steps(0, last, (a.step, 0), (b.step, pieces), *more)
    a.finish()
    b.finish()
    if shift:
        a.receive()
        b.receive()
    for item in scatters + tasks:
        item.finish()


def back_attn(dresid, kept, spots, weights, groups, q_heads, k_heads, cid, shift, sums=()):
    norm_one, wqkv, wout, norm_two, wgate, wup, wdown = weights
    x, q, kv, lse, mixed, resid, gate, up, act = kept
    count, width = x.shape
    keys = kv.shape[0]
    pieces = 5
    vmem = pl.BlockSpec(memory_space=pltpu.VMEM)
    far = pl.BlockSpec(memory_space=pl.ANY)
    outs = [
        jax.ShapeDtypeStruct((count, width), BF16),
        jax.ShapeDtypeStruct((1, width), F32),
        jax.ShapeDtypeStruct((count, wqkv.shape[1]), BF16),
    ]
    if shift:
        outs.append(jax.ShapeDtypeStruct((count, width), BF16))
    scratch = [
        pltpu.VMEM(wout.shape, BF16),
        pltpu.VMEM(wqkv.shape, BF16),
        pltpu.VMEM((count, width), BF16),
        pltpu.VMEM(q.shape, BF16),
        pltpu.VMEM(kv.shape, F32),
        pltpu.SemaphoreType.DMA((2,)),
    ]
    for _ in range(k_heads):
        scratch += [pltpu.VMEM((keys, 2 * LANES), BF16), pltpu.VMEM((count, 2 * LANES), F32)]
        scratch += Scatter.scratch(groups, count, 2 * LANES, 5, BF16)
    plans = []
    for value in sums:
        rows = value.shape[0] // groups
        parts = max(1, min(8, rows // 16))
        while rows % (parts * 16):
            parts -= 1
        plans.append((rows, parts))
        outs.append(jax.ShapeDtypeStruct((rows, value.shape[1]), F32))
        scratch += Scatter.scratch(groups, rows, value.shape[1], parts, BF16)
    scratch += Line.scratch(count // 4, pieces, width, bool(shift)) * 2
    return pl.pallas_call(
        functools.partial(back_attn_kernel, groups, q_heads, k_heads, pieces, shift, plans),
        out_shape=outs,
        in_specs=[vmem] * 11 + [far] * 2 + [vmem] * len(sums),
        out_specs=[vmem] * len(outs),
        scratch_shapes=scratch,
        compiler_params=pltpu.CompilerParams(
            collective_id=cid, has_side_effects=True, vmem_limit_bytes=VMEM_LIMIT
        ),
        name="back_attn_%d" % cid,
    )(dresid, x, q, kv, lse, *spots, norm_one[None], wout, wqkv, *sums)


def announce(sems, neighbours):
    for here, where, k in neighbours:

        @pl.when(here)
        def _():
            pl.semaphore_signal(sems.at[k], inc=1, device_id=where, device_id_type=MESH)


def heard(sems, neighbours):
    for k, (here, _, _) in enumerate(neighbours):

        @pl.when(here)
        def _():
            pl.semaphore_wait(sems.at[k], 1)


def main_kernel(groups, q_heads, k_heads, pieces, *refs):
    refs = list(refs)

    def take(count):
        taken = refs[:count]
        del refs[:count]
        return taken

    cosine, sine, qcode, qstart, kcode, gain_one, gain_two, holder, chosen = take(9)
    packed, own_second, extra_second = take(3)
    far_weights = take(5)
    y_out, dx_out, back_out = take(3)
    far_state = take(14)
    gsum_one, gsum_two = take(2)
    near_state = xs, q, kv, lse, mixed, resid, gate, up, act, dys, dresid, dgate, dup, dqkv = take(14)
    state_sem = take(1)[0]
    wqkv, wout, wgate, wup, wdown = near_weights = take(5)
    part_one, part_two, normed, y, dmixed, dkv, w_sem, io_sem, meet_sem = take(9)
    levels = dp_bits(groups)
    gather_sems = take(2)
    line_scratch = [take(12) for _ in range(4)]
    forth_s, forth_r, back_s, back_r = take(4)
    spares, returned = take(2)
    spare = returned.shape[0]
    give_lag = Line.lag_o + pieces
    give = OwnScatter(groups, spare, spare // 32, [spares, returned] + take(OwnScatter.refs(groups)))
    second = Gather(groups, spare, spares, *take(2))
    count, width = part_one.shape
    keys = groups * count
    quarter = count // 4
    half = 2 * quarter
    shares, owns, scatters = [], [], []
    for g in range(k_heads):
        share, own = take(2)
        shares.append(share)
        owns.append(own)
        scatters.append(Scatter(groups, count, 5, [share, own] + take(4 * levels - 1)))
    section = lax.axis_index("section")
    t = lax.axis_index("tensor")
    tiles, wide = gate.shape[1] // WIDE, width // WIDE
    repeat = q_heads // k_heads
    rows = block_rows(keys)
    blocks = half // rows
    scale = HD ** (-0.5)

    def span(first, size):
        return pl.ds(pl.multiple_of(first, 32), size)

    neighbours = [
        (t > 0, {"tensor": jnp.maximum(t - 1, 0)}, 1),
        (t < 3, {"tensor": jnp.minimum(t + 1, 3)}, 0),
    ]
    for k in range(levels):
        neighbours.append((t >= 0, dp_partner(k)[0], 2 + k))

    for _, where, _ in neighbours[2:]:
        greet(where)
    Line.greet()
    greet({"section": 1 - section})

    loads = load_all(list(zip(far_weights, near_weights)), w_sem)

    def fetch(target):
        return (
            pltpu.make_async_copy(packed, target.at[:count], io_sem.at[0]),
            pltpu.make_async_copy(own_second, target.at[count:], io_sem.at[1]),
        )

    place = span(lax.axis_index("dp") * spare, spare)
    fetch_extra = pltpu.make_async_copy(extra_second, spares.at[place], io_sem.at[2])
    fetch_extra.start()
    for which, target in enumerate((xs, dys)):

        @pl.when(section == which)
        def _():
            for item in fetch(target):
                item.start()

    pl.semaphore_wait(pltpu.get_barrier_semaphore(), jnp.where(jnp.logical_or(t == 1, t == 2), 2, 1) + levels + 1)
    announce(meet_sem, neighbours)
    gsum_one[...] = jnp.zeros_like(gsum_one)
    gsum_two[...] = jnp.zeros_like(gsum_two)
    for which, target in enumerate((xs, dys)):

        @pl.when(section == which)
        def _():
            for item in fetch(target):
                item.wait()

    fetch_extra.wait()

    def keep(index, slot):
        near, there = near_state[index], far_state[index]
        part = near.shape[0] // 2
        here = span(slot * part, part)
        return pltpu.make_async_copy(near.at[here], there.at[here], state_sem.at[index, slot])

    def projected(target, left, right, first, left_at, each=None):
        here, there = span(first, half), span(first + left_at, half)

        def one(i, c):
            target[here, lanes(i, WIDE)] = times(left[there], right[:, lanes(i, WIDE)]).astype(BF16)
            if each:
                each(i)
            return c

        lax.fori_loop(0, wide, one, 0)

    def give_back(slot, now, line):
        @pl.when(now)
        def _():
            spares[...] = times(holder[span(slot * groups * spare, groups * spare)], y[...]).astype(BF16)
            give.start()

        def one(i, c):
            line.step(i)

            @pl.when(now)
            def _():
                give.step(i, give_lag)

            return c

        lax.fori_loop(0, line.steps, one, 0)

    def give_rest(now, line, begun):
        def one(i, c):
            line.step(i)

            @pl.when(now)
            def _():
                give.step(i - begun + give_lag, give_lag)

            return c

        lax.fori_loop(begun, max(line.steps, begun + give.steps(give_lag) - give_lag), one, 0)

    def given(slot, now):
        @pl.when(now)
        def _():
            give.finish()
            pltpu.make_async_copy(returned, back_out.at[span(slot * spare, spare)], io_sem.at[1]).start()
            pltpu.make_async_copy(returned, back_out.at[span(slot * spare, spare)], io_sem.at[1]).wait()

    def forward(slot, carry):
        base = slot * count
        whole = span(base, count)
        moved = (xs, 1)
        lines = []
        for k in range(4):
            first = (k % 2) * half
            scratch = list(line_scratch[k])
            if k < 2:
                lines.append(Line(first, quarter, pieces, part_one, xs, resid, scratch, at=(base, base, 0)))
            else:
                scratch += [forth_s.at[k - 2], forth_r.at[2 * slot + k - 2]]
                lines.append(
                    Line(first, quarter, pieces, part_two, resid, y, scratch, moved=moved, at=(base, 0, base))
                )
        one_a, one_b, two_a, two_b = lines
        gather = Gather(groups, count, kv.at[span(slot * keys, keys)], *gather_sems)
        two_a.receive()
        two_b.receive()
        normalize_into(normed, xs, gain_one, 0, count, source_at=base)

        @pl.when(slot == 0)
        def _():
            loads[0].wait()

        mine = span(slot * keys + lax.axis_index("dp") * count, count)
        middle = (q_heads + k_heads) * LANES
        value = times(normed[...], wqkv[:, q_heads * LANES : middle])
        for g in range(k_heads):
            here = slice(g * LANES, (g + 1) * LANES)
            kv[mine, here] = rolled(value[:, here], cosine[whole], sine[whole]).astype(BF16)
        kv[mine, k_heads * LANES :] = times(normed[...], wqkv[:, middle:]).astype(BF16)
        heard(meet_sem, neighbours)
        gather.start(levels - 1)
        for first in range(0, q_heads, 2):
            value = times(normed[...], wqkv[:, first * LANES : (first + 2) * LANES])
            for h in range(2):
                here = slice((first + h) * LANES, (first + h + 1) * LANES)
                q[whole, here] = rolled(
                    value[:, h * LANES : (h + 1) * LANES], cosine[whole], sine[whole]
                ).astype(BF16)
        for level in range(levels - 1, -1, -1):
            gather.arrive(level)
            if level:
                gather.start(level - 1)

        @pl.when(slot == 0)
        def _():
            second.start(levels - 1)

        def attend(first, each=None):
            def one(i, c):
                h, b = i // blocks, lax.rem(i, blocks)
                g = h // repeat
                here = span(base + first + b * rows, rows)
                scores = with_transpose(q[here, lanes(h)], kv[span(slot * keys, keys), lanes(g)]) * scale
                code = kcode[slot]
                allowed = jnp.logical_and(code <= qcode[here], code >= qstart[here])
                scores = jnp.where(allowed, scores, negative)
                row_max = jnp.max(scores, axis=-1, keepdims=True)
                expo = jnp.exp(scores - row_max)
                row_total = jnp.sum(expo, axis=-1, keepdims=True)
                prob = (expo * (1.0 / row_total)).astype(BF16)
                mixed[here, lanes(h)] = times(prob, kv[span(slot * keys, keys), lanes(k_heads + g)]).astype(BF16)
                lse[span((slot * q_heads + h) * count + first + b * rows, rows)] = jnp.broadcast_to(
                    row_max + jnp.log(row_total), (rows, LANES)
                )
                if each:
                    each(i)
                return c

            lax.fori_loop(0, q_heads * blocks, one, 0)

        attend(0)

        @pl.when(slot == 0)
        def _():
            loads[1].wait()

        projected(part_one, mixed, wout, 0, base)
        one_a.start()
        attend(half)
        projected(part_one, mixed, wout, half, base)
        one_b.start()
        give_back(0, slot == 1, one_a)

        @pl.when(slot == 0)
        def _():
            for item in loads[2:]:
                item.wait()
            for level in range(levels - 1, 0, -1):
                second.arrive(level)
                second.start(level - 1)

        def hidden(first, each):
            here, there = span(first, half), span(base + first, half)
            normalize_into(normed, resid, gain_two, first, half, source_at=base)

            def one(i, c):
                columns = lanes(i, WIDE)
                gate_pre = times(normed[here], wgate[:, columns])
                up_pre = times(normed[here], wup[:, columns])
                gate[there, columns] = gate_pre.astype(BF16)
                up[there, columns] = up_pre.astype(BF16)
                act[there, columns] = (gate_pre * jax.nn.sigmoid(gate_pre) * up_pre).astype(BF16)
                each(i)
                return c

            lax.fori_loop(0, tiles, one, 0)

        hidden(0, one_b.step)
        projected(part_two, act, wdown, 0, base)
        two_a.start()
        give_rest(slot == 1, one_b, tiles)
        hidden(half, two_a.step)
        projected(part_two, act, wdown, half, base)
        two_b.start()

        @pl.when(slot == 0)
        def _():
            second.arrive(0)
            brought = times(chosen[...], spares[...])
            for which, target in enumerate((xs, dys)):

                @pl.when(section == which)
                def _():
                    target[count:] = (target[count:].astype(F32) + brought).astype(BF16)

        run_steps(tiles, two_a.steps, (two_a.step, 0))
        run_steps(0, two_b.steps, (two_b.step, 0))
        out = pltpu.make_async_copy(y, y_out.at[whole], io_sem.at[0])
        out.start()
        gather.finish()
        for line in lines:
            line.finish()
        given(0, slot == 1)

        @pl.when(slot == 0)
        def _():
            second.finish()

        out.wait()
        for index in range(9):
            keep(index, slot).start()
        announce(meet_sem, neighbours)
        return carry

    lax.fori_loop(0, 2, forward, 0)

    def backward(tick, carry):
        slot = 1 - tick
        base = slot * count
        whole = span(base, count)
        lines = []
        for k in range(4):
            first = (k % 2) * half
            scratch = list(line_scratch[k])
            if k < 2:
                norm = (resid, gain_two, gsum_two)
                lines.append(Line(first, quarter, pieces, part_one, dys, dresid, scratch, norm=norm, at=(base, base, 0)))
            else:
                scratch += [back_s.at[k - 2], back_r.at[2 * slot + k - 2]]
                norm = (xs, gain_one, gsum_one)
                lines.append(
                    Line(
                        first, quarter, pieces, part_two, dresid, y, scratch, norm=norm, moved=(dys, -1), at=(base, 0, base)
                    )
                )
        one_a, one_b, two_a, two_b = lines
        two_a.receive()
        two_b.receive()
        dkv[...] = jnp.zeros_like(dkv)
        heard(meet_sem, neighbours)

        def hidden(first, each=None):
            here = span(base + first, half)

            def one(i, c):
                columns = lanes(i, WIDE)
                d_act = with_transpose(dys[here], wdown[columns, :])
                gate_pre, up_pre = gate[here, columns].astype(F32), up[here, columns].astype(F32)
                sigma = jax.nn.sigmoid(gate_pre)
                d_silu = d_act * sigma
                dup[here, columns] = (d_silu * gate_pre).astype(BF16)
                dgate[here, columns] = (d_silu * up_pre * (1.0 + gate_pre * (1.0 - sigma))).astype(BF16)
                if each:
                    each(i)
                return c

            lax.fori_loop(0, tiles, one, 0)

        def back_hidden(first):
            here, there = span(first, half), span(base + first, half)

            def one(i, c):
                columns = lanes(i, WIDE)
                total = with_transpose(dgate[there], wgate[columns, :]) + with_transpose(dup[there], wup[columns, :])
                part_one[here, columns] = total.astype(BF16)
                return c

            lax.fori_loop(0, wide, one, 0)

        hidden(0)
        back_hidden(0)
        one_a.start()
        hidden(half)
        back_hidden(half)
        one_b.start()
        give_back(1, tick == 0, one_a)

        def attend(first, g, each=None):
            def one(i, c):
                h, n = g * repeat + i // blocks, lax.rem(i, blocks)
                here = span(base + first + n * rows, rows)
                near = span(first + n * rows, rows)
                k_rows = kv[span(slot * keys, keys), lanes(g)]
                scores = with_transpose(q[here, lanes(h)], k_rows) * scale
                code = kcode[slot]
                allowed = jnp.logical_and(code <= qcode[here], code >= qstart[here])
                known = lse[span((slot * q_heads + h) * count + first + n * rows, rows)][:, :1]
                prob = jnp.where(allowed, jnp.exp(scores - known), 0.0)
                dm = dmixed[near, lanes(h)]
                d_prob = with_transpose(dm, kv[span(slot * keys, keys), lanes(k_heads + g)])
                row_dot = jnp.sum(prob * d_prob, axis=-1, keepdims=True)
                d_scores = (prob * (d_prob - row_dot)).astype(BF16)
                d_query = times(d_scores, k_rows) * scale
                dqkv[here, lanes(h)] = rolled(d_query, cosine[here], -sine[here]).astype(BF16)
                dkv[lanes(g), :] += rows_contract(q[here, lanes(h)], d_scores) * scale
                dkv[lanes(k_heads + g), :] += rows_contract(dm, prob.astype(BF16))
                if each:
                    each(i)
                return c

            lax.fori_loop(0, repeat * blocks, one, 0)

        def mix(first):
            here, there = span(first, half), span(base + first, half)

            def one(h, c):
                dmixed[here, lanes(h)] = with_transpose(dresid[there], wout[lanes(h), :]).astype(BF16)
                return c

            lax.fori_loop(0, q_heads, one, 0)

        mix(0)
        turns = repeat * blocks
        for g in range(k_heads):
            attend(0, g, lambda i: one_b.step(g * turns + i))
        give_rest(tick == 0, one_b, k_heads * turns)
        mix(half)
        for g in range(k_heads):
            attend(half, g)

            shares[g][:, :LANES] = jnp.transpose(dkv[lanes(g), :]).astype(BF16)
            shares[g][:, LANES:] = jnp.transpose(dkv[lanes(k_heads + g), :]).astype(BF16)
            scatters[g].start()
        run_steps(0, scatters[0].steps(1), *[(functools.partial(lambda s, i: s.step(i, 1), s), 0) for s in scatters])
        for g in range(k_heads):
            dqkv[whole, lanes(q_heads + g)] = rolled(owns[g][:, :LANES], cosine[whole], -sine[whole]).astype(BF16)
            dqkv[whole, lanes(q_heads + k_heads + g)] = owns[g][:, LANES:].astype(BF16)

        def back(first, each=None):
            here, there = span(first, half), span(base + first, half)

            def one(i, c):
                columns = lanes(i, WIDE)
                part_two[here, columns] = with_transpose(dqkv[there], wqkv[columns, :]).astype(BF16)
                if each:
                    each(i)
                return c

            lax.fori_loop(0, wide, one, 0)

        back(0)
        two_a.start()
        back(half)
        two_b.start()
        run_steps(0, two_a.steps, (two_a.step, 0))
        run_steps(0, two_b.steps, (two_b.step, 0))
        out = pltpu.make_async_copy(y, dx_out.at[whole], io_sem.at[0])
        out.start()
        for line in lines:
            line.finish()
        for item in scatters:
            item.finish()
        given(1, tick == 0)
        out.wait()
        for index in range(9, 14):
            keep(index, slot).start()
        announce(meet_sem, neighbours)
        return carry

    lax.fori_loop(0, 1 + section, backward, 0)
    heard(meet_sem, neighbours)
    for k in range(2):
        Line(
            k * half,
            quarter,
            pieces,
            part_two,
            dresid,
            y,
            list(line_scratch[2 + k]) + [back_s.at[k], back_r.at[k]],
            moved=(dys, -1),
        ).receive()
    for index in range(14):
        keep(index, 1).wait()
        if index < 9:
            keep(index, 0).wait()

    @pl.when(section > 0)
    def _():
        for index in range(9, 14):
            keep(index, 0).wait()

    @pl.when(section == 0)
    def _():
        keep(9, 0).start()
        keep(9, 0).wait()


def main_ticks(packed, second, spots, holder, weights, groups, q_heads, k_heads, cid):
    norm_one, wqkv, wout, norm_two, wgate, wup, wdown = weights
    count, width = packed.shape
    own_second, extra_second, chosen = second
    hidden, keys = wgate.shape[1], groups * count
    pieces = 5
    vmem = pl.BlockSpec(memory_space=pltpu.VMEM)
    far = pl.BlockSpec(memory_space=pl.ANY)
    dma = pltpu.SemaphoreType.DMA

    def shape(columns, rows=2 * count, dtype=BF16):
        return jax.ShapeDtypeStruct((rows, columns), dtype)

    heads, both = q_heads * LANES, (q_heads + 2 * k_heads) * LANES
    spare = holder.shape[0] // (2 * groups)
    outs = [
        shape(width),
        shape(width),
        shape(width, 2 * spare),
    ]
    state = [
        shape(width),
        shape(heads),
        shape(2 * k_heads * LANES, 2 * keys),
        shape(LANES, 2 * q_heads * count, F32),
        shape(heads),
        shape(width),
        shape(hidden),
        shape(hidden),
        shape(hidden),
        shape(width),
        shape(width),
        shape(hidden),
        shape(hidden),
        shape(both),
    ]
    outs += state + [shape(width, 1, F32)] * 2
    far_weights = [wqkv, wout, wgate, wup, wdown]
    scratch = [pltpu.VMEM(item.shape, item.dtype) for item in state] + [dma((14, 2))]
    scratch += [pltpu.VMEM(item.shape, BF16) for item in far_weights]
    scratch += [pltpu.VMEM((count, width), BF16)] * 4 + [
        pltpu.VMEM((count, heads), BF16),
        pltpu.VMEM((2 * k_heads * LANES, keys), F32),
        dma((5,)),
        dma((3,)),
        pltpu.SemaphoreType.REGULAR((2 + dp_bits(groups),)),
    ]
    scratch += Gather.scratch(groups)
    for k in range(4):
        scratch += Line.scratch(quarter_rows(count), pieces, width, False)
    scratch += [dma((2, 2, pieces)), dma((4, 2, pieces))] * 2
    scratch += [pltpu.VMEM((groups * spare, width), BF16), pltpu.VMEM((spare, width), BF16)]
    scratch += OwnScatter.scratch(groups, spare, width, spare // 32, BF16)
    scratch += Gather.scratch(groups)
    for _ in range(k_heads):
        scratch += [pltpu.VMEM((keys, 2 * LANES), BF16), pltpu.VMEM((count, 2 * LANES), F32)]
        scratch += Scatter.scratch(groups, count, 2 * LANES, 5, BF16)
    return pl.pallas_call(
        functools.partial(main_kernel, groups, q_heads, k_heads, pieces),
        out_shape=outs,
        in_specs=[vmem] * 9 + [far] * 8,
        out_specs=[far] * (len(outs) - 2) + [vmem] * 2,
        scratch_shapes=scratch,
        compiler_params=pltpu.CompilerParams(
            collective_id=cid, has_side_effects=True, vmem_limit_bytes=VMEM_LIMIT
        ),
        name="main_ticks",
    )(*spots, norm_one[None], norm_two[None], holder, chosen, packed, own_second, extra_second, *far_weights)


def quarter_rows(count):
    return count // 4


def weight_job(target, left, right, i, block=256):
    here = lanes(i, block)
    target[here, :] = rows_contract(left[:, here], right[...]).astype(BF16)


def last_ffn_kernel(groups, pieces, chunks, *refs):
    refs = list(refs)

    def take(count):
        taken = refs[:count]
        del refs[:count]
        return taken

    (gain,) = take(1)
    sources = take(11)
    first_dresid, gsum, g_up, down_sum, gate_sum = take(5)
    wdown, wgate, wup, dys, act, gate, up, dgate, dup, resid = kept = take(10)
    n2, part, g_down, g_gate, w_sem = take(5)
    (scratch,) = (take(12),)
    count, width = part.shape
    half = count // 2
    line_a, line_b = [
        Line(k * half, half // 2, pieces, part, dys, first_dresid, item, norm=(resid, gain, gsum))
        for k, item in enumerate((scratch, take(12)))
    ]
    down = OwnScatter(groups, width // groups, chunks, [g_down, down_sum] + take(OwnScatter.refs(groups)))
    gated = OwnScatter(groups, width // groups, chunks, [g_gate, gate_sum] + take(OwnScatter.refs(groups)))
    section = lax.axis_index("section")
    mine = section == 0
    tiles, wide, blocks = act.shape[1] // WIDE, width // WIDE, width // TILE

    def load(k):
        if k in (7, 8):
            return pltpu.make_async_copy(sources[k].at[count:], kept[k].at[count:], w_sem.at[k])
        return pltpu.make_async_copy(sources[k], kept[k], w_sem.at[k])

    lacks = [
        pltpu.make_async_copy(sources[7].at[:count], kept[7].at[:count], w_sem.at[10]),
        pltpu.make_async_copy(sources[8].at[:count], kept[8].at[:count], w_sem.at[11]),
        pltpu.make_async_copy(sources[10].at[:count], first_dresid, w_sem.at[12]),
    ]
    loads = [load(k) for k in range(10)]
    for k in (3, 0, 5, 6, 1, 2, 4, 9, 7, 8):
        loads[k].start()

    @pl.when(section > 0)
    def _():
        for item in lacks:
            item.start()

    Line.greet()
    for where, _ in down.links:
        greet(where)
    gsum[...] = jnp.zeros_like(gsum)
    line_a.enter(down.levels)
    for k in (3, 0, 5, 6):
        loads[k].wait()

    def hidden(first):
        here = pl.ds(first, half)

        def one(i, c):
            columns = lanes(i, WIDE)
            d_act = with_transpose(dys[here], wdown[columns, :])
            gate_pre, up_pre = gate[here, columns].astype(F32), up[here, columns].astype(F32)
            sigma = jax.nn.sigmoid(gate_pre)
            d_silu = d_act * sigma
            dup[here, columns] = (d_silu * gate_pre).astype(BF16)
            dgate[here, columns] = (d_silu * up_pre * (1.0 + gate_pre * (1.0 - sigma))).astype(BF16)
            return c

        lax.fori_loop(0, tiles, one, 0)

    def back(first):
        here = pl.ds(first, half)

        def one(i, c):
            columns = lanes(i, WIDE)
            total = with_transpose(dgate[here], wgate[columns, :]) + with_transpose(dup[here], wup[columns, :])
            part[here, columns] = total.astype(BF16)
            return c

        lax.fori_loop(0, wide, one, 0)

    @pl.when(mine)
    def _():
        hidden(0)

    loads[1].wait()
    loads[2].wait()

    @pl.when(mine)
    def _():
        back(0)
        line_a.start()

    loads[4].wait()

    def down_job(i, c):
        weight_job(g_down, dys, act, i)
        return c

    lax.fori_loop(0, blocks, down_job, 0)
    down.start()

    @pl.when(mine)
    def _():
        hidden(half)
        back(half)
        line_b.start()

    for k in (9, 7, 8):
        loads[k].wait()

    @pl.when(section > 0)
    def _():
        lacks[0].wait()
        lacks[1].wait()

    late = 100
    spans = 5
    norm_rows = 2 * count // spans

    def step(i, c):
        @pl.when(mine)
        def _():
            line_a.step(i)
            line_b.step(i - line_a.steps)

        down.step(i, late)

        @pl.when(i < spans)
        def _():
            normalize_into(n2, resid, gain, i * norm_rows, norm_rows)

        @pl.when(jnp.logical_and(i >= spans, i < spans + blocks))
        def _():
            weight_job(g_gate, n2, dgate, i - spans)

        @pl.when(i == spans + blocks - 1)
        def _():
            gated.start()

        gated.step(i - spans - blocks, late)

        @pl.when(jnp.logical_and(i >= spans + blocks, i < spans + 2 * blocks))
        def _():
            weight_job(g_up, n2, dup, i - spans - blocks)

        return c

    lax.fori_loop(0, max(line_a.steps + line_b.steps, spans + 2 * blocks, spans + blocks + chunks), step, 0)
    run_steps(late, late + chunks, (lambda i: down.step(i, late), 0), (lambda i: gated.step(i, late), 0))

    @pl.when(mine)
    def _():
        line_a.finish()
        line_b.finish()

    @pl.when(section > 0)
    def _():
        lacks[2].wait()

    down.finish()
    gated.finish()


def last_ffn(known, weights, groups, cid):
    norm_one, wqkv, wout, norm_two, wgate, wup, wdown = weights
    dys, act, gate, up, dgate, dup, resid, dresid = known
    count, width = dys.shape[0] // 2, dys.shape[1]
    hidden = act.shape[1]
    pieces, chunks = 5, 8
    vmem = pl.BlockSpec(memory_space=pltpu.VMEM)
    far = pl.BlockSpec(memory_space=pl.ANY)
    sources = [wdown, wgate, wup, dys, act, gate, up, dgate, dup, resid]
    scratch = [pltpu.VMEM(item.shape, BF16) for item in sources]
    scratch += [
        pltpu.VMEM((2 * count, width), BF16),
        pltpu.VMEM((count, width), BF16),
        pltpu.VMEM((width, hidden), BF16),
        pltpu.VMEM((width, hidden), BF16),
        pltpu.SemaphoreType.DMA((13,)),
    ]
    scratch += Line.scratch(count // 4, pieces, width, False) * 2
    scratch += OwnScatter.scratch(groups, width // groups, hidden, chunks, BF16) * 2
    return pl.pallas_call(
        functools.partial(last_ffn_kernel, groups, pieces, chunks),
        out_shape=[
            jax.ShapeDtypeStruct((count, width), BF16),
            jax.ShapeDtypeStruct((1, width), F32),
            jax.ShapeDtypeStruct((width, hidden), BF16),
            jax.ShapeDtypeStruct((width // groups, hidden), F32),
            jax.ShapeDtypeStruct((width // groups, hidden), F32),
        ],
        in_specs=[vmem] + [far] * 11,
        out_specs=[vmem] * 5,
        scratch_shapes=scratch,
        compiler_params=pltpu.CompilerParams(
            collective_id=cid, has_side_effects=True, vmem_limit_bytes=VMEM_LIMIT
        ),
        name="last_ffn",
    )(norm_two[None], *sources, dresid)


def last_attn_kernel(groups, q_heads, k_heads, pieces, chunks, spare_chunks, *refs):
    refs = list(refs)

    def take(count):
        taken = refs[:count]
        del refs[:count]
        return taken

    cosine, sine, qcode, qstart, kcode, gain, dresid, holder, gains, spread_q, spread_k, spread_v, spread_o = take(13)
    sources = take(10)
    (dx_known,) = take(1)
    dx, returned, returned_second, gains_out, up_sum, attn_sum = take(6)
    wout, wqkv, x, q, kv, lse, mixed, dqkv, other_dresid, g_up = kept = take(10)
    plain, plain_mixed = take(2)
    part, dmixed, dkv, n1, g_attn, spares, spares_second, gsum, gains_own, gains_all, gains_sum, w_sem, g_s, g_r = take(14)
    levels = dp_bits(groups)
    count, width = part.shape
    half = count // 2
    keys = kv.shape[0]
    shares, owns, scatters = [], [], []
    for g in range(k_heads):
        share, own = take(2)
        shares.append(share)
        owns.append(own)
        scatters.append(OwnScatter(groups, count, 5, [share, own] + take(OwnScatter.refs(groups))))
    block = width // groups
    up_task, attn_task = [
        OwnScatter(groups, block, chunks, [value, total] + take(OwnScatter.refs(groups)))
        for value, total in ((g_up, up_sum), (g_attn, attn_sum))
    ]
    spare = spares.shape[0] // groups
    back_task = OwnScatter(groups, spare, spare_chunks, [spares, returned] + take(OwnScatter.refs(groups)))
    give = OwnScatter(groups, spare, spare_chunks, [spares_second, returned_second] + take(OwnScatter.refs(groups)))
    small = OwnScatter(groups, 8, 1, [gains_sum, gains_out] + take(OwnScatter.refs(groups)))
    line_a, line_b = [
        Line(k * half, half // 2, pieces, part, dresid, dx, take(12), norm=(x, gain, gsum)) for k in range(2)
    ]
    section, t = lax.axis_index("section"), lax.axis_index("tensor")
    mine = section == 0
    order = [9, 0, 3, 4, 5, 1, 2, 6, 7, 8]
    loads = [pltpu.make_async_copy(sources[k].at[: kept[k].shape[0]], kept[k], w_sem.at[k]) for k in range(10)]
    for k in order:
        loads[k].start()
    known = pltpu.make_async_copy(dx_known.at[:count], dx, w_sem.at[11])
    second = pltpu.make_async_copy(dx_known.at[count:], part, w_sem.at[10])
    second.start()

    @pl.when(section > 0)
    def _():
        known.start()

    for k in range(1, 4):
        greet({"tensor": lax.rem(t + k, 4)})
    for where, _ in up_task.links:
        greet(where)
    gsum[...] = jnp.zeros_like(gsum)
    dkv[...] = jnp.zeros_like(dkv)
    pl.semaphore_wait(pltpu.get_barrier_semaphore(), 3 + levels)
    loads[9].wait()
    up_task.start()
    for k in order[1:]:
        loads[k].wait()

    wide, jobs = width // WIDE, width // TILE
    repeat = q_heads // k_heads
    rows = block_rows(keys)
    blocks = half // rows
    turns = repeat * blocks
    scale = HD ** (-0.5)
    late = 100
    begun = 2 * k_heads * turns

    def early(i):
        @pl.when(lax.rem(i, 2) == 1)
        def _():
            up_task.step(i // 2, late)

    def mix(first):
        here = pl.ds(first, half)

        def one(h, c):
            dmixed[here, lanes(h)] = with_transpose(dresid[here], wout[lanes(h), :]).astype(BF16)
            return c

        lax.fori_loop(0, q_heads, one, 0)

    def attend(first, g, each):
        def one(i, c):
            h, n = g * repeat + i // blocks, lax.rem(i, blocks)
            here = pl.ds(pl.multiple_of(first + n * rows, rows), rows)
            scores, allowed = score_rows(q, kv, h, g, here, qcode, qstart, kcode)
            there = pl.ds(pl.multiple_of(h * count + first + n * rows, rows), rows)
            prob = jnp.where(allowed, jnp.exp(scores - lse[there][:, :1]), 0.0)
            dm = dmixed[here, lanes(h)]
            d_prob = with_transpose(dm, kv[:, lanes(k_heads + g)])
            row_dot = jnp.sum(prob * d_prob, axis=-1, keepdims=True)
            d_scores = (prob * (d_prob - row_dot)).astype(BF16)
            d_query = times(d_scores, kv[:, lanes(g)]) * scale
            dqkv[here, lanes(h)] = rolled(d_query, cosine[here], -sine[here]).astype(BF16)
            dkv[lanes(g), :] += rows_contract(q[here, lanes(h)], d_scores) * scale
            dkv[lanes(k_heads + g), :] += rows_contract(dm, prob.astype(BF16))
            each(i)
            return c

        lax.fori_loop(0, turns, one, 0)

    def back(first):
        here = pl.ds(first, half)

        def one(i, c):
            columns = lanes(i, WIDE)
            part[here, columns] = with_transpose(dqkv[here], wqkv[columns, :]).astype(BF16)
            return c

        lax.fori_loop(0, wide, one, 0)

    @pl.when(mine)
    def _():
        mix(0)
        mix(half)
        for g in range(k_heads):
            for first in (0, half):
                at = 2 * g * turns + (turns if first else 0)
                attend(first, g, lambda i: early(at + i))

            shares[g][:, :LANES] = jnp.transpose(dkv[lanes(g), :]).astype(BF16)
            shares[g][:, LANES:] = jnp.transpose(dkv[lanes(k_heads + g), :]).astype(BF16)
            scatters[g].start()
        run_steps(0, scatters[0].chunks, *[(functools.partial(lambda s, i: s.step(i, late), s), 0) for s in scatters])

    @pl.when(section > 0)
    def _():
        run_steps(0, begun, (early, 0))
        known.wait()

    ends = [0]
    for item in (spread_q, spread_k, spread_v, spread_o):
        ends.append(ends[-1] + item.shape[0])
    starts = [0, q_heads, q_heads + k_heads, q_heads + 2 * k_heads]
    second.wait()
    spares_second[...] = times(holder[groups * spare :], part[...]).astype(BF16)
    give.start()
    normalize_into(n1, x, gain, 0, 2 * count)
    plain_mixed[...] = with_transpose(mixed[...], spread_o[...]).astype(BF16)
    other_dresid[:count] = dresid[...]

    def out_job(i, c):
        here = lanes(i, TILE)
        g_attn[here, ends[3] :] = rows_contract(other_dresid[:, here], plain_mixed[...]).astype(BF16)
        return c

    lax.fori_loop(0, jobs, out_job, 0)

    @pl.when(mine)
    def _():
        ending = late + scatters[0].chunks
        run_steps(late, ending, *[(functools.partial(lambda s, i: s.step(i, late), s), 0) for s in scatters])
        for g in range(k_heads):
            dqkv[:count, lanes(q_heads + g)] = rolled(owns[g][:, :LANES], cosine[...], -sine[...]).astype(BF16)
            dqkv[:count, lanes(q_heads + k_heads + g)] = owns[g][:, LANES:].astype(BF16)
        back(0)
        line_a.start()
        back(half)
        line_b.start()

    def spread(k):
        return remote(gains_own, gains_all.at[k - 1], g_s.at[k - 1], g_r.at[k - 1], {"tensor": lax.rem(t + k, 4)})

    first_job = begun // 2

    def step(i, c):
        @pl.when(mine)
        def _():
            line_a.step(i)
            line_b.step(i - line_a.steps)

        up_task.step(i + first_job, late)

        @pl.when(i == 0)
        def _():
            for a, b, n, item in zip(starts, starts[1:], ends, (spread_q, spread_k, spread_v)):
                plain[:, n : n + item.shape[0]] = with_transpose(
                    dqkv[:, a * LANES : b * LANES], item[...]
                ).astype(BF16)

        @pl.when(jnp.logical_and(i >= 1, i <= jobs))
        def _():
            here = lanes(jnp.clip(i - 1, 0, jobs - 1), TILE)
            g_attn[here, : ends[3]] = rows_contract(n1[:, here], plain[...]).astype(BF16)

        @pl.when(i == jobs)
        def _():
            attn_task.start()

        give.step(i - first_job, late)
        attn_task.step(i - jobs - 1, late)
        return c

    lax.fori_loop(0, max(line_a.steps + line_b.steps, jobs + 1 + chunks), step, 0)
    spares[...] = times(holder[: groups * spare], dx[...]).astype(BF16)
    back_task.start()
    section_one = jnp.where(mine, 1.0, 0.0)
    gains_own[...] = gains[...]
    gains_own[:1] = gains[:1] + gsum[...] * section_one
    for k in range(1, 4):
        spread(k).start()
    for k in range(1, 4):
        spread(k).wait()
    total = gains_own[...] + gains_all[0] + gains_all[1] + gains_all[2]
    part_width = width // groups
    for d in range(groups):
        gains_sum[8 * d : 8 * d + 8, :] = total[:, d * part_width : (d + 1) * part_width]
    small.start()

    def close(i, c):
        back_task.step(i, late)
        small.step(i, 2)
        up_task.step(late + i, late)
        attn_task.step(late + i, late)
        give.step(late + i, late)
        return c

    lax.fori_loop(0, max(chunks, spare_chunks, small.steps(2)), close, 0)
    run_steps(late, late + spare_chunks, (lambda i: back_task.step(i, late), 0))

    @pl.when(mine)
    def _():
        line_a.finish()
        line_b.finish()
        for item in scatters:
            item.finish()

    for item in (up_task, attn_task, back_task, give, small):
        item.finish()


def last_attn(known, spots, dresid, dx, holder, gains, spreads, grads, weights, groups, q_heads, k_heads, cid):
    norm_one, wqkv, wout, norm_two, wgate, wup, wdown = weights
    x, q, kv, lse, mixed, dqkv, other_dresid = known
    count, width = dresid.shape
    keys = groups * count
    spare = holder.shape[0] // (2 * groups)
    pieces, chunks, spare_chunks = 5, 8, spare // 32
    vmem = pl.BlockSpec(memory_space=pltpu.VMEM)
    far = pl.BlockSpec(memory_space=pl.ANY)
    dma = pltpu.SemaphoreType.DMA
    sources = [wout, wqkv, x, q, kv, lse, mixed, dqkv, other_dresid, *grads]
    attn_width = sum(item.shape[0] for item in spreads)
    block = width // groups
    first_only = {3: count, 4: keys, 5: q_heads * count}
    scratch = [
        pltpu.VMEM((first_only.get(k, item.shape[0]),) + item.shape[1:], item.dtype) for k, item in enumerate(sources)
    ]
    scratch += [
        pltpu.VMEM((2 * count, attn_width - spreads[3].shape[0]), BF16),
        pltpu.VMEM((2 * count, spreads[3].shape[0]), BF16),
        pltpu.VMEM((count, width), BF16),
        pltpu.VMEM((count, q.shape[1]), BF16),
        pltpu.VMEM((kv.shape[1], keys), F32),
        pltpu.VMEM((2 * count, width), BF16),
        pltpu.VMEM((width, attn_width), BF16),
        pltpu.VMEM((groups * spare, width), BF16),
        pltpu.VMEM((groups * spare, width), BF16),
        pltpu.VMEM((1, width), F32),
        pltpu.VMEM(gains.shape, F32),
        pltpu.VMEM((3,) + gains.shape, F32),
        pltpu.VMEM((groups * 8, block), F32),
        dma((12,)),
        dma((3,)),
        dma((3,)),
    ]
    for _ in range(k_heads):
        scratch += [pltpu.VMEM((keys, 2 * LANES), BF16), pltpu.VMEM((count, 2 * LANES), F32)]
        scratch += OwnScatter.scratch(groups, count, 2 * LANES, 5, BF16)
    for columns in (grads[0].shape[1], attn_width):
        scratch += OwnScatter.scratch(groups, block, columns, chunks, BF16)
    scratch += OwnScatter.scratch(groups, spare, width, spare_chunks, BF16) * 2
    scratch += OwnScatter.scratch(groups, 8, block, 1, F32)
    scratch += Line.scratch(count // 4, pieces, width, False) * 2
    return pl.pallas_call(
        functools.partial(last_attn_kernel, groups, q_heads, k_heads, pieces, chunks, spare_chunks),
        out_shape=[
            jax.ShapeDtypeStruct((count, width), BF16),
            jax.ShapeDtypeStruct((spare, width), BF16),
            jax.ShapeDtypeStruct((spare, width), BF16),
            jax.ShapeDtypeStruct((8, block), F32),
            jax.ShapeDtypeStruct((block, grads[0].shape[1]), F32),
            jax.ShapeDtypeStruct((block, attn_width), F32),
        ],
        in_specs=[vmem] * 13 + [far] * 11,
        out_specs=[vmem] * 6,
        scratch_shapes=scratch,
        compiler_params=pltpu.CompilerParams(
            collective_id=cid, has_side_effects=True, vmem_limit_bytes=VMEM_LIMIT
        ),
        name="last_attn",
    )(*spots, norm_one[None], dresid, holder, gains, *spreads, *sources, dx)


def finish_kernel(groups, parts, *refs):
    refs = list(refs)

    def take(count):
        taken = refs[:count]
        del refs[:count]
        return taken

    (live,) = take(1)
    through, y, y_back, cot, dx_first, dx_second, back_first, back_second = take(8)
    gate, up, down, attn = take(4)
    acts, backs = take(2)
    outs = take(7)
    tiles = take(4)
    rows = take(4)
    backs_near = take(4)
    down_near, down_turned, attn_near, *attn_parts = take(7)
    plain_near = take(2)
    sems, out_sems = take(2)
    count, spare = rows[0].shape[0], backs_near[0].shape[0]
    seq = count + spare
    whole = [
        (through.at[0, 0], y.at[:count], y_back.at[:spare], acts.at[0, 0, 0]),
        (through.at[1, 0], y.at[count:], y_back.at[spare:], acts.at[0, 1, 0]),
        (cot.at[0, 0], dx_first, back_first, backs.at[0, 0, 0]),
        (cot.at[1, 0], dx_second.at[count:], back_second, backs.at[0, 1, 0]),
    ]
    query_out, key_out, value_out, out_out, gate_out, up_out, down_out = outs
    plain_in = [pltpu.make_async_copy(a, b, sems.at[14 + k]) for k, (a, b) in enumerate(zip((gate, up), plain_near))]
    plain = [pltpu.make_async_copy(a, b, out_sems.at[k]) for k, (a, b) in enumerate(zip(plain_near, (gate_out.at[0], up_out.at[0])))]
    load_down = pltpu.make_async_copy(down, down_near, sems.at[12])
    load_attn = pltpu.make_async_copy(attn, attn_near, sems.at[13])
    loads = []
    for k, (a, b, c, _) in enumerate(whole):
        loads.append(
            [
                pltpu.make_async_copy(src, dst, sems.at[3 * k + n])
                for n, (src, dst) in enumerate(((a, tiles[k]), (b, rows[k]), (c, backs_near[k])))
            ]
        )
    load_attn.start()
    load_down.start()
    for item in plain_in:
        item.start()
    for group in loads:
        for item in group:
            item.start()
    stores = []
    load_attn.wait()
    at = 0
    for k, (size, near, there) in enumerate(zip(parts, attn_parts, (query_out, key_out, value_out, out_out))):
        value = attn_near[:, at : at + size]
        near[...] = value if k == 0 else jnp.transpose(value)
        at += size
        stores.append(pltpu.make_async_copy(near, there.at[0], out_sems.at[2 + k]))
        stores[-1].start()
    for before, item in zip(plain_in, plain):
        before.wait()
        item.start()
    load_down.wait()
    down_turned[...] = jnp.transpose(down_near[...])
    stores.append(pltpu.make_async_copy(down_turned, down_out.at[0], out_sems.at[6]))
    stores[-1].start()
    for k, group in enumerate(loads):
        for item in group:
            item.wait()
        first = (k % 2) * seq

        def one(i, c):
            here = pl.ds(pl.multiple_of(i * 64, 64), 64)
            alive = live[pl.ds(pl.multiple_of(first + i * 64, 64), 64)] > 0
            tiles[k][here] = jnp.where(alive, rows[k][here], tiles[k][here])
            return c

        lax.fori_loop(0, count // 64, one, 0)

        def two(i, c):
            near = pl.ds(pl.multiple_of(i * 64, 64), 64)
            here = pl.ds(pl.multiple_of(count + i * 64, 64), 64)
            alive = live[pl.ds(pl.multiple_of(first + count + i * 64, 64), 64)] > 0
            tiles[k][here] = jnp.where(alive, backs_near[k][near], tiles[k][here])
            return c

        lax.fori_loop(0, spare // 64, two, 0)
        stores.append(pltpu.make_async_copy(tiles[k], whole[k][3], out_sems.at[7 + k]))
        stores[-1].start()
    for item in stores + plain:
        item.wait()


def finish(live, through, y, y_back, cot, dx_first, dx_second, back_first, back_second, grads, parts, groups):
    count, width = dx_first.shape
    spare = back_first.shape[0]
    gate, up, down, attn = grads
    block, hidden = down.shape
    vmem = pl.BlockSpec(memory_space=pltpu.VMEM)
    far = pl.BlockSpec(memory_space=pl.ANY)
    shapes = [(block, parts[0])] + [(size, block) for size in parts[1:]]
    outs = [jax.ShapeDtypeStruct((1, 2, 1, count + spare, width), BF16)] * 2
    outs += [jax.ShapeDtypeStruct((1,) + item, F32) for item in shapes + [gate.shape, up.shape, (hidden, block)]]
    scratch = [pltpu.VMEM((count + spare, width), BF16)] * 4
    scratch += [pltpu.VMEM((count, width), BF16)] * 4 + [pltpu.VMEM((spare, width), BF16)] * 4
    scratch += [pltpu.VMEM(down.shape, F32), pltpu.VMEM((hidden, block), F32), pltpu.VMEM(attn.shape, F32)]
    scratch += [pltpu.VMEM(item, F32) for item in shapes]
    scratch += [pltpu.VMEM(gate.shape, F32), pltpu.VMEM(up.shape, F32)]
    scratch += [pltpu.SemaphoreType.DMA((16,)), pltpu.SemaphoreType.DMA((11,))]
    return pl.pallas_call(
        functools.partial(finish_kernel, groups, parts),
        out_shape=outs,
        in_specs=[vmem] + [far] * 12,
        out_specs=[far] * 9,
        scratch_shapes=scratch,
        compiler_params=pltpu.CompilerParams(vmem_limit_bytes=VMEM_LIMIT),
        name="finish",
    )(live, through, y, y_back, cot, dx_first, dx_second, back_first, back_second, gate, up, down, attn)


def rope_tables(pos):
    half_width = HD // 2
    inverse = rope_base ** (-(jnp.arange(half_width, dtype=F32) * 2.0 / HD))
    angle = pos.astype(F32)[:, None] * inverse[None, :]
    blank = jnp.zeros((pos.shape[0], LANES // 2 - half_width), F32)
    cosine, sine = jnp.cos(angle), jnp.sin(angle)
    return (
        jnp.concatenate([cosine, blank, cosine, blank], axis=1),
        jnp.concatenate([-sine, blank, sine, blank], axis=1),
    )


def spreader(heads, turned):
    feature = jnp.arange(HD)
    place = jnp.where(feature < HD // 2, feature, feature - HD // 2 + LANES // 2) if turned else feature
    lane = (jnp.arange(heads)[:, None] * LANES + place[None, :]).reshape(-1)
    return (lane[:, None] == jnp.arange(heads * LANES)[None, :]).astype(BF16)


def slots_of(lens, count):
    groups = lens.shape[0]
    kept = jnp.minimum(lens, count)
    free, extra = count - kept, lens - kept
    free_off = jnp.cumsum(free) - free
    extra_end = jnp.cumsum(extra)
    slot = jnp.arange(count)
    own = slot[None, :] < kept[:, None]
    index = free_off[:, None] + slot[None, :] - kept[:, None]
    source = jnp.sum(index[:, :, None] >= extra_end[None, None, :], axis=-1)
    begins = jnp.sum(jnp.where(index[:, :, None] >= extra_end[None, None, :], extra[None, None, :], 0), axis=-1)
    seq = jnp.where(own, jnp.arange(groups)[:, None], source)
    pos = jnp.where(own, slot[None, :], count + index - begins)
    return seq, pos, own


def on_device(
    inputs,
    cotangent,
    lengths,
    norm_attn,
    w_query,
    w_key,
    w_value,
    w_out,
    norm_ffn,
    w_gate,
    w_up,
    w_down,
):
    first = lax.axis_index("section") == 0
    me = lax.axis_index("dp")
    groups = lax.axis_size("dp")
    micro, seq_len, width = inputs.shape[0], inputs.shape[2], inputs.shape[3]
    count = seq_len * 5 // 8
    spare = seq_len - count
    q_heads, k_heads = w_query.shape[2] // HD, w_key.shape[2] // HD
    spread_q, spread_k = spreader(q_heads, True), spreader(k_heads, True)
    spread_v, spread_o = spreader(k_heads, False), spreader(q_heads, False)
    wqkv = jnp.concatenate(
        [times(w_query[0], spread_q), times(w_key[0], spread_k), times(w_value[0], spread_v)], axis=1
    ).astype(BF16)
    wout = rows_contract(spread_o, w_out[0]).astype(BF16)
    weights = (norm_attn[0], wqkv, wout, norm_ffn[0], w_gate[0], w_up[0], w_down[0])

    all_in_one = micro == 2 and groups == 4

    source = jnp.where(first, inputs[:, 0], cotangent[:, 0])
    first_extra = lax.all_gather(source[0, count:], "dp", axis=0, tiled=True)
    length_rows = jnp.broadcast_to(lengths[:, 0].astype(F32)[:, None], (micro, LANES))
    length_rows = jnp.concatenate([length_rows, jnp.zeros((8 - micro, LANES), F32)], axis=0)
    (length_all,) = gather_rows([length_rows], groups, 4)
    lens = length_all.reshape(groups, 8, LANES)[:, :micro, 0].T.astype(jnp.int32)
    packed, slots, chosen, kept_own = [], [], [], []
    for b in range(micro):
        seq, pos, own = slots_of(lens[b], count)
        slots.append((seq, pos))
        wanted = seq[me] * spare + pos[me] - count
        chosen.append(
            jnp.logical_and(jnp.arange(groups * spare)[None, :] == wanted[:, None], ~own[me][:, None]).astype(BF16)
        )
        kept_own.append(jnp.where(own[me][:, None], source[b, :count], jnp.zeros((), BF16)))
    for b in range(1 if all_in_one else micro):
        extra = first_extra if b == 0 else lax.all_gather(source[b, count:], "dp", axis=0, tiled=True)
        brought = times(chosen[b], extra)
        packed.append((kept_own[b].astype(F32) + brought).astype(BF16))

    def spots_of(b):
        seq, pos = slots[b]
        code = seq * seq_len + pos
        return rope_tables(pos[me]) + (code[me][:, None], (seq[me] * seq_len)[:, None], code.reshape(1, -1))

    spots = [spots_of(b) for b in range(micro)]

    def holder(b):
        seq, pos = slots[b]
        row = jnp.arange(groups * spare)[:, None]
        return jnp.logical_and(row == seq[me][None, :] * spare + pos[me][None, :] - count, pos[me][None, :] >= count)

    def spread(rows, b):
        return jnp.dot(holder(b).astype(BF16), rows, preferred_element_type=F32).astype(BF16)

    def unpack(rows, back, b, through):
        live = (jnp.arange(seq_len) < lens[b, me])[:, None]
        return jnp.where(live, jnp.concatenate([rows, back], axis=0), through)

    def come_back(rows, b):
        return lax.psum_scatter(spread(rows, b), "dp", scatter_dimension=0, tiled=True)

    norm_one, norm_two = weights[0], weights[3]
    empty = jnp.zeros((count, width), BF16)

    def spots_at(tick):
        early, late = spots[min(tick, micro - 1)], spots[max(tick - 1, 0)]
        return tuple(jnp.where(first, a, b) for a, b in zip(early, late))

    grads_in, before, gain_sums = [], [], []
    if all_in_one:
        joined = [jnp.concatenate(items, axis=0) for items in zip(*spots)]
        joined[4] = joined[4][:, None]
        held = jnp.concatenate([holder(b) for b in range(micro)], axis=0).astype(BF16)
        y, dx, y_back, x, q, kv, lse, mixed, resid, gate, up, act, dy, d_resid, d_gate, d_up, d_qkv, gain_one, gain_two = main_ticks(
            packed[0],
            (kept_own[1], source[1, count:], chosen[1]),
            joined,
            held,
            weights,
            groups,
            q_heads,
            k_heads,
            0,
        )
        first_dresid, gain_last, grad_up, grad_down, grad_gate = last_ffn(
            (dy, act, gate, up, d_gate, d_up, resid, d_resid), weights, groups, 1
        )
        gain_last = jnp.where(first, gain_last, jnp.zeros_like(gain_last))
        gains = jnp.concatenate([gain_one, gain_two + gain_last, jnp.zeros((6, width), F32)], axis=0)
        last_dx, back_first, back_second, gains, grad_up, grad_attn = last_attn(
            (x, q, kv, lse, mixed, d_qkv, d_resid),
            spots[0],
            first_dresid,
            dx,
            held,
            gains,
            (spread_q, spread_k, spread_v, spread_o),
            (grad_up,),
            weights,
            groups,
            q_heads,
            k_heads,
            2,
        )
        live = (jnp.arange(seq_len)[None, :] < lens[:, me][:, None]).astype(jnp.int32).reshape(-1, 1)
        acts, backs, *grads = finish(
            live,
            inputs,
            y,
            y_back,
            cotangent,
            last_dx,
            dx,
            back_first,
            back_second,
            (grad_gate, grad_up, grad_down, grad_attn),
            [w_query.shape[2], w_key.shape[2], w_value.shape[2], w_query.shape[2]],
            groups,
        )
        grads[1:3] = [jnp.swapaxes(item, 1, 2) for item in grads[1:3]]
        return (acts, backs, gains[:1], *grads[:4], gains[1:2], *grads[4:])

    else:
        arriving = empty
        results, saved = [], []
        for tick in range(micro + 1):
            stream = jnp.where(first, packed[tick] if tick < micro else empty, arriving)
            result, arriving, kept = forward_tick(stream, spots_at(tick), weights, groups, q_heads, k_heads, 0)
            results.append(result)
            saved.append(kept)
        results = [jnp.where(first, results[b], results[b + 1]) for b in range(micro)]
        arriving = empty
        for tick in range(micro):
            kept = saved[micro - tick]
            incoming = jnp.where(first, arriving, packed[micro - 1 - tick])
            d_resid, gain_two, d_gate, d_up = back_ffn(incoming, kept, weights, 1)
            d_stream, gain_one, d_qkv, arriving = back_attn(
                d_resid, kept, spots_at(micro - tick), weights, groups, q_heads, k_heads, 2, -1
            )
            before.append((kept[5], d_gate, d_up, incoming, kept[8], kept[0], d_qkv, d_resid, kept[4]))
            grads_in.append(d_stream)
            gain_sums.append(jnp.concatenate([gain_one, gain_two], axis=0))
        kept_last = saved[0]
        last_in, last_spots = jnp.where(first, arriving, empty), spots_at(0)
        grads_at = [grads_in[micro - 1 - b] if b == 0 else jnp.where(first, grads_in[micro - b], grads_in[micro - 1 - b]) for b in range(micro)]

        def all_rows(now, index):
            old = [item[index] for item in before]
            return jnp.concatenate([jnp.where(first, now, old[0])] + old[1:], axis=0)

        x, mixed, resid, act = kept_last[0], kept_last[4], kept_last[5], kept_last[8]
        d_resid, gain_two, d_gate, d_up = back_ffn(last_in, kept_last, weights, 1)
        n2 = normalize(all_rows(resid, 0), norm_two)
        grad_gate = rows_contract(n2, all_rows(d_gate, 1)).astype(BF16)
        grad_up = rows_contract(n2, all_rows(d_up, 2)).astype(BF16)
        grad_down = rows_contract(all_rows(last_in, 3), all_rows(act, 4)).astype(BF16)
        ffn_grads = (grad_gate, grad_up, grad_down)
        beside = len(ffn_grads) if groups * count <= 2048 else 1
        d_stream, gain_one, d_qkv, *ffn_sums = back_attn(
            d_resid, kept_last, last_spots, weights, groups, q_heads, k_heads, 3, 0, sums=ffn_grads[:beside]
        )
        n1 = normalize(all_rows(x, 5), norm_one)
        back_spread = [(spread_q, 0, q_heads), (spread_k, q_heads, k_heads), (spread_v, q_heads + k_heads, k_heads)]
        dqkv = all_rows(d_qkv, 6)
        dqkv = jnp.concatenate(
            [with_transpose(dqkv[:, i * LANES : (i + n) * LANES], item) for item, i, n in back_spread], axis=1
        ).astype(BF16)
        mix = with_transpose(all_rows(mixed, 8), spread_o).astype(BF16)
        grad_attn = jnp.concatenate(
            [rows_contract(n1, dqkv).astype(BF16), rows_contract(all_rows(d_resid, 7), mix).astype(BF16)], axis=1
        )
        grads_at[0] = jnp.where(first, d_stream, grads_at[0])
        last_gains = jnp.concatenate([gain_one, gain_two], axis=0)
        gain_sums.append(jnp.where(first, last_gains, jnp.zeros_like(last_gains)))

        gains = sum(gain_sums[1:], gain_sums[0])
        gains = jnp.concatenate([gains, jnp.zeros((6, width), F32)], axis=0)
        gains = gains.reshape(8, groups, -1).transpose(1, 0, 2).reshape(groups * 8, -1)

    acts = []
    for b in range(micro):
        rows = results[b]
        acts.append(unpack(rows, come_back(rows, b), b, inputs[b, 0]))
    backs = []
    for b in range(micro):
        rows = grads_at[b]
        if b == 0:
            back, gains, grad_attn, *rest = return_rows(
                spread(rows, b), gains, (grad_attn,) + ffn_grads[beside:], groups, 5, spare // 16
            )
            grad_gate, grad_up, grad_down = ffn_sums + rest
        else:
            back = come_back(rows, b)
        backs.append(unpack(rows, back, b, cotangent[b, 0]))
    acts, backs = jnp.stack(acts), jnp.stack(backs)
    ends = [0]
    for item in (w_query, w_key, w_value, w_query):
        ends.append(ends[-1] + item.shape[2])
    grad_query, grad_key, grad_value, grad_out = (grad_attn[:, a:b] for a, b in zip(ends, ends[1:]))
    final = (
        gains[0],
        grad_query,
        grad_key,
        grad_value,
        grad_out.T,
        gains[1],
        grad_gate,
        grad_up,
        grad_down.T,
    )
    return (acts[None, :, None], backs[None, :, None]) + tuple(item[None] for item in final)


def solution(mesh):
    placed = (
        P(None, "dp", None, None),
        P(None, "dp", None, None),
        P(None, "dp"),
        P("section", None),
        P("section", None, "tensor"),
        P("section", None, "tensor"),
        P("section", None, "tensor"),
        P("section", "tensor", None),
        P("section", None),
        P("section", None, "tensor"),
        P("section", None, "tensor"),
        P("section", "tensor", None),
    )
    return jax.shard_map(
        on_device,
        mesh=mesh,
        in_specs=placed,
        out_specs=(
            P("section", None, "dp", None, None),
            P("section", None, "dp", None, None),
            P("section", "dp"),
            P("section", "dp", "tensor"),
            P("section", "dp", "tensor"),
            P("section", "dp", "tensor"),
            P("section", "tensor", "dp"),
            P("section", "dp"),
            P("section", "dp", "tensor"),
            P("section", "dp", "tensor"),
            P("section", "tensor", "dp"),
        ),
        check_vma=False,
    )
```

```python
import functools

import jax
import jax.numpy as jnp
from jax import lax
from jax.experimental import pallas as pl
from jax.experimental.pallas import tpu as pltpu
from jax.sharding import PartitionSpec as P

HD = 96

epsilon = 1e-05
rope_base = 100000.0
negative = -1e30
MESH = pl.DeviceIdType.MESH
F32 = jnp.float32
BF16 = jnp.bfloat16


def remote(src, dst, s_sem, r_sem, where):
    return pltpu.make_async_remote_copy(
        src_ref=src, dst_ref=dst, send_sem=s_sem, recv_sem=r_sem, device_id=where, device_id_type=MESH
    )


def greet(where):
    pl.semaphore_signal(pltpu.get_barrier_semaphore(), inc=1, device_id=where, device_id_type=MESH)


def dp_bits(groups):
    return groups.bit_length() - 1


def dp_partner(level):
    me = lax.axis_index("dp")
    bit = lax.rem(me // (1 << level), 2)
    return {"dp": me + (1 - 2 * bit) * (1 << level)}, bit


class Scatter:
    def __init__(self, groups, rows, chunks, refs):
        self.levels = dp_bits(groups)
        self.groups, self.rows, self.chunks, self.size = groups, rows, chunks, rows // chunks
        self.value, self.out = refs[0], refs[1]
        m = self.levels
        self.arrive = refs[2 : 2 + m]
        self.held = refs[2 + m : 1 + 2 * m]
        self.s_sem = refs[1 + 2 * m : 1 + 3 * m]
        self.r_sem = refs[1 + 3 * m : 1 + 4 * m]
        self.links = [dp_partner(k) for k in range(m)]

    @staticmethod
    def scratch(groups, rows, width, chunks, dtype):
        m = dp_bits(groups)
        sizes = [groups >> (k + 1) for k in range(m)]
        return (
            [pltpu.VMEM((size * rows, width), dtype) for size in sizes]
            + [pltpu.VMEM((size * rows, width), dtype) for size in sizes[:-1]]
            + [pltpu.SemaphoreType.DMA((size, chunks)) for size in sizes] * 2
        )

    def at(self, block, c):
        return pl.ds(pl.multiple_of(block * self.rows + c * self.size, self.size), self.size)

    def copy(self, level, slot, c):
        where, bit = self.links[level]
        source = self.value if level == 0 else self.held[level - 1]
        return remote(
            source.at[self.at(2 * slot + 1 - bit, c)],
            self.arrive[level].at[self.at(slot, c)],
            self.s_sem[level].at[slot, c],
            self.r_sem[level].at[slot, c],
            where,
        )

    def order(self, level):
        count = self.groups >> (level + 1)
        if count == 1:
            return [(0, False)]
        bit = self.links[level + 1][1]
        return [(2 * i + 1 - bit, True) for i in range(count // 2)] + [(2 * i + bit, False) for i in range(count // 2)]

    def start(self):
        def one(c, carry):
            for slot, _ in self.order(0):
                self.copy(0, slot, c).start()
            return carry

        lax.fori_loop(0, self.chunks, one, 0)

    def step(self, i, lag):
        for level in range(self.levels):
            c = i - level * lag

            @pl.when(jnp.logical_and(c >= 0, c < self.chunks))
            def _():
                bit = self.links[level][1]
                source = self.value if level == 0 else self.held[level - 1]
                for slot, goes in self.order(level):
                    self.copy(level, slot, c).wait_recv()
                    here = self.at(slot, c)
                    total = source[self.at(2 * slot + bit, c)].astype(F32) + self.arrive[level][here].astype(F32)
                    if level == self.levels - 1:
                        self.out[here] = total.astype(self.out.dtype)
                    else:
                        self.held[level][here] = total.astype(self.held[level].dtype)
                        if goes:
                            self.copy(level + 1, slot // 2, c).start()

    def steps(self, lag):
        return self.chunks + (self.levels - 1) * lag

    def finish(self):
        def one(c, carry):
            for level in range(self.levels):
                for slot in range(self.groups >> (level + 1)):
                    self.copy(level, slot, c).wait_send()
            return carry

        lax.fori_loop(0, self.chunks, one, 0)


def return_kernel(groups, rows, chunks, plans, *refs):
    refs = list(refs)

    def take(count):
        taken = refs[:count]
        del refs[:count]
        return taken

    m = dp_bits(groups)
    count = 4 * m - 1
    value, gains = take(2)
    grads = take(len(plans))
    out, gains_out = take(2)
    totals = take(len(plans))
    gains_all, gains_sum, g_s, g_r = take(4)
    task = Scatter(groups, rows, chunks, [value, out] + take(count))
    small = Scatter(groups, 8, 1, [gains_sum, gains_out] + take(count))
    large = [
        Scatter(groups, block, parts, [grad, total] + take(count))
        for (block, parts), grad, total in zip(plans, grads, totals)
    ]
    t = lax.axis_index("tensor")
    for where, _ in task.links:
        greet(where)
    for k in range(1, 4):
        greet({"tensor": lax.rem(t + k, 4)})
    pl.semaphore_wait(pltpu.get_barrier_semaphore(), m + 3)

    def spread(k):
        return remote(gains, gains_all.at[k - 1], g_s.at[k - 1], g_r.at[k - 1], {"tensor": lax.rem(t + k, 4)})

    for k in range(1, 4):
        spread(k).start()
    task.start()
    for item in large:
        item.start()
    for k in range(1, 4):
        spread(k).wait()
    gains_sum[...] = gains[...] + gains_all[0] + gains_all[1] + gains_all[2]
    small.start()

    def body(i, c):
        small.step(i, 1)
        task.step(i, 2)
        for item in large:
            item.step(i, 4)
        return c

    lax.fori_loop(0, max([task.steps(2), small.steps(1)] + [item.steps(4) for item in large]), body, 0)
    small.finish()
    task.finish()
    for item in large:
        item.finish()


def return_rows(value, gains, grads, groups, cid, chunks):
    rows, width = value.shape[0] // groups, value.shape[1]
    vmem = pl.BlockSpec(memory_space=pltpu.VMEM)
    part = gains.shape[1]
    plans, outs = [], [jax.ShapeDtypeStruct((rows, width), BF16), jax.ShapeDtypeStruct((8, part), F32)]
    scratch = [
        pltpu.VMEM((3,) + gains.shape, F32),
        pltpu.VMEM(gains.shape, F32),
        pltpu.SemaphoreType.DMA((3,)),
        pltpu.SemaphoreType.DMA((3,)),
    ]
    scratch += Scatter.scratch(groups, rows, width, chunks, BF16) + Scatter.scratch(groups, 8, part, 1, F32)
    for grad in grads:
        block = grad.shape[0] // groups
        plans.append((block, max(1, block // 48)))
        outs.append(jax.ShapeDtypeStruct((block, grad.shape[1]), F32))
        scratch += Scatter.scratch(groups, block, grad.shape[1], plans[-1][1], BF16)
    return pl.pallas_call(
        functools.partial(return_kernel, groups, rows, chunks, plans),
        out_shape=outs,
        in_specs=[vmem] * (2 + len(grads)),
        out_specs=[vmem] * len(outs),
        scratch_shapes=scratch,
        compiler_params=pltpu.CompilerParams(
            collective_id=cid, has_side_effects=True, vmem_limit_bytes=VMEM_LIMIT
        ),
        name="return_%d" % cid,
    )(value, gains, *grads)


def gather_kernel(groups, count, *refs):
    values, outs = refs[:count], refs[count : 2 * count]
    s_sem, r_sem, own = refs[2 * count :]
    m = dp_bits(groups)
    me = lax.axis_index("dp")
    links = [dp_partner(k) for k in range(m)]
    for where, _ in links:
        greet(where)
    pl.semaphore_wait(pltpu.get_barrier_semaphore(), m)

    def place(a, block):
        rows = values[a].shape[0]
        return outs[a].at[pl.ds(pl.multiple_of(block * rows, rows), rows)]

    def copy(a, level, i, mine):
        where, bit = links[level]
        low = lax.rem(me, 1 << (level + 1))
        if not mine:
            low = low + (1 - 2 * bit) * (1 << level)
        block = i * (1 << (level + 1)) + low
        return remote(place(a, block), place(a, block), s_sem.at[a, level, i], r_sem.at[a, level, i], where)

    locals_ = [pltpu.make_async_copy(values[a], place(a, me), own.at[a]) for a in range(count)]
    for item in locals_:
        item.start()
    for item in locals_:
        item.wait()
    for level in reversed(range(m)):
        for i in range(groups >> (level + 1)):
            for a in range(count):
                copy(a, level, i, True).start()
        for i in range(groups >> (level + 1)):
            for a in range(count):
                copy(a, level, i, False).wait_recv()
    for level in range(m):
        for i in range(groups >> (level + 1)):
            for a in range(count):
                copy(a, level, i, True).wait_send()


def gather_rows(values, groups, cid):
    vmem = pl.BlockSpec(memory_space=pltpu.VMEM)
    m, count = dp_bits(groups), len(values)
    dma = pltpu.SemaphoreType.DMA
    return pl.pallas_call(
        functools.partial(gather_kernel, groups, count),
        out_shape=[jax.ShapeDtypeStruct((groups * v.shape[0], v.shape[1]), v.dtype) for v in values],
        in_specs=[vmem] * count,
        out_specs=[vmem] * count,
        scratch_shapes=[dma((count, m, groups // 2)), dma((count, m, groups // 2)), dma((count,))],
        compiler_params=pltpu.CompilerParams(
            collective_id=cid, has_side_effects=True, vmem_limit_bytes=48 * 2**20
        ),
        name="gather_%d" % cid,
    )(*values)


class OwnScatter(Scatter):
    def __init__(self, groups, rows, chunks, refs):
        m = dp_bits(groups)
        super().__init__(groups, rows, chunks, list(refs[: 2 + m]) + [None] * (m - 1) + list(refs[2 + m :]))
        self.me = lax.axis_index("dp")

    @staticmethod
    def scratch(groups, rows, width, chunks, dtype):
        m = dp_bits(groups)
        kinds = Scatter.scratch(groups, rows, width, chunks, dtype)
        return kinds[:m] + kinds[2 * m - 1 :]

    @staticmethod
    def refs(groups):
        return 3 * dp_bits(groups)

    def whole(self, level, slot, c):
        return self.at(slot * (1 << level) + lax.rem(self.me, 1 << level), c)

    def copy(self, level, slot, c):
        where, bit = self.links[level]
        return remote(
            self.value.at[self.whole(level, 2 * slot + 1 - bit, c)],
            self.arrive[level].at[self.at(slot, c)],
            self.s_sem[level].at[slot, c],
            self.r_sem[level].at[slot, c],
            where,
        )

    def step(self, i, lag):
        for level in range(self.levels):
            c = i - level * lag

            @pl.when(jnp.logical_and(c >= 0, c < self.chunks))
            def _():
                bit = self.links[level][1]
                for slot, goes in self.order(level):
                    self.copy(level, slot, c).wait_recv()
                    here, there = self.whole(level, 2 * slot + bit, c), self.at(slot, c)
                    if level == self.levels - 1:
                        total = self.value[here].astype(F32) + self.arrive[level][there].astype(F32)
                        self.out[self.at(0, c)] = total.astype(self.out.dtype)
                    else:
                        self.value[here] = self.value[here] + self.arrive[level][there]
                        if goes:
                            self.copy(level + 1, slot // 2, c).start()


class Line:
    lag_b, lag_c, lag_o = 2, 4, 5

    def __init__(self, first, half, pieces, part, base, out, scratch, norm=None, moved=None, at=(0, 0, 0), turns=1):
        self.first, self.half, self.size = first, half, half // pieces
        self.each, self.pieces = pieces, pieces * turns
        self.base_at, self.out_at, self.moved_at = at
        self.part, self.base, self.out = part, base, out
        (self.rin, self.smid, self.rmid) = scratch[:3]
        (self.s_up, self.r_up, self.s_mid, self.r_mid, self.s_b1, self.s_b2, self.r_b, self.s_c, self.r_c) = scratch[3:12]
        self.norm, self.moved = norm, moved
        if moved:
            self.arrived, self.shift = moved
            self.s_s, self.r_s = scratch[12:14]
            section = lax.axis_index("section")
            self.sends = section == (0 if self.shift > 0 else 1)
            self.partner = {"section": 1 - section}
        t = lax.axis_index("tensor")
        self.mid = jnp.logical_or(t == 1, t == 2)
        self.outside = jnp.logical_not(self.mid)
        self.outer = {"tensor": jnp.where(t == 1, 0, 3)}
        self.other = {"tensor": jnp.where(t == 1, 2, 1)}
        self.nbr = {"tensor": jnp.where(t == 0, 1, 2)}
        self.near = jnp.where(t < 2, 0, half)
        self.far = half - self.near

    @staticmethod
    def scratch(half, pieces, width, moved, turns=1):
        dma = pltpu.SemaphoreType.DMA
        half, pieces = half * turns, pieces * turns
        kinds = [
            pltpu.VMEM((2 * half, width), BF16),
            pltpu.VMEM((half, width), BF16),
            pltpu.VMEM((half, width), BF16),
            dma((2, pieces)),
            dma((2, pieces)),
        ] + [dma((pieces,))] * 7
        return kinds + ([dma((2, pieces))] * 2 if moved else [])

    @staticmethod
    def greet():
        t = lax.axis_index("tensor")

        @pl.when(t > 0)
        def _():
            greet({"tensor": jnp.maximum(t - 1, 0)})

        @pl.when(t < 3)
        def _():
            greet({"tensor": jnp.minimum(t + 1, 3)})

    def greet_sender(self):
        if self.moved:

            @pl.when(jnp.logical_not(self.sends))
            def _():
                greet(self.partner)

    def enter(self, others):
        bar = pltpu.get_barrier_semaphore()
        count = jnp.where(self.mid, 2, 1) + others
        if self.moved:
            count = count + jnp.where(self.sends, 1, 0)
        pl.semaphore_wait(bar, count)

    def local(self, start, p):
        if self.each < self.pieces:
            start, p = start + (p // self.each) * (2 * self.half), lax.rem(p, self.each)
        return pl.ds(pl.multiple_of(start + p * self.size, self.size), self.size)

    def own(self, p):
        return pl.ds(pl.multiple_of(p * self.size, self.size), self.size)

    def rows(self, start, p, at=0):
        return self.local(self.first + at + start, p)

    def shifted(self, start, p):
        side = start // self.half
        here, there = self.rows(start, p, self.out_at), self.rows(start, p, self.moved_at)
        return remote(self.out.at[here], self.arrived.at[there], self.s_s.at[side, p], self.r_s.at[side, p], self.partner)

    def pass_on(self, start, p):
        if self.moved:

            @pl.when(self.sends)
            def _():
                self.shifted(start, p).start()

    def outcome(self, s_sem, r_sem, where, start, p):
        here = self.rows(start, p, self.out_at)
        return remote(self.out.at[here], self.out.at[here], s_sem.at[p], r_sem.at[p], where)

    def up(self, start, p, k, where):
        return remote(
            self.part.at[self.rows(start, p)], self.rin.at[self.local(start, p)], self.s_up.at[k, p], self.r_up.at[k, p], where
        )

    def cross(self, p):
        return remote(
            self.smid.at[self.own(p)], self.rmid.at[self.own(p)], self.s_mid.at[p], self.r_mid.at[p], self.other
        )

    def start(self, turn=0):
        @pl.when(self.outside)
        def _():
            def begin(p, c):
                self.up(self.far, p, 0, self.nbr).start()
                self.up(self.near, p, 1, self.nbr).start()
                return c

            lax.fori_loop(turn * self.each, (turn + 1) * self.each, begin, 0)

    def outer_step(self, i):
        p = i - self.lag_o

        @pl.when(jnp.logical_and(p >= 0, p < self.pieces))
        def _():
            self.outcome(self.s_b2, self.r_b, self.nbr, self.near, p).wait_recv()
            self.pass_on(self.near, p)
            self.outcome(self.s_c, self.r_c, self.nbr, self.far, p).wait_recv()
            self.pass_on(self.far, p)

    def mid_step(self, i):
        @pl.when(jnp.logical_and(i >= 0, i < self.pieces))
        def _():
            self.up(self.far, i, 0, self.outer).wait_recv()
            total = self.part[self.rows(self.far, i)].astype(F32) + self.rin[self.local(self.far, i)].astype(F32)
            self.smid[self.own(i)] = total.astype(BF16)
            self.cross(i).start()

        j = i - self.lag_b

        @pl.when(jnp.logical_and(j >= 0, j < self.pieces))
        def _():
            self.up(self.near, j, 1, self.outer).wait_recv()
            self.cross(j).wait_recv()
            here = self.rows(self.near, j, self.base_at)
            total = self.part[self.rows(self.near, j)].astype(F32) + self.rin[self.local(self.near, j)].astype(F32)
            total = total + self.rmid[self.own(j)].astype(F32)
            if self.norm:
                xrow, gain, gsum, norm_at = self.norm
                x = xrow[self.rows(self.near, j, norm_at)].astype(F32)
                scale = lax.rsqrt(jnp.mean(x * x, axis=-1, keepdims=True) + epsilon)
                unit = x * scale
                gsum[...] += jnp.sum(total * unit, axis=0, keepdims=True)
                inner = total * gain[...]
                total = scale * (inner - unit * jnp.mean(inner * unit, axis=-1, keepdims=True))
            total = self.base[here].astype(F32) + total
            self.out[self.rows(self.near, j, self.out_at)] = total.astype(BF16)
            self.outcome(self.s_b1, self.r_b, self.other, self.near, j).start()
            self.outcome(self.s_b2, self.r_b, self.outer, self.near, j).start()
            self.pass_on(self.near, j)

        k = i - self.lag_c

        @pl.when(jnp.logical_and(k >= 0, k < self.pieces))
        def _():
            self.outcome(self.s_b1, self.r_b, self.other, self.far, k).wait_recv()
            self.outcome(self.s_c, self.r_c, self.outer, self.far, k).start()
            self.pass_on(self.far, k)

    @property
    def steps(self):
        return self.pieces + self.lag_o

    def step(self, i):
        @pl.when(self.mid)
        def _():
            self.mid_step(i)

        @pl.when(self.outside)
        def _():
            self.outer_step(i)

    def finish(self):
        @pl.when(self.mid)
        def _():
            def one(p, c):
                self.cross(p).wait_send()
                self.outcome(self.s_b1, self.r_b, self.other, self.near, p).wait_send()
                self.outcome(self.s_b2, self.r_b, self.outer, self.near, p).wait_send()
                self.outcome(self.s_c, self.r_c, self.outer, self.far, p).wait_send()
                return c

            lax.fori_loop(0, self.pieces, one, 0)

        @pl.when(self.outside)
        def _():
            def one(p, c):
                self.up(self.far, p, 0, self.nbr).wait_send()
                self.up(self.near, p, 1, self.nbr).wait_send()
                return c

            lax.fori_loop(0, self.pieces, one, 0)

        if self.moved:

            @pl.when(self.sends)
            def _():
                def close(p, c):
                    self.shifted(0, p).wait_send()
                    self.shifted(self.half, p).wait_send()
                    return c

                lax.fori_loop(0, self.pieces, close, 0)

    def receive(self):
        @pl.when(jnp.logical_not(self.sends))
        def _():
            def close(p, c):
                self.shifted(0, p).wait_recv()
                self.shifted(self.half, p).wait_recv()
                return c

            lax.fori_loop(0, self.pieces, close, 0)


def run_steps(begin, end, *planned):
    def body(i, c):
        for step, offset in planned:
            step(i - offset)
        return c

    lax.fori_loop(begin, end, body, 0)


class Gather:
    def __init__(self, groups, rows, out, s_sem, r_sem):
        self.groups, self.rows, self.out, self.s_sem, self.r_sem = groups, rows, out, s_sem, r_sem
        self.levels = dp_bits(groups)
        self.links = [dp_partner(k) for k in range(self.levels)]
        self.me = lax.axis_index("dp")

    @staticmethod
    def scratch(groups):
        return [pltpu.SemaphoreType.DMA((dp_bits(groups), groups // 2))] * 2

    def copy(self, level, i, mine):
        where, bit = self.links[level]
        low = lax.rem(self.me, 1 << (level + 1))
        if not mine:
            low = low + (1 - 2 * bit) * (1 << level)
        block = i * (1 << (level + 1)) + low
        place = self.out.at[pl.ds(pl.multiple_of(block * self.rows, self.rows), self.rows)]
        return remote(place, place, self.s_sem.at[level, i], self.r_sem.at[level, i], where)

    def start(self, level):
        for i in range(self.groups >> (level + 1)):
            self.copy(level, i, True).start()

    def arrive(self, level):
        for i in range(self.groups >> (level + 1)):
            self.copy(level, i, False).wait_recv()

    def finish(self):
        for level in range(self.levels):
            for i in range(self.groups >> (level + 1)):
                self.copy(level, i, True).wait_send()


def with_transpose(left, right):
    return lax.dot_general(left, right, (((1,), (1,)), ((), ())), preferred_element_type=F32)


def rows_contract(left, right):
    return lax.dot_general(left, right, (((0,), (0,)), ((), ())), preferred_element_type=F32)


def times(left, right):
    return jnp.dot(left, right, preferred_element_type=F32)


LANES = 128
TILE = 256
WIDE = 512


def lanes(i, size=LANES):
    return pl.ds(pl.multiple_of(i * size, size), size)


def normalize(rows, gain):
    rows = rows.astype(F32)
    scale = lax.rsqrt(jnp.mean(rows * rows, axis=-1, keepdims=True) + epsilon)
    return (rows * scale * gain).astype(BF16)


def normalize_into(target, source, gain, first, count, block=32, source_at=0):
    def one(i, c):
        here = pl.ds(pl.multiple_of(first + i * block, block), block)
        there = pl.ds(pl.multiple_of(source_at + first + i * block, block), block)
        target[here] = normalize(source[there], gain[...])
        return c

    lax.fori_loop(0, count // block, one, 0)


def rolled(value, cosine, sine):
    return value * cosine + pltpu.roll(value, LANES // 2, 1) * sine


def block_rows(keys):
    for rows in (160, 80, 32):
        if rows * keys <= 160 * 1280:
            return rows
    return 16


def score_rows(q, kv, h, g, here, qcode, qstart, kcode):
    scores = with_transpose(q[here, lanes(h)], kv[:, lanes(g)]) * HD ** (-0.5)
    code = kcode[...]
    return scores, jnp.logical_and(code <= qcode[here], code >= qstart[here])


def load_all(pairs, sems):
    copies = [pltpu.make_async_copy(src, dst, sems.at[i]) for i, (src, dst) in enumerate(pairs)]
    for item in copies:
        item.start()
    return copies


def forward_kernel(groups, q_heads, k_heads, pieces, *refs):
    refs = list(refs)

    def take(count):
        taken = refs[:count]
        del refs[:count]
        return taken

    x, cosine, sine, qcode, qstart, kcode, gain_one, gain_two = take(8)
    far_weights = take(5)
    q, kv, lse, mixed, resid, gate, up, act, y, arrived = take(10)
    near_weights = take(5)
    wqkv, wout, wgate, wup, wdown = near_weights
    part_one, part_two, n1, n2, w_sem = take(5)
    gather = Gather(groups, x.shape[0], kv, *take(2))
    count, width = x.shape
    quarter = count // 4
    lines = []
    for k in range(4):
        first = (k % 2) * 2 * quarter
        source = (part_one, x, resid) if k < 2 else (part_two, resid, y)
        lines.append(
            Line(first, quarter, pieces, *source, take(12 if k < 2 else 14), moved=None if k < 2 else (arrived, 1))
        )
    one_a, one_b, two_a, two_b = lines

    loads = load_all(list(zip(far_weights, near_weights)), w_sem)
    Line.greet()
    two_a.greet_sender()
    for where, _ in gather.links:
        greet(where)
    normalize_into(n1, x, gain_one, 0, count)
    loads[0].wait()

    mine = pl.ds(pl.multiple_of(lax.axis_index("dp") * count, count), count)
    for g in range(k_heads):
        column = (q_heads + g) * LANES
        value = times(n1[...], wqkv[:, column : column + LANES])
        kv[mine, g * LANES : (g + 1) * LANES] = rolled(value, cosine[...], sine[...]).astype(BF16)
        column += k_heads * LANES
        kv[mine, (k_heads + g) * LANES : (k_heads + g + 1) * LANES] = times(
            n1[...], wqkv[:, column : column + LANES]
        ).astype(BF16)

    two_a.enter(gather.levels)

    top = gather.levels - 1
    gather.start(top)

    def queries(h, c):
        value = times(n1[...], wqkv[:, lanes(h)])
        q[:, lanes(h)] = rolled(value, cosine[...], sine[...]).astype(BF16)
        return c

    lax.fori_loop(0, q_heads, queries, 0)
    for level in range(top, -1, -1):
        gather.arrive(level)
        if level:
            gather.start(level - 1)

    rows = block_rows(kv.shape[0])
    blocks = count // rows

    def attend(i, c):
        h, b = i // blocks, lax.rem(i, blocks)
        g = h // (q_heads // k_heads)
        here = pl.ds(pl.multiple_of(b * rows, rows), rows)
        scores, allowed = score_rows(q, kv, h, g, here, qcode, qstart, kcode)
        scores = jnp.where(allowed, scores, negative)
        row_max = jnp.max(scores, axis=-1, keepdims=True)
        expo = jnp.exp(scores - row_max)
        row_total = jnp.sum(expo, axis=-1, keepdims=True)
        prob = (expo * (1.0 / row_total)).astype(BF16)
        mixed[here, lanes(h)] = times(prob, kv[:, lanes(k_heads + g)]).astype(BF16)
        there = pl.ds(pl.multiple_of(h * count + b * rows, rows), rows)
        lse[there] = jnp.broadcast_to(row_max + jnp.log(row_total), (rows, LANES))
        return c

    lax.fori_loop(0, q_heads * blocks, attend, 0)
    loads[1].wait()

    def projected(target, left, right, first, each=None):
        here = pl.ds(first, 2 * quarter)

        def one(i, c):
            target[here, lanes(i, TILE)] = times(left[here], right[:, lanes(i, TILE)]).astype(BF16)
            if each:
                each(i)
            return c

        lax.fori_loop(0, width // TILE, one, 0)

    projected(part_one, mixed, wout, 0)
    one_a.start()
    projected(part_one, mixed, wout, 2 * quarter)
    one_b.start()
    run_steps(0, one_a.steps, (one_a.step, 0), (one_b.step, pieces))
    loads[2].wait()
    loads[3].wait()
    loads[4].wait()

    def hidden(first, each):
        here = pl.ds(first, 2 * quarter)
        normalize_into(n2, resid, gain_two, first, 2 * quarter)

        def one(i, c):
            columns = lanes(i, TILE)
            gate_pre = times(n2[here], wgate[:, columns])
            up_pre = times(n2[here], wup[:, columns])
            gate[here, columns] = gate_pre.astype(BF16)
            up[here, columns] = up_pre.astype(BF16)
            act[here, columns] = (gate_pre * jax.nn.sigmoid(gate_pre) * up_pre).astype(BF16)
            each(i)
            return c

        lax.fori_loop(0, gate.shape[1] // TILE, one, 0)

    tiles = gate.shape[1] // TILE
    done = one_a.steps - pieces
    hidden(0, lambda i: one_b.step(done + i))
    projected(part_two, act, wdown, 0)
    two_a.start()
    run_steps(done + tiles, one_b.steps, (one_b.step, 0))
    hidden(2 * quarter, lambda i: two_a.step(i))
    projected(part_two, act, wdown, 2 * quarter)
    two_b.start()
    run_steps(tiles, two_b.steps + tiles, (two_a.step, 0), (two_b.step, tiles))
    gather.finish()
    for line in lines:
        line.finish()
    two_a.receive()
    two_b.receive()


VMEM_LIMIT = 60 * 2**20


def forward_tick(x, spots, weights, groups, q_heads, k_heads, cid):
    norm_one, wqkv, wout, norm_two, wgate, wup, wdown = weights
    count, width = x.shape
    hidden = wgate.shape[1]
    pieces = 5
    vmem = pl.BlockSpec(memory_space=pltpu.VMEM)
    far = pl.BlockSpec(memory_space=pl.ANY)

    def shape(*dims, dtype=BF16):
        return jax.ShapeDtypeStruct(dims, dtype)

    outs = [
        shape(count, q_heads * LANES),
        shape(groups * count, 2 * k_heads * LANES),
        shape(q_heads * count, LANES, dtype=F32),
        shape(count, q_heads * LANES),
        shape(count, width),
        shape(count, hidden),
        shape(count, hidden),
        shape(count, hidden),
        shape(count, width),
        shape(count, width),
    ]
    far_weights = [wqkv, wout, wgate, wup, wdown]
    scratch = [pltpu.VMEM(item.shape, BF16) for item in far_weights]
    scratch += [pltpu.VMEM((count, width), BF16)] * 4 + [pltpu.SemaphoreType.DMA((5,))]
    scratch += Gather.scratch(groups)
    for k in range(4):
        scratch += Line.scratch(count // 4, pieces, width, k >= 2)
    q, kv, lse, mixed, resid, gate, up, act, y, arrived = pl.pallas_call(
        functools.partial(forward_kernel, groups, q_heads, k_heads, pieces),
        out_shape=outs,
        in_specs=[vmem] * 8 + [far] * 5,
        out_specs=[vmem] * len(outs),
        scratch_shapes=scratch,
        compiler_params=pltpu.CompilerParams(
            collective_id=cid, has_side_effects=True, vmem_limit_bytes=VMEM_LIMIT
        ),
        name="forward_tick",
    )(x, *spots, norm_one[None], norm_two[None], *far_weights)
    return y, arrived, (x, q, kv, lse, mixed, resid, gate, up, act)


def back_ffn_kernel(pieces, *refs):
    dy, gate, up, resid, gain = refs[:5]
    far_weights = refs[5:8]
    dresid, gsum, dgate, dup = refs[8:12]
    wdown, wgate, wup = near_weights = refs[12:15]
    part, w_sem = refs[15:17]
    count, width = dy.shape
    quarter = count // 4
    a, b = [
        Line(k * 2 * quarter, quarter, pieces, part, dy, dresid, refs[17 + 12 * k : 29 + 12 * k], norm=(resid, gain, gsum, 0))
        for k in range(2)
    ]
    loads = load_all(list(zip(far_weights, near_weights)), w_sem)
    Line.greet()
    gsum[...] = jnp.zeros_like(gsum)

    def hidden(first, each=None):
        here = pl.ds(first, 2 * quarter)

        def one(i, c):
            columns = lanes(i, TILE)
            d_act = with_transpose(dy[here], wdown[columns, :])
            gate_pre, up_pre = gate[here, columns].astype(F32), up[here, columns].astype(F32)
            sigma = jax.nn.sigmoid(gate_pre)
            d_silu = d_act * sigma
            dup[here, columns] = (d_silu * gate_pre).astype(BF16)
            dgate[here, columns] = (d_silu * up_pre * (1.0 + gate_pre * (1.0 - sigma))).astype(BF16)
            if each:
                each(i)
            return c

        lax.fori_loop(0, gate.shape[1] // TILE, one, 0)

    def back(first):
        here = pl.ds(first, 2 * quarter)

        def one(i, c):
            columns = lanes(i, TILE)
            total = with_transpose(dgate[here], wgate[columns, :]) + with_transpose(dup[here], wup[columns, :])
            part[here, columns] = total.astype(BF16)
            return c

        lax.fori_loop(0, width // TILE, one, 0)

    loads[0].wait()
    hidden(0)
    loads[1].wait()
    loads[2].wait()
    back(0)
    a.enter(0)
    a.start()
    tiles = gate.shape[1] // TILE
    hidden(2 * quarter, lambda i: a.step(i))
    back(2 * quarter)
    b.start()
    run_steps(tiles, b.steps + tiles, (a.step, 0), (b.step, tiles))
    a.finish()
    b.finish()


def back_ffn(dy, kept, weights, cid):
    norm_one, wqkv, wout, norm_two, wgate, wup, wdown = weights
    x, q, kv, lse, mixed, resid, gate, up, act = kept
    count, width = dy.shape
    pieces = 5
    vmem = pl.BlockSpec(memory_space=pltpu.VMEM)
    far = pl.BlockSpec(memory_space=pl.ANY)
    far_weights = [wdown, wgate, wup]
    scratch = [pltpu.VMEM(item.shape, BF16) for item in far_weights]
    scratch += [pltpu.VMEM((count, width), BF16), pltpu.SemaphoreType.DMA((3,))]
    scratch += Line.scratch(count // 4, pieces, width, False) * 2
    return pl.pallas_call(
        functools.partial(back_ffn_kernel, pieces),
        out_shape=[
            jax.ShapeDtypeStruct((count, width), BF16),
            jax.ShapeDtypeStruct((1, width), F32),
            jax.ShapeDtypeStruct(gate.shape, BF16),
            jax.ShapeDtypeStruct(gate.shape, BF16),
        ],
        in_specs=[vmem] * 5 + [far] * 3,
        out_specs=[vmem] * 4,
        scratch_shapes=scratch,
        compiler_params=pltpu.CompilerParams(
            collective_id=cid, has_side_effects=True, vmem_limit_bytes=VMEM_LIMIT
        ),
        name="back_ffn",
    )(dy, gate, up, resid, norm_two[None], *far_weights)


def back_attn_kernel(groups, q_heads, k_heads, pieces, shift, plans, *refs):
    refs = list(refs)

    def take(count):
        taken = refs[:count]
        del refs[:count]
        return taken

    dresid, x, q, kv, lse, cosine, sine, qcode, qstart, kcode, gain = take(11)
    far_weights = take(2)
    values = take(len(plans))
    dx, gsum, dqkv = take(3)
    (arrived,) = take(1) if shift else (None,)
    totals = take(len(plans))
    wout, wqkv = near_weights = take(2)
    part, dmixed, dkv, w_sem = take(4)
    levels = dp_bits(groups)
    count, width = x.shape
    quarter = count // 4
    keys = kv.shape[0]
    shares, owns, scatters = [], [], []
    for g in range(k_heads):
        share, own = take(2)
        shares.append(share)
        owns.append(own)
        scatters.append(Scatter(groups, count, 5, [share, own] + take(4 * levels - 1)))
    tasks = [
        Scatter(groups, rows, chunks, [value, total] + take(4 * levels - 1))
        for (rows, chunks), value, total in zip(plans, values, totals)
    ]
    moved = (arrived, shift) if shift else None
    a, b = [
        Line(
            k * 2 * quarter,
            quarter,
            pieces,
            part,
            dresid,
            dx,
            take(14 if shift else 12),
            norm=(x, gain, gsum, 0),
            moved=moved,
        )
        for k in range(2)
    ]
    loads = load_all(list(zip(far_weights, near_weights)), w_sem)
    Line.greet()
    for where, _ in scatters[0].links:
        greet(where)
    a.greet_sender()
    gsum[...] = jnp.zeros_like(gsum)
    dkv[...] = jnp.zeros_like(dkv)
    a.enter(levels)
    for task in tasks:
        task.start()
    loads[0].wait()

    def mix(h, c):
        dmixed[:, lanes(h)] = with_transpose(dresid[...], wout[lanes(h), :]).astype(BF16)
        return c

    lax.fori_loop(0, q_heads, mix, 0)
    rows = block_rows(keys)
    blocks = count // rows
    repeat = q_heads // k_heads
    lag = 4
    scale = HD ** (-0.5)

    for g in range(k_heads):

        def one(i, c):
            h, n = g * repeat + i // blocks, lax.rem(i, blocks)
            here = pl.ds(pl.multiple_of(n * rows, rows), rows)
            there = pl.ds(pl.multiple_of(h * count + n * rows, rows), rows)
            scores, allowed = score_rows(q, kv, h, g, here, qcode, qstart, kcode)
            prob = jnp.where(allowed, jnp.exp(scores - lse[there][:, :1]), 0.0)
            dm = dmixed[here, lanes(h)]
            d_prob = with_transpose(dm, kv[:, lanes(k_heads + g)])
            row_dot = jnp.sum(prob * d_prob, axis=-1, keepdims=True)
            d_scores = (prob * (d_prob - row_dot)).astype(BF16)
            d_query = times(d_scores, kv[:, lanes(g)]) * scale
            dqkv[here, lanes(h)] = rolled(d_query, cosine[here], -sine[here]).astype(BF16)
            dkv[:, lanes(g)] += rows_contract(d_scores, q[here, lanes(h)]) * scale
            dkv[:, lanes(k_heads + g)] += rows_contract(prob.astype(BF16), dm)
            for task in tasks:
                task.step(g * repeat * blocks + i, lag)
            return c

        lax.fori_loop(0, repeat * blocks, one, 0)

        def narrow(i, c):
            here = pl.ds(pl.multiple_of(i * LANES, LANES), LANES)
            shares[g][here, :LANES] = dkv[here, lanes(g)].astype(BF16)
            shares[g][here, LANES:] = dkv[here, lanes(k_heads + g)].astype(BF16)
            return c

        lax.fori_loop(0, keys // LANES, narrow, 0)
        scatters[g].start()
    run_steps(0, scatters[0].steps(1), *[(functools.partial(lambda s, i: s.step(i, 1), s), 0) for s in scatters])
    for g in range(k_heads):
        dqkv[:, lanes(q_heads + g)] = rolled(owns[g][:, :LANES], cosine[...], -sine[...]).astype(BF16)
        dqkv[:, lanes(q_heads + k_heads + g)] = owns[g][:, LANES:].astype(BF16)
    loads[1].wait()

    def back(first, each=None):
        here = pl.ds(first, 2 * quarter)

        def one(i, c):
            columns = lanes(i, TILE)
            part[here, columns] = with_transpose(dqkv[here], wqkv[columns, :]).astype(BF16)
            if each:
                each(i)
            return c

        lax.fori_loop(0, width // TILE, one, 0)

    back(0)
    a.start()
    back(2 * quarter)
    b.start()
    begun = q_heads * blocks
    more = [(functools.partial(lambda s, i: s.step(i + begun, lag), s), 0) for s in tasks]
    last = max([b.steps + pieces] + [s.steps(lag) - begun for s in tasks])
    run_steps(0, last, (a.step, 0), (b.step, pieces), *more)
    a.finish()
    b.finish()
    if shift:
        a.receive()
        b.receive()
    for item in scatters + tasks:
        item.finish()


def back_attn(dresid, kept, spots, weights, groups, q_heads, k_heads, cid, shift, sums=()):
    norm_one, wqkv, wout, norm_two, wgate, wup, wdown = weights
    x, q, kv, lse, mixed, resid, gate, up, act = kept
    count, width = x.shape
    keys = kv.shape[0]
    pieces = 5
    vmem = pl.BlockSpec(memory_space=pltpu.VMEM)
    far = pl.BlockSpec(memory_space=pl.ANY)
    outs = [
        jax.ShapeDtypeStruct((count, width), BF16),
        jax.ShapeDtypeStruct((1, width), F32),
        jax.ShapeDtypeStruct((count, wqkv.shape[1]), BF16),
    ]
    if shift:
        outs.append(jax.ShapeDtypeStruct((count, width), BF16))
    scratch = [
        pltpu.VMEM(wout.shape, BF16),
        pltpu.VMEM(wqkv.shape, BF16),
        pltpu.VMEM((count, width), BF16),
        pltpu.VMEM(q.shape, BF16),
        pltpu.VMEM(kv.shape, F32),
        pltpu.SemaphoreType.DMA((2,)),
    ]
    for _ in range(k_heads):
        scratch += [pltpu.VMEM((keys, 2 * LANES), BF16), pltpu.VMEM((count, 2 * LANES), F32)]
        scratch += Scatter.scratch(groups, count, 2 * LANES, 5, BF16)
    plans = []
    for value in sums:
        rows = value.shape[0] // groups
        parts = max(1, min(8, rows // 16))
        while rows % (parts * 16):
            parts -= 1
        plans.append((rows, parts))
        outs.append(jax.ShapeDtypeStruct((rows, value.shape[1]), F32))
        scratch += Scatter.scratch(groups, rows, value.shape[1], parts, BF16)
    scratch += Line.scratch(count // 4, pieces, width, bool(shift)) * 2
    return pl.pallas_call(
        functools.partial(back_attn_kernel, groups, q_heads, k_heads, pieces, shift, plans),
        out_shape=outs,
        in_specs=[vmem] * 11 + [far] * 2 + [vmem] * len(sums),
        out_specs=[vmem] * len(outs),
        scratch_shapes=scratch,
        compiler_params=pltpu.CompilerParams(
            collective_id=cid, has_side_effects=True, vmem_limit_bytes=VMEM_LIMIT
        ),
        name="back_attn_%d" % cid,
    )(dresid, x, q, kv, lse, *spots, norm_one[None], wout, wqkv, *sums)


def announce(sems, neighbours):
    for here, where, k in neighbours:

        @pl.when(here)
        def _():
            pl.semaphore_signal(sems.at[k], inc=1, device_id=where, device_id_type=MESH)


def heard(sems, neighbours):
    for k, (here, _, _) in enumerate(neighbours):

        @pl.when(here)
        def _():
            pl.semaphore_wait(sems.at[k], 1)


def main_kernel(groups, q_heads, k_heads, pieces, *refs):
    refs = list(refs)

    def take(count):
        taken = refs[:count]
        del refs[:count]
        return taken

    cosine, sine, qcode, qstart, kcode, gain_one, gain_two, holder, chosen = take(9)
    packed, own_second, extra_second = take(3)
    far_weights = take(5)
    y_out, dx_out, back_out, normed_one, normed_two = take(5)
    far_state = take(14)
    gsum_one, gsum_two = take(2)
    near_state = xs, q, kv, lse, mixed, resid, gate, up, act, dys, dresid, dgate, dup, dqkv = take(14)
    state_sem = take(1)[0]
    wqkv, wout, wgate, wup, wdown = near_weights = take(5)
    part_one, part_two, normed, y, dmixed, dkv, w_sem, io_sem, meet_sem = take(9)
    levels = dp_bits(groups)
    gather_sems = take(2)
    line_scratch = [take(12) for _ in range(4)]
    forth_s, forth_r, back_s, back_r = take(4)
    spares, returned = take(2)
    spare = returned.shape[0]
    give_lag = Line.lag_o + pieces
    give = OwnScatter(groups, spare, spare // 32, [spares, returned] + take(OwnScatter.refs(groups)))
    second = Gather(groups, spare, spares, *take(2))
    count, width = part_one.shape
    keys = groups * count
    quarter = count // 4
    half = 2 * quarter
    shares, owns, scatters = [], [], []
    for g in range(k_heads):
        share, own = take(2)
        shares.append(share)
        owns.append(own)
        scatters.append(Scatter(groups, count, 5, [share, own] + take(4 * levels - 1)))
    section = lax.axis_index("section")
    t = lax.axis_index("tensor")
    tiles, wide = gate.shape[1] // WIDE, width // WIDE
    repeat = q_heads // k_heads
    rows = block_rows(keys)
    blocks = half // rows
    scale = HD ** (-0.5)

    def span(first, size):
        return pl.ds(pl.multiple_of(first, 32), size)

    neighbours = [
        (t > 0, {"tensor": jnp.maximum(t - 1, 0)}, 1),
        (t < 3, {"tensor": jnp.minimum(t + 1, 3)}, 0),
    ]
    for k in range(levels):
        neighbours.append((t >= 0, dp_partner(k)[0], 2 + k))

    for _, where, _ in neighbours[2:]:
        greet(where)
    Line.greet()
    greet({"section": 1 - section})

    loads = load_all(list(zip(far_weights, near_weights)), w_sem)

    def fetch(target):
        return (
            pltpu.make_async_copy(packed, target.at[:count], io_sem.at[0]),
            pltpu.make_async_copy(own_second, target.at[count:], io_sem.at[1]),
        )

    place = span(lax.axis_index("dp") * spare, spare)
    fetch_extra = pltpu.make_async_copy(extra_second, spares.at[place], io_sem.at[2])
    fetch_extra.start()
    for which, target in enumerate((xs, dys)):

        @pl.when(section == which)
        def _():
            for item in fetch(target):
                item.start()

    pl.semaphore_wait(pltpu.get_barrier_semaphore(), jnp.where(jnp.logical_or(t == 1, t == 2), 2, 1) + levels + 1)
    announce(meet_sem, neighbours)
    gsum_one[...] = jnp.zeros_like(gsum_one)
    gsum_two[...] = jnp.zeros_like(gsum_two)
    for which, target in enumerate((xs, dys)):

        @pl.when(section == which)
        def _():
            for item in fetch(target):
                item.wait()

    fetch_extra.wait()

    def keep(index, slot):
        near, there = near_state[index], far_state[index]
        part = near.shape[0] // 2
        here = span(slot * part, part)
        return pltpu.make_async_copy(near.at[here], there.at[here], state_sem.at[index, slot])

    def projected(target, left, right, first, left_at, each=None):
        here, there = span(first, half), span(first + left_at, half)

        def one(i, c):
            target[here, lanes(i, WIDE)] = times(left[there], right[:, lanes(i, WIDE)]).astype(BF16)
            if each:
                each(i)
            return c

        lax.fori_loop(0, wide, one, 0)

    def give_back(slot, now, line):
        @pl.when(now)
        def _():
            spares[...] = times(holder[span(slot * groups * spare, groups * spare)], y[...]).astype(BF16)
            give.start()

        def one(i, c):
            line.step(i)

            @pl.when(now)
            def _():
                give.step(i, give_lag)

            return c

        lax.fori_loop(0, line.steps, one, 0)

    def give_rest(now, line, begun):
        def one(i, c):
            line.step(i)

            @pl.when(now)
            def _():
                give.step(i - begun + give_lag, give_lag)

            return c

        lax.fori_loop(begun, max(line.steps, begun + give.steps(give_lag) - give_lag), one, 0)

    def given(place, now):
        @pl.when(now)
        def _():
            give.finish()
            pltpu.make_async_copy(returned, back_out.at[span(place * spare, spare)], io_sem.at[1]).start()
            pltpu.make_async_copy(returned, back_out.at[span(place * spare, spare)], io_sem.at[1]).wait()

    def back_lines(slot):
        base = slot * count
        made = []
        for k in range(4):
            first = (k % 2) * half
            scratch = list(line_scratch[k])
            if k < 2:
                norm = (resid, gain_two, gsum_two, base)
                made.append(Line(first, quarter, pieces, part_one, dys, dresid, scratch, norm=norm, at=(base, base, 0)))
            else:
                scratch += [back_s.at[k - 2], back_r.at[2 * slot + k - 2]]
                norm = (xs, gain_one, gsum_one, base)
                made.append(
                    Line(
                        first, quarter, pieces, part_two, dresid, y, scratch, norm=norm, moved=(dys, -1), at=(base, 0, base)
                    )
                )
        return made

    def forward(slot):
        base = slot * count
        pending = jnp.logical_and(section == 1, slot == 1)
        left_a, left_b = back_lines(0)[2:]
        whole = span(base, count)
        moved = (xs, 1)
        lines = []
        for k in range(4):
            first = (k % 2) * half
            scratch = list(line_scratch[k])
            if k < 2:
                lines.append(Line(first, quarter, pieces, part_one, xs, resid, scratch, at=(base, base, 0)))
            else:
                scratch += [forth_s.at[k - 2], forth_r.at[2 * slot + k - 2]]
                lines.append(
                    Line(first, quarter, pieces, part_two, resid, y, scratch, moved=moved, at=(base, 0, base))
                )
        one_a, one_b, two_a, two_b = lines
        gather = Gather(groups, count, kv.at[span(slot * keys, keys)], *gather_sems)
        two_a.receive()
        two_b.receive()
        normalize_into(normed, xs, gain_one, 0, count, source_at=base)
        keep_one = pltpu.make_async_copy(normed, normed_one.at[whole], io_sem.at[1])
        keep_two = pltpu.make_async_copy(normed, normed_two.at[whole], io_sem.at[2])
        keep_one.start()

        @pl.when(slot == 0)
        def _():
            loads[0].wait()

        mine = span(slot * keys + lax.axis_index("dp") * count, count)
        middle = (q_heads + k_heads) * LANES
        value = times(normed[...], wqkv[:, q_heads * LANES : middle])
        for g in range(k_heads):
            here = slice(g * LANES, (g + 1) * LANES)
            kv[mine, here] = rolled(value[:, here], cosine[whole], sine[whole]).astype(BF16)
        kv[mine, k_heads * LANES :] = times(normed[...], wqkv[:, middle:]).astype(BF16)
        heard(meet_sem, neighbours)
        gather.start(levels - 1)
        for first in range(0, q_heads, 2):
            value = times(normed[...], wqkv[:, first * LANES : (first + 2) * LANES])
            for h in range(2):
                here = slice((first + h) * LANES, (first + h + 1) * LANES)
                q[whole, here] = rolled(
                    value[:, h * LANES : (h + 1) * LANES], cosine[whole], sine[whole]
                ).astype(BF16)
        for level in range(levels - 1, 0, -1):
            gather.arrive(level)
            gather.start(level - 1)

        @pl.when(pending)
        def _():
            run_steps(0, left_a.steps, (left_a.step, 0))

        gather.arrive(0)

        @pl.when(slot == 0)
        def _():
            second.start(levels - 1)

        def attend(first, each=None):
            def one(i, c):
                h, b = i // blocks, lax.rem(i, blocks)
                g = h // repeat
                here = span(base + first + b * rows, rows)
                scores = with_transpose(q[here, lanes(h)], kv[span(slot * keys, keys), lanes(g)]) * scale
                code = kcode[slot]
                allowed = jnp.logical_and(code <= qcode[here], code >= qstart[here])
                scores = jnp.where(allowed, scores, negative)
                row_max = jnp.max(scores, axis=-1, keepdims=True)
                expo = jnp.exp(scores - row_max)
                row_total = jnp.sum(expo, axis=-1, keepdims=True)
                prob = (expo * (1.0 / row_total)).astype(BF16)
                mixed[here, lanes(h)] = times(prob, kv[span(slot * keys, keys), lanes(k_heads + g)]).astype(BF16)
                lse[span((slot * q_heads + h) * count + first + b * rows, rows)] = jnp.broadcast_to(
                    row_max + jnp.log(row_total), (rows, LANES)
                )
                if each:
                    each(i)
                return c

            lax.fori_loop(0, q_heads * blocks, one, 0)

        attend(0)

        @pl.when(slot == 0)
        def _():
            loads[1].wait()

        projected(part_one, mixed, wout, 0, base)
        one_a.start()

        @pl.when(pending)
        def _():
            run_steps(0, left_b.steps, (left_b.step, 0))
            left_out = pltpu.make_async_copy(y, dx_out.at[:count], io_sem.at[0])
            left_out.start()
            left_a.finish()
            left_b.finish()
            left_out.wait()

        attend(half)
        projected(part_one, mixed, wout, half, base)
        one_b.start()
        giving = jnp.logical_and(slot == 1, section == 0)
        give_back(0, giving, one_a)

        @pl.when(slot == 0)
        def _():
            for item in loads[2:]:
                item.wait()
            for level in range(levels - 1, 0, -1):
                second.arrive(level)
                second.start(level - 1)

        def hidden(first, each):
            here, there = span(first, half), span(base + first, half)
            normalize_into(normed, resid, gain_two, first, half, source_at=base)

            def one(i, c):
                columns = lanes(i, WIDE)
                gate_pre = times(normed[here], wgate[:, columns])
                up_pre = times(normed[here], wup[:, columns])
                gate[there, columns] = gate_pre.astype(BF16)
                up[there, columns] = up_pre.astype(BF16)
                act[there, columns] = (gate_pre * jax.nn.sigmoid(gate_pre) * up_pre).astype(BF16)
                each(i)
                return c

            lax.fori_loop(0, tiles, one, 0)

        keep_one.wait()
        hidden(0, one_b.step)

        @pl.when(section == 0)
        def _():
            projected(part_two, act, wdown, 0, base)
            two_a.start()

        give_rest(giving, one_b, tiles)

        def early(i):
            @pl.when(section == 0)
            def _():
                two_a.step(i)

        hidden(half, early)
        keep_two.start()

        @pl.when(section == 0)
        def _():
            projected(part_two, act, wdown, half, base)
            two_b.start()

        @pl.when(slot == 0)
        def _():
            second.arrive(0)
            brought = times(chosen[...], spares[...])
            for which, target in enumerate((xs, dys)):

                @pl.when(section == which)
                def _():
                    target[count:] = (target[count:].astype(F32) + brought).astype(BF16)

        out = pltpu.make_async_copy(y, y_out.at[whole], io_sem.at[0])

        @pl.when(section == 0)
        def _():
            run_steps(tiles, two_a.steps, (two_a.step, 0))
            run_steps(0, two_b.steps, (two_b.step, 0))
            out.start()
            two_a.finish()
            two_b.finish()

        gather.finish()
        one_a.finish()
        one_b.finish()
        keep_two.wait()
        given(0, giving)

        @pl.when(slot == 0)
        def _():
            second.finish()

        @pl.when(section == 0)
        def _():
            out.wait()

        for index in range(9):
            keep(index, slot).start()
        announce(meet_sem, neighbours)

    def backward(slot):
        giving = jnp.logical_or(section == 0, slot == 1)
        later = jnp.logical_and(section == 1, slot == 0)
        base = slot * count
        whole = span(base, count)
        lines = back_lines(slot)
        one_a, one_b, two_a, two_b = lines
        two_a.receive()
        two_b.receive()
        dkv[...] = jnp.zeros_like(dkv)
        heard(meet_sem, neighbours)

        def hidden(first, each=None):
            here = span(base + first, half)

            def one(i, c):
                columns = lanes(i, WIDE)
                d_act = with_transpose(dys[here], wdown[columns, :])
                gate_pre, up_pre = gate[here, columns].astype(F32), up[here, columns].astype(F32)
                sigma = jax.nn.sigmoid(gate_pre)
                d_silu = d_act * sigma
                dup[here, columns] = (d_silu * gate_pre).astype(BF16)
                dgate[here, columns] = (d_silu * up_pre * (1.0 + gate_pre * (1.0 - sigma))).astype(BF16)
                if each:
                    each(i)
                return c

            lax.fori_loop(0, tiles, one, 0)

        def back_hidden(first):
            here, there = span(first, half), span(base + first, half)

            def one(i, c):
                columns = lanes(i, WIDE)
                total = with_transpose(dgate[there], wgate[columns, :]) + with_transpose(dup[there], wup[columns, :])
                part_one[here, columns] = total.astype(BF16)
                return c

            lax.fori_loop(0, wide, one, 0)

        hidden(0)
        back_hidden(0)
        one_a.start()
        hidden(half)
        back_hidden(half)
        one_b.start()
        give_back(1 - section, giving, one_a)

        def attend(first, g, each=None):
            def one(i, c):
                h, n = g * repeat + i // blocks, lax.rem(i, blocks)
                here = span(base + first + n * rows, rows)
                near = span(first + n * rows, rows)
                k_rows = kv[span(slot * keys, keys), lanes(g)]
                scores = with_transpose(q[here, lanes(h)], k_rows) * scale
                code = kcode[slot]
                allowed = jnp.logical_and(code <= qcode[here], code >= qstart[here])
                known = lse[span((slot * q_heads + h) * count + first + n * rows, rows)][:, :1]
                prob = jnp.where(allowed, jnp.exp(scores - known), 0.0)
                dm = dmixed[near, lanes(h)]
                d_prob = with_transpose(dm, kv[span(slot * keys, keys), lanes(k_heads + g)])
                row_dot = jnp.sum(prob * d_prob, axis=-1, keepdims=True)
                d_scores = (prob * (d_prob - row_dot)).astype(BF16)
                d_query = times(d_scores, k_rows) * scale
                dqkv[here, lanes(h)] = rolled(d_query, cosine[here], -sine[here]).astype(BF16)
                dkv[lanes(g), :] += rows_contract(q[here, lanes(h)], d_scores) * scale
                dkv[lanes(k_heads + g), :] += rows_contract(dm, prob.astype(BF16))
                if each:
                    each(i)
                return c

            lax.fori_loop(0, repeat * blocks, one, 0)

        def mix(first):
            here, there = span(first, half), span(base + first, half)

            def one(h, c):
                dmixed[here, lanes(h)] = with_transpose(dresid[there], wout[lanes(h), :]).astype(BF16)
                return c

            lax.fori_loop(0, q_heads, one, 0)

        mix(0)
        turns = repeat * blocks
        for g in range(k_heads):
            attend(0, g, lambda i: one_b.step(g * turns + i))
        give_rest(giving, one_b, k_heads * turns)
        mix(half)
        for g in range(k_heads):
            attend(half, g)

            shares[g][:, :LANES] = jnp.transpose(dkv[lanes(g), :]).astype(BF16)
            shares[g][:, LANES:] = jnp.transpose(dkv[lanes(k_heads + g), :]).astype(BF16)
            scatters[g].start()
        run_steps(0, scatters[0].steps(1), *[(functools.partial(lambda s, i: s.step(i, 1), s), 0) for s in scatters])
        for g in range(k_heads):
            dqkv[whole, lanes(q_heads + g)] = rolled(owns[g][:, :LANES], cosine[whole], -sine[whole]).astype(BF16)
            dqkv[whole, lanes(q_heads + k_heads + g)] = owns[g][:, LANES:].astype(BF16)

        def back(first, each=None):
            here, there = span(first, half), span(base + first, half)

            def one(i, c):
                columns = lanes(i, WIDE)
                part_two[here, columns] = with_transpose(dqkv[there], wqkv[columns, :]).astype(BF16)
                if each:
                    each(i)
                return c

            lax.fori_loop(0, wide, one, 0)

        back(0)
        two_a.start()
        back(half)
        two_b.start()

        @pl.when(jnp.logical_not(later))
        def _():
            run_steps(0, two_a.steps, (two_a.step, 0))
            run_steps(0, two_b.steps, (two_b.step, 0))
            out = pltpu.make_async_copy(y, dx_out.at[whole], io_sem.at[0])
            out.start()
            two_a.finish()
            two_b.finish()
            out.wait()

        one_a.finish()
        one_b.finish()
        for item in scatters:
            item.finish()
        given(1 + section, giving)
        for index in range(9, 14):
            keep(index, slot).start()
        announce(meet_sem, neighbours)

    def turn(k, carry):
        @pl.when(jnp.where(section == 0, k < 2, lax.rem(k, 2) == 0))
        def _():
            forward(jnp.where(section == 0, jnp.minimum(k, 1), k // 2))

        @pl.when(jnp.where(section == 0, k == 2, lax.rem(k, 2) == 1))
        def _():
            backward(jnp.where(section == 0, 0, k // 2))

        return carry

    lax.fori_loop(0, 3 + section, turn, 0)
    heard(meet_sem, neighbours)

    @pl.when(section == 0)
    def _():
        spares[...] = times(holder[: groups * spare], y[...]).astype(BF16)
        give.start()
        run_steps(0, give.steps(give_lag), (lambda i: give.step(i, give_lag), 0))

    given(2, section == 0)
    for k in range(2):
        Line(
            k * half,
            quarter,
            pieces,
            part_two,
            dresid,
            y,
            list(line_scratch[2 + k]) + [back_s.at[k], back_r.at[2 + k]],
            moved=(dys, -1),
            at=(0, 0, count),
        ).receive()
    for index in range(14):
        keep(index, 0).wait()
        if index < 9:
            keep(index, 1).wait()

    @pl.when(section > 0)
    def _():
        for index in range(9, 14):
            keep(index, 1).wait()

    @pl.when(section == 0)
    def _():
        keep(9, 1).start()
        keep(9, 1).wait()


def main_ticks(packed, second, spots, holder, weights, groups, q_heads, k_heads, cid):
    norm_one, wqkv, wout, norm_two, wgate, wup, wdown = weights
    count, width = packed.shape
    own_second, extra_second, chosen = second
    hidden, keys = wgate.shape[1], groups * count
    pieces = 5
    vmem = pl.BlockSpec(memory_space=pltpu.VMEM)
    far = pl.BlockSpec(memory_space=pl.ANY)
    dma = pltpu.SemaphoreType.DMA

    def shape(columns, rows=2 * count, dtype=BF16):
        return jax.ShapeDtypeStruct((rows, columns), dtype)

    heads, both = q_heads * LANES, (q_heads + 2 * k_heads) * LANES
    spare = holder.shape[0] // (2 * groups)
    outs = [
        shape(width),
        shape(width),
        shape(width, 3 * spare),
        shape(width),
        shape(width),
    ]
    state = [
        shape(width),
        shape(heads),
        shape(2 * k_heads * LANES, 2 * keys),
        shape(LANES, 2 * q_heads * count, F32),
        shape(heads),
        shape(width),
        shape(hidden),
        shape(hidden),
        shape(hidden),
        shape(width),
        shape(width),
        shape(hidden),
        shape(hidden),
        shape(both),
    ]
    outs += state + [shape(width, 1, F32)] * 2
    far_weights = [wqkv, wout, wgate, wup, wdown]
    scratch = [pltpu.VMEM(item.shape, item.dtype) for item in state] + [dma((14, 2))]
    scratch += [pltpu.VMEM(item.shape, BF16) for item in far_weights]
    scratch += [pltpu.VMEM((count, width), BF16)] * 4 + [
        pltpu.VMEM((count, heads), BF16),
        pltpu.VMEM((2 * k_heads * LANES, keys), F32),
        dma((5,)),
        dma((3,)),
        pltpu.SemaphoreType.REGULAR((2 + dp_bits(groups),)),
    ]
    scratch += Gather.scratch(groups)
    for k in range(4):
        scratch += Line.scratch(quarter_rows(count), pieces, width, False)
    scratch += [dma((2, 2, pieces)), dma((4, 2, pieces))] * 2
    scratch += [pltpu.VMEM((groups * spare, width), BF16), pltpu.VMEM((spare, width), BF16)]
    scratch += OwnScatter.scratch(groups, spare, width, spare // 32, BF16)
    scratch += Gather.scratch(groups)
    for _ in range(k_heads):
        scratch += [pltpu.VMEM((keys, 2 * LANES), BF16), pltpu.VMEM((count, 2 * LANES), F32)]
        scratch += Scatter.scratch(groups, count, 2 * LANES, 5, BF16)
    return pl.pallas_call(
        functools.partial(main_kernel, groups, q_heads, k_heads, pieces),
        out_shape=outs,
        in_specs=[vmem] * 9 + [far] * 8,
        out_specs=[far] * (len(outs) - 2) + [vmem] * 2,
        scratch_shapes=scratch,
        compiler_params=pltpu.CompilerParams(
            collective_id=cid, has_side_effects=True, vmem_limit_bytes=VMEM_LIMIT
        ),
        name="main_ticks",
    )(*spots, norm_one[None], norm_two[None], holder, chosen, packed, own_second, extra_second, *far_weights)


def quarter_rows(count):
    return count // 4


def weight_job(target, left, right, i, block=256):
    here = lanes(i, block)
    target[here, :] = rows_contract(left[:, here], right[...]).astype(BF16)


def last_ffn_kernel(groups, pieces, chunks, *refs):
    refs = list(refs)

    def take(count):
        taken = refs[:count]
        del refs[:count]
        return taken

    gain, holder = take(2)
    sources = take(14)
    last_dresid, gsum, g_up, down_sum, gate_sum, y, returned = take(7)
    wdown, wgate, wup, dys, act, gate, up, dgate, dup, resid = kept = take(10)
    n2, part, g_down, g_gate, spares, w_sem = take(6)
    line_scratch = [take(12) for _ in range(4)]
    count, width = last_dresid.shape
    half = count // 2
    line_a, line_b = [
        Line(
            k * half,
            half // 2,
            pieces,
            part,
            dys,
            last_dresid,
            line_scratch[k],
            norm=(resid, gain, gsum, count),
            at=(count, 0, 0),
        )
        for k in range(2)
    ]
    results = [Line(k * half, half // 2, pieces, part, resid, y, line_scratch[k]) for k in range(4)]
    down = OwnScatter(groups, width // groups, chunks, [g_down, down_sum] + take(OwnScatter.refs(groups)))
    gated = OwnScatter(groups, width // groups, chunks, [g_gate, gate_sum] + take(OwnScatter.refs(groups)))
    spare = returned.shape[0]
    give = OwnScatter(groups, spare, spare // 32, [spares, returned] + take(OwnScatter.refs(groups)))
    section = lax.axis_index("section")
    mine = section == 0
    tiles, wide, blocks = act.shape[1] // WIDE, width // WIDE, width // TILE

    def load(k):
        if k in (7, 8):
            return pltpu.make_async_copy(sources[k].at[:count], kept[k].at[:count], w_sem.at[k])
        return pltpu.make_async_copy(sources[k], kept[k], w_sem.at[k])

    lacks = [
        pltpu.make_async_copy(sources[7].at[count:], kept[7].at[count:], w_sem.at[10]),
        pltpu.make_async_copy(sources[8].at[count:], kept[8].at[count:], w_sem.at[11]),
        pltpu.make_async_copy(sources[10].at[count:], last_dresid, w_sem.at[12]),
    ]
    known = [
        pltpu.make_async_copy(sources[11], y, w_sem.at[13]),
        pltpu.make_async_copy(sources[12].at[:spare], returned, w_sem.at[14]),
    ]
    loads = [load(k) for k in range(10)] + [pltpu.make_async_copy(sources[13], n2, w_sem.at[15])]
    for k in (3, 0, 5, 6, 1, 2, 4, 9, 10, 7, 8):
        loads[k].start()

    @pl.when(section > 0)
    def _():
        for item in lacks:
            item.start()

    @pl.when(mine)
    def _():
        for item in known:
            item.start()

    Line.greet()
    for where, _ in down.links:
        greet(where)
    gsum[...] = jnp.zeros_like(gsum)
    line_a.enter(down.levels)
    for k in (3, 0, 5, 6):
        loads[k].wait()

    def hidden(first):
        here = pl.ds(count + first, half)

        def one(i, c):
            columns = lanes(i, WIDE)
            d_act = with_transpose(dys[here], wdown[columns, :])
            gate_pre, up_pre = gate[here, columns].astype(F32), up[here, columns].astype(F32)
            sigma = jax.nn.sigmoid(gate_pre)
            d_silu = d_act * sigma
            dup[here, columns] = (d_silu * gate_pre).astype(BF16)
            dgate[here, columns] = (d_silu * up_pre * (1.0 + gate_pre * (1.0 - sigma))).astype(BF16)
            return c

        lax.fori_loop(0, tiles, one, 0)

    def back(first):
        here, there = pl.ds(first, half), pl.ds(count + first, half)

        def one(i, c):
            columns = lanes(i, WIDE)
            total = with_transpose(dgate[there], wgate[columns, :]) + with_transpose(dup[there], wup[columns, :])
            part[here, columns] = total.astype(BF16)
            return c

        lax.fori_loop(0, wide, one, 0)

    @pl.when(mine)
    def _():
        hidden(0)

    loads[1].wait()
    loads[2].wait()

    @pl.when(mine)
    def _():
        back(0)
        line_a.start()

    loads[4].wait()

    @pl.when(section > 0)
    def _():
        for k in range(4):
            here = pl.ds(k * half, half)

            def one(i, c):
                part[here, lanes(i, WIDE)] = times(act[here], wdown[:, lanes(i, WIDE)]).astype(BF16)
                return c

            lax.fori_loop(0, wide, one, 0)
            results[k].start()

        loads[9].wait()

    def down_job(i, c):
        weight_job(g_down, dys, act, i)
        return c

    lax.fori_loop(0, blocks, down_job, 0)
    down.start()

    @pl.when(mine)
    def _():
        hidden(half)
        back(half)
        line_b.start()

    @pl.when(mine)
    def _():
        loads[9].wait()

    for k in (10, 7, 8):
        loads[k].wait()

    @pl.when(section > 0)
    def _():
        lacks[0].wait()
        lacks[1].wait()

    late = 100
    spans = 0

    first_done = line_a.steps + pieces

    def step(i, c):
        @pl.when(mine)
        def _():
            line_a.step(i)
            line_b.step(i - line_a.steps)

        @pl.when(section > 0)
        def _():
            for k, item in enumerate(results):
                item.step(i - k * pieces)

            @pl.when(i == first_done)
            def _():
                spares[...] = times(holder[...], y[:count]).astype(BF16)
                give.start()

            give.step(i - first_done, late)

        @pl.when(i < late)
        def _():
            down.step(i, late)
            gated.step(i - spans - blocks, late)

        @pl.when(jnp.logical_and(i >= spans, i < spans + blocks))
        def _():
            weight_job(g_gate, n2, dgate, i - spans)

        @pl.when(i == spans + blocks - 1)
        def _():
            gated.start()

        @pl.when(jnp.logical_and(i >= spans + blocks, i < spans + 2 * blocks))
        def _():
            weight_job(g_up, n2, dup, i - spans - blocks)

        return c

    enough = max(line_a.steps + line_b.steps, spans + 2 * blocks, spans + blocks + chunks)
    lax.fori_loop(0, jnp.where(mine, enough, max(enough, line_a.steps + 3 * pieces, first_done + give.chunks)), step, 0)
    run_steps(late, late + chunks, (lambda i: down.step(i, late), 0), (lambda i: gated.step(i, late), 0))

    @pl.when(mine)
    def _():
        line_a.finish()
        line_b.finish()

        for item in known:
            item.wait()

    @pl.when(section > 0)
    def _():
        lacks[2].wait()
        run_steps(late, late + give.chunks, (lambda i: give.step(i, late), 0))
        give.finish()
        for item in results:
            item.finish()

    down.finish()
    gated.finish()


def last_ffn(known, holder, weights, groups, cid):
    norm_one, wqkv, wout, norm_two, wgate, wup, wdown = weights
    dys, act, gate, up, dgate, dup, resid, dresid, y, y_back, normed_two = known
    spare = holder.shape[0] // groups
    count, width = dys.shape[0] // 2, dys.shape[1]
    hidden = act.shape[1]
    pieces, chunks = 5, 8
    vmem = pl.BlockSpec(memory_space=pltpu.VMEM)
    far = pl.BlockSpec(memory_space=pl.ANY)
    sources = [wdown, wgate, wup, dys, act, gate, up, dgate, dup, resid]
    scratch = [pltpu.VMEM(item.shape, BF16) for item in sources]
    scratch += [
        pltpu.VMEM((2 * count, width), BF16),
        pltpu.VMEM((2 * count, width), BF16),
        pltpu.VMEM((width, hidden), BF16),
        pltpu.VMEM((width, hidden), BF16),
        pltpu.VMEM((groups * spare, width), BF16),
        pltpu.SemaphoreType.DMA((16,)),
    ]
    scratch += Line.scratch(count // 4, pieces, width, False) * 4
    scratch += OwnScatter.scratch(groups, width // groups, hidden, chunks, BF16) * 2
    scratch += OwnScatter.scratch(groups, spare, width, spare // 32, BF16)
    return pl.pallas_call(
        functools.partial(last_ffn_kernel, groups, pieces, chunks),
        out_shape=[
            jax.ShapeDtypeStruct((count, width), BF16),
            jax.ShapeDtypeStruct((1, width), F32),
            jax.ShapeDtypeStruct((width, hidden), BF16),
            jax.ShapeDtypeStruct((width // groups, hidden), F32),
            jax.ShapeDtypeStruct((width // groups, hidden), F32),
            jax.ShapeDtypeStruct((2 * count, width), BF16),
            jax.ShapeDtypeStruct((spare, width), BF16),
        ],
        in_specs=[vmem] * 2 + [far] * 14,
        out_specs=[vmem] * 7,
        scratch_shapes=scratch,
        compiler_params=pltpu.CompilerParams(
            collective_id=cid, has_side_effects=True, vmem_limit_bytes=VMEM_LIMIT
        ),
        name="last_ffn",
    )(norm_two[None], holder, *sources, dresid, y, y_back, normed_two)


def last_attn_kernel(groups, q_heads, k_heads, pieces, chunks, spare_chunks, *refs):
    refs = list(refs)

    def take(count):
        taken = refs[:count]
        del refs[:count]
        return taken

    cosine, sine, qcode, qstart, kcode, gain, dresid, holder, gains, spread_q, spread_k, spread_v, spread_o = take(13)
    sources = take(10)
    dx_known, y, y_back, normed_one = take(4)
    dx, returned, returned_y, gains_out, up_sum, attn_sum = take(6)
    wout, wqkv, x, q, kv, lse, mixed, dqkv, other_dresid, g_up = kept = take(10)
    plain, plain_mixed = take(2)
    part, dmixed, dkv, n1, g_attn, spares, spares_y, gsum, gains_own, gains_all, gains_sum, w_sem, g_s, g_r = take(14)
    levels = dp_bits(groups)
    count, width = part.shape
    half = count // 2
    keys = kv.shape[0]
    shares, owns, scatters = [], [], []
    for g in range(k_heads):
        share, own = take(2)
        shares.append(share)
        owns.append(own)
        scatters.append(OwnScatter(groups, count, 5, [share, own] + take(OwnScatter.refs(groups))))
    block = width // groups
    up_task, attn_task = [
        OwnScatter(groups, block, chunks, [value, total] + take(OwnScatter.refs(groups)))
        for value, total in ((g_up, up_sum), (g_attn, attn_sum))
    ]
    spare = spares.shape[0] // groups
    back_task = OwnScatter(groups, spare, spare_chunks, [spares, returned] + take(OwnScatter.refs(groups)))
    give_y = OwnScatter(groups, spare, spare_chunks, [spares_y, returned_y] + take(OwnScatter.refs(groups)))
    small = OwnScatter(groups, 8, 1, [gains_sum, gains_out] + take(OwnScatter.refs(groups)))
    line_a, line_b = [
        Line(k * half, half // 2, pieces, part, dresid, dx, take(12), norm=(x, gain, gsum, count)) for k in range(2)
    ]
    section, t = lax.axis_index("section"), lax.axis_index("tensor")
    mine = section == 0
    order = [9, 0, 3, 4, 5, 1, 2, 6, 7, 8]
    loads = [pltpu.make_async_copy(sources[k].at[sources[k].shape[0] - kept[k].shape[0] :], kept[k], w_sem.at[k]) for k in range(10)]
    for k in order:
        loads[k].start()
    known = pltpu.make_async_copy(dx_known.at[count:], dx, w_sem.at[11])
    load_n1 = pltpu.make_async_copy(normed_one, n1, w_sem.at[10])
    load_n1.start()
    known_y = pltpu.make_async_copy(y_back.at[spare : 2 * spare], returned_y, w_sem.at[12])
    load_y = pltpu.make_async_copy(y.at[count:], part, w_sem.at[12])

    @pl.when(mine)
    def _():
        known_y.start()

    @pl.when(section > 0)
    def _():
        known.start()

    for k in range(1, 4):
        greet({"tensor": lax.rem(t + k, 4)})
    for where, _ in up_task.links:
        greet(where)
    gsum[...] = jnp.zeros_like(gsum)
    dkv[...] = jnp.zeros_like(dkv)
    pl.semaphore_wait(pltpu.get_barrier_semaphore(), 3 + levels)
    loads[9].wait()
    up_task.start()
    for k in order[1:]:
        loads[k].wait()

    wide, jobs = width // WIDE, width // TILE
    repeat = q_heads // k_heads
    rows = block_rows(keys)
    blocks = half // rows
    turns = repeat * blocks
    scale = HD ** (-0.5)
    late = 100
    begun = 2 * k_heads * turns

    def early(i):
        @pl.when(lax.rem(i, 2) == 1)
        def _():
            up_task.step(i // 2, late)

    def mix(first):
        here = pl.ds(first, half)

        def one(h, c):
            dmixed[here, lanes(h)] = with_transpose(dresid[here], wout[lanes(h), :]).astype(BF16)
            return c

        lax.fori_loop(0, q_heads, one, 0)

    def attend(first, g, each):
        def one(i, c):
            h, n = g * repeat + i // blocks, lax.rem(i, blocks)
            here = pl.ds(pl.multiple_of(first + n * rows, rows), rows)
            scores, allowed = score_rows(q, kv, h, g, here, qcode, qstart, kcode)
            there = pl.ds(pl.multiple_of(h * count + first + n * rows, rows), rows)
            prob = jnp.where(allowed, jnp.exp(scores - lse[there][:, :1]), 0.0)
            dm = dmixed[here, lanes(h)]
            d_prob = with_transpose(dm, kv[:, lanes(k_heads + g)])
            row_dot = jnp.sum(prob * d_prob, axis=-1, keepdims=True)
            d_scores = (prob * (d_prob - row_dot)).astype(BF16)
            d_query = times(d_scores, kv[:, lanes(g)]) * scale
            there = pl.ds(pl.multiple_of(count + first + n * rows, rows), rows)
            dqkv[there, lanes(h)] = rolled(d_query, cosine[here], -sine[here]).astype(BF16)
            dkv[lanes(g), :] += rows_contract(q[here, lanes(h)], d_scores) * scale
            dkv[lanes(k_heads + g), :] += rows_contract(dm, prob.astype(BF16))
            each(i)
            return c

        lax.fori_loop(0, turns, one, 0)

    def back(first):
        here, there = pl.ds(first, half), pl.ds(count + first, half)

        def one(i, c):
            columns = lanes(i, WIDE)
            part[here, columns] = with_transpose(dqkv[there], wqkv[columns, :]).astype(BF16)
            return c

        lax.fori_loop(0, wide, one, 0)

    @pl.when(mine)
    def _():
        mix(0)
        mix(half)
        for g in range(k_heads):
            for first in (0, half):
                at = 2 * g * turns + (turns if first else 0)
                attend(first, g, lambda i: early(at + i))

            shares[g][:, :LANES] = jnp.transpose(dkv[lanes(g), :]).astype(BF16)
            shares[g][:, LANES:] = jnp.transpose(dkv[lanes(k_heads + g), :]).astype(BF16)
            scatters[g].start()
        run_steps(0, scatters[0].chunks, *[(functools.partial(lambda s, i: s.step(i, late), s), 0) for s in scatters])

    @pl.when(section > 0)
    def _():
        run_steps(0, begun, (early, 0))
        known.wait()

    ends = [0]
    for item in (spread_q, spread_k, spread_v, spread_o):
        ends.append(ends[-1] + item.shape[0])
    starts = [0, q_heads, q_heads + k_heads, q_heads + 2 * k_heads]

    @pl.when(section > 0)
    def _():
        load_y.start()
        load_y.wait()
        spares_y[...] = times(holder[...], part[...]).astype(BF16)
        give_y.start()

    load_n1.wait()
    plain_mixed[...] = with_transpose(mixed[...], spread_o[...]).astype(BF16)
    other_dresid[count:] = dresid[...]

    def out_job(i, c):
        here = lanes(i, TILE)
        g_attn[here, ends[3] :] = rows_contract(other_dresid[:, here], plain_mixed[...]).astype(BF16)
        return c

    lax.fori_loop(0, jobs, out_job, 0)

    @pl.when(mine)
    def _():
        ending = late + scatters[0].chunks
        run_steps(late, ending, *[(functools.partial(lambda s, i: s.step(i, late), s), 0) for s in scatters])
        for g in range(k_heads):
            dqkv[count:, lanes(q_heads + g)] = rolled(owns[g][:, :LANES], cosine[...], -sine[...]).astype(BF16)
            dqkv[count:, lanes(q_heads + k_heads + g)] = owns[g][:, LANES:].astype(BF16)
        back(0)
        line_a.start()
        back(half)
        line_b.start()

    def spread(k):
        return remote(gains_own, gains_all.at[k - 1], g_s.at[k - 1], g_r.at[k - 1], {"tensor": lax.rem(t + k, 4)})

    first_job = begun // 2

    def step(i, c):
        @pl.when(mine)
        def _():
            line_a.step(i)
            line_b.step(i - line_a.steps)

        up_task.step(i + first_job, late)

        @pl.when(i == 0)
        def _():
            for a, b, n, item in zip(starts, starts[1:], ends, (spread_q, spread_k, spread_v)):
                plain[:, n : n + item.shape[0]] = with_transpose(
                    dqkv[:, a * LANES : b * LANES], item[...]
                ).astype(BF16)

        @pl.when(jnp.logical_and(i >= 1, i <= jobs))
        def _():
            here = lanes(jnp.clip(i - 1, 0, jobs - 1), TILE)
            g_attn[here, : ends[3]] = rows_contract(n1[:, here], plain[...]).astype(BF16)

        @pl.when(i == jobs)
        def _():
            attn_task.start()

        attn_task.step(i - jobs - 1, late)

        @pl.when(section > 0)
        def _():
            give_y.step(i - first_job, late)

        return c

    lax.fori_loop(0, max(line_a.steps + line_b.steps, jobs + 1 + chunks), step, 0)
    spares[...] = times(holder[...], dx[...]).astype(BF16)
    back_task.start()
    gains_own[...] = gains[...]
    gains_own[:1] = gains[:1] + gsum[...] * jnp.where(mine, 1.0, 0.0)
    for k in range(1, 4):
        spread(k).start()
    run_steps(0, spare_chunks, (lambda i: back_task.step(i, late), 0))
    for k in range(1, 4):
        spread(k).wait()
    total = gains_own[...] + gains_all[0] + gains_all[1] + gains_all[2]
    part_width = width // groups
    for d in range(groups):
        gains_sum[8 * d : 8 * d + 8, :] = total[:, d * part_width : (d + 1) * part_width]
    small.start()

    def close(i, c):
        up_task.step(late + i, late)
        attn_task.step(late + i, late)

        @pl.when(section > 0)
        def _():
            give_y.step(late + i, late)

        small.step(i, 4)
        return c

    lax.fori_loop(0, max(chunks, spare_chunks, small.steps(4)), close, 0)
    run_steps(late, late + spare_chunks, (lambda i: back_task.step(i, late), 0))

    @pl.when(mine)
    def _():
        line_a.finish()
        line_b.finish()
        for item in scatters:
            item.finish()
        known_y.wait()

    @pl.when(section > 0)
    def _():
        give_y.finish()

    for item in (up_task, attn_task, back_task, small):
        item.finish()


def last_attn(known, spots, dresid, dx, y, y_back, normed_one, holder, gains, spreads, grads, weights, groups, q_heads, k_heads, cid):
    norm_one, wqkv, wout, norm_two, wgate, wup, wdown = weights
    x, q, kv, lse, mixed, dqkv, other_dresid = known
    count, width = dresid.shape
    keys = groups * count
    spare = holder.shape[0] // groups
    pieces, chunks, spare_chunks = 5, 8, spare // 32
    vmem = pl.BlockSpec(memory_space=pltpu.VMEM)
    far = pl.BlockSpec(memory_space=pl.ANY)
    dma = pltpu.SemaphoreType.DMA
    sources = [wout, wqkv, x, q, kv, lse, mixed, dqkv, other_dresid, *grads]
    attn_width = sum(item.shape[0] for item in spreads)
    block = width // groups
    first_only = {3: count, 4: keys, 5: q_heads * count}
    scratch = [
        pltpu.VMEM((first_only.get(k, item.shape[0]),) + item.shape[1:], item.dtype) for k, item in enumerate(sources)
    ]
    scratch += [
        pltpu.VMEM((2 * count, attn_width - spreads[3].shape[0]), BF16),
        pltpu.VMEM((2 * count, spreads[3].shape[0]), BF16),
        pltpu.VMEM((count, width), BF16),
        pltpu.VMEM((count, q.shape[1]), BF16),
        pltpu.VMEM((kv.shape[1], keys), F32),
        pltpu.VMEM((2 * count, width), BF16),
        pltpu.VMEM((width, attn_width), BF16),
        pltpu.VMEM((groups * spare, width), BF16),
        pltpu.VMEM((groups * spare, width), BF16),
        pltpu.VMEM((1, width), F32),
        pltpu.VMEM(gains.shape, F32),
        pltpu.VMEM((3,) + gains.shape, F32),
        pltpu.VMEM((groups * 8, block), F32),
        dma((13,)),
        dma((3,)),
        dma((3,)),
    ]
    for _ in range(k_heads):
        scratch += [pltpu.VMEM((keys, 2 * LANES), BF16), pltpu.VMEM((count, 2 * LANES), F32)]
        scratch += OwnScatter.scratch(groups, count, 2 * LANES, 5, BF16)
    for columns in (grads[0].shape[1], attn_width):
        scratch += OwnScatter.scratch(groups, block, columns, chunks, BF16)
    scratch += OwnScatter.scratch(groups, spare, width, spare_chunks, BF16) * 2
    scratch += OwnScatter.scratch(groups, 8, block, 1, F32)
    scratch += Line.scratch(count // 4, pieces, width, False) * 2
    return pl.pallas_call(
        functools.partial(last_attn_kernel, groups, q_heads, k_heads, pieces, chunks, spare_chunks),
        out_shape=[
            jax.ShapeDtypeStruct((count, width), BF16),
            jax.ShapeDtypeStruct((spare, width), BF16),
            jax.ShapeDtypeStruct((spare, width), BF16),
            jax.ShapeDtypeStruct((8, block), F32),
            jax.ShapeDtypeStruct((block, grads[0].shape[1]), F32),
            jax.ShapeDtypeStruct((block, attn_width), F32),
        ],
        in_specs=[vmem] * 13 + [far] * 14,
        out_specs=[vmem] * 6,
        scratch_shapes=scratch,
        compiler_params=pltpu.CompilerParams(
            collective_id=cid, has_side_effects=True, vmem_limit_bytes=VMEM_LIMIT
        ),
        name="last_attn",
    )(*spots, norm_one[None], dresid, holder, gains, *spreads, *sources, dx, y, y_back, normed_one)


def finish_kernel(groups, parts, *refs):
    refs = list(refs)

    def take(count):
        taken = refs[:count]
        del refs[:count]
        return taken

    (live,) = take(1)
    through, y, y_first, y_second, cot, dx_first, dx_second, back_first, back_second = take(9)
    gate, up, down, attn = take(4)
    acts, backs = take(2)
    outs = take(7)
    tiles = take(4)
    rows = take(4)
    backs_near = take(4)
    down_near, down_turned, attn_near, *attn_parts = take(7)
    plain_near = take(2)
    sems, out_sems = take(2)
    count, spare = rows[0].shape[0], backs_near[0].shape[0]
    seq = count + spare
    whole = [
        (through.at[0, 0], y.at[:count], y_first, acts.at[0, 0, 0]),
        (through.at[1, 0], y.at[count:], y_second, acts.at[0, 1, 0]),
        (cot.at[0, 0], dx_first.at[:count], back_first.at[2 * spare :], backs.at[0, 0, 0]),
        (cot.at[1, 0], dx_second, back_second, backs.at[0, 1, 0]),
    ]
    query_out, key_out, value_out, out_out, gate_out, up_out, down_out = outs
    plain_in = [pltpu.make_async_copy(a, b, sems.at[14 + k]) for k, (a, b) in enumerate(zip((gate, up), plain_near))]
    plain = [pltpu.make_async_copy(a, b, out_sems.at[k]) for k, (a, b) in enumerate(zip(plain_near, (gate_out.at[0], up_out.at[0])))]
    load_down = pltpu.make_async_copy(down, down_near, sems.at[12])
    load_attn = pltpu.make_async_copy(attn, attn_near, sems.at[13])
    loads = []
    for k, (a, b, c, _) in enumerate(whole):
        loads.append(
            [
                pltpu.make_async_copy(src, dst, sems.at[3 * k + n])
                for n, (src, dst) in enumerate(((a, tiles[k]), (b, rows[k]), (c, backs_near[k])))
            ]
        )
    load_attn.start()
    load_down.start()
    for item in plain_in:
        item.start()
    for group in loads:
        for item in group:
            item.start()
    stores = []
    load_attn.wait()
    at = 0
    for k, (size, near, there) in enumerate(zip(parts, attn_parts, (query_out, key_out, value_out, out_out))):
        value = attn_near[:, at : at + size]
        near[...] = value if k == 0 else jnp.transpose(value)
        at += size
        stores.append(pltpu.make_async_copy(near, there.at[0], out_sems.at[2 + k]))
        stores[-1].start()
    for before, item in zip(plain_in, plain):
        before.wait()
        item.start()
    load_down.wait()
    down_turned[...] = jnp.transpose(down_near[...])
    stores.append(pltpu.make_async_copy(down_turned, down_out.at[0], out_sems.at[6]))
    stores[-1].start()
    for k, group in enumerate(loads):
        for item in group:
            item.wait()
        first = (k % 2) * seq

        def one(i, c):
            here = pl.ds(pl.multiple_of(i * 64, 64), 64)
            alive = live[pl.ds(pl.multiple_of(first + i * 64, 64), 64)] > 0
            tiles[k][here] = jnp.where(alive, rows[k][here], tiles[k][here])
            return c

        lax.fori_loop(0, count // 64, one, 0)

        def two(i, c):
            near = pl.ds(pl.multiple_of(i * 64, 64), 64)
            here = pl.ds(pl.multiple_of(count + i * 64, 64), 64)
            alive = live[pl.ds(pl.multiple_of(first + count + i * 64, 64), 64)] > 0
            tiles[k][here] = jnp.where(alive, backs_near[k][near], tiles[k][here])
            return c

        lax.fori_loop(0, spare // 64, two, 0)
        stores.append(pltpu.make_async_copy(tiles[k], whole[k][3], out_sems.at[7 + k]))
        stores[-1].start()
    for item in stores + plain:
        item.wait()


def finish(live, through, y, y_backs, cot, dx_first, dx_second, back_first, back_second, grads, parts, groups):
    count, width = dx_second.shape
    spare = back_second.shape[0]
    gate, up, down, attn = grads
    block, hidden = down.shape
    vmem = pl.BlockSpec(memory_space=pltpu.VMEM)
    far = pl.BlockSpec(memory_space=pl.ANY)
    shapes = [(block, parts[0])] + [(size, block) for size in parts[1:]]
    outs = [jax.ShapeDtypeStruct((1, 2, 1, count + spare, width), BF16)] * 2
    outs += [jax.ShapeDtypeStruct((1,) + item, F32) for item in shapes + [gate.shape, up.shape, (hidden, block)]]
    scratch = [pltpu.VMEM((count + spare, width), BF16)] * 4
    scratch += [pltpu.VMEM((count, width), BF16)] * 4 + [pltpu.VMEM((spare, width), BF16)] * 4
    scratch += [pltpu.VMEM(down.shape, F32), pltpu.VMEM((hidden, block), F32), pltpu.VMEM(attn.shape, F32)]
    scratch += [pltpu.VMEM(item, F32) for item in shapes]
    scratch += [pltpu.VMEM(gate.shape, F32), pltpu.VMEM(up.shape, F32)]
    scratch += [pltpu.SemaphoreType.DMA((16,)), pltpu.SemaphoreType.DMA((11,))]
    return pl.pallas_call(
        functools.partial(finish_kernel, groups, parts),
        out_shape=outs,
        in_specs=[vmem] + [far] * 13,
        out_specs=[far] * 9,
        scratch_shapes=scratch,
        compiler_params=pltpu.CompilerParams(vmem_limit_bytes=VMEM_LIMIT),
        name="finish",
    )(live, through, y, *y_backs, cot, dx_first, dx_second, back_first, back_second, gate, up, down, attn)


def rope_tables(pos):
    half_width = HD // 2
    inverse = rope_base ** (-(jnp.arange(half_width, dtype=F32) * 2.0 / HD))
    angle = pos.astype(F32)[:, None] * inverse[None, :]
    blank = jnp.zeros((pos.shape[0], LANES // 2 - half_width), F32)
    cosine, sine = jnp.cos(angle), jnp.sin(angle)
    return (
        jnp.concatenate([cosine, blank, cosine, blank], axis=1),
        jnp.concatenate([-sine, blank, sine, blank], axis=1),
    )


def spreader(heads, turned):
    feature = jnp.arange(HD)
    place = jnp.where(feature < HD // 2, feature, feature - HD // 2 + LANES // 2) if turned else feature
    lane = (jnp.arange(heads)[:, None] * LANES + place[None, :]).reshape(-1)
    return (lane[:, None] == jnp.arange(heads * LANES)[None, :]).astype(BF16)


def slots_of(lens, count):
    groups = lens.shape[0]
    kept = jnp.minimum(lens, count)
    free, extra = count - kept, lens - kept
    free_off = jnp.cumsum(free) - free
    extra_end = jnp.cumsum(extra)
    slot = jnp.arange(count)
    own = slot[None, :] < kept[:, None]
    index = free_off[:, None] + slot[None, :] - kept[:, None]
    source = jnp.sum(index[:, :, None] >= extra_end[None, None, :], axis=-1)
    begins = jnp.sum(jnp.where(index[:, :, None] >= extra_end[None, None, :], extra[None, None, :], 0), axis=-1)
    seq = jnp.where(own, jnp.arange(groups)[:, None], source)
    pos = jnp.where(own, slot[None, :], count + index - begins)
    return seq, pos, own


def on_device(
    inputs,
    cotangent,
    lengths,
    norm_attn,
    w_query,
    w_key,
    w_value,
    w_out,
    norm_ffn,
    w_gate,
    w_up,
    w_down,
):
    first = lax.axis_index("section") == 0
    me = lax.axis_index("dp")
    groups = lax.axis_size("dp")
    micro, seq_len, width = inputs.shape[0], inputs.shape[2], inputs.shape[3]
    count = seq_len * 5 // 8
    spare = seq_len - count
    q_heads, k_heads = w_query.shape[2] // HD, w_key.shape[2] // HD
    spread_q, spread_k = spreader(q_heads, True), spreader(k_heads, True)
    spread_v, spread_o = spreader(k_heads, False), spreader(q_heads, False)
    wqkv = jnp.concatenate(
        [times(w_query[0], spread_q), times(w_key[0], spread_k), times(w_value[0], spread_v)], axis=1
    ).astype(BF16)
    wout = rows_contract(spread_o, w_out[0]).astype(BF16)
    weights = (norm_attn[0], wqkv, wout, norm_ffn[0], w_gate[0], w_up[0], w_down[0])

    all_in_one = micro == 2 and groups == 4

    source = jnp.where(first, inputs[:, 0], cotangent[:, 0])
    first_extra = lax.all_gather(source[0, count:], "dp", axis=0, tiled=True)
    length_rows = jnp.broadcast_to(lengths[:, 0].astype(F32)[:, None], (micro, LANES))
    length_rows = jnp.concatenate([length_rows, jnp.zeros((8 - micro, LANES), F32)], axis=0)
    (length_all,) = gather_rows([length_rows], groups, 4)
    lens = length_all.reshape(groups, 8, LANES)[:, :micro, 0].T.astype(jnp.int32)
    packed, slots, chosen, kept_own = [], [], [], []
    for b in range(micro):
        seq, pos, own = slots_of(lens[b], count)
        slots.append((seq, pos))
        wanted = seq[me] * spare + pos[me] - count
        chosen.append(
            jnp.logical_and(jnp.arange(groups * spare)[None, :] == wanted[:, None], ~own[me][:, None]).astype(BF16)
        )
        kept_own.append(jnp.where(own[me][:, None], source[b, :count], jnp.zeros((), BF16)))
    for b in range(1 if all_in_one else micro):
        extra = first_extra if b == 0 else lax.all_gather(source[b, count:], "dp", axis=0, tiled=True)
        brought = times(chosen[b], extra)
        packed.append((kept_own[b].astype(F32) + brought).astype(BF16))

    def spots_of(b):
        seq, pos = slots[b]
        code = seq * seq_len + pos
        return rope_tables(pos[me]) + (code[me][:, None], (seq[me] * seq_len)[:, None], code.reshape(1, -1))

    spots = [spots_of(b) for b in range(micro)]

    def holder(b):
        seq, pos = slots[b]
        row = jnp.arange(groups * spare)[:, None]
        return jnp.logical_and(row == seq[me][None, :] * spare + pos[me][None, :] - count, pos[me][None, :] >= count)

    def spread(rows, b):
        return jnp.dot(holder(b).astype(BF16), rows, preferred_element_type=F32).astype(BF16)

    def unpack(rows, back, b, through):
        live = (jnp.arange(seq_len) < lens[b, me])[:, None]
        return jnp.where(live, jnp.concatenate([rows, back], axis=0), through)

    def come_back(rows, b):
        return lax.psum_scatter(spread(rows, b), "dp", scatter_dimension=0, tiled=True)

    norm_one, norm_two = weights[0], weights[3]
    empty = jnp.zeros((count, width), BF16)

    def spots_at(tick):
        early, late = spots[min(tick, micro - 1)], spots[max(tick - 1, 0)]
        return tuple(jnp.where(first, a, b) for a, b in zip(early, late))

    grads_in, before, gain_sums = [], [], []
    if all_in_one:
        joined = [jnp.concatenate(items, axis=0) for items in zip(*spots)]
        joined[4] = joined[4][:, None]
        held = jnp.concatenate([holder(b) for b in range(micro)], axis=0).astype(BF16)
        y, dx, y_back, normed_one, normed_two, x, q, kv, lse, mixed, resid, gate, up, act, dy, d_resid, d_gate, d_up, d_qkv, gain_one, gain_two = main_ticks(
            packed[0],
            (kept_own[1], source[1, count:], chosen[1]),
            joined,
            held,
            weights,
            groups,
            q_heads,
            k_heads,
            0,
        )
        last_dresid, gain_last, grad_up, grad_down, grad_gate, y, y_first = last_ffn(
            (dy, act, gate, up, d_gate, d_up, resid, d_resid, y, y_back, normed_two), held[: groups * spare], weights, groups, 1
        )
        gain_last = jnp.where(first, gain_last, jnp.zeros_like(gain_last))
        gains = jnp.concatenate([gain_one, gain_two + gain_last, jnp.zeros((6, width), F32)], axis=0)
        last_dx, back_second, y_second, gains, grad_up, grad_attn = last_attn(
            (x, q, kv, lse, mixed, d_qkv, d_resid),
            spots[1],
            last_dresid,
            dx,
            y,
            y_back,
            normed_one,
            held[groups * spare :],
            gains,
            (spread_q, spread_k, spread_v, spread_o),
            (grad_up,),
            weights,
            groups,
            q_heads,
            k_heads,
            2,
        )
        live = (jnp.arange(seq_len)[None, :] < lens[:, me][:, None]).astype(jnp.int32).reshape(-1, 1)
        acts, backs, *grads = finish(
            live,
            inputs,
            y,
            (y_first, y_second),
            cotangent,
            dx,
            last_dx,
            y_back,
            back_second,
            (grad_gate, grad_up, grad_down, grad_attn),
            [w_query.shape[2], w_key.shape[2], w_value.shape[2], w_query.shape[2]],
            groups,
        )
        grads[1:3] = [jnp.swapaxes(item, 1, 2) for item in grads[1:3]]
        return (acts, backs, gains[:1], *grads[:4], gains[1:2], *grads[4:])

    else:
        arriving = empty
        results, saved = [], []
        for tick in range(micro + 1):
            stream = jnp.where(first, packed[tick] if tick < micro else empty, arriving)
            result, arriving, kept = forward_tick(stream, spots_at(tick), weights, groups, q_heads, k_heads, 0)
            results.append(result)
            saved.append(kept)
        results = [jnp.where(first, results[b], results[b + 1]) for b in range(micro)]
        arriving = empty
        for tick in range(micro):
            kept = saved[micro - tick]
            incoming = jnp.where(first, arriving, packed[micro - 1 - tick])
            d_resid, gain_two, d_gate, d_up = back_ffn(incoming, kept, weights, 1)
            d_stream, gain_one, d_qkv, arriving = back_attn(
                d_resid, kept, spots_at(micro - tick), weights, groups, q_heads, k_heads, 2, -1
            )
            before.append((kept[5], d_gate, d_up, incoming, kept[8], kept[0], d_qkv, d_resid, kept[4]))
            grads_in.append(d_stream)
            gain_sums.append(jnp.concatenate([gain_one, gain_two], axis=0))
        kept_last = saved[0]
        last_in, last_spots = jnp.where(first, arriving, empty), spots_at(0)
        grads_at = [grads_in[micro - 1 - b] if b == 0 else jnp.where(first, grads_in[micro - b], grads_in[micro - 1 - b]) for b in range(micro)]

        def all_rows(now, index):
            old = [item[index] for item in before]
            return jnp.concatenate([jnp.where(first, now, old[0])] + old[1:], axis=0)

        x, mixed, resid, act = kept_last[0], kept_last[4], kept_last[5], kept_last[8]
        d_resid, gain_two, d_gate, d_up = back_ffn(last_in, kept_last, weights, 1)
        n2 = normalize(all_rows(resid, 0), norm_two)
        grad_gate = rows_contract(n2, all_rows(d_gate, 1)).astype(BF16)
        grad_up = rows_contract(n2, all_rows(d_up, 2)).astype(BF16)
        grad_down = rows_contract(all_rows(last_in, 3), all_rows(act, 4)).astype(BF16)
        ffn_grads = (grad_gate, grad_up, grad_down)
        beside = len(ffn_grads) if groups * count <= 2048 else 1
        d_stream, gain_one, d_qkv, *ffn_sums = back_attn(
            d_resid, kept_last, last_spots, weights, groups, q_heads, k_heads, 3, 0, sums=ffn_grads[:beside]
        )
        n1 = normalize(all_rows(x, 5), norm_one)
        back_spread = [(spread_q, 0, q_heads), (spread_k, q_heads, k_heads), (spread_v, q_heads + k_heads, k_heads)]
        dqkv = all_rows(d_qkv, 6)
        dqkv = jnp.concatenate(
            [with_transpose(dqkv[:, i * LANES : (i + n) * LANES], item) for item, i, n in back_spread], axis=1
        ).astype(BF16)
        mix = with_transpose(all_rows(mixed, 8), spread_o).astype(BF16)
        grad_attn = jnp.concatenate(
            [rows_contract(n1, dqkv).astype(BF16), rows_contract(all_rows(d_resid, 7), mix).astype(BF16)], axis=1
        )
        grads_at[0] = jnp.where(first, d_stream, grads_at[0])
        last_gains = jnp.concatenate([gain_one, gain_two], axis=0)
        gain_sums.append(jnp.where(first, last_gains, jnp.zeros_like(last_gains)))

        gains = sum(gain_sums[1:], gain_sums[0])
        gains = jnp.concatenate([gains, jnp.zeros((6, width), F32)], axis=0)
        gains = gains.reshape(8, groups, -1).transpose(1, 0, 2).reshape(groups * 8, -1)

    acts = []
    for b in range(micro):
        rows = results[b]
        acts.append(unpack(rows, come_back(rows, b), b, inputs[b, 0]))
    backs = []
    for b in range(micro):
        rows = grads_at[b]
        if b == 0:
            back, gains, grad_attn, *rest = return_rows(
                spread(rows, b), gains, (grad_attn,) + ffn_grads[beside:], groups, 5, spare // 16
            )
            grad_gate, grad_up, grad_down = ffn_sums + rest
        else:
            back = come_back(rows, b)
        backs.append(unpack(rows, back, b, cotangent[b, 0]))
    acts, backs = jnp.stack(acts), jnp.stack(backs)
    ends = [0]
    for item in (w_query, w_key, w_value, w_query):
        ends.append(ends[-1] + item.shape[2])
    grad_query, grad_key, grad_value, grad_out = (grad_attn[:, a:b] for a, b in zip(ends, ends[1:]))
    final = (
        gains[0],
        grad_query,
        grad_key,
        grad_value,
        grad_out.T,
        gains[1],
        grad_gate,
        grad_up,
        grad_down.T,
    )
    return (acts[None, :, None], backs[None, :, None]) + tuple(item[None] for item in final)


def solution(mesh):
    placed = (
        P(None, "dp", None, None),
        P(None, "dp", None, None),
        P(None, "dp"),
        P("section", None),
        P("section", None, "tensor"),
        P("section", None, "tensor"),
        P("section", None, "tensor"),
        P("section", "tensor", None),
        P("section", None),
        P("section", None, "tensor"),
        P("section", None, "tensor"),
        P("section", "tensor", None),
    )
    return jax.shard_map(
        on_device,
        mesh=mesh,
        in_specs=placed,
        out_specs=(
            P("section", None, "dp", None, None),
            P("section", None, "dp", None, None),
            P("section", "dp"),
            P("section", "dp", "tensor"),
            P("section", "dp", "tensor"),
            P("section", "dp", "tensor"),
            P("section", "tensor", "dp"),
            P("section", "dp"),
            P("section", "dp", "tensor"),
            P("section", "dp", "tensor"),
            P("section", "tensor", "dp"),
        ),
        check_vma=False,
    )
```

```python
import functools

import jax
import jax.numpy as jnp
import numpy as np
from jax import lax
from jax.experimental import pallas as pl
from jax.experimental.pallas import tpu as pltpu
from jax.sharding import PartitionSpec as P

HD = 96

epsilon = 1e-05
rope_base = 100000.0
negative = -1e30
MESH = pl.DeviceIdType.MESH
F32 = jnp.float32
BF16 = jnp.bfloat16


def remote(src, dst, s_sem, r_sem, where):
    return pltpu.make_async_remote_copy(
        src_ref=src, dst_ref=dst, send_sem=s_sem, recv_sem=r_sem, device_id=where, device_id_type=MESH
    )


def greet(where):
    pl.semaphore_signal(pltpu.get_barrier_semaphore(), inc=1, device_id=where, device_id_type=MESH)


def dp_bits(groups):
    return groups.bit_length() - 1


def dp_partner(level):
    me = lax.axis_index("dp")
    bit = lax.rem(me // (1 << level), 2)
    return {"dp": me + (1 - 2 * bit) * (1 << level)}, bit


class Scatter:
    def __init__(self, groups, rows, chunks, refs):
        self.levels = dp_bits(groups)
        self.groups, self.rows, self.chunks, self.size = groups, rows, chunks, rows // chunks
        self.value, self.out = refs[0], refs[1]
        m = self.levels
        self.arrive = refs[2 : 2 + m]
        self.held = refs[2 + m : 1 + 2 * m]
        self.s_sem = refs[1 + 2 * m : 1 + 3 * m]
        self.r_sem = refs[1 + 3 * m : 1 + 4 * m]
        self.links = [dp_partner(k) for k in range(m)]

    @staticmethod
    def scratch(groups, rows, width, chunks, dtype):
        m = dp_bits(groups)
        sizes = [groups >> (k + 1) for k in range(m)]
        return (
            [pltpu.VMEM((size * rows, width), dtype) for size in sizes]
            + [pltpu.VMEM((size * rows, width), dtype) for size in sizes[:-1]]
            + [pltpu.SemaphoreType.DMA((size, chunks)) for size in sizes] * 2
        )

    def at(self, block, c):
        return pl.ds(pl.multiple_of(block * self.rows + c * self.size, self.size), self.size)

    def copy(self, level, slot, c):
        where, bit = self.links[level]
        source = self.value if level == 0 else self.held[level - 1]
        return remote(
            source.at[self.at(2 * slot + 1 - bit, c)],
            self.arrive[level].at[self.at(slot, c)],
            self.s_sem[level].at[slot, c],
            self.r_sem[level].at[slot, c],
            where,
        )

    def order(self, level):
        count = self.groups >> (level + 1)
        if count == 1:
            return [(0, False)]
        bit = self.links[level + 1][1]
        return [(2 * i + 1 - bit, True) for i in range(count // 2)] + [(2 * i + bit, False) for i in range(count // 2)]

    def start(self):
        def one(c, carry):
            for slot, _ in self.order(0):
                self.copy(0, slot, c).start()
            return carry

        lax.fori_loop(0, self.chunks, one, 0)

    def step(self, i, lag):
        for level in range(self.levels):
            c = i - level * lag

            @pl.when(jnp.logical_and(c >= 0, c < self.chunks))
            def _():
                bit = self.links[level][1]
                source = self.value if level == 0 else self.held[level - 1]
                for slot, goes in self.order(level):
                    self.copy(level, slot, c).wait_recv()
                    here = self.at(slot, c)
                    total = source[self.at(2 * slot + bit, c)].astype(F32) + self.arrive[level][here].astype(F32)
                    if level == self.levels - 1:
                        self.out[here] = total.astype(self.out.dtype)
                    else:
                        self.held[level][here] = total.astype(self.held[level].dtype)
                        if goes:
                            self.copy(level + 1, slot // 2, c).start()

    def steps(self, lag):
        return self.chunks + (self.levels - 1) * lag

    def finish(self):
        def one(c, carry):
            for level in range(self.levels):
                for slot in range(self.groups >> (level + 1)):
                    self.copy(level, slot, c).wait_send()
            return carry

        lax.fori_loop(0, self.chunks, one, 0)


def return_kernel(groups, rows, chunks, plans, *refs):
    refs = list(refs)

    def take(count):
        taken = refs[:count]
        del refs[:count]
        return taken

    m = dp_bits(groups)
    count = 4 * m - 1
    value, gains = take(2)
    grads = take(len(plans))
    out, gains_out = take(2)
    totals = take(len(plans))
    gains_all, gains_sum, g_s, g_r = take(4)
    task = Scatter(groups, rows, chunks, [value, out] + take(count))
    small = Scatter(groups, 8, 1, [gains_sum, gains_out] + take(count))
    large = [
        Scatter(groups, block, parts, [grad, total] + take(count))
        for (block, parts), grad, total in zip(plans, grads, totals)
    ]
    t = lax.axis_index("tensor")
    for where, _ in task.links:
        greet(where)
    for k in range(1, 4):
        greet({"tensor": lax.rem(t + k, 4)})
    pl.semaphore_wait(pltpu.get_barrier_semaphore(), m + 3)

    def spread(k):
        return remote(gains, gains_all.at[k - 1], g_s.at[k - 1], g_r.at[k - 1], {"tensor": lax.rem(t + k, 4)})

    for k in range(1, 4):
        spread(k).start()
    task.start()
    for item in large:
        item.start()
    for k in range(1, 4):
        spread(k).wait()
    gains_sum[...] = gains[...] + gains_all[0] + gains_all[1] + gains_all[2]
    small.start()

    def body(i, c):
        small.step(i, 1)
        task.step(i, 2)
        for item in large:
            item.step(i, 4)
        return c

    lax.fori_loop(0, max([task.steps(2), small.steps(1)] + [item.steps(4) for item in large]), body, 0)
    small.finish()
    task.finish()
    for item in large:
        item.finish()


def return_rows(value, gains, grads, groups, cid, chunks):
    rows, width = value.shape[0] // groups, value.shape[1]
    vmem = pl.BlockSpec(memory_space=pltpu.VMEM)
    part = gains.shape[1]
    plans, outs = [], [jax.ShapeDtypeStruct((rows, width), BF16), jax.ShapeDtypeStruct((8, part), F32)]
    scratch = [
        pltpu.VMEM((3,) + gains.shape, F32),
        pltpu.VMEM(gains.shape, F32),
        pltpu.SemaphoreType.DMA((3,)),
        pltpu.SemaphoreType.DMA((3,)),
    ]
    scratch += Scatter.scratch(groups, rows, width, chunks, BF16) + Scatter.scratch(groups, 8, part, 1, F32)
    for grad in grads:
        block = grad.shape[0] // groups
        plans.append((block, max(1, block // 48)))
        outs.append(jax.ShapeDtypeStruct((block, grad.shape[1]), F32))
        scratch += Scatter.scratch(groups, block, grad.shape[1], plans[-1][1], BF16)
    return pl.pallas_call(
        functools.partial(return_kernel, groups, rows, chunks, plans),
        out_shape=outs,
        in_specs=[vmem] * (2 + len(grads)),
        out_specs=[vmem] * len(outs),
        scratch_shapes=scratch,
        compiler_params=pltpu.CompilerParams(
            collective_id=cid, has_side_effects=True, vmem_limit_bytes=VMEM_LIMIT
        ),
        name="return_%d" % cid,
    )(value, gains, *grads)


def gather_kernel(groups, count, *refs):
    values, outs = refs[:count], refs[count : 2 * count]
    s_sem, r_sem, own = refs[2 * count :]
    m = dp_bits(groups)
    me = lax.axis_index("dp")
    links = [dp_partner(k) for k in range(m)]
    for where, _ in links:
        greet(where)
    pl.semaphore_wait(pltpu.get_barrier_semaphore(), m)

    def place(a, block):
        rows = values[a].shape[0]
        return outs[a].at[pl.ds(pl.multiple_of(block * rows, rows), rows)]

    def copy(a, level, i, mine):
        where, bit = links[level]
        low = lax.rem(me, 1 << (level + 1))
        if not mine:
            low = low + (1 - 2 * bit) * (1 << level)
        block = i * (1 << (level + 1)) + low
        return remote(place(a, block), place(a, block), s_sem.at[a, level, i], r_sem.at[a, level, i], where)

    locals_ = [pltpu.make_async_copy(values[a], place(a, me), own.at[a]) for a in range(count)]
    for item in locals_:
        item.start()
    for item in locals_:
        item.wait()
    for level in reversed(range(m)):
        for i in range(groups >> (level + 1)):
            for a in range(count):
                copy(a, level, i, True).start()
        for i in range(groups >> (level + 1)):
            for a in range(count):
                copy(a, level, i, False).wait_recv()
    for level in range(m):
        for i in range(groups >> (level + 1)):
            for a in range(count):
                copy(a, level, i, True).wait_send()


def gather_rows(values, groups, cid):
    vmem = pl.BlockSpec(memory_space=pltpu.VMEM)
    m, count = dp_bits(groups), len(values)
    dma = pltpu.SemaphoreType.DMA
    return pl.pallas_call(
        functools.partial(gather_kernel, groups, count),
        out_shape=[jax.ShapeDtypeStruct((groups * v.shape[0], v.shape[1]), v.dtype) for v in values],
        in_specs=[vmem] * count,
        out_specs=[vmem] * count,
        scratch_shapes=[dma((count, m, groups // 2)), dma((count, m, groups // 2)), dma((count,))],
        compiler_params=pltpu.CompilerParams(
            collective_id=cid, has_side_effects=True, vmem_limit_bytes=48 * 2**20
        ),
        name="gather_%d" % cid,
    )(*values)


class OwnScatter(Scatter):
    def __init__(self, groups, rows, chunks, refs):
        m = dp_bits(groups)
        super().__init__(groups, rows, chunks, list(refs[: 2 + m]) + [None] * (m - 1) + list(refs[2 + m :]))
        self.me = lax.axis_index("dp")

    @staticmethod
    def scratch(groups, rows, width, chunks, dtype):
        m = dp_bits(groups)
        kinds = Scatter.scratch(groups, rows, width, chunks, dtype)
        return kinds[:m] + kinds[2 * m - 1 :]

    @staticmethod
    def refs(groups):
        return 3 * dp_bits(groups)

    def whole(self, level, slot, c):
        return self.at(slot * (1 << level) + lax.rem(self.me, 1 << level), c)

    def copy(self, level, slot, c):
        where, bit = self.links[level]
        return remote(
            self.value.at[self.whole(level, 2 * slot + 1 - bit, c)],
            self.arrive[level].at[self.at(slot, c)],
            self.s_sem[level].at[slot, c],
            self.r_sem[level].at[slot, c],
            where,
        )

    def step(self, i, lag):
        for level in range(self.levels):
            c = i - level * lag

            @pl.when(jnp.logical_and(c >= 0, c < self.chunks))
            def _():
                bit = self.links[level][1]
                for slot, goes in self.order(level):
                    self.copy(level, slot, c).wait_recv()
                    here, there = self.whole(level, 2 * slot + bit, c), self.at(slot, c)
                    if level == self.levels - 1:
                        total = self.value[here].astype(F32) + self.arrive[level][there].astype(F32)
                        self.out[self.at(0, c)] = total.astype(self.out.dtype)
                    else:
                        self.value[here] = self.value[here] + self.arrive[level][there]
                        if goes:
                            self.copy(level + 1, slot // 2, c).start()


class Line:
    lag_b, lag_c, lag_o = 2, 4, 5

    def __init__(self, first, half, pieces, part, base, out, scratch, norm=None, moved=None, at=(0, 0, 0), turns=1):
        self.first, self.half, self.size = first, half, half // pieces
        self.each, self.pieces = pieces, pieces * turns
        self.base_at, self.out_at, self.moved_at = at
        self.part, self.base, self.out = part, base, out
        (self.rin, self.smid, self.rmid) = scratch[:3]
        (self.s_up, self.r_up, self.s_mid, self.r_mid, self.s_b1, self.s_b2, self.r_b, self.s_c, self.r_c) = scratch[3:12]
        self.norm, self.moved = norm, moved
        if moved:
            self.arrived, self.shift = moved
            self.s_s, self.r_s = scratch[12:14]
            section = lax.axis_index("section")
            self.sends = section == (0 if self.shift > 0 else 1)
            self.partner = {"section": 1 - section}
        t = lax.axis_index("tensor")
        self.mid = jnp.logical_or(t == 1, t == 2)
        self.outside = jnp.logical_not(self.mid)
        self.outer = {"tensor": jnp.where(t == 1, 0, 3)}
        self.other = {"tensor": jnp.where(t == 1, 2, 1)}
        self.nbr = {"tensor": jnp.where(t == 0, 1, 2)}
        self.near = jnp.where(t < 2, 0, half)
        self.far = half - self.near

    @staticmethod
    def scratch(half, pieces, width, moved, turns=1):
        dma = pltpu.SemaphoreType.DMA
        half, pieces = half * turns, pieces * turns
        kinds = [
            pltpu.VMEM((2 * half, width), BF16),
            pltpu.VMEM((half, width), BF16),
            pltpu.VMEM((half, width), BF16),
            dma((2, pieces)),
            dma((2, pieces)),
        ] + [dma((pieces,))] * 7
        return kinds + ([dma((2, pieces))] * 2 if moved else [])

    @staticmethod
    def greet():
        t = lax.axis_index("tensor")

        @pl.when(t > 0)
        def _():
            greet({"tensor": jnp.maximum(t - 1, 0)})

        @pl.when(t < 3)
        def _():
            greet({"tensor": jnp.minimum(t + 1, 3)})

    def greet_sender(self):
        if self.moved:

            @pl.when(jnp.logical_not(self.sends))
            def _():
                greet(self.partner)

    def enter(self, others):
        bar = pltpu.get_barrier_semaphore()
        count = jnp.where(self.mid, 2, 1) + others
        if self.moved:
            count = count + jnp.where(self.sends, 1, 0)
        pl.semaphore_wait(bar, count)

    def local(self, start, p):
        if self.each < self.pieces:
            start, p = start + (p // self.each) * (2 * self.half), lax.rem(p, self.each)
        return pl.ds(pl.multiple_of(start + p * self.size, self.size), self.size)

    def own(self, p):
        return pl.ds(pl.multiple_of(p * self.size, self.size), self.size)

    def rows(self, start, p, at=0):
        return self.local(self.first + at + start, p)

    def shifted(self, start, p):
        side = start // self.half
        here, there = self.rows(start, p, self.out_at), self.rows(start, p, self.moved_at)
        return remote(self.out.at[here], self.arrived.at[there], self.s_s.at[side, p], self.r_s.at[side, p], self.partner)

    def pass_on(self, start, p):
        if self.moved:

            @pl.when(self.sends)
            def _():
                self.shifted(start, p).start()

    def outcome(self, s_sem, r_sem, where, start, p):
        here = self.rows(start, p, self.out_at)
        return remote(self.out.at[here], self.out.at[here], s_sem.at[p], r_sem.at[p], where)

    def up(self, start, p, k, where):
        return remote(
            self.part.at[self.rows(start, p)], self.rin.at[self.local(start, p)], self.s_up.at[k, p], self.r_up.at[k, p], where
        )

    def cross(self, p):
        return remote(
            self.smid.at[self.own(p)], self.rmid.at[self.own(p)], self.s_mid.at[p], self.r_mid.at[p], self.other
        )

    def start(self, turn=0):
        @pl.when(self.outside)
        def _():
            def begin(p, c):
                self.up(self.far, p, 0, self.nbr).start()
                self.up(self.near, p, 1, self.nbr).start()
                return c

            lax.fori_loop(turn * self.each, (turn + 1) * self.each, begin, 0)

    def outer_step(self, i):
        p = i - self.lag_o

        @pl.when(jnp.logical_and(p >= 0, p < self.pieces))
        def _():
            self.outcome(self.s_b2, self.r_b, self.nbr, self.near, p).wait_recv()
            self.pass_on(self.near, p)
            self.outcome(self.s_c, self.r_c, self.nbr, self.far, p).wait_recv()
            self.pass_on(self.far, p)

    def mid_step(self, i):
        @pl.when(jnp.logical_and(i >= 0, i < self.pieces))
        def _():
            self.up(self.far, i, 0, self.outer).wait_recv()
            total = self.part[self.rows(self.far, i)].astype(F32) + self.rin[self.local(self.far, i)].astype(F32)
            self.smid[self.own(i)] = total.astype(BF16)
            self.cross(i).start()

        j = i - self.lag_b

        @pl.when(jnp.logical_and(j >= 0, j < self.pieces))
        def _():
            self.up(self.near, j, 1, self.outer).wait_recv()
            self.cross(j).wait_recv()
            here = self.rows(self.near, j, self.base_at)
            total = self.part[self.rows(self.near, j)].astype(F32) + self.rin[self.local(self.near, j)].astype(F32)
            total = total + self.rmid[self.own(j)].astype(F32)
            if self.norm:
                xrow, gain, gsum, norm_at = self.norm
                x = xrow[self.rows(self.near, j, norm_at)].astype(F32)
                scale = lax.rsqrt(jnp.mean(x * x, axis=-1, keepdims=True) + epsilon)
                unit = x * scale
                gsum[...] += jnp.sum(total * unit, axis=0, keepdims=True)
                inner = total * gain[...]
                total = scale * (inner - unit * jnp.mean(inner * unit, axis=-1, keepdims=True))
            total = self.base[here].astype(F32) + total
            self.out[self.rows(self.near, j, self.out_at)] = total.astype(BF16)
            self.outcome(self.s_b1, self.r_b, self.other, self.near, j).start()
            self.outcome(self.s_b2, self.r_b, self.outer, self.near, j).start()
            self.pass_on(self.near, j)

        k = i - self.lag_c

        @pl.when(jnp.logical_and(k >= 0, k < self.pieces))
        def _():
            self.outcome(self.s_b1, self.r_b, self.other, self.far, k).wait_recv()
            self.outcome(self.s_c, self.r_c, self.outer, self.far, k).start()
            self.pass_on(self.far, k)

    @property
    def steps(self):
        return self.pieces + self.lag_o

    def step(self, i):
        @pl.when(self.mid)
        def _():
            self.mid_step(i)

        @pl.when(self.outside)
        def _():
            self.outer_step(i)

    def finish(self):
        @pl.when(self.mid)
        def _():
            def one(p, c):
                self.cross(p).wait_send()
                self.outcome(self.s_b1, self.r_b, self.other, self.near, p).wait_send()
                self.outcome(self.s_b2, self.r_b, self.outer, self.near, p).wait_send()
                self.outcome(self.s_c, self.r_c, self.outer, self.far, p).wait_send()
                return c

            lax.fori_loop(0, self.pieces, one, 0)

        @pl.when(self.outside)
        def _():
            def one(p, c):
                self.up(self.far, p, 0, self.nbr).wait_send()
                self.up(self.near, p, 1, self.nbr).wait_send()
                return c

            lax.fori_loop(0, self.pieces, one, 0)

        if self.moved:

            @pl.when(self.sends)
            def _():
                def close(p, c):
                    self.shifted(0, p).wait_send()
                    self.shifted(self.half, p).wait_send()
                    return c

                lax.fori_loop(0, self.pieces, close, 0)

    def receive(self):
        @pl.when(jnp.logical_not(self.sends))
        def _():
            def close(p, c):
                self.shifted(0, p).wait_recv()
                self.shifted(self.half, p).wait_recv()
                return c

            lax.fori_loop(0, self.pieces, close, 0)


def run_steps(begin, end, *planned):
    def body(i, c):
        for step, offset in planned:
            step(i - offset)
        return c

    lax.fori_loop(begin, end, body, 0)


class Gather:
    def __init__(self, groups, rows, out, s_sem, r_sem, first=0, size=None):
        self.first, self.size = first, size or rows
        self.groups, self.rows, self.out, self.s_sem, self.r_sem = groups, rows, out, s_sem, r_sem
        self.levels = dp_bits(groups)
        self.links = [dp_partner(k) for k in range(self.levels)]
        self.me = lax.axis_index("dp")

    @staticmethod
    def scratch(groups):
        return [pltpu.SemaphoreType.DMA((dp_bits(groups), groups // 2))] * 2

    def copy(self, level, i, mine):
        where, bit = self.links[level]
        low = lax.rem(self.me, 1 << (level + 1))
        if not mine:
            low = low + (1 - 2 * bit) * (1 << level)
        block = i * (1 << (level + 1)) + low
        place = self.out.at[pl.ds(pl.multiple_of(block * self.rows + self.first, self.size), self.size)]
        return remote(place, place, self.s_sem.at[level, i], self.r_sem.at[level, i], where)

    def start(self, level):
        for i in range(self.groups >> (level + 1)):
            self.copy(level, i, True).start()

    def arrive(self, level):
        for i in range(self.groups >> (level + 1)):
            self.copy(level, i, False).wait_recv()

    def finish(self):
        for level in range(self.levels):
            for i in range(self.groups >> (level + 1)):
                self.copy(level, i, True).wait_send()


def with_transpose(left, right):
    return lax.dot_general(left, right, (((1,), (1,)), ((), ())), preferred_element_type=F32)


def rows_contract(left, right):
    return lax.dot_general(left, right, (((0,), (0,)), ((), ())), preferred_element_type=F32)


def times(left, right):
    return jnp.dot(left, right, preferred_element_type=F32)


LANES = 128
TILE = 256
WIDE = 512


def lanes(i, size=LANES):
    return pl.ds(pl.multiple_of(i * size, size), size)


def normalize(rows, gain):
    rows = rows.astype(F32)
    scale = lax.rsqrt(jnp.mean(rows * rows, axis=-1, keepdims=True) + epsilon)
    return (rows * scale * gain).astype(BF16)


def normalize_into(target, source, gain, first, count, block=32, source_at=0):
    def one(i, c):
        here = pl.ds(pl.multiple_of(first + i * block, block), block)
        there = pl.ds(pl.multiple_of(source_at + first + i * block, block), block)
        target[here] = normalize(source[there], gain[...])
        return c

    lax.fori_loop(0, count // block, one, 0)


def rolled(value, cosine, sine):
    return value * cosine + pltpu.roll(value, LANES // 2, 1) * sine


def block_rows(keys):
    for rows in (160, 80, 32):
        if rows * keys <= 160 * 1280:
            return rows
    return 16


def score_rows(q, kv, h, g, here, qcode, qstart, kcode):
    scores = with_transpose(q[here, lanes(h)], kv[:, lanes(g)]) * HD ** (-0.5)
    code = kcode[...]
    return scores, jnp.logical_and(code <= qcode[here][:, :1], code >= qstart[here][:, :1])


def load_all(pairs, sems):
    copies = [pltpu.make_async_copy(src, dst, sems.at[i]) for i, (src, dst) in enumerate(pairs)]
    for item in copies:
        item.start()
    return copies


def forward_kernel(groups, q_heads, k_heads, pieces, *refs):
    refs = list(refs)

    def take(count):
        taken = refs[:count]
        del refs[:count]
        return taken

    x, cosine, sine, qcode, qstart, kcode, gain_one, gain_two = take(8)
    far_weights = take(5)
    q, kv, lse, mixed, resid, gate, up, act, y, arrived = take(10)
    near_weights = take(5)
    wqkv, wout, wgate, wup, wdown = near_weights
    part_one, part_two, n1, n2, w_sem = take(5)
    gather = Gather(groups, x.shape[0], kv, *take(2))
    count, width = x.shape
    quarter = count // 4
    lines = []
    for k in range(4):
        first = (k % 2) * 2 * quarter
        source = (part_one, x, resid) if k < 2 else (part_two, resid, y)
        lines.append(
            Line(first, quarter, pieces, *source, take(12 if k < 2 else 14), moved=None if k < 2 else (arrived, 1))
        )
    one_a, one_b, two_a, two_b = lines

    loads = load_all(list(zip(far_weights, near_weights)), w_sem)
    Line.greet()
    two_a.greet_sender()
    for where, _ in gather.links:
        greet(where)
    normalize_into(n1, x, gain_one, 0, count)
    loads[0].wait()

    mine = pl.ds(pl.multiple_of(lax.axis_index("dp") * count, count), count)
    for g in range(k_heads):
        column = (q_heads + g) * LANES
        value = times(n1[...], wqkv[:, column : column + LANES])
        kv[mine, g * LANES : (g + 1) * LANES] = rolled(value, cosine[...], sine[...]).astype(BF16)
        column += k_heads * LANES
        kv[mine, (k_heads + g) * LANES : (k_heads + g + 1) * LANES] = times(
            n1[...], wqkv[:, column : column + LANES]
        ).astype(BF16)

    two_a.enter(gather.levels)

    top = gather.levels - 1
    gather.start(top)

    def queries(h, c):
        value = times(n1[...], wqkv[:, lanes(h)])
        q[:, lanes(h)] = rolled(value, cosine[...], sine[...]).astype(BF16)
        return c

    lax.fori_loop(0, q_heads, queries, 0)
    for level in range(top, -1, -1):
        gather.arrive(level)
        if level:
            gather.start(level - 1)

    rows = block_rows(kv.shape[0])
    blocks = count // rows

    def attend(i, c):
        h, b = i // blocks, lax.rem(i, blocks)
        g = h // (q_heads // k_heads)
        here = pl.ds(pl.multiple_of(b * rows, rows), rows)
        scores, allowed = score_rows(q, kv, h, g, here, qcode, qstart, kcode)
        scores = jnp.where(allowed, scores, negative)
        row_max = jnp.max(scores, axis=-1, keepdims=True)
        expo = jnp.exp(scores - row_max)
        row_total = jnp.sum(expo, axis=-1, keepdims=True)
        prob = (expo * (1.0 / row_total)).astype(BF16)
        mixed[here, lanes(h)] = times(prob, kv[:, lanes(k_heads + g)]).astype(BF16)
        there = pl.ds(pl.multiple_of(h * count + b * rows, rows), rows)
        lse[there] = jnp.broadcast_to(row_max + jnp.log(row_total), (rows, LANES))
        return c

    lax.fori_loop(0, q_heads * blocks, attend, 0)
    loads[1].wait()

    def projected(target, left, right, first, each=None):
        here = pl.ds(first, 2 * quarter)

        def one(i, c):
            target[here, lanes(i, TILE)] = times(left[here], right[:, lanes(i, TILE)]).astype(BF16)
            if each:
                each(i)
            return c

        lax.fori_loop(0, width // TILE, one, 0)

    projected(part_one, mixed, wout, 0)
    one_a.start()
    projected(part_one, mixed, wout, 2 * quarter)
    one_b.start()
    run_steps(0, one_a.steps, (one_a.step, 0), (one_b.step, pieces))
    loads[2].wait()
    loads[3].wait()
    loads[4].wait()

    def hidden(first, each):
        here = pl.ds(first, 2 * quarter)
        normalize_into(n2, resid, gain_two, first, 2 * quarter)

        def one(i, c):
            columns = lanes(i, TILE)
            gate_pre = times(n2[here], wgate[:, columns])
            up_pre = times(n2[here], wup[:, columns])
            gate[here, columns] = gate_pre.astype(BF16)
            up[here, columns] = up_pre.astype(BF16)
            act[here, columns] = (gate_pre * jax.nn.sigmoid(gate_pre) * up_pre).astype(BF16)
            each(i)
            return c

        lax.fori_loop(0, gate.shape[1] // TILE, one, 0)

    tiles = gate.shape[1] // TILE
    done = one_a.steps - pieces
    hidden(0, lambda i: one_b.step(done + i))
    projected(part_two, act, wdown, 0)
    two_a.start()
    run_steps(done + tiles, one_b.steps, (one_b.step, 0))
    hidden(2 * quarter, lambda i: two_a.step(i))
    projected(part_two, act, wdown, 2 * quarter)
    two_b.start()
    run_steps(tiles, two_b.steps + tiles, (two_a.step, 0), (two_b.step, tiles))
    gather.finish()
    for line in lines:
        line.finish()
    two_a.receive()
    two_b.receive()


VMEM_LIMIT = 60 * 2**20


def forward_tick(x, spots, weights, groups, q_heads, k_heads, cid):
    norm_one, wqkv, wout, norm_two, wgate, wup, wdown = weights
    count, width = x.shape
    hidden = wgate.shape[1]
    pieces = 5
    vmem = pl.BlockSpec(memory_space=pltpu.VMEM)
    far = pl.BlockSpec(memory_space=pl.ANY)

    def shape(*dims, dtype=BF16):
        return jax.ShapeDtypeStruct(dims, dtype)

    outs = [
        shape(count, q_heads * LANES),
        shape(groups * count, 2 * k_heads * LANES),
        shape(q_heads * count, LANES, dtype=F32),
        shape(count, q_heads * LANES),
        shape(count, width),
        shape(count, hidden),
        shape(count, hidden),
        shape(count, hidden),
        shape(count, width),
        shape(count, width),
    ]
    far_weights = [wqkv, wout, wgate, wup, wdown]
    scratch = [pltpu.VMEM(item.shape, BF16) for item in far_weights]
    scratch += [pltpu.VMEM((count, width), BF16)] * 4 + [pltpu.SemaphoreType.DMA((5,))]
    scratch += Gather.scratch(groups)
    for k in range(4):
        scratch += Line.scratch(count // 4, pieces, width, k >= 2)
    q, kv, lse, mixed, resid, gate, up, act, y, arrived = pl.pallas_call(
        functools.partial(forward_kernel, groups, q_heads, k_heads, pieces),
        out_shape=outs,
        in_specs=[vmem] * 8 + [far] * 5,
        out_specs=[vmem] * len(outs),
        scratch_shapes=scratch,
        compiler_params=pltpu.CompilerParams(
            collective_id=cid, has_side_effects=True, vmem_limit_bytes=VMEM_LIMIT
        ),
        name="forward_tick",
    )(x, *spots, norm_one[None], norm_two[None], *far_weights)
    return y, arrived, (x, q, kv, lse, mixed, resid, gate, up, act)


def back_ffn_kernel(pieces, *refs):
    dy, gate, up, resid, gain = refs[:5]
    far_weights = refs[5:8]
    dresid, gsum, dgate, dup = refs[8:12]
    wdown, wgate, wup = near_weights = refs[12:15]
    part, w_sem = refs[15:17]
    count, width = dy.shape
    quarter = count // 4
    a, b = [
        Line(k * 2 * quarter, quarter, pieces, part, dy, dresid, refs[17 + 12 * k : 29 + 12 * k], norm=(resid, gain, gsum, 0))
        for k in range(2)
    ]
    loads = load_all(list(zip(far_weights, near_weights)), w_sem)
    Line.greet()
    gsum[...] = jnp.zeros_like(gsum)

    def hidden(first, each=None):
        here = pl.ds(first, 2 * quarter)

        def one(i, c):
            columns = lanes(i, TILE)
            d_act = with_transpose(dy[here], wdown[columns, :])
            gate_pre, up_pre = gate[here, columns].astype(F32), up[here, columns].astype(F32)
            sigma = jax.nn.sigmoid(gate_pre)
            d_silu = d_act * sigma
            dup[here, columns] = (d_silu * gate_pre).astype(BF16)
            dgate[here, columns] = (d_silu * up_pre * (1.0 + gate_pre * (1.0 - sigma))).astype(BF16)
            if each:
                each(i)
            return c

        lax.fori_loop(0, gate.shape[1] // TILE, one, 0)

    def back(first):
        here = pl.ds(first, 2 * quarter)

        def one(i, c):
            columns = lanes(i, TILE)
            total = with_transpose(dgate[here], wgate[columns, :]) + with_transpose(dup[here], wup[columns, :])
            part[here, columns] = total.astype(BF16)
            return c

        lax.fori_loop(0, width // TILE, one, 0)

    loads[0].wait()
    hidden(0)
    loads[1].wait()
    loads[2].wait()
    back(0)
    a.enter(0)
    a.start()
    tiles = gate.shape[1] // TILE
    hidden(2 * quarter, lambda i: a.step(i))
    back(2 * quarter)
    b.start()
    run_steps(tiles, b.steps + tiles, (a.step, 0), (b.step, tiles))
    a.finish()
    b.finish()


def back_ffn(dy, kept, weights, cid):
    norm_one, wqkv, wout, norm_two, wgate, wup, wdown = weights
    x, q, kv, lse, mixed, resid, gate, up, act = kept
    count, width = dy.shape
    pieces = 5
    vmem = pl.BlockSpec(memory_space=pltpu.VMEM)
    far = pl.BlockSpec(memory_space=pl.ANY)
    far_weights = [wdown, wgate, wup]
    scratch = [pltpu.VMEM(item.shape, BF16) for item in far_weights]
    scratch += [pltpu.VMEM((count, width), BF16), pltpu.SemaphoreType.DMA((3,))]
    scratch += Line.scratch(count // 4, pieces, width, False) * 2
    return pl.pallas_call(
        functools.partial(back_ffn_kernel, pieces),
        out_shape=[
            jax.ShapeDtypeStruct((count, width), BF16),
            jax.ShapeDtypeStruct((1, width), F32),
            jax.ShapeDtypeStruct(gate.shape, BF16),
            jax.ShapeDtypeStruct(gate.shape, BF16),
        ],
        in_specs=[vmem] * 5 + [far] * 3,
        out_specs=[vmem] * 4,
        scratch_shapes=scratch,
        compiler_params=pltpu.CompilerParams(
            collective_id=cid, has_side_effects=True, vmem_limit_bytes=VMEM_LIMIT
        ),
        name="back_ffn",
    )(dy, gate, up, resid, norm_two[None], *far_weights)


def back_attn_kernel(groups, q_heads, k_heads, pieces, shift, plans, *refs):
    refs = list(refs)

    def take(count):
        taken = refs[:count]
        del refs[:count]
        return taken

    dresid, x, q, kv, lse, cosine, sine, qcode, qstart, kcode, gain = take(11)
    far_weights = take(2)
    values = take(len(plans))
    dx, gsum, dqkv = take(3)
    (arrived,) = take(1) if shift else (None,)
    totals = take(len(plans))
    wout, wqkv = near_weights = take(2)
    part, dmixed, dkv, w_sem = take(4)
    levels = dp_bits(groups)
    count, width = x.shape
    quarter = count // 4
    keys = kv.shape[0]
    shares, owns, scatters = [], [], []
    for g in range(k_heads):
        share, own = take(2)
        shares.append(share)
        owns.append(own)
        scatters.append(Scatter(groups, count, 5, [share, own] + take(4 * levels - 1)))
    tasks = [
        Scatter(groups, rows, chunks, [value, total] + take(4 * levels - 1))
        for (rows, chunks), value, total in zip(plans, values, totals)
    ]
    moved = (arrived, shift) if shift else None
    a, b = [
        Line(
            k * 2 * quarter,
            quarter,
            pieces,
            part,
            dresid,
            dx,
            take(14 if shift else 12),
            norm=(x, gain, gsum, 0),
            moved=moved,
        )
        for k in range(2)
    ]
    loads = load_all(list(zip(far_weights, near_weights)), w_sem)
    Line.greet()
    for where, _ in scatters[0].links:
        greet(where)
    a.greet_sender()
    gsum[...] = jnp.zeros_like(gsum)
    dkv[...] = jnp.zeros_like(dkv)
    a.enter(levels)
    for task in tasks:
        task.start()
    loads[0].wait()

    def mix(h, c):
        dmixed[:, lanes(h)] = with_transpose(dresid[...], wout[lanes(h), :]).astype(BF16)
        return c

    lax.fori_loop(0, q_heads, mix, 0)
    rows = block_rows(keys)
    blocks = count // rows
    repeat = q_heads // k_heads
    lag = 4
    scale = HD ** (-0.5)

    for g in range(k_heads):

        def one(i, c):
            h, n = g * repeat + i // blocks, lax.rem(i, blocks)
            here = pl.ds(pl.multiple_of(n * rows, rows), rows)
            there = pl.ds(pl.multiple_of(h * count + n * rows, rows), rows)
            scores, allowed = score_rows(q, kv, h, g, here, qcode, qstart, kcode)
            prob = jnp.where(allowed, jnp.exp(scores - lse[there][:, :1]), 0.0)
            dm = dmixed[here, lanes(h)]
            d_prob = with_transpose(dm, kv[:, lanes(k_heads + g)])
            row_dot = jnp.sum(prob * d_prob, axis=-1, keepdims=True)
            d_scores = (prob * (d_prob - row_dot)).astype(BF16)
            d_query = times(d_scores, kv[:, lanes(g)]) * scale
            dqkv[here, lanes(h)] = rolled(d_query, cosine[here], -sine[here]).astype(BF16)
            dkv[:, lanes(g)] += rows_contract(d_scores, q[here, lanes(h)]) * scale
            dkv[:, lanes(k_heads + g)] += rows_contract(prob.astype(BF16), dm)
            for task in tasks:
                task.step(g * repeat * blocks + i, lag)
            return c

        lax.fori_loop(0, repeat * blocks, one, 0)

        def narrow(i, c):
            here = pl.ds(pl.multiple_of(i * LANES, LANES), LANES)
            shares[g][here, :LANES] = dkv[here, lanes(g)].astype(BF16)
            shares[g][here, LANES:] = dkv[here, lanes(k_heads + g)].astype(BF16)
            return c

        lax.fori_loop(0, keys // LANES, narrow, 0)
        scatters[g].start()
    run_steps(0, scatters[0].steps(1), *[(functools.partial(lambda s, i: s.step(i, 1), s), 0) for s in scatters])
    for g in range(k_heads):
        dqkv[:, lanes(q_heads + g)] = rolled(owns[g][:, :LANES], cosine[...], -sine[...]).astype(BF16)
        dqkv[:, lanes(q_heads + k_heads + g)] = owns[g][:, LANES:].astype(BF16)
    loads[1].wait()

    def back(first, each=None):
        here = pl.ds(first, 2 * quarter)

        def one(i, c):
            columns = lanes(i, TILE)
            part[here, columns] = with_transpose(dqkv[here], wqkv[columns, :]).astype(BF16)
            if each:
                each(i)
            return c

        lax.fori_loop(0, width // TILE, one, 0)

    back(0)
    a.start()
    back(2 * quarter)
    b.start()
    begun = q_heads * blocks
    more = [(functools.partial(lambda s, i: s.step(i + begun, lag), s), 0) for s in tasks]
    last = max([b.steps + pieces] + [s.steps(lag) - begun for s in tasks])
    run_steps(0, last, (a.step, 0), (b.step, pieces), *more)
    a.finish()
    b.finish()
    if shift:
        a.receive()
        b.receive()
    for item in scatters + tasks:
        item.finish()


def back_attn(dresid, kept, spots, weights, groups, q_heads, k_heads, cid, shift, sums=()):
    norm_one, wqkv, wout, norm_two, wgate, wup, wdown = weights
    x, q, kv, lse, mixed, resid, gate, up, act = kept
    count, width = x.shape
    keys = kv.shape[0]
    pieces = 5
    vmem = pl.BlockSpec(memory_space=pltpu.VMEM)
    far = pl.BlockSpec(memory_space=pl.ANY)
    outs = [
        jax.ShapeDtypeStruct((count, width), BF16),
        jax.ShapeDtypeStruct((1, width), F32),
        jax.ShapeDtypeStruct((count, wqkv.shape[1]), BF16),
    ]
    if shift:
        outs.append(jax.ShapeDtypeStruct((count, width), BF16))
    scratch = [
        pltpu.VMEM(wout.shape, BF16),
        pltpu.VMEM(wqkv.shape, BF16),
        pltpu.VMEM((count, width), BF16),
        pltpu.VMEM(q.shape, BF16),
        pltpu.VMEM(kv.shape, F32),
        pltpu.SemaphoreType.DMA((2,)),
    ]
    for _ in range(k_heads):
        scratch += [pltpu.VMEM((keys, 2 * LANES), BF16), pltpu.VMEM((count, 2 * LANES), F32)]
        scratch += Scatter.scratch(groups, count, 2 * LANES, 5, BF16)
    plans = []
    for value in sums:
        rows = value.shape[0] // groups
        parts = max(1, min(8, rows // 16))
        while rows % (parts * 16):
            parts -= 1
        plans.append((rows, parts))
        outs.append(jax.ShapeDtypeStruct((rows, value.shape[1]), F32))
        scratch += Scatter.scratch(groups, rows, value.shape[1], parts, BF16)
    scratch += Line.scratch(count // 4, pieces, width, bool(shift)) * 2
    return pl.pallas_call(
        functools.partial(back_attn_kernel, groups, q_heads, k_heads, pieces, shift, plans),
        out_shape=outs,
        in_specs=[vmem] * 11 + [far] * 2 + [vmem] * len(sums),
        out_specs=[vmem] * len(outs),
        scratch_shapes=scratch,
        compiler_params=pltpu.CompilerParams(
            collective_id=cid, has_side_effects=True, vmem_limit_bytes=VMEM_LIMIT
        ),
        name="back_attn_%d" % cid,
    )(dresid, x, q, kv, lse, *spots, norm_one[None], wout, wqkv, *sums)


def announce(sems, neighbours):
    for here, where, k in neighbours:

        @pl.when(here)
        def _():
            pl.semaphore_signal(sems.at[k], inc=1, device_id=where, device_id_type=MESH)


def heard(sems, neighbours):
    for k, (here, _, _) in enumerate(neighbours):

        @pl.when(here)
        def _():
            pl.semaphore_wait(sems.at[k], 1)


def main_kernel(groups, q_heads, k_heads, pieces, *refs):
    refs = list(refs)

    def take(count):
        taken = refs[:count]
        del refs[:count]
        return taken

    cosine, sine, qcode, qstart, kcode, gain_one, gain_two, holder, chosen = take(9)
    own_rows, extra_first, extra_second = take(3)
    far_weights = take(7)
    y_out, dx_out, back_out, normed_one, normed_two = take(5)
    far_state = take(14)
    gsum_one, gsum_two = take(2)
    near_state = xs, q, kv, lse, mixed, resid, gate, up, act, dys, dresid, dgate, dup, dqkv = take(14)
    state_sem = take(1)[0]
    wqkv, wout, wgate, wup, wdown = near_weights = take(5)
    part_one, part_two, normed, y, dmixed, dkv, w_sem, io_sem, meet_sem = take(9)
    levels = dp_bits(groups)
    gather_sems = [take(2) for _ in range(2)]
    line_scratch = [take(12) for _ in range(4)]
    forth_s, forth_r, back_s, back_r = take(4)
    spares, returned = take(2)
    spare = returned.shape[0]
    give_lag = Line.lag_o + pieces
    give = OwnScatter(groups, spare, spare // 32, [spares, returned] + take(OwnScatter.refs(groups)))
    second = Gather(groups, spare, spares, *take(2))
    count, width = part_one.shape
    keys = groups * count
    quarter = count // 4
    half = 2 * quarter
    shares, owns, scatters = [], [], []
    for g in range(k_heads):
        share, own = take(2)
        shares.append(share)
        owns.append(own)
        scatters.append(Scatter(groups, count, 5, [share, own] + take(4 * levels - 1)))
    section = lax.axis_index("section")
    t = lax.axis_index("tensor")
    tiles, wide = gate.shape[1] // WIDE, width // WIDE
    repeat = q_heads // k_heads
    rows = block_rows(keys)
    blocks = half // rows
    scale = HD ** (-0.5)

    def span(first, size):
        return pl.ds(pl.multiple_of(first, 32), size)

    neighbours = [
        (t > 0, {"tensor": jnp.maximum(t - 1, 0)}, 1),
        (t < 3, {"tensor": jnp.minimum(t + 1, 3)}, 0),
    ]
    for k in range(levels):
        neighbours.append((t >= 0, dp_partner(k)[0], 2 + k))

    for _, where, _ in neighbours[2:]:
        greet(where)
    Line.greet()
    greet({"section": 1 - section})

    ends = [0]
    for item in far_weights[:3]:
        ends.append(ends[-1] + item.shape[1])
    parts = [wqkv.at[:, a:b] for a, b in zip(ends, ends[1:])]
    copies = load_all(list(zip(far_weights, parts + list(near_weights[1:]))), w_sem)
    loads = [copies[:3], *[[item] for item in copies[3:]]]

    place = span(lax.axis_index("dp") * spare, spare)
    fetch_first = pltpu.make_async_copy(extra_first, spares, io_sem.at[2])
    fetch_extra = pltpu.make_async_copy(extra_second, spares.at[place], io_sem.at[2])
    fetch_first.start()
    for which, target in enumerate((xs, dys)):

        @pl.when(section == which)
        def _():
            pltpu.make_async_copy(own_rows, target, io_sem.at[0]).start()

    pl.semaphore_wait(pltpu.get_barrier_semaphore(), jnp.where(jnp.logical_or(t == 1, t == 2), 2, 1) + levels + 1)
    announce(meet_sem, neighbours)
    gsum_one[...] = jnp.zeros_like(gsum_one)
    gsum_two[...] = jnp.zeros_like(gsum_two)
    fetch_first.wait()
    brought_first = times(chosen[:count], spares[...])
    for which, target in enumerate((xs, dys)):

        @pl.when(section == which)
        def _():
            pltpu.make_async_copy(own_rows, target, io_sem.at[0]).wait()
            target[:count] = (target[:count].astype(F32) + brought_first).astype(BF16)

    fetch_extra.start()
    fetch_extra.wait()

    def keep(index, slot):
        near, there = near_state[index], far_state[index]
        part = near.shape[0] // 2
        here = span(slot * part, part)
        return pltpu.make_async_copy(near.at[here], there.at[here], state_sem.at[index, slot])

    def projected(target, left, right, first, left_at, each=None):
        here, there = span(first, half), span(first + left_at, half)

        def one(i, c):
            target[here, lanes(i, WIDE)] = times(left[there], right[:, lanes(i, WIDE)]).astype(BF16)
            if each:
                each(i)
            return c

        lax.fori_loop(0, wide, one, 0)

    def give_back(slot, now, line):
        @pl.when(now)
        def _():
            spares[...] = times(holder[span(slot * groups * spare, groups * spare)], y[...]).astype(BF16)
            give.start()

        def one(i, c):
            line.step(i)

            @pl.when(now)
            def _():
                give.step(i, give_lag)

            return c

        lax.fori_loop(0, line.steps, one, 0)

    def give_rest(now, line, begun):
        def one(i, c):
            line.step(i)

            @pl.when(now)
            def _():
                give.step(i - begun + give_lag, give_lag)

            return c

        lax.fori_loop(begun, max(line.steps, begun + give.steps(give_lag) - give_lag), one, 0)

    def given(place, now):
        @pl.when(now)
        def _():
            give.finish()
            pltpu.make_async_copy(returned, back_out.at[span(place * spare, spare)], io_sem.at[1]).start()
            pltpu.make_async_copy(returned, back_out.at[span(place * spare, spare)], io_sem.at[1]).wait()

    def ffn_back(slot, first, each=None):
        here, there = span(first, half), span(slot * count + first, half)

        def one(i, c):
            columns = lanes(i, WIDE)
            d_act = with_transpose(dys[there], wdown[columns, :])
            gate_pre, up_pre = gate[there, columns].astype(F32), up[there, columns].astype(F32)
            sigma = jax.nn.sigmoid(gate_pre)
            d_silu = d_act * sigma
            dup[there, columns] = (d_silu * gate_pre).astype(BF16)
            dgate[there, columns] = (d_silu * up_pre * (1.0 + gate_pre * (1.0 - sigma))).astype(BF16)
            if each:
                each(i)
            return c

        lax.fori_loop(0, tiles, one, 0)

        def two(i, c):
            columns = lanes(i, WIDE)
            total = with_transpose(dgate[there], wgate[columns, :]) + with_transpose(dup[there], wup[columns, :])
            part_one[here, columns] = total.astype(BF16)
            if each:
                each(tiles + i)
            return c

        lax.fori_loop(0, wide, two, 0)

    def back_lines(slot):
        base = slot * count
        made = []
        for k in range(4):
            first = (k % 2) * half
            scratch = list(line_scratch[k])
            if k < 2:
                norm = (resid, gain_two, gsum_two, base)
                made.append(Line(first, quarter, pieces, part_one, dys, dresid, scratch, norm=norm, at=(base, base, 0)))
            else:
                scratch += [back_s.at[k - 2], back_r.at[2 * slot + k - 2]]
                norm = (xs, gain_one, gsum_one, base)
                made.append(
                    Line(
                        first, quarter, pieces, part_two, dresid, y, scratch, norm=norm, moved=(dys, -1), at=(base, 0, base)
                    )
                )
        return made

    def forward_lines(slot):
        base = slot * count
        made = []
        for k in range(4):
            first = (k % 2) * half
            scratch = list(line_scratch[k])
            if k < 2:
                made.append(Line(first, quarter, pieces, part_one, xs, resid, scratch, at=(base, base, 0)))
            else:
                scratch += [forth_s.at[k - 2], forth_r.at[2 * slot + k - 2]]
                made.append(
                    Line(first, quarter, pieces, part_two, resid, y, scratch, moved=(xs, 1), at=(base, 0, base))
                )
        return made

    def gathers_of(slot):
        place = kv.at[span(slot * keys, keys)]
        return [Gather(groups, count, place, *gather_sems[h], h * half, half) for h in range(2)]

    def keep_normed(slot):
        return pltpu.make_async_copy(normed, normed_one.at[span(slot * count, count)], io_sem.at[1])

    def begin(slot, sync):
        base = slot * count
        middle = (q_heads + k_heads) * LANES
        for h, (line, gather) in enumerate(zip(forward_lines(slot)[2:], gathers_of(slot))):
            line.receive()
            normalize_into(normed, xs, gain_one, h * half, half, source_at=base)
            if h == 0:

                @pl.when(slot == 0)
                def _():
                    for item in loads[0]:
                        item.wait()

            here, there = span(h * half, half), span(base + h * half, half)
            mine = span(slot * keys + lax.axis_index("dp") * count + h * half, half)
            value = times(normed[here], wqkv[:, q_heads * LANES : middle])
            for g in range(k_heads):
                columns = slice(g * LANES, (g + 1) * LANES)
                kv[mine, columns] = rolled(value[:, columns], cosine[there], sine[there]).astype(BF16)
            kv[mine, k_heads * LANES :] = times(normed[here], wqkv[:, middle:]).astype(BF16)
            if h == 0 and sync:
                heard(meet_sem, neighbours)
            gather.start(levels - 1)
        keep_normed(slot).start()
        whole = span(base, count)
        for first in range(0, q_heads, 2):
            value = times(normed[...], wqkv[:, first * LANES : (first + 2) * LANES])
            for h in range(2):
                columns = slice((first + h) * LANES, (first + h + 1) * LANES)
                q[whole, columns] = rolled(
                    value[:, h * LANES : (h + 1) * LANES], cosine[whole], sine[whole]
                ).astype(BF16)

    def forward(slot):
        base = slot * count
        whole = span(base, count)
        pending = jnp.logical_and(section == 1, slot == 1)
        left_a, left_b = back_lines(0)[2:]
        one_a, one_b, two_a, two_b = forward_lines(slot)
        gathers = gathers_of(slot)
        keep_one = keep_normed(slot)
        keep_two = pltpu.make_async_copy(normed, normed_two.at[whole], io_sem.at[2])

        @pl.when(jnp.logical_not(pending))
        def _():
            begin(slot, True)

        for level in range(levels - 1, 0, -1):
            for gather in gathers:
                gather.arrive(level)
                gather.start(level - 1)

        @pl.when(pending)
        def _():
            run_steps(0, left_a.steps, (left_a.step, 0))

        for gather in gathers:
            gather.arrive(0)

        @pl.when(slot == 0)
        def _():
            second.start(levels - 1)

        def attend(first, each=None):
            def one(i, c):
                h, b = i // blocks, lax.rem(i, blocks)
                g = h // repeat
                here = span(base + first + b * rows, rows)
                scores = with_transpose(q[here, lanes(h)], kv[span(slot * keys, keys), lanes(g)]) * scale
                code = kcode[slot]
                allowed = jnp.logical_and(code <= qcode[here][:, :1], code >= qstart[here][:, :1])
                scores = jnp.where(allowed, scores, negative)
                row_max = jnp.max(scores, axis=-1, keepdims=True)
                expo = jnp.exp(scores - row_max)
                row_total = jnp.sum(expo, axis=-1, keepdims=True)
                prob = (expo * (1.0 / row_total)).astype(BF16)
                mixed[here, lanes(h)] = times(prob, kv[span(slot * keys, keys), lanes(k_heads + g)]).astype(BF16)
                lse[span((slot * q_heads + h) * count + first + b * rows, rows)] = jnp.broadcast_to(
                    row_max + jnp.log(row_total), (rows, LANES)
                )
                if each:
                    each(i)
                return c

            lax.fori_loop(0, q_heads * blocks, one, 0)

        attend(0)

        @pl.when(slot == 0)
        def _():
            loads[1][0].wait()

        projected(part_one, mixed, wout, 0, base)

        @pl.when(pending)
        def _():
            heard(meet_sem, neighbours)

        one_a.start()

        @pl.when(pending)
        def _():
            run_steps(0, left_b.steps, (left_b.step, 0))
            left_out = pltpu.make_async_copy(y, dx_out.at[:count], io_sem.at[0])
            left_out.start()
            left_a.finish()
            left_b.finish()
            left_out.wait()

        attend(half)
        projected(part_one, mixed, wout, half, base)
        one_b.start()
        run_steps(0, one_a.steps, (one_a.step, 0))

        @pl.when(slot == 0)
        def _():
            for (item,) in loads[2:]:
                item.wait()
            for level in range(levels - 1, 0, -1):
                second.arrive(level)
                second.start(level - 1)

        def hidden(first, each):
            here, there = span(first, half), span(base + first, half)
            normalize_into(normed, resid, gain_two, first, half, source_at=base)

            def one(i, c):
                columns = lanes(i, WIDE)
                gate_pre = times(normed[here], wgate[:, columns])
                up_pre = times(normed[here], wup[:, columns])
                gate[there, columns] = gate_pre.astype(BF16)
                up[there, columns] = up_pre.astype(BF16)
                act[there, columns] = (gate_pre * jax.nn.sigmoid(gate_pre) * up_pre).astype(BF16)
                each(i)
                return c

            lax.fori_loop(0, tiles, one, 0)

        keep_one.wait()
        hidden(0, one_b.step)

        @pl.when(section == 0)
        def _():
            projected(part_two, act, wdown, 0, base)
            two_a.start()

        @pl.when(slot == 0)
        def _():
            second.arrive(0)
            brought = times(chosen[count:], spares[...])
            for which, target in enumerate((xs, dys)):

                @pl.when(section == which)
                def _():
                    target[count:] = (target[count:].astype(F32) + brought).astype(BF16)

        @pl.when(section == 1)
        def _():
            one_a.finish()
            ffn_back(slot, 0, lambda i: one_b.step(tiles + i))
            run_steps(2 * tiles + wide, one_b.steps, (one_b.step, 0))

        @pl.when(section == 0)
        def _():
            run_steps(tiles, one_b.steps, (one_b.step, 0))

        @pl.when(section == 1)
        def _():
            one_b.finish()
            for gather in gathers:
                gather.finish()
            announce(meet_sem, neighbours)

        def early(i):
            @pl.when(section == 0)
            def _():
                two_a.step(i)

        hidden(half, early)
        keep_two.start()
        out = pltpu.make_async_copy(y, y_out.at[whole], io_sem.at[0])

        @pl.when(section == 0)
        def _():
            projected(part_two, act, wdown, half, base)
            two_b.start()
            run_steps(tiles, two_a.steps, (two_a.step, 0))
            run_steps(0, two_b.steps, (two_b.step, 0))
            out.start()
            two_a.finish()
            two_b.finish()
            for gather in gathers:
                gather.finish()
            one_a.finish()
            one_b.finish()

        keep_two.wait()

        @pl.when(slot == 0)
        def _():
            second.finish()

        for index in range(9):
            keep(index, slot).start()

        @pl.when(section == 0)
        def _():
            out.wait()
            announce(meet_sem, neighbours)

    def backward(slot):
        giving = jnp.logical_and(section == 1, slot == 1)
        later = jnp.logical_and(section == 1, slot == 0)
        base = slot * count
        whole = span(base, count)
        lines = back_lines(slot)
        one_a, one_b, two_a, two_b = lines
        two_a.receive()
        two_b.receive()
        dkv[...] = jnp.zeros_like(dkv)
        heard(meet_sem, neighbours)

        @pl.when(section == 0)
        def _():
            ffn_back(slot, 0)

        one_a.start()
        ffn_back(slot, half)
        one_b.start()
        give_back(0, giving, one_a)

        def attend(first, g, each=None):
            def one(i, c):
                h, n = g * repeat + i // blocks, lax.rem(i, blocks)
                here = span(base + first + n * rows, rows)
                near = span(first + n * rows, rows)
                k_rows = kv[span(slot * keys, keys), lanes(g)]
                scores = with_transpose(q[here, lanes(h)], k_rows) * scale
                code = kcode[slot]
                allowed = jnp.logical_and(code <= qcode[here][:, :1], code >= qstart[here][:, :1])
                known = lse[span((slot * q_heads + h) * count + first + n * rows, rows)][:, :1]
                prob = jnp.where(allowed, jnp.exp(scores - known), 0.0)
                dm = dmixed[near, lanes(h)]
                d_prob = with_transpose(dm, kv[span(slot * keys, keys), lanes(k_heads + g)])
                row_dot = jnp.sum(prob * d_prob, axis=-1, keepdims=True)
                d_scores = (prob * (d_prob - row_dot)).astype(BF16)
                d_query = times(d_scores, k_rows) * scale
                dqkv[here, lanes(h)] = rolled(d_query, cosine[here], -sine[here]).astype(BF16)
                dkv[lanes(g), :] += rows_contract(q[here, lanes(h)], d_scores) * scale
                dkv[lanes(k_heads + g), :] += rows_contract(dm, prob.astype(BF16))
                if each:
                    each(i)
                return c

            lax.fori_loop(0, repeat * blocks, one, 0)

        def mix(first):
            here, there = span(first, half), span(base + first, half)

            def one(h, c):
                dmixed[here, lanes(h)] = with_transpose(dresid[there], wout[lanes(h), :]).astype(BF16)
                return c

            lax.fori_loop(0, q_heads, one, 0)

        mix(0)
        turns = repeat * blocks
        for g in range(k_heads):
            attend(0, g, lambda i: one_b.step(g * turns + i))
        give_rest(giving, one_b, k_heads * turns)
        mix(half)
        for g in range(k_heads):
            attend(half, g)

            shares[g][:, :LANES] = jnp.transpose(dkv[lanes(g), :]).astype(BF16)
            shares[g][:, LANES:] = jnp.transpose(dkv[lanes(k_heads + g), :]).astype(BF16)
            scatters[g].start()
        far = give_lag
        everyone = [(functools.partial(lambda s, i: s.step(i, far), s), 0) for s in scatters]
        run_steps(0, scatters[0].chunks, *everyone)

        @pl.when(later)
        def _():
            begin(1, False)

        run_steps(far, far + scatters[0].chunks, *everyone)
        for g in range(k_heads):
            dqkv[whole, lanes(q_heads + g)] = rolled(owns[g][:, :LANES], cosine[whole], -sine[whole]).astype(BF16)
            dqkv[whole, lanes(q_heads + k_heads + g)] = owns[g][:, LANES:].astype(BF16)

        def back(first, each=None):
            here, there = span(first, half), span(base + first, half)

            def one(i, c):
                columns = lanes(i, WIDE)
                part_two[here, columns] = with_transpose(dqkv[there], wqkv[columns, :]).astype(BF16)
                if each:
                    each(i)
                return c

            lax.fori_loop(0, wide, one, 0)

        back(0)
        two_a.start()
        back(half)
        two_b.start()

        @pl.when(jnp.logical_not(later))
        def _():
            run_steps(0, two_a.steps, (two_a.step, 0))
            run_steps(0, two_b.steps, (two_b.step, 0))
            out = pltpu.make_async_copy(y, dx_out.at[whole], io_sem.at[0])
            out.start()
            two_a.finish()
            two_b.finish()
            out.wait()

        one_a.finish()
        one_b.finish()
        for item in scatters:
            item.finish()
        given(2, giving)
        for index in range(9, 14):
            keep(index, slot).start()
        announce(meet_sem, neighbours)

    def give_alone(slot, place):
        heard(meet_sem, neighbours)
        spares[...] = times(holder[slot * groups * spare : (slot + 1) * groups * spare], y[...]).astype(BF16)
        give.start()
        run_steps(0, give.steps(give_lag), (lambda i: give.step(i, give_lag), 0))
        given(place, section == 0)
        announce(meet_sem, neighbours)

    def turn(k, carry):
        @pl.when(jnp.where(section == 0, k < 2, lax.rem(k, 2) == 0))
        def _():
            forward(jnp.where(section == 0, jnp.minimum(k, 1), k // 2))

        @pl.when(jnp.logical_and(section == 0, k == 2))
        def _():
            give_alone(1, 1)
            again = pltpu.make_async_copy(y_out.at[:count], y, io_sem.at[0])
            again.start()
            again.wait()
            give_alone(0, 0)

        @pl.when(jnp.where(section == 0, k == 2, lax.rem(k, 2) == 1))
        def _():
            backward(jnp.where(section == 0, 0, k // 2))

        return carry

    lax.fori_loop(0, 3 + section, turn, 0)

    @pl.when(section == 0)
    def _():
        give_alone(0, 2)

    heard(meet_sem, neighbours)
    for k in range(2):
        Line(
            k * half,
            quarter,
            pieces,
            part_two,
            dresid,
            y,
            list(line_scratch[2 + k]) + [back_s.at[k], back_r.at[2 + k]],
            moved=(dys, -1),
            at=(0, 0, count),
        ).receive()
    for index in range(14):
        keep(index, 0).wait()
        if index < 9:
            keep(index, 1).wait()

    @pl.when(section > 0)
    def _():
        for index in range(9, 14):
            keep(index, 1).wait()

    @pl.when(section == 0)
    def _():
        keep(9, 1).start()
        keep(9, 1).wait()


def main_ticks(rows, spots, holder, weights, qkv, groups, q_heads, k_heads, cid):
    norm_one, wqkv, wout, norm_two, wgate, wup, wdown = weights
    own_rows, extra_first, extra_second, chosen = rows
    count, width = own_rows.shape[0] // 2, own_rows.shape[1]
    hidden, keys = wgate.shape[1], groups * count
    pieces = 5
    vmem = pl.BlockSpec(memory_space=pltpu.VMEM)
    far = pl.BlockSpec(memory_space=pl.ANY)
    dma = pltpu.SemaphoreType.DMA

    def shape(columns, rows=2 * count, dtype=BF16):
        return jax.ShapeDtypeStruct((rows, columns), dtype)

    heads, both = q_heads * LANES, (q_heads + 2 * k_heads) * LANES
    spare = holder.shape[0] // (2 * groups)
    outs = [
        shape(width),
        shape(width),
        shape(width, 3 * spare),
        shape(width),
        shape(width),
    ]
    state = [
        shape(width),
        shape(heads),
        shape(2 * k_heads * LANES, 2 * keys),
        shape(LANES, 2 * q_heads * count, F32),
        shape(heads),
        shape(width),
        shape(hidden),
        shape(hidden),
        shape(hidden),
        shape(width),
        shape(width),
        shape(hidden),
        shape(hidden),
        shape(both),
    ]
    outs += state + [shape(width, 1, F32)] * 2
    near_weights = [wqkv, wout, wgate, wup, wdown]
    far_weights = [*qkv, wout, wgate, wup, wdown]
    scratch = [pltpu.VMEM(item.shape, item.dtype) for item in state] + [dma((14, 2))]
    scratch += [pltpu.VMEM(item.shape, BF16) for item in near_weights]
    scratch += [pltpu.VMEM((count, width), BF16)] * 4 + [
        pltpu.VMEM((count, heads), BF16),
        pltpu.VMEM((2 * k_heads * LANES, keys), F32),
        dma((7,)),
        dma((3,)),
        pltpu.SemaphoreType.REGULAR((2 + dp_bits(groups),)),
    ]
    scratch += Gather.scratch(groups) * 2
    for k in range(4):
        scratch += Line.scratch(quarter_rows(count), pieces, width, False)
    scratch += [dma((2, 2, pieces)), dma((4, 2, pieces))] * 2
    scratch += [pltpu.VMEM((groups * spare, width), BF16), pltpu.VMEM((spare, width), BF16)]
    scratch += OwnScatter.scratch(groups, spare, width, spare // 32, BF16)
    scratch += Gather.scratch(groups)
    for _ in range(k_heads):
        scratch += [pltpu.VMEM((keys, 2 * LANES), BF16), pltpu.VMEM((count, 2 * LANES), F32)]
        scratch += Scatter.scratch(groups, count, 2 * LANES, 5, BF16)
    return pl.pallas_call(
        functools.partial(main_kernel, groups, q_heads, k_heads, pieces),
        out_shape=outs,
        in_specs=[vmem] * 9 + [far] * 10,
        out_specs=[far] * (len(outs) - 2) + [vmem] * 2,
        scratch_shapes=scratch,
        compiler_params=pltpu.CompilerParams(
            collective_id=cid, has_side_effects=True, vmem_limit_bytes=VMEM_LIMIT
        ),
        name="main_ticks",
    )(*spots, norm_one[None], norm_two[None], holder, chosen, own_rows, extra_first, extra_second, *far_weights)


def quarter_rows(count):
    return count // 4


def weight_job(target, left, right, i, block=256):
    here = lanes(i, block)
    target[here, :] = rows_contract(left[:, here], right[...]).astype(BF16)


def last_ffn_kernel(groups, pieces, chunks, *refs):
    refs = list(refs)

    def take(count):
        taken = refs[:count]
        del refs[:count]
        return taken

    gain, holder = take(2)
    sources = take(14)
    last_dresid, gsum, g_up, down_sum, gate_sum, y, returned = take(7)
    wdown, wgate, wup, dys, act, gate, up, dgate, dup, resid = kept = take(10)
    n2, part, g_down, g_gate, spares, w_sem = take(6)
    line_scratch = [take(12) for _ in range(4)]
    count, width = last_dresid.shape
    half = count // 2
    line_a, line_b = [
        Line(
            k * half,
            half // 2,
            pieces,
            part,
            dys,
            last_dresid,
            line_scratch[k],
            norm=(resid, gain, gsum, count),
            at=(count, 0, 0),
        )
        for k in range(2)
    ]
    results = [Line(k * half, half // 2, pieces, part, resid, y, line_scratch[k]) for k in range(4)]
    down = OwnScatter(groups, width // groups, chunks, [g_down, down_sum] + take(OwnScatter.refs(groups)))
    gated = OwnScatter(groups, width // groups, chunks, [g_gate, gate_sum] + take(OwnScatter.refs(groups)))
    spare = returned.shape[0]
    give = OwnScatter(groups, spare, spare // 32, [spares, returned] + take(OwnScatter.refs(groups)))
    section = lax.axis_index("section")
    mine = section == 0
    tiles, wide, blocks = act.shape[1] // WIDE, width // WIDE, width // TILE

    def load(k):
        if k in (7, 8):
            return pltpu.make_async_copy(sources[k].at[:count], kept[k].at[:count], w_sem.at[k])
        return pltpu.make_async_copy(sources[k], kept[k], w_sem.at[k])

    lacks = [
        pltpu.make_async_copy(sources[7].at[count:], kept[7].at[count:], w_sem.at[10]),
        pltpu.make_async_copy(sources[8].at[count:], kept[8].at[count:], w_sem.at[11]),
        pltpu.make_async_copy(sources[10].at[count:], last_dresid, w_sem.at[12]),
    ]
    known = [
        pltpu.make_async_copy(sources[11], y, w_sem.at[13]),
        pltpu.make_async_copy(sources[12].at[:spare], returned, w_sem.at[14]),
    ]
    loads = [load(k) for k in range(10)] + [pltpu.make_async_copy(sources[13], n2, w_sem.at[15])]
    for k in (3, 0, 5, 6, 1, 2, 4, 9, 10, 7, 8):
        loads[k].start()

    @pl.when(section > 0)
    def _():
        for item in lacks:
            item.start()

    @pl.when(mine)
    def _():
        for item in known:
            item.start()

    Line.greet()
    for where, _ in down.links:
        greet(where)
    gsum[...] = jnp.zeros_like(gsum)
    line_a.enter(down.levels)
    for k in (3, 0, 5, 6):
        loads[k].wait()

    def hidden(first):
        here = pl.ds(count + first, half)

        def one(i, c):
            columns = lanes(i, WIDE)
            d_act = with_transpose(dys[here], wdown[columns, :])
            gate_pre, up_pre = gate[here, columns].astype(F32), up[here, columns].astype(F32)
            sigma = jax.nn.sigmoid(gate_pre)
            d_silu = d_act * sigma
            dup[here, columns] = (d_silu * gate_pre).astype(BF16)
            dgate[here, columns] = (d_silu * up_pre * (1.0 + gate_pre * (1.0 - sigma))).astype(BF16)
            return c

        lax.fori_loop(0, tiles, one, 0)

    def back(first):
        here, there = pl.ds(first, half), pl.ds(count + first, half)

        def one(i, c):
            columns = lanes(i, WIDE)
            total = with_transpose(dgate[there], wgate[columns, :]) + with_transpose(dup[there], wup[columns, :])
            part[here, columns] = total.astype(BF16)
            return c

        lax.fori_loop(0, wide, one, 0)

    @pl.when(mine)
    def _():
        hidden(0)

    loads[1].wait()
    loads[2].wait()

    @pl.when(mine)
    def _():
        back(0)
        line_a.start()

    loads[4].wait()

    @pl.when(section > 0)
    def _():
        for k in range(4):
            here = pl.ds(k * half, half)

            def one(i, c):
                part[here, lanes(i, WIDE)] = times(act[here], wdown[:, lanes(i, WIDE)]).astype(BF16)
                return c

            lax.fori_loop(0, wide, one, 0)
            results[k].start()

        loads[9].wait()

    def down_job(i, c):
        weight_job(g_down, dys, act, i)
        return c

    lax.fori_loop(0, blocks, down_job, 0)
    down.start()

    @pl.when(mine)
    def _():
        hidden(half)
        back(half)
        line_b.start()

    @pl.when(mine)
    def _():
        loads[9].wait()

    for k in (10, 7, 8):
        loads[k].wait()

    @pl.when(section > 0)
    def _():
        lacks[0].wait()
        lacks[1].wait()

    late = 100
    spans = 0

    first_done = line_a.steps + pieces

    def step(i, c):
        @pl.when(mine)
        def _():
            line_a.step(i)
            line_b.step(i - line_a.steps)

        @pl.when(section > 0)
        def _():
            for k, item in enumerate(results):
                item.step(i - k * pieces)

            @pl.when(i == first_done)
            def _():
                spares[...] = times(holder[...], y[:count]).astype(BF16)
                give.start()

            give.step(i - first_done, late)

        @pl.when(i < late)
        def _():
            down.step(i, late)
            gated.step(i - spans - blocks, late)

        @pl.when(jnp.logical_and(i >= spans, i < spans + blocks))
        def _():
            weight_job(g_gate, n2, dgate, i - spans)

        @pl.when(i == spans + blocks - 1)
        def _():
            gated.start()

        @pl.when(jnp.logical_and(i >= spans + blocks, i < spans + 2 * blocks))
        def _():
            weight_job(g_up, n2, dup, i - spans - blocks)

        return c

    enough = max(line_a.steps + line_b.steps, spans + 2 * blocks, spans + blocks + chunks)
    lax.fori_loop(0, jnp.where(mine, enough, max(enough, line_a.steps + 3 * pieces, first_done + give.chunks)), step, 0)
    run_steps(late, late + chunks, (lambda i: down.step(i, late), 0), (lambda i: gated.step(i, late), 0))

    @pl.when(mine)
    def _():
        line_a.finish()
        line_b.finish()

        for item in known:
            item.wait()

    @pl.when(section > 0)
    def _():
        lacks[2].wait()
        run_steps(late, late + give.chunks, (lambda i: give.step(i, late), 0))
        give.finish()
        for item in results:
            item.finish()

    down.finish()
    gated.finish()


def last_ffn(known, holder, weights, groups, cid):
    norm_one, wqkv, wout, norm_two, wgate, wup, wdown = weights
    dys, act, gate, up, dgate, dup, resid, dresid, y, y_back, normed_two = known
    spare = holder.shape[0] // groups
    count, width = dys.shape[0] // 2, dys.shape[1]
    hidden = act.shape[1]
    pieces, chunks = 5, 8
    vmem = pl.BlockSpec(memory_space=pltpu.VMEM)
    far = pl.BlockSpec(memory_space=pl.ANY)
    sources = [wdown, wgate, wup, dys, act, gate, up, dgate, dup, resid]
    scratch = [pltpu.VMEM(item.shape, BF16) for item in sources]
    scratch += [
        pltpu.VMEM((2 * count, width), BF16),
        pltpu.VMEM((2 * count, width), BF16),
        pltpu.VMEM((width, hidden), BF16),
        pltpu.VMEM((width, hidden), BF16),
        pltpu.VMEM((groups * spare, width), BF16),
        pltpu.SemaphoreType.DMA((16,)),
    ]
    scratch += Line.scratch(count // 4, pieces, width, False) * 4
    scratch += OwnScatter.scratch(groups, width // groups, hidden, chunks, BF16) * 2
    scratch += OwnScatter.scratch(groups, spare, width, spare // 32, BF16)
    return pl.pallas_call(
        functools.partial(last_ffn_kernel, groups, pieces, chunks),
        out_shape=[
            jax.ShapeDtypeStruct((count, width), BF16),
            jax.ShapeDtypeStruct((1, width), F32),
            jax.ShapeDtypeStruct((width, hidden), BF16),
            jax.ShapeDtypeStruct((width // groups, hidden), F32),
            jax.ShapeDtypeStruct((width // groups, hidden), F32),
            jax.ShapeDtypeStruct((2 * count, width), BF16),
            jax.ShapeDtypeStruct((spare, width), BF16),
        ],
        in_specs=[vmem] * 2 + [far] * 14,
        out_specs=[vmem] * 7,
        scratch_shapes=scratch,
        compiler_params=pltpu.CompilerParams(
            collective_id=cid, has_side_effects=True, vmem_limit_bytes=VMEM_LIMIT
        ),
        name="last_ffn",
    )(norm_two[None], holder, *sources, dresid, y, y_back, normed_two)


def last_attn_kernel(groups, q_heads, k_heads, pieces, chunks, spare_chunks, *refs):
    refs = list(refs)

    def take(count):
        taken = refs[:count]
        del refs[:count]
        return taken

    cosine, sine, qcode, qstart, kcode, gain, dresid, holder, gains, spread_q, spread_k, spread_v, spread_o = take(13)
    sources = take(10)
    dx_known, y, y_back, normed_one = take(4)
    dx, returned, returned_y, gains_out, up_sum, attn_sum = take(6)
    wout, wqkv, x, q, kv, lse, mixed, dqkv, other_dresid, g_up = kept = take(10)
    plain, plain_mixed = take(2)
    part, dmixed, dkv, n1, g_attn, spares, spares_y, gsum, gains_own, gains_all, gains_sum, w_sem, g_s, g_r = take(14)
    levels = dp_bits(groups)
    count, width = part.shape
    half = count // 2
    keys = kv.shape[0]
    shares, owns, scatters = [], [], []
    for g in range(k_heads):
        share, own = take(2)
        shares.append(share)
        owns.append(own)
        scatters.append(OwnScatter(groups, count, 5, [share, own] + take(OwnScatter.refs(groups))))
    block = width // groups
    up_task, attn_task = [
        OwnScatter(groups, block, chunks, [value, total] + take(OwnScatter.refs(groups)))
        for value, total in ((g_up, up_sum), (g_attn, attn_sum))
    ]
    spare = spares.shape[0] // groups
    back_task = OwnScatter(groups, spare, spare_chunks, [spares, returned] + take(OwnScatter.refs(groups)))
    give_y = OwnScatter(groups, spare, spare_chunks, [spares_y, returned_y] + take(OwnScatter.refs(groups)))
    small = OwnScatter(groups, 8, 1, [gains_sum, gains_out] + take(OwnScatter.refs(groups)))
    line_a, line_b = [
        Line(k * half, half // 2, pieces, part, dresid, dx, take(12), norm=(x, gain, gsum, count)) for k in range(2)
    ]
    section, t = lax.axis_index("section"), lax.axis_index("tensor")
    mine = section == 0
    order = [9, 0, 3, 4, 5, 1, 2, 6, 7, 8]

    def load(k):
        here, there = sources[k].at[sources[k].shape[0] - kept[k].shape[0] :], kept[k]
        if k in (7, 8):
            here, there = sources[k].at[:count], kept[k].at[:count]
        return pltpu.make_async_copy(here, there, w_sem.at[k])

    lack = pltpu.make_async_copy(sources[7].at[count:], dqkv.at[count:], w_sem.at[13])
    loads = [load(k) for k in range(10)]
    for k in order:
        loads[k].start()
    known = pltpu.make_async_copy(dx_known.at[count:], dx, w_sem.at[11])
    load_n1 = pltpu.make_async_copy(normed_one, n1, w_sem.at[10])
    load_n1.start()
    known_y = pltpu.make_async_copy(y_back.at[spare : 2 * spare], returned_y, w_sem.at[12])
    load_y = pltpu.make_async_copy(y.at[count:], part, w_sem.at[12])

    @pl.when(mine)
    def _():
        known_y.start()

    @pl.when(section > 0)
    def _():
        known.start()
        lack.start()

    for k in range(1, 4):
        greet({"tensor": lax.rem(t + k, 4)})
    for where, _ in up_task.links:
        greet(where)
    gsum[...] = jnp.zeros_like(gsum)
    dkv[...] = jnp.zeros_like(dkv)
    pl.semaphore_wait(pltpu.get_barrier_semaphore(), 3 + levels)
    loads[9].wait()
    up_task.start()
    for k in (0, 3, 4, 5):
        loads[k].wait()

    wide, jobs = width // WIDE, width // TILE
    repeat = q_heads // k_heads
    rows = block_rows(keys)
    blocks = half // rows
    turns = repeat * blocks
    scale = HD ** (-0.5)
    late = 100
    begun = 2 * k_heads * turns

    def early(i):
        @pl.when(lax.rem(i, 2) == 1)
        def _():
            up_task.step(i // 2, late)

    def mix(first):
        here = pl.ds(first, half)

        def one(h, c):
            dmixed[here, lanes(h)] = with_transpose(dresid[here], wout[lanes(h), :]).astype(BF16)
            return c

        lax.fori_loop(0, q_heads, one, 0)

    def attend(first, g, each):
        def one(i, c):
            h, n = g * repeat + i // blocks, lax.rem(i, blocks)
            here = pl.ds(pl.multiple_of(first + n * rows, rows), rows)
            scores, allowed = score_rows(q, kv, h, g, here, qcode, qstart, kcode)
            there = pl.ds(pl.multiple_of(h * count + first + n * rows, rows), rows)
            prob = jnp.where(allowed, jnp.exp(scores - lse[there][:, :1]), 0.0)
            dm = dmixed[here, lanes(h)]
            d_prob = with_transpose(dm, kv[:, lanes(k_heads + g)])
            row_dot = jnp.sum(prob * d_prob, axis=-1, keepdims=True)
            d_scores = (prob * (d_prob - row_dot)).astype(BF16)
            d_query = times(d_scores, kv[:, lanes(g)]) * scale
            there = pl.ds(pl.multiple_of(count + first + n * rows, rows), rows)
            dqkv[there, lanes(h)] = rolled(d_query, cosine[here], -sine[here]).astype(BF16)
            dkv[lanes(g), :] += rows_contract(q[here, lanes(h)], d_scores) * scale
            dkv[lanes(k_heads + g), :] += rows_contract(dm, prob.astype(BF16))
            each(i)
            return c

        lax.fori_loop(0, turns, one, 0)

    def back(first):
        here, there = pl.ds(first, half), pl.ds(count + first, half)

        def one(i, c):
            columns = lanes(i, WIDE)
            part[here, columns] = with_transpose(dqkv[there], wqkv[columns, :]).astype(BF16)
            return c

        lax.fori_loop(0, wide, one, 0)

    @pl.when(mine)
    def _():
        mix(0)
        mix(half)
        for g in range(k_heads):
            for first in (0, half):
                at = 2 * g * turns + (turns if first else 0)
                attend(first, g, lambda i: early(at + i))

            shares[g][:, :LANES] = jnp.transpose(dkv[lanes(g), :]).astype(BF16)
            shares[g][:, LANES:] = jnp.transpose(dkv[lanes(k_heads + g), :]).astype(BF16)
            scatters[g].start()
        run_steps(0, scatters[0].chunks, *[(functools.partial(lambda s, i: s.step(i, late), s), 0) for s in scatters])

    @pl.when(section > 0)
    def _():
        run_steps(0, begun, (early, 0))
        known.wait()
        lack.wait()

    ends = [0]
    for item in (spread_q, spread_k, spread_v, spread_o):
        ends.append(ends[-1] + item.shape[0])
    starts = [0, q_heads, q_heads + k_heads, q_heads + 2 * k_heads]

    @pl.when(section > 0)
    def _():
        load_y.start()
        load_y.wait()
        spares_y[...] = times(holder[...], part[...]).astype(BF16)
        give_y.start()

    for k in (1, 2, 6, 7, 8):
        loads[k].wait()
    load_n1.wait()
    plain_mixed[...] = with_transpose(mixed[...], spread_o[...]).astype(BF16)
    other_dresid[count:] = dresid[...]

    def out_job(i, c):
        here = lanes(i, TILE)
        g_attn[here, ends[3] :] = rows_contract(other_dresid[:, here], plain_mixed[...]).astype(BF16)
        return c

    lax.fori_loop(0, jobs, out_job, 0)

    @pl.when(mine)
    def _():
        ending = late + scatters[0].chunks
        run_steps(late, ending, *[(functools.partial(lambda s, i: s.step(i, late), s), 0) for s in scatters])
        for g in range(k_heads):
            dqkv[count:, lanes(q_heads + g)] = rolled(owns[g][:, :LANES], cosine[...], -sine[...]).astype(BF16)
            dqkv[count:, lanes(q_heads + k_heads + g)] = owns[g][:, LANES:].astype(BF16)
        back(0)
        line_a.start()
        back(half)
        line_b.start()

    def spread(k):
        return remote(gains_own, gains_all.at[k - 1], g_s.at[k - 1], g_r.at[k - 1], {"tensor": lax.rem(t + k, 4)})

    first_job = begun // 2

    def step(i, c):
        @pl.when(mine)
        def _():
            line_a.step(i)
            line_b.step(i - line_a.steps)

        up_task.step(i + first_job, late)

        @pl.when(i == 0)
        def _():
            for a, b, n, item in zip(starts, starts[1:], ends, (spread_q, spread_k, spread_v)):
                plain[:, n : n + item.shape[0]] = with_transpose(
                    dqkv[:, a * LANES : b * LANES], item[...]
                ).astype(BF16)

        @pl.when(jnp.logical_and(i >= 1, i <= jobs))
        def _():
            here = lanes(jnp.clip(i - 1, 0, jobs - 1), TILE)
            g_attn[here, : ends[3]] = rows_contract(n1[:, here], plain[...]).astype(BF16)

        @pl.when(i == jobs)
        def _():
            attn_task.start()

        attn_task.step(i - jobs - 1, late)

        @pl.when(section > 0)
        def _():
            give_y.step(i - first_job, late)

        return c

    lax.fori_loop(0, max(line_a.steps + line_b.steps, jobs + 1 + chunks), step, 0)
    spares[...] = times(holder[...], dx[...]).astype(BF16)
    back_task.start()
    gains_own[...] = gains[...]
    gains_own[:1] = gains[:1] + gsum[...] * jnp.where(mine, 1.0, 0.0)
    for k in range(1, 4):
        spread(k).start()
    run_steps(0, spare_chunks, (lambda i: back_task.step(i, late), 0))
    for k in range(1, 4):
        spread(k).wait()
    total = gains_own[...] + gains_all[0] + gains_all[1] + gains_all[2]
    part_width = width // groups
    for d in range(groups):
        gains_sum[8 * d : 8 * d + 8, :] = total[:, d * part_width : (d + 1) * part_width]
    small.start()

    def close(i, c):
        up_task.step(late + i, late)
        attn_task.step(late + i, late)

        @pl.when(section > 0)
        def _():
            give_y.step(late + i, late)

        small.step(i, 4)
        return c

    lax.fori_loop(0, max(chunks, spare_chunks, small.steps(4)), close, 0)
    run_steps(late, late + spare_chunks, (lambda i: back_task.step(i, late), 0))

    @pl.when(mine)
    def _():
        line_a.finish()
        line_b.finish()
        for item in scatters:
            item.finish()
        known_y.wait()

    @pl.when(section > 0)
    def _():
        give_y.finish()

    for item in (up_task, attn_task, back_task, small):
        item.finish()


def last_attn(known, spots, dresid, dx, y, y_back, normed_one, holder, gains, spreads, grads, weights, groups, q_heads, k_heads, cid):
    norm_one, wqkv, wout, norm_two, wgate, wup, wdown = weights
    x, q, kv, lse, mixed, dqkv, other_dresid = known
    count, width = dresid.shape
    keys = groups * count
    spare = holder.shape[0] // groups
    pieces, chunks, spare_chunks = 5, 8, spare // 32
    vmem = pl.BlockSpec(memory_space=pltpu.VMEM)
    far = pl.BlockSpec(memory_space=pl.ANY)
    dma = pltpu.SemaphoreType.DMA
    sources = [wout, wqkv, x, q, kv, lse, mixed, dqkv, other_dresid, *grads]
    attn_width = sum(item.shape[0] for item in spreads)
    block = width // groups
    first_only = {3: count, 4: keys, 5: q_heads * count}
    scratch = [
        pltpu.VMEM((first_only.get(k, item.shape[0]),) + item.shape[1:], item.dtype) for k, item in enumerate(sources)
    ]
    scratch += [
        pltpu.VMEM((2 * count, attn_width - spreads[3].shape[0]), BF16),
        pltpu.VMEM((2 * count, spreads[3].shape[0]), BF16),
        pltpu.VMEM((count, width), BF16),
        pltpu.VMEM((count, q.shape[1]), BF16),
        pltpu.VMEM((kv.shape[1], keys), F32),
        pltpu.VMEM((2 * count, width), BF16),
        pltpu.VMEM((width, attn_width), BF16),
        pltpu.VMEM((groups * spare, width), BF16),
        pltpu.VMEM((groups * spare, width), BF16),
        pltpu.VMEM((1, width), F32),
        pltpu.VMEM(gains.shape, F32),
        pltpu.VMEM((3,) + gains.shape, F32),
        pltpu.VMEM((groups * 8, block), F32),
        dma((14,)),
        dma((3,)),
        dma((3,)),
    ]
    for _ in range(k_heads):
        scratch += [pltpu.VMEM((keys, 2 * LANES), BF16), pltpu.VMEM((count, 2 * LANES), F32)]
        scratch += OwnScatter.scratch(groups, count, 2 * LANES, 5, BF16)
    for columns in (grads[0].shape[1], attn_width):
        scratch += OwnScatter.scratch(groups, block, columns, chunks, BF16)
    scratch += OwnScatter.scratch(groups, spare, width, spare_chunks, BF16) * 2
    scratch += OwnScatter.scratch(groups, 8, block, 1, F32)
    scratch += Line.scratch(count // 4, pieces, width, False) * 2
    return pl.pallas_call(
        functools.partial(last_attn_kernel, groups, q_heads, k_heads, pieces, chunks, spare_chunks),
        out_shape=[
            jax.ShapeDtypeStruct((count, width), BF16),
            jax.ShapeDtypeStruct((spare, width), BF16),
            jax.ShapeDtypeStruct((spare, width), BF16),
            jax.ShapeDtypeStruct((8, block), F32),
            jax.ShapeDtypeStruct((block, grads[0].shape[1]), F32),
            jax.ShapeDtypeStruct((block, attn_width), F32),
        ],
        in_specs=[vmem] * 13 + [far] * 14,
        out_specs=[vmem] * 6,
        scratch_shapes=scratch,
        compiler_params=pltpu.CompilerParams(
            collective_id=cid, has_side_effects=True, vmem_limit_bytes=VMEM_LIMIT
        ),
        name="last_attn",
    )(*spots, norm_one[None], dresid, holder, gains, *spreads, *sources, dx, y, y_back, normed_one)


def finish_kernel(groups, parts, *refs):
    refs = list(refs)

    def take(count):
        taken = refs[:count]
        del refs[:count]
        return taken

    (live,) = take(1)
    through, y, y_first, y_second, cot, dx_first, dx_second, back_first, back_second = take(9)
    gate, up, down, attn = take(4)
    acts, backs = take(2)
    outs = take(7)
    tiles = take(4)
    rows = take(4)
    backs_near = take(4)
    down_near, down_turned, attn_near, *attn_parts = take(7)
    plain_near = take(2)
    sems, out_sems = take(2)
    count, spare = rows[0].shape[0], backs_near[0].shape[0]
    seq = count + spare
    whole = [
        (through.at[0, 0], y.at[:count], y_first, acts.at[0, 0, 0]),
        (through.at[1, 0], y.at[count:], y_second, acts.at[0, 1, 0]),
        (cot.at[0, 0], dx_first.at[:count], back_first.at[2 * spare :], backs.at[0, 0, 0]),
        (cot.at[1, 0], dx_second, back_second, backs.at[0, 1, 0]),
    ]
    query_out, key_out, value_out, out_out, gate_out, up_out, down_out = outs
    plain_in = [pltpu.make_async_copy(a, b, sems.at[14 + k]) for k, (a, b) in enumerate(zip((gate, up), plain_near))]
    plain = [pltpu.make_async_copy(a, b, out_sems.at[k]) for k, (a, b) in enumerate(zip(plain_near, (gate_out.at[0], up_out.at[0])))]
    load_down = pltpu.make_async_copy(down, down_near, sems.at[12])
    load_attn = pltpu.make_async_copy(attn, attn_near, sems.at[13])
    loads = []
    for k, (a, b, c, _) in enumerate(whole):
        loads.append(
            [
                pltpu.make_async_copy(src, dst, sems.at[3 * k + n])
                for n, (src, dst) in enumerate(((a, tiles[k]), (b, rows[k]), (c, backs_near[k])))
            ]
        )
    load_attn.start()
    load_down.start()
    for item in plain_in:
        item.start()
    for group in loads:
        for item in group:
            item.start()
    stores = []
    load_attn.wait()
    at = 0
    for k, (size, near, there) in enumerate(zip(parts, attn_parts, (query_out, key_out, value_out, out_out))):
        value = attn_near[:, at : at + size]
        near[...] = value if k == 0 else jnp.transpose(value)
        at += size
        stores.append(pltpu.make_async_copy(near, there.at[0], out_sems.at[2 + k]))
        stores[-1].start()
    for before, item in zip(plain_in, plain):
        before.wait()
        item.start()
    load_down.wait()
    down_turned[...] = jnp.transpose(down_near[...])
    stores.append(pltpu.make_async_copy(down_turned, down_out.at[0], out_sems.at[6]))
    stores[-1].start()
    for k, group in enumerate(loads):
        for item in group:
            item.wait()
        first = (k % 2) * seq

        def one(i, c):
            here = pl.ds(pl.multiple_of(i * 64, 64), 64)
            alive = live[pl.ds(pl.multiple_of(first + i * 64, 64), 64)] > 0
            tiles[k][here] = jnp.where(alive, rows[k][here], tiles[k][here])
            return c

        lax.fori_loop(0, count // 64, one, 0)

        def two(i, c):
            near = pl.ds(pl.multiple_of(i * 64, 64), 64)
            here = pl.ds(pl.multiple_of(count + i * 64, 64), 64)
            alive = live[pl.ds(pl.multiple_of(first + count + i * 64, 64), 64)] > 0
            tiles[k][here] = jnp.where(alive, backs_near[k][near], tiles[k][here])
            return c

        lax.fori_loop(0, spare // 64, two, 0)
        stores.append(pltpu.make_async_copy(tiles[k], whole[k][3], out_sems.at[7 + k]))
        stores[-1].start()
    for item in stores + plain:
        item.wait()


def finish(live, through, y, y_backs, cot, dx_first, dx_second, back_first, back_second, grads, parts, groups):
    count, width = dx_second.shape
    spare = back_second.shape[0]
    gate, up, down, attn = grads
    block, hidden = down.shape
    vmem = pl.BlockSpec(memory_space=pltpu.VMEM)
    far = pl.BlockSpec(memory_space=pl.ANY)
    shapes = [(block, parts[0])] + [(size, block) for size in parts[1:]]
    outs = [jax.ShapeDtypeStruct((1, 2, 1, count + spare, width), BF16)] * 2
    outs += [jax.ShapeDtypeStruct((1,) + item, F32) for item in shapes + [gate.shape, up.shape, (hidden, block)]]
    scratch = [pltpu.VMEM((count + spare, width), BF16)] * 4
    scratch += [pltpu.VMEM((count, width), BF16)] * 4 + [pltpu.VMEM((spare, width), BF16)] * 4
    scratch += [pltpu.VMEM(down.shape, F32), pltpu.VMEM((hidden, block), F32), pltpu.VMEM(attn.shape, F32)]
    scratch += [pltpu.VMEM(item, F32) for item in shapes]
    scratch += [pltpu.VMEM(gate.shape, F32), pltpu.VMEM(up.shape, F32)]
    scratch += [pltpu.SemaphoreType.DMA((16,)), pltpu.SemaphoreType.DMA((11,))]
    return pl.pallas_call(
        functools.partial(finish_kernel, groups, parts),
        out_shape=outs,
        in_specs=[vmem] + [far] * 13,
        out_specs=[far] * 9,
        scratch_shapes=scratch,
        compiler_params=pltpu.CompilerParams(vmem_limit_bytes=VMEM_LIMIT),
        name="finish",
    )(live, through, y, *y_backs, cot, dx_first, dx_second, back_first, back_second, gate, up, down, attn)


def rope_tables(seq_len):
    half_width = HD // 2
    inverse = np.float32(rope_base) ** (-(np.arange(half_width, dtype=np.float32) * np.float32(2.0) / np.float32(HD)))
    angle = np.arange(seq_len, dtype=np.float32)[:, None] * inverse[None, :].astype(np.float32)
    cosine, sine = np.cos(angle), np.sin(angle)
    table = np.zeros((seq_len, 4, LANES // 2), np.float32)
    table[:, 0, :half_width] = cosine
    table[:, 1, :half_width] = cosine
    table[:, 2, :half_width] = -sine
    table[:, 3, :half_width] = sine
    return table.reshape(seq_len, 2 * LANES)


def spreader(heads, turned):
    feature = jnp.arange(HD)
    place = jnp.where(feature < HD // 2, feature, feature - HD // 2 + LANES // 2) if turned else feature
    lane = (jnp.arange(heads)[:, None] * LANES + place[None, :]).reshape(-1)
    return (lane[:, None] == jnp.arange(heads * LANES)[None, :]).astype(BF16)


def slots_of(lens, count):
    groups = lens.shape[0]
    kept = jnp.minimum(lens, count)
    free, extra = count - kept, lens - kept
    free_off = jnp.cumsum(free) - free
    extra_end = jnp.cumsum(extra)
    slot = jnp.arange(count)
    own = slot[None, :] < kept[:, None]
    index = free_off[:, None] + slot[None, :] - kept[:, None]
    source = jnp.sum(index[:, :, None] >= extra_end[None, None, :], axis=-1)
    begins = jnp.sum(jnp.where(index[:, :, None] >= extra_end[None, None, :], extra[None, None, :], 0), axis=-1)
    seq = jnp.where(own, jnp.arange(groups)[:, None], source)
    pos = jnp.where(own, slot[None, :], count + index - begins)
    return seq, pos, own


def on_device(
    inputs,
    cotangent,
    lengths,
    norm_attn,
    w_query,
    w_key,
    w_value,
    w_out,
    norm_ffn,
    w_gate,
    w_up,
    w_down,
):
    first = lax.axis_index("section") == 0
    me = lax.axis_index("dp")
    groups = lax.axis_size("dp")
    micro, seq_len, width = inputs.shape[0], inputs.shape[2], inputs.shape[3]
    count = seq_len * 5 // 8
    spare = seq_len - count
    q_heads, k_heads = w_query.shape[2] // HD, w_key.shape[2] // HD
    spread_q, spread_k = spreader(q_heads, True), spreader(k_heads, True)
    spread_v, spread_o = spreader(k_heads, False), spreader(q_heads, False)
    qkv = [
        times(item[0], spread).astype(BF16)
        for item, spread in ((w_query, spread_q), (w_key, spread_k), (w_value, spread_v))
    ]
    wqkv = jnp.concatenate(qkv, axis=1)
    wout = rows_contract(spread_o, w_out[0]).astype(BF16)
    weights = (norm_attn[0], wqkv, wout, norm_ffn[0], w_gate[0], w_up[0], w_down[0])

    all_in_one = micro == 2 and groups == 4

    extras = [jnp.where(first, inputs[b, 0, count:], cotangent[b, 0, count:]) for b in range(micro)]
    first_extra = lax.all_gather(extras[0], "dp", axis=0, tiled=True)
    length_rows = jnp.broadcast_to(lengths[:, 0].astype(F32)[:, None], (micro, LANES))
    length_rows = jnp.concatenate([length_rows, jnp.zeros((8 - micro, LANES), F32)], axis=0)
    (length_all,) = gather_rows([length_rows], groups, 4)
    lens = length_all.reshape(groups, 8, LANES)[:, :micro, 0].T.astype(jnp.int32)
    packed, slots, spots, chosen, kept_own = [], [], [], [], []
    for b in range(micro):
        seq, pos, own = slots_of(lens[b], count)
        slots.append((seq, pos))
        my_seq, my_pos, own = seq[me][:, None], pos[me][:, None], own[me][:, None]
        here = (jnp.arange(seq_len)[None, :] == my_pos).astype(F32)
        turned = jnp.dot(here, rope_tables(seq_len), precision=lax.Precision.HIGHEST)
        code = (seq * seq_len + pos).reshape(1, -1)
        spots.append((turned[:, :LANES], turned[:, LANES:], my_seq * seq_len + my_pos, my_seq * seq_len, code))
        wanted = jnp.where(own, -1, my_seq * spare + my_pos - count)
        chosen.append((jnp.arange(groups * spare)[None, :] == wanted).astype(BF16))
        kept = jnp.where(first, inputs[b, 0, :count], cotangent[b, 0, :count])
        kept_own.append(jnp.where(own, kept, jnp.zeros((), BF16)))
    for b in range(0 if all_in_one else micro):
        extra = first_extra if b == 0 else lax.all_gather(extras[b], "dp", axis=0, tiled=True)
        packed.append((kept_own[b].astype(F32) + times(chosen[b], extra)).astype(BF16))

    def holder(b):
        seq, pos = slots[b]
        row = jnp.arange(groups * spare)[:, None]
        return jnp.logical_and(row == seq[me][None, :] * spare + pos[me][None, :] - count, pos[me][None, :] >= count)

    def spread(rows, b):
        return jnp.dot(holder(b).astype(BF16), rows, preferred_element_type=F32).astype(BF16)

    def unpack(rows, back, b, through):
        live = (jnp.arange(seq_len) < lens[b, me])[:, None]
        return jnp.where(live, jnp.concatenate([rows, back], axis=0), through)

    def come_back(rows, b):
        return lax.psum_scatter(spread(rows, b), "dp", scatter_dimension=0, tiled=True)

    norm_one, norm_two = weights[0], weights[3]
    empty = jnp.zeros((count, width), BF16)

    def spots_at(tick):
        early, late = spots[min(tick, micro - 1)], spots[max(tick - 1, 0)]
        return tuple(jnp.where(first, a, b) for a, b in zip(early, late))

    grads_in, before, gain_sums = [], [], []
    if all_in_one:
        joined = [jnp.concatenate(items, axis=0) for items in zip(*spots)]
        joined[4] = joined[4][:, None]
        held = jnp.concatenate([holder(b) for b in range(micro)], axis=0).astype(BF16)
        y, dx, y_back, normed_one, normed_two, x, q, kv, lse, mixed, resid, gate, up, act, dy, d_resid, d_gate, d_up, d_qkv, gain_one, gain_two = main_ticks(
            (jnp.concatenate(kept_own, axis=0), first_extra, extras[1], jnp.concatenate(chosen, axis=0)),
            joined,
            held,
            weights,
            qkv,
            groups,
            q_heads,
            k_heads,
            0,
        )
        last_dresid, gain_last, grad_up, grad_down, grad_gate, y, y_first = last_ffn(
            (dy, act, gate, up, d_gate, d_up, resid, d_resid, y, y_back, normed_two), held[: groups * spare], weights, groups, 1
        )
        gain_last = jnp.where(first, gain_last, jnp.zeros_like(gain_last))
        gains = jnp.concatenate([gain_one, gain_two + gain_last, jnp.zeros((6, width), F32)], axis=0)
        last_dx, back_second, y_second, gains, grad_up, grad_attn = last_attn(
            (x, q, kv, lse, mixed, d_qkv, d_resid),
            spots[1],
            last_dresid,
            dx,
            y,
            y_back,
            normed_one,
            held[groups * spare :],
            gains,
            (spread_q, spread_k, spread_v, spread_o),
            (grad_up,),
            weights,
            groups,
            q_heads,
            k_heads,
            2,
        )
        live = (jnp.arange(seq_len)[None, :] < lens[:, me][:, None]).astype(jnp.int32).reshape(-1, 1)
        acts, backs, *grads = finish(
            live,
            inputs,
            y,
            (y_first, y_second),
            cotangent,
            dx,
            last_dx,
            y_back,
            back_second,
            (grad_gate, grad_up, grad_down, grad_attn),
            [w_query.shape[2], w_key.shape[2], w_value.shape[2], w_query.shape[2]],
            groups,
        )
        grads[1:3] = [jnp.swapaxes(item, 1, 2) for item in grads[1:3]]
        return (acts, backs, gains[:1], *grads[:4], gains[1:2], *grads[4:])

    else:
        arriving = empty
        results, saved = [], []
        for tick in range(micro + 1):
            stream = jnp.where(first, packed[tick] if tick < micro else empty, arriving)
            result, arriving, kept = forward_tick(stream, spots_at(tick), weights, groups, q_heads, k_heads, 0)
            results.append(result)
            saved.append(kept)
        results = [jnp.where(first, results[b], results[b + 1]) for b in range(micro)]
        arriving = empty
        for tick in range(micro):
            kept = saved[micro - tick]
            incoming = jnp.where(first, arriving, packed[micro - 1 - tick])
            d_resid, gain_two, d_gate, d_up = back_ffn(incoming, kept, weights, 1)
            d_stream, gain_one, d_qkv, arriving = back_attn(
                d_resid, kept, spots_at(micro - tick), weights, groups, q_heads, k_heads, 2, -1
            )
            before.append((kept[5], d_gate, d_up, incoming, kept[8], kept[0], d_qkv, d_resid, kept[4]))
            grads_in.append(d_stream)
            gain_sums.append(jnp.concatenate([gain_one, gain_two], axis=0))
        kept_last = saved[0]
        last_in, last_spots = jnp.where(first, arriving, empty), spots_at(0)
        grads_at = [grads_in[micro - 1 - b] if b == 0 else jnp.where(first, grads_in[micro - b], grads_in[micro - 1 - b]) for b in range(micro)]

        def all_rows(now, index):
            old = [item[index] for item in before]
            return jnp.concatenate([jnp.where(first, now, old[0])] + old[1:], axis=0)

        x, mixed, resid, act = kept_last[0], kept_last[4], kept_last[5], kept_last[8]
        d_resid, gain_two, d_gate, d_up = back_ffn(last_in, kept_last, weights, 1)
        n2 = normalize(all_rows(resid, 0), norm_two)
        grad_gate = rows_contract(n2, all_rows(d_gate, 1)).astype(BF16)
        grad_up = rows_contract(n2, all_rows(d_up, 2)).astype(BF16)
        grad_down = rows_contract(all_rows(last_in, 3), all_rows(act, 4)).astype(BF16)
        ffn_grads = (grad_gate, grad_up, grad_down)
        beside = len(ffn_grads) if groups * count <= 2048 else 1
        d_stream, gain_one, d_qkv, *ffn_sums = back_attn(
            d_resid, kept_last, last_spots, weights, groups, q_heads, k_heads, 3, 0, sums=ffn_grads[:beside]
        )
        n1 = normalize(all_rows(x, 5), norm_one)
        back_spread = [(spread_q, 0, q_heads), (spread_k, q_heads, k_heads), (spread_v, q_heads + k_heads, k_heads)]
        dqkv = all_rows(d_qkv, 6)
        dqkv = jnp.concatenate(
            [with_transpose(dqkv[:, i * LANES : (i + n) * LANES], item) for item, i, n in back_spread], axis=1
        ).astype(BF16)
        mix = with_transpose(all_rows(mixed, 8), spread_o).astype(BF16)
        grad_attn = jnp.concatenate(
            [rows_contract(n1, dqkv).astype(BF16), rows_contract(all_rows(d_resid, 7), mix).astype(BF16)], axis=1
        )
        grads_at[0] = jnp.where(first, d_stream, grads_at[0])
        last_gains = jnp.concatenate([gain_one, gain_two], axis=0)
        gain_sums.append(jnp.where(first, last_gains, jnp.zeros_like(last_gains)))

        gains = sum(gain_sums[1:], gain_sums[0])
        gains = jnp.concatenate([gains, jnp.zeros((6, width), F32)], axis=0)
        gains = gains.reshape(8, groups, -1).transpose(1, 0, 2).reshape(groups * 8, -1)

    acts = []
    for b in range(micro):
        rows = results[b]
        acts.append(unpack(rows, come_back(rows, b), b, inputs[b, 0]))
    backs = []
    for b in range(micro):
        rows = grads_at[b]
        if b == 0:
            back, gains, grad_attn, *rest = return_rows(
                spread(rows, b), gains, (grad_attn,) + ffn_grads[beside:], groups, 5, spare // 16
            )
            grad_gate, grad_up, grad_down = ffn_sums + rest
        else:
            back = come_back(rows, b)
        backs.append(unpack(rows, back, b, cotangent[b, 0]))
    acts, backs = jnp.stack(acts), jnp.stack(backs)
    ends = [0]
    for item in (w_query, w_key, w_value, w_query):
        ends.append(ends[-1] + item.shape[2])
    grad_query, grad_key, grad_value, grad_out = (grad_attn[:, a:b] for a, b in zip(ends, ends[1:]))
    final = (
        gains[0],
        grad_query,
        grad_key,
        grad_value,
        grad_out.T,
        gains[1],
        grad_gate,
        grad_up,
        grad_down.T,
    )
    return (acts[None, :, None], backs[None, :, None]) + tuple(item[None] for item in final)


def solution(mesh):
    placed = (
        P(None, "dp", None, None),
        P(None, "dp", None, None),
        P(None, "dp"),
        P("section", None),
        P("section", None, "tensor"),
        P("section", None, "tensor"),
        P("section", None, "tensor"),
        P("section", "tensor", None),
        P("section", None),
        P("section", None, "tensor"),
        P("section", None, "tensor"),
        P("section", "tensor", None),
    )
    return jax.shard_map(
        on_device,
        mesh=mesh,
        in_specs=placed,
        out_specs=(
            P("section", None, "dp", None, None),
            P("section", None, "dp", None, None),
            P("section", "dp"),
            P("section", "dp", "tensor"),
            P("section", "dp", "tensor"),
            P("section", "dp", "tensor"),
            P("section", "tensor", "dp"),
            P("section", "dp"),
            P("section", "dp", "tensor"),
            P("section", "dp", "tensor"),
            P("section", "tensor", "dp"),
        ),
        check_vma=False,
    )
```

```python
import functools

import jax
import jax.numpy as jnp
import numpy as np
from jax import lax
from jax.experimental import pallas as pl
from jax.experimental.pallas import tpu as pltpu
from jax.sharding import PartitionSpec as P

HD = 96

epsilon = 1e-05
rope_base = 100000.0
negative = -1e30
MESH = pl.DeviceIdType.MESH
F32 = jnp.float32
BF16 = jnp.bfloat16


def remote(src, dst, s_sem, r_sem, where):
    return pltpu.make_async_remote_copy(
        src_ref=src, dst_ref=dst, send_sem=s_sem, recv_sem=r_sem, device_id=where, device_id_type=MESH
    )


def greet(where):
    pl.semaphore_signal(pltpu.get_barrier_semaphore(), inc=1, device_id=where, device_id_type=MESH)


def dp_bits(groups):
    return groups.bit_length() - 1


def dp_partner(level):
    me = lax.axis_index("dp")
    bit = lax.rem(me // (1 << level), 2)
    return {"dp": me + (1 - 2 * bit) * (1 << level)}, bit


class Scatter:
    def __init__(self, groups, rows, chunks, refs):
        self.levels = dp_bits(groups)
        self.groups, self.rows, self.chunks, self.size = groups, rows, chunks, rows // chunks
        self.value, self.out = refs[0], refs[1]
        m = self.levels
        self.arrive = refs[2 : 2 + m]
        self.held = refs[2 + m : 1 + 2 * m]
        self.s_sem = refs[1 + 2 * m : 1 + 3 * m]
        self.r_sem = refs[1 + 3 * m : 1 + 4 * m]
        self.links = [dp_partner(k) for k in range(m)]

    @staticmethod
    def scratch(groups, rows, width, chunks, dtype):
        m = dp_bits(groups)
        sizes = [groups >> (k + 1) for k in range(m)]
        return (
            [pltpu.VMEM((size * rows, width), dtype) for size in sizes]
            + [pltpu.VMEM((size * rows, width), dtype) for size in sizes[:-1]]
            + [pltpu.SemaphoreType.DMA((size, chunks)) for size in sizes] * 2
        )

    def at(self, block, c):
        return pl.ds(pl.multiple_of(block * self.rows + c * self.size, self.size), self.size)

    def copy(self, level, slot, c):
        where, bit = self.links[level]
        source = self.value if level == 0 else self.held[level - 1]
        return remote(
            source.at[self.at(2 * slot + 1 - bit, c)],
            self.arrive[level].at[self.at(slot, c)],
            self.s_sem[level].at[slot, c],
            self.r_sem[level].at[slot, c],
            where,
        )

    def order(self, level):
        count = self.groups >> (level + 1)
        if count == 1:
            return [(0, False)]
        bit = self.links[level + 1][1]
        return [(2 * i + 1 - bit, True) for i in range(count // 2)] + [(2 * i + bit, False) for i in range(count // 2)]

    def start(self):
        def one(c, carry):
            for slot, _ in self.order(0):
                self.copy(0, slot, c).start()
            return carry

        lax.fori_loop(0, self.chunks, one, 0)

    def step(self, i, lag):
        for level in range(self.levels):
            c = i - level * lag

            @pl.when(jnp.logical_and(c >= 0, c < self.chunks))
            def _():
                bit = self.links[level][1]
                source = self.value if level == 0 else self.held[level - 1]
                for slot, goes in self.order(level):
                    self.copy(level, slot, c).wait_recv()
                    here = self.at(slot, c)
                    total = source[self.at(2 * slot + bit, c)].astype(F32) + self.arrive[level][here].astype(F32)
                    if level == self.levels - 1:
                        self.out[here] = total.astype(self.out.dtype)
                    else:
                        self.held[level][here] = total.astype(self.held[level].dtype)
                        if goes:
                            self.copy(level + 1, slot // 2, c).start()

    def steps(self, lag):
        return self.chunks + (self.levels - 1) * lag

    def finish(self):
        def one(c, carry):
            for level in range(self.levels):
                for slot in range(self.groups >> (level + 1)):
                    self.copy(level, slot, c).wait_send()
            return carry

        lax.fori_loop(0, self.chunks, one, 0)


def return_kernel(groups, rows, chunks, plans, *refs):
    refs = list(refs)

    def take(count):
        taken = refs[:count]
        del refs[:count]
        return taken

    m = dp_bits(groups)
    count = 4 * m - 1
    value, gains = take(2)
    grads = take(len(plans))
    out, gains_out = take(2)
    totals = take(len(plans))
    gains_all, gains_sum, g_s, g_r = take(4)
    task = Scatter(groups, rows, chunks, [value, out] + take(count))
    small = Scatter(groups, 8, 1, [gains_sum, gains_out] + take(count))
    large = [
        Scatter(groups, block, parts, [grad, total] + take(count))
        for (block, parts), grad, total in zip(plans, grads, totals)
    ]
    t = lax.axis_index("tensor")
    for where, _ in task.links:
        greet(where)
    for k in range(1, 4):
        greet({"tensor": lax.rem(t + k, 4)})
    pl.semaphore_wait(pltpu.get_barrier_semaphore(), m + 3)

    def spread(k):
        return remote(gains, gains_all.at[k - 1], g_s.at[k - 1], g_r.at[k - 1], {"tensor": lax.rem(t + k, 4)})

    for k in range(1, 4):
        spread(k).start()
    task.start()
    for item in large:
        item.start()
    for k in range(1, 4):
        spread(k).wait()
    gains_sum[...] = gains[...] + gains_all[0] + gains_all[1] + gains_all[2]
    small.start()

    def body(i, c):
        small.step(i, 1)
        task.step(i, 2)
        for item in large:
            item.step(i, 4)
        return c

    lax.fori_loop(0, max([task.steps(2), small.steps(1)] + [item.steps(4) for item in large]), body, 0)
    small.finish()
    task.finish()
    for item in large:
        item.finish()


def return_rows(value, gains, grads, groups, cid, chunks):
    rows, width = value.shape[0] // groups, value.shape[1]
    vmem = pl.BlockSpec(memory_space=pltpu.VMEM)
    part = gains.shape[1]
    plans, outs = [], [jax.ShapeDtypeStruct((rows, width), BF16), jax.ShapeDtypeStruct((8, part), F32)]
    scratch = [
        pltpu.VMEM((3,) + gains.shape, F32),
        pltpu.VMEM(gains.shape, F32),
        pltpu.SemaphoreType.DMA((3,)),
        pltpu.SemaphoreType.DMA((3,)),
    ]
    scratch += Scatter.scratch(groups, rows, width, chunks, BF16) + Scatter.scratch(groups, 8, part, 1, F32)
    for grad in grads:
        block = grad.shape[0] // groups
        plans.append((block, max(1, block // 48)))
        outs.append(jax.ShapeDtypeStruct((block, grad.shape[1]), F32))
        scratch += Scatter.scratch(groups, block, grad.shape[1], plans[-1][1], BF16)
    return pl.pallas_call(
        functools.partial(return_kernel, groups, rows, chunks, plans),
        out_shape=outs,
        in_specs=[vmem] * (2 + len(grads)),
        out_specs=[vmem] * len(outs),
        scratch_shapes=scratch,
        compiler_params=pltpu.CompilerParams(
            collective_id=cid, has_side_effects=True, vmem_limit_bytes=VMEM_LIMIT
        ),
        name="return_%d" % cid,
    )(value, gains, *grads)


def gather_kernel(groups, count, *refs):
    values, outs = refs[:count], refs[count : 2 * count]
    s_sem, r_sem, own = refs[2 * count :]
    m = dp_bits(groups)
    me = lax.axis_index("dp")
    links = [dp_partner(k) for k in range(m)]
    for where, _ in links:
        greet(where)
    pl.semaphore_wait(pltpu.get_barrier_semaphore(), m)

    def place(a, block):
        rows = values[a].shape[0]
        return outs[a].at[pl.ds(pl.multiple_of(block * rows, rows), rows)]

    def copy(a, level, i, mine):
        where, bit = links[level]
        low = lax.rem(me, 1 << (level + 1))
        if not mine:
            low = low + (1 - 2 * bit) * (1 << level)
        block = i * (1 << (level + 1)) + low
        return remote(place(a, block), place(a, block), s_sem.at[a, level, i], r_sem.at[a, level, i], where)

    locals_ = [pltpu.make_async_copy(values[a], place(a, me), own.at[a]) for a in range(count)]
    for item in locals_:
        item.start()
    for item in locals_:
        item.wait()
    for level in reversed(range(m)):
        for i in range(groups >> (level + 1)):
            for a in range(count):
                copy(a, level, i, True).start()
        for i in range(groups >> (level + 1)):
            for a in range(count):
                copy(a, level, i, False).wait_recv()
    for level in range(m):
        for i in range(groups >> (level + 1)):
            for a in range(count):
                copy(a, level, i, True).wait_send()


def gather_rows(values, groups, cid):
    vmem = pl.BlockSpec(memory_space=pltpu.VMEM)
    m, count = dp_bits(groups), len(values)
    dma = pltpu.SemaphoreType.DMA
    return pl.pallas_call(
        functools.partial(gather_kernel, groups, count),
        out_shape=[jax.ShapeDtypeStruct((groups * v.shape[0], v.shape[1]), v.dtype) for v in values],
        in_specs=[vmem] * count,
        out_specs=[vmem] * count,
        scratch_shapes=[dma((count, m, groups // 2)), dma((count, m, groups // 2)), dma((count,))],
        compiler_params=pltpu.CompilerParams(
            collective_id=cid, has_side_effects=True, vmem_limit_bytes=48 * 2**20
        ),
        name="gather_%d" % cid,
    )(*values)


class OwnScatter(Scatter):
    def __init__(self, groups, rows, chunks, refs):
        m = dp_bits(groups)
        super().__init__(groups, rows, chunks, list(refs[: 2 + m]) + [None] * (m - 1) + list(refs[2 + m :]))
        self.me = lax.axis_index("dp")

    @staticmethod
    def scratch(groups, rows, width, chunks, dtype):
        m = dp_bits(groups)
        kinds = Scatter.scratch(groups, rows, width, chunks, dtype)
        return kinds[:m] + kinds[2 * m - 1 :]

    @staticmethod
    def refs(groups):
        return 3 * dp_bits(groups)

    def whole(self, level, slot, c):
        return self.at(slot * (1 << level) + lax.rem(self.me, 1 << level), c)

    def copy(self, level, slot, c):
        where, bit = self.links[level]
        return remote(
            self.value.at[self.whole(level, 2 * slot + 1 - bit, c)],
            self.arrive[level].at[self.at(slot, c)],
            self.s_sem[level].at[slot, c],
            self.r_sem[level].at[slot, c],
            where,
        )

    def step(self, i, lag):
        for level in range(self.levels):
            c = i - level * lag

            @pl.when(jnp.logical_and(c >= 0, c < self.chunks))
            def _():
                bit = self.links[level][1]
                for slot, goes in self.order(level):
                    self.copy(level, slot, c).wait_recv()
                    here, there = self.whole(level, 2 * slot + bit, c), self.at(slot, c)
                    if level == self.levels - 1:
                        total = self.value[here].astype(F32) + self.arrive[level][there].astype(F32)
                        self.out[self.at(0, c)] = total.astype(self.out.dtype)
                    else:
                        self.value[here] = self.value[here] + self.arrive[level][there]
                        if goes:
                            self.copy(level + 1, slot // 2, c).start()


class Line:
    lag_b, lag_c, lag_o = 2, 4, 5

    def __init__(self, first, half, pieces, part, base, out, scratch, norm=None, moved=None, at=(0, 0, 0), turns=1):
        self.first, self.half, self.size = first, half, half // pieces
        self.each, self.pieces = pieces, pieces * turns
        self.base_at, self.out_at, self.moved_at = at
        self.part, self.base, self.out = part, base, out
        (self.rin, self.smid, self.rmid) = scratch[:3]
        (self.s_up, self.r_up, self.s_mid, self.r_mid, self.s_b1, self.s_b2, self.r_b, self.s_c, self.r_c) = scratch[3:12]
        self.norm, self.moved = norm, moved
        if moved:
            self.arrived, self.shift = moved
            self.s_s, self.r_s = scratch[12:14]
            section = lax.axis_index("section")
            self.sends = section == (0 if self.shift > 0 else 1)
            self.partner = {"section": 1 - section}
        t = lax.axis_index("tensor")
        self.mid = jnp.logical_or(t == 1, t == 2)
        self.outside = jnp.logical_not(self.mid)
        self.outer = {"tensor": jnp.where(t == 1, 0, 3)}
        self.other = {"tensor": jnp.where(t == 1, 2, 1)}
        self.nbr = {"tensor": jnp.where(t == 0, 1, 2)}
        self.near = jnp.where(t < 2, 0, half)
        self.far = half - self.near

    @staticmethod
    def scratch(half, pieces, width, moved, turns=1):
        dma = pltpu.SemaphoreType.DMA
        half, pieces = half * turns, pieces * turns
        kinds = [
            pltpu.VMEM((2 * half, width), BF16),
            pltpu.VMEM((half, width), BF16),
            pltpu.VMEM((half, width), BF16),
            dma((2, pieces)),
            dma((2, pieces)),
        ] + [dma((pieces,))] * 7
        return kinds + ([dma((2, pieces))] * 2 if moved else [])

    @staticmethod
    def greet():
        t = lax.axis_index("tensor")

        @pl.when(t > 0)
        def _():
            greet({"tensor": jnp.maximum(t - 1, 0)})

        @pl.when(t < 3)
        def _():
            greet({"tensor": jnp.minimum(t + 1, 3)})

    def greet_sender(self):
        if self.moved:

            @pl.when(jnp.logical_not(self.sends))
            def _():
                greet(self.partner)

    def enter(self, others):
        bar = pltpu.get_barrier_semaphore()
        count = jnp.where(self.mid, 2, 1) + others
        if self.moved:
            count = count + jnp.where(self.sends, 1, 0)
        pl.semaphore_wait(bar, count)

    def local(self, start, p):
        if self.each < self.pieces:
            start, p = start + (p // self.each) * (2 * self.half), lax.rem(p, self.each)
        return pl.ds(pl.multiple_of(start + p * self.size, self.size), self.size)

    def own(self, p):
        return pl.ds(pl.multiple_of(p * self.size, self.size), self.size)

    def rows(self, start, p, at=0):
        return self.local(self.first + at + start, p)

    def shifted(self, start, p):
        side = start // self.half
        here, there = self.rows(start, p, self.out_at), self.rows(start, p, self.moved_at)
        return remote(self.out.at[here], self.arrived.at[there], self.s_s.at[side, p], self.r_s.at[side, p], self.partner)

    def pass_on(self, start, p):
        if self.moved:

            @pl.when(self.sends)
            def _():
                self.shifted(start, p).start()

    def outcome(self, s_sem, r_sem, where, start, p):
        here = self.rows(start, p, self.out_at)
        return remote(self.out.at[here], self.out.at[here], s_sem.at[p], r_sem.at[p], where)

    def up(self, start, p, k, where):
        return remote(
            self.part.at[self.rows(start, p)], self.rin.at[self.local(start, p)], self.s_up.at[k, p], self.r_up.at[k, p], where
        )

    def cross(self, p):
        return remote(
            self.smid.at[self.own(p)], self.rmid.at[self.own(p)], self.s_mid.at[p], self.r_mid.at[p], self.other
        )

    def start(self, turn=0):
        @pl.when(self.outside)
        def _():
            def begin(p, c):
                self.up(self.far, p, 0, self.nbr).start()
                self.up(self.near, p, 1, self.nbr).start()
                return c

            lax.fori_loop(turn * self.each, (turn + 1) * self.each, begin, 0)

    def outer_step(self, i):
        p = i - self.lag_o

        @pl.when(jnp.logical_and(p >= 0, p < self.pieces))
        def _():
            self.outcome(self.s_b2, self.r_b, self.nbr, self.near, p).wait_recv()
            self.pass_on(self.near, p)
            self.outcome(self.s_c, self.r_c, self.nbr, self.far, p).wait_recv()
            self.pass_on(self.far, p)

    def mid_step(self, i):
        @pl.when(jnp.logical_and(i >= 0, i < self.pieces))
        def _():
            self.up(self.far, i, 0, self.outer).wait_recv()
            total = self.part[self.rows(self.far, i)].astype(F32) + self.rin[self.local(self.far, i)].astype(F32)
            self.smid[self.own(i)] = total.astype(BF16)
            self.cross(i).start()

        j = i - self.lag_b

        @pl.when(jnp.logical_and(j >= 0, j < self.pieces))
        def _():
            self.up(self.near, j, 1, self.outer).wait_recv()
            self.cross(j).wait_recv()
            here = self.rows(self.near, j, self.base_at)
            total = self.part[self.rows(self.near, j)].astype(F32) + self.rin[self.local(self.near, j)].astype(F32)
            total = total + self.rmid[self.own(j)].astype(F32)
            if self.norm:
                xrow, gain, gsum, norm_at = self.norm
                x = xrow[self.rows(self.near, j, norm_at)].astype(F32)
                scale = lax.rsqrt(jnp.mean(x * x, axis=-1, keepdims=True) + epsilon)
                unit = x * scale
                gsum[...] += jnp.sum(total * unit, axis=0, keepdims=True)
                inner = total * gain[...]
                total = scale * (inner - unit * jnp.mean(inner * unit, axis=-1, keepdims=True))
            total = self.base[here].astype(F32) + total
            self.out[self.rows(self.near, j, self.out_at)] = total.astype(BF16)
            self.outcome(self.s_b1, self.r_b, self.other, self.near, j).start()
            self.outcome(self.s_b2, self.r_b, self.outer, self.near, j).start()
            self.pass_on(self.near, j)

        k = i - self.lag_c

        @pl.when(jnp.logical_and(k >= 0, k < self.pieces))
        def _():
            self.outcome(self.s_b1, self.r_b, self.other, self.far, k).wait_recv()
            self.outcome(self.s_c, self.r_c, self.outer, self.far, k).start()
            self.pass_on(self.far, k)

    @property
    def steps(self):
        return self.pieces + self.lag_o

    def step(self, i):
        @pl.when(self.mid)
        def _():
            self.mid_step(i)

        @pl.when(self.outside)
        def _():
            self.outer_step(i)

    def finish(self):
        @pl.when(self.mid)
        def _():
            def one(p, c):
                self.cross(p).wait_send()
                self.outcome(self.s_b1, self.r_b, self.other, self.near, p).wait_send()
                self.outcome(self.s_b2, self.r_b, self.outer, self.near, p).wait_send()
                self.outcome(self.s_c, self.r_c, self.outer, self.far, p).wait_send()
                return c

            lax.fori_loop(0, self.pieces, one, 0)

        @pl.when(self.outside)
        def _():
            def one(p, c):
                self.up(self.far, p, 0, self.nbr).wait_send()
                self.up(self.near, p, 1, self.nbr).wait_send()
                return c

            lax.fori_loop(0, self.pieces, one, 0)

        if self.moved:

            @pl.when(self.sends)
            def _():
                def close(p, c):
                    self.shifted(0, p).wait_send()
                    self.shifted(self.half, p).wait_send()
                    return c

                lax.fori_loop(0, self.pieces, close, 0)

    def receive(self):
        @pl.when(jnp.logical_not(self.sends))
        def _():
            def close(p, c):
                self.shifted(0, p).wait_recv()
                self.shifted(self.half, p).wait_recv()
                return c

            lax.fori_loop(0, self.pieces, close, 0)


def run_steps(begin, end, *planned):
    def body(i, c):
        for step, offset in planned:
            step(i - offset)
        return c

    lax.fori_loop(begin, end, body, 0)


class Gather:
    def __init__(self, groups, rows, out, s_sem, r_sem, first=0, size=None):
        self.first, self.size = first, size or rows
        self.groups, self.rows, self.out, self.s_sem, self.r_sem = groups, rows, out, s_sem, r_sem
        self.levels = dp_bits(groups)
        self.links = [dp_partner(k) for k in range(self.levels)]
        self.me = lax.axis_index("dp")

    @staticmethod
    def scratch(groups):
        return [pltpu.SemaphoreType.DMA((dp_bits(groups), groups // 2))] * 2

    def copy(self, level, i, mine):
        where, bit = self.links[level]
        low = lax.rem(self.me, 1 << (level + 1))
        if not mine:
            low = low + (1 - 2 * bit) * (1 << level)
        block = i * (1 << (level + 1)) + low
        place = self.out.at[pl.ds(pl.multiple_of(block * self.rows + self.first, self.size), self.size)]
        return remote(place, place, self.s_sem.at[level, i], self.r_sem.at[level, i], where)

    def start(self, level):
        for i in range(self.groups >> (level + 1)):
            self.copy(level, i, True).start()

    def arrive(self, level):
        for i in range(self.groups >> (level + 1)):
            self.copy(level, i, False).wait_recv()

    def finish(self):
        for level in range(self.levels):
            for i in range(self.groups >> (level + 1)):
                self.copy(level, i, True).wait_send()


def with_transpose(left, right):
    return lax.dot_general(left, right, (((1,), (1,)), ((), ())), preferred_element_type=F32)


def rows_contract(left, right):
    return lax.dot_general(left, right, (((0,), (0,)), ((), ())), preferred_element_type=F32)


def times(left, right):
    return jnp.dot(left, right, preferred_element_type=F32)


LANES = 128
TILE = 256
WIDE = 512


def lanes(i, size=LANES):
    return pl.ds(pl.multiple_of(i * size, size), size)


def normalize(rows, gain):
    rows = rows.astype(F32)
    scale = lax.rsqrt(jnp.mean(rows * rows, axis=-1, keepdims=True) + epsilon)
    return (rows * scale * gain).astype(BF16)


def normalize_into(target, source, gain, first, count, block=32, source_at=0):
    def one(i, c):
        here = pl.ds(pl.multiple_of(first + i * block, block), block)
        there = pl.ds(pl.multiple_of(source_at + first + i * block, block), block)
        target[here] = normalize(source[there], gain[...])
        return c

    lax.fori_loop(0, count // block, one, 0)


def rolled(value, cosine, sine):
    return value * cosine + pltpu.roll(value, LANES // 2, 1) * sine


def block_rows(keys):
    for rows in (160, 80, 32):
        if rows * keys <= 160 * 1280:
            return rows
    return 16


def score_rows(q, kv, h, g, here, qcode, qstart, kcode):
    scores = with_transpose(q[here, lanes(h)], kv[:, lanes(g)]) * HD ** (-0.5)
    code = kcode[...]
    return scores, jnp.logical_and(code <= qcode[here][:, :1], code >= qstart[here][:, :1])


def load_all(pairs, sems):
    copies = [pltpu.make_async_copy(src, dst, sems.at[i]) for i, (src, dst) in enumerate(pairs)]
    for item in copies:
        item.start()
    return copies


def forward_kernel(groups, q_heads, k_heads, pieces, *refs):
    refs = list(refs)

    def take(count):
        taken = refs[:count]
        del refs[:count]
        return taken

    x, cosine, sine, qcode, qstart, kcode, gain_one, gain_two = take(8)
    far_weights = take(5)
    q, kv, lse, mixed, resid, gate, up, act, y, arrived = take(10)
    near_weights = take(5)
    wqkv, wout, wgate, wup, wdown = near_weights
    part_one, part_two, n1, n2, w_sem = take(5)
    gather = Gather(groups, x.shape[0], kv, *take(2))
    count, width = x.shape
    quarter = count // 4
    lines = []
    for k in range(4):
        first = (k % 2) * 2 * quarter
        source = (part_one, x, resid) if k < 2 else (part_two, resid, y)
        lines.append(
            Line(first, quarter, pieces, *source, take(12 if k < 2 else 14), moved=None if k < 2 else (arrived, 1))
        )
    one_a, one_b, two_a, two_b = lines

    loads = load_all(list(zip(far_weights, near_weights)), w_sem)
    Line.greet()
    two_a.greet_sender()
    for where, _ in gather.links:
        greet(where)
    normalize_into(n1, x, gain_one, 0, count)
    loads[0].wait()

    mine = pl.ds(pl.multiple_of(lax.axis_index("dp") * count, count), count)
    for g in range(k_heads):
        column = (q_heads + g) * LANES
        value = times(n1[...], wqkv[:, column : column + LANES])
        kv[mine, g * LANES : (g + 1) * LANES] = rolled(value, cosine[...], sine[...]).astype(BF16)
        column += k_heads * LANES
        kv[mine, (k_heads + g) * LANES : (k_heads + g + 1) * LANES] = times(
            n1[...], wqkv[:, column : column + LANES]
        ).astype(BF16)

    two_a.enter(gather.levels)

    top = gather.levels - 1
    gather.start(top)

    def queries(h, c):
        value = times(n1[...], wqkv[:, lanes(h)])
        q[:, lanes(h)] = rolled(value, cosine[...], sine[...]).astype(BF16)
        return c

    lax.fori_loop(0, q_heads, queries, 0)
    for level in range(top, -1, -1):
        gather.arrive(level)
        if level:
            gather.start(level - 1)

    rows = block_rows(kv.shape[0])
    blocks = count // rows

    def attend(i, c):
        h, b = i // blocks, lax.rem(i, blocks)
        g = h // (q_heads // k_heads)
        here = pl.ds(pl.multiple_of(b * rows, rows), rows)
        scores, allowed = score_rows(q, kv, h, g, here, qcode, qstart, kcode)
        scores = jnp.where(allowed, scores, negative)
        row_max = jnp.max(scores, axis=-1, keepdims=True)
        expo = jnp.exp(scores - row_max)
        row_total = jnp.sum(expo, axis=-1, keepdims=True)
        prob = (expo * (1.0 / row_total)).astype(BF16)
        mixed[here, lanes(h)] = times(prob, kv[:, lanes(k_heads + g)]).astype(BF16)
        there = pl.ds(pl.multiple_of(h * count + b * rows, rows), rows)
        lse[there] = jnp.broadcast_to(row_max + jnp.log(row_total), (rows, LANES))
        return c

    lax.fori_loop(0, q_heads * blocks, attend, 0)
    loads[1].wait()

    def projected(target, left, right, first, each=None):
        here = pl.ds(first, 2 * quarter)

        def one(i, c):
            target[here, lanes(i, TILE)] = times(left[here], right[:, lanes(i, TILE)]).astype(BF16)
            if each:
                each(i)
            return c

        lax.fori_loop(0, width // TILE, one, 0)

    projected(part_one, mixed, wout, 0)
    one_a.start()
    projected(part_one, mixed, wout, 2 * quarter)
    one_b.start()
    run_steps(0, one_a.steps, (one_a.step, 0), (one_b.step, pieces))
    loads[2].wait()
    loads[3].wait()
    loads[4].wait()

    def hidden(first, each):
        here = pl.ds(first, 2 * quarter)
        normalize_into(n2, resid, gain_two, first, 2 * quarter)

        def one(i, c):
            columns = lanes(i, TILE)
            gate_pre = times(n2[here], wgate[:, columns])
            up_pre = times(n2[here], wup[:, columns])
            gate[here, columns] = gate_pre.astype(BF16)
            up[here, columns] = up_pre.astype(BF16)
            act[here, columns] = (gate_pre * jax.nn.sigmoid(gate_pre) * up_pre).astype(BF16)
            each(i)
            return c

        lax.fori_loop(0, gate.shape[1] // TILE, one, 0)

    tiles = gate.shape[1] // TILE
    done = one_a.steps - pieces
    hidden(0, lambda i: one_b.step(done + i))
    projected(part_two, act, wdown, 0)
    two_a.start()
    run_steps(done + tiles, one_b.steps, (one_b.step, 0))
    hidden(2 * quarter, lambda i: two_a.step(i))
    projected(part_two, act, wdown, 2 * quarter)
    two_b.start()
    run_steps(tiles, two_b.steps + tiles, (two_a.step, 0), (two_b.step, tiles))
    gather.finish()
    for line in lines:
        line.finish()
    two_a.receive()
    two_b.receive()


VMEM_LIMIT = 60 * 2**20


def forward_tick(x, spots, weights, groups, q_heads, k_heads, cid):
    norm_one, wqkv, wout, norm_two, wgate, wup, wdown = weights
    count, width = x.shape
    hidden = wgate.shape[1]
    pieces = 5
    vmem = pl.BlockSpec(memory_space=pltpu.VMEM)
    far = pl.BlockSpec(memory_space=pl.ANY)

    def shape(*dims, dtype=BF16):
        return jax.ShapeDtypeStruct(dims, dtype)

    outs = [
        shape(count, q_heads * LANES),
        shape(groups * count, 2 * k_heads * LANES),
        shape(q_heads * count, LANES, dtype=F32),
        shape(count, q_heads * LANES),
        shape(count, width),
        shape(count, hidden),
        shape(count, hidden),
        shape(count, hidden),
        shape(count, width),
        shape(count, width),
    ]
    far_weights = [wqkv, wout, wgate, wup, wdown]
    scratch = [pltpu.VMEM(item.shape, BF16) for item in far_weights]
    scratch += [pltpu.VMEM((count, width), BF16)] * 4 + [pltpu.SemaphoreType.DMA((5,))]
    scratch += Gather.scratch(groups)
    for k in range(4):
        scratch += Line.scratch(count // 4, pieces, width, k >= 2)
    q, kv, lse, mixed, resid, gate, up, act, y, arrived = pl.pallas_call(
        functools.partial(forward_kernel, groups, q_heads, k_heads, pieces),
        out_shape=outs,
        in_specs=[vmem] * 8 + [far] * 5,
        out_specs=[vmem] * len(outs),
        scratch_shapes=scratch,
        compiler_params=pltpu.CompilerParams(
            collective_id=cid, has_side_effects=True, vmem_limit_bytes=VMEM_LIMIT
        ),
        name="forward_tick",
    )(x, *spots, norm_one[None], norm_two[None], *far_weights)
    return y, arrived, (x, q, kv, lse, mixed, resid, gate, up, act)


def back_ffn_kernel(pieces, *refs):
    dy, gate, up, resid, gain = refs[:5]
    far_weights = refs[5:8]
    dresid, gsum, dgate, dup = refs[8:12]
    wdown, wgate, wup = near_weights = refs[12:15]
    part, w_sem = refs[15:17]
    count, width = dy.shape
    quarter = count // 4
    a, b = [
        Line(k * 2 * quarter, quarter, pieces, part, dy, dresid, refs[17 + 12 * k : 29 + 12 * k], norm=(resid, gain, gsum, 0))
        for k in range(2)
    ]
    loads = load_all(list(zip(far_weights, near_weights)), w_sem)
    Line.greet()
    gsum[...] = jnp.zeros_like(gsum)

    def hidden(first, each=None):
        here = pl.ds(first, 2 * quarter)

        def one(i, c):
            columns = lanes(i, TILE)
            d_act = with_transpose(dy[here], wdown[columns, :])
            gate_pre, up_pre = gate[here, columns].astype(F32), up[here, columns].astype(F32)
            sigma = jax.nn.sigmoid(gate_pre)
            d_silu = d_act * sigma
            dup[here, columns] = (d_silu * gate_pre).astype(BF16)
            dgate[here, columns] = (d_silu * up_pre * (1.0 + gate_pre * (1.0 - sigma))).astype(BF16)
            if each:
                each(i)
            return c

        lax.fori_loop(0, gate.shape[1] // TILE, one, 0)

    def back(first):
        here = pl.ds(first, 2 * quarter)

        def one(i, c):
            columns = lanes(i, TILE)
            total = with_transpose(dgate[here], wgate[columns, :]) + with_transpose(dup[here], wup[columns, :])
            part[here, columns] = total.astype(BF16)
            return c

        lax.fori_loop(0, width // TILE, one, 0)

    loads[0].wait()
    hidden(0)
    loads[1].wait()
    loads[2].wait()
    back(0)
    a.enter(0)
    a.start()
    tiles = gate.shape[1] // TILE
    hidden(2 * quarter, lambda i: a.step(i))
    back(2 * quarter)
    b.start()
    run_steps(tiles, b.steps + tiles, (a.step, 0), (b.step, tiles))
    a.finish()
    b.finish()


def back_ffn(dy, kept, weights, cid):
    norm_one, wqkv, wout, norm_two, wgate, wup, wdown = weights
    x, q, kv, lse, mixed, resid, gate, up, act = kept
    count, width = dy.shape
    pieces = 5
    vmem = pl.BlockSpec(memory_space=pltpu.VMEM)
    far = pl.BlockSpec(memory_space=pl.ANY)
    far_weights = [wdown, wgate, wup]
    scratch = [pltpu.VMEM(item.shape, BF16) for item in far_weights]
    scratch += [pltpu.VMEM((count, width), BF16), pltpu.SemaphoreType.DMA((3,))]
    scratch += Line.scratch(count // 4, pieces, width, False) * 2
    return pl.pallas_call(
        functools.partial(back_ffn_kernel, pieces),
        out_shape=[
            jax.ShapeDtypeStruct((count, width), BF16),
            jax.ShapeDtypeStruct((1, width), F32),
            jax.ShapeDtypeStruct(gate.shape, BF16),
            jax.ShapeDtypeStruct(gate.shape, BF16),
        ],
        in_specs=[vmem] * 5 + [far] * 3,
        out_specs=[vmem] * 4,
        scratch_shapes=scratch,
        compiler_params=pltpu.CompilerParams(
            collective_id=cid, has_side_effects=True, vmem_limit_bytes=VMEM_LIMIT
        ),
        name="back_ffn",
    )(dy, gate, up, resid, norm_two[None], *far_weights)


def back_attn_kernel(groups, q_heads, k_heads, pieces, shift, plans, *refs):
    refs = list(refs)

    def take(count):
        taken = refs[:count]
        del refs[:count]
        return taken

    dresid, x, q, kv, lse, cosine, sine, qcode, qstart, kcode, gain = take(11)
    far_weights = take(2)
    values = take(len(plans))
    dx, gsum, dqkv = take(3)
    (arrived,) = take(1) if shift else (None,)
    totals = take(len(plans))
    wout, wqkv = near_weights = take(2)
    part, dmixed, dkv, w_sem = take(4)
    levels = dp_bits(groups)
    count, width = x.shape
    quarter = count // 4
    keys = kv.shape[0]
    shares, owns, scatters = [], [], []
    for g in range(k_heads):
        share, own = take(2)
        shares.append(share)
        owns.append(own)
        scatters.append(Scatter(groups, count, 5, [share, own] + take(4 * levels - 1)))
    tasks = [
        Scatter(groups, rows, chunks, [value, total] + take(4 * levels - 1))
        for (rows, chunks), value, total in zip(plans, values, totals)
    ]
    moved = (arrived, shift) if shift else None
    a, b = [
        Line(
            k * 2 * quarter,
            quarter,
            pieces,
            part,
            dresid,
            dx,
            take(14 if shift else 12),
            norm=(x, gain, gsum, 0),
            moved=moved,
        )
        for k in range(2)
    ]
    loads = load_all(list(zip(far_weights, near_weights)), w_sem)
    Line.greet()
    for where, _ in scatters[0].links:
        greet(where)
    a.greet_sender()
    gsum[...] = jnp.zeros_like(gsum)
    dkv[...] = jnp.zeros_like(dkv)
    a.enter(levels)
    for task in tasks:
        task.start()
    loads[0].wait()

    def mix(h, c):
        dmixed[:, lanes(h)] = with_transpose(dresid[...], wout[lanes(h), :]).astype(BF16)
        return c

    lax.fori_loop(0, q_heads, mix, 0)
    rows = block_rows(keys)
    blocks = count // rows
    repeat = q_heads // k_heads
    lag = 4
    scale = HD ** (-0.5)

    for g in range(k_heads):

        def one(i, c):
            h, n = g * repeat + i // blocks, lax.rem(i, blocks)
            here = pl.ds(pl.multiple_of(n * rows, rows), rows)
            there = pl.ds(pl.multiple_of(h * count + n * rows, rows), rows)
            scores, allowed = score_rows(q, kv, h, g, here, qcode, qstart, kcode)
            prob = jnp.where(allowed, jnp.exp(scores - lse[there][:, :1]), 0.0)
            dm = dmixed[here, lanes(h)]
            d_prob = with_transpose(dm, kv[:, lanes(k_heads + g)])
            row_dot = jnp.sum(prob * d_prob, axis=-1, keepdims=True)
            d_scores = (prob * (d_prob - row_dot)).astype(BF16)
            d_query = times(d_scores, kv[:, lanes(g)]) * scale
            dqkv[here, lanes(h)] = rolled(d_query, cosine[here], -sine[here]).astype(BF16)
            dkv[:, lanes(g)] += rows_contract(d_scores, q[here, lanes(h)]) * scale
            dkv[:, lanes(k_heads + g)] += rows_contract(prob.astype(BF16), dm)
            for task in tasks:
                task.step(g * repeat * blocks + i, lag)
            return c

        lax.fori_loop(0, repeat * blocks, one, 0)

        def narrow(i, c):
            here = pl.ds(pl.multiple_of(i * LANES, LANES), LANES)
            shares[g][here, :LANES] = dkv[here, lanes(g)].astype(BF16)
            shares[g][here, LANES:] = dkv[here, lanes(k_heads + g)].astype(BF16)
            return c

        lax.fori_loop(0, keys // LANES, narrow, 0)
        scatters[g].start()
    run_steps(0, scatters[0].steps(1), *[(functools.partial(lambda s, i: s.step(i, 1), s), 0) for s in scatters])
    for g in range(k_heads):
        dqkv[:, lanes(q_heads + g)] = rolled(owns[g][:, :LANES], cosine[...], -sine[...]).astype(BF16)
        dqkv[:, lanes(q_heads + k_heads + g)] = owns[g][:, LANES:].astype(BF16)
    loads[1].wait()

    def back(first, each=None):
        here = pl.ds(first, 2 * quarter)

        def one(i, c):
            columns = lanes(i, TILE)
            part[here, columns] = with_transpose(dqkv[here], wqkv[columns, :]).astype(BF16)
            if each:
                each(i)
            return c

        lax.fori_loop(0, width // TILE, one, 0)

    back(0)
    a.start()
    back(2 * quarter)
    b.start()
    begun = q_heads * blocks
    more = [(functools.partial(lambda s, i: s.step(i + begun, lag), s), 0) for s in tasks]
    last = max([b.steps + pieces] + [s.steps(lag) - begun for s in tasks])
    run_steps(0, last, (a.step, 0), (b.step, pieces), *more)
    a.finish()
    b.finish()
    if shift:
        a.receive()
        b.receive()
    for item in scatters + tasks:
        item.finish()


def back_attn(dresid, kept, spots, weights, groups, q_heads, k_heads, cid, shift, sums=()):
    norm_one, wqkv, wout, norm_two, wgate, wup, wdown = weights
    x, q, kv, lse, mixed, resid, gate, up, act = kept
    count, width = x.shape
    keys = kv.shape[0]
    pieces = 5
    vmem = pl.BlockSpec(memory_space=pltpu.VMEM)
    far = pl.BlockSpec(memory_space=pl.ANY)
    outs = [
        jax.ShapeDtypeStruct((count, width), BF16),
        jax.ShapeDtypeStruct((1, width), F32),
        jax.ShapeDtypeStruct((count, wqkv.shape[1]), BF16),
    ]
    if shift:
        outs.append(jax.ShapeDtypeStruct((count, width), BF16))
    scratch = [
        pltpu.VMEM(wout.shape, BF16),
        pltpu.VMEM(wqkv.shape, BF16),
        pltpu.VMEM((count, width), BF16),
        pltpu.VMEM(q.shape, BF16),
        pltpu.VMEM(kv.shape, F32),
        pltpu.SemaphoreType.DMA((2,)),
    ]
    for _ in range(k_heads):
        scratch += [pltpu.VMEM((keys, 2 * LANES), BF16), pltpu.VMEM((count, 2 * LANES), F32)]
        scratch += Scatter.scratch(groups, count, 2 * LANES, 5, BF16)
    plans = []
    for value in sums:
        rows = value.shape[0] // groups
        parts = max(1, min(8, rows // 16))
        while rows % (parts * 16):
            parts -= 1
        plans.append((rows, parts))
        outs.append(jax.ShapeDtypeStruct((rows, value.shape[1]), F32))
        scratch += Scatter.scratch(groups, rows, value.shape[1], parts, BF16)
    scratch += Line.scratch(count // 4, pieces, width, bool(shift)) * 2
    return pl.pallas_call(
        functools.partial(back_attn_kernel, groups, q_heads, k_heads, pieces, shift, plans),
        out_shape=outs,
        in_specs=[vmem] * 11 + [far] * 2 + [vmem] * len(sums),
        out_specs=[vmem] * len(outs),
        scratch_shapes=scratch,
        compiler_params=pltpu.CompilerParams(
            collective_id=cid, has_side_effects=True, vmem_limit_bytes=VMEM_LIMIT
        ),
        name="back_attn_%d" % cid,
    )(dresid, x, q, kv, lse, *spots, norm_one[None], wout, wqkv, *sums)


def announce(sems, neighbours):
    for here, where, k in neighbours:

        @pl.when(here)
        def _():
            pl.semaphore_signal(sems.at[k], inc=1, device_id=where, device_id_type=MESH)


def heard(sems, neighbours):
    for k, (here, _, _) in enumerate(neighbours):

        @pl.when(here)
        def _():
            pl.semaphore_wait(sems.at[k], 1)


def main_kernel(groups, q_heads, k_heads, pieces, *refs):
    refs = list(refs)

    def take(count):
        taken = refs[:count]
        del refs[:count]
        return taken

    cosine, sine, qcode, qstart, kcode, gain_one, gain_two, holder, chosen = take(9)
    own_rows, extra_first, extra_second = take(3)
    far_weights = take(7)
    y_out, dx_out, back_out, normed_one, normed_two = take(5)
    far_state = take(14)
    gsum_one, gsum_two = take(2)
    near_state = xs, q, kv, lse, mixed, resid, gate, up, act, dys, dresid, dgate, dup, dqkv = take(14)
    state_sem = take(1)[0]
    wqkv, wout, wgate, wup, wdown = near_weights = take(5)
    part_one, part_two, normed, y, dmixed, dkv, w_sem, io_sem, meet_sem = take(9)
    levels = dp_bits(groups)
    gather_sems = [take(2) for _ in range(2)]
    line_scratch = [take(12) for _ in range(4)]
    forth_s, forth_r, back_s, back_r = take(4)
    spares, returned = take(2)
    spare = returned.shape[0]
    give_lag = Line.lag_o + pieces
    give = OwnScatter(groups, spare, spare // 32, [spares, returned] + take(OwnScatter.refs(groups)))
    second = Gather(groups, spare, spares, *take(2))
    count, width = part_one.shape
    keys = groups * count
    quarter = count // 4
    half = 2 * quarter
    shares, owns, scatters = [], [], []
    for g in range(k_heads):
        share, own = take(2)
        shares.append(share)
        owns.append(own)
        scatters.append(Scatter(groups, count, 5, [share, own] + take(4 * levels - 1)))
    section = lax.axis_index("section")
    t = lax.axis_index("tensor")
    tiles, wide = gate.shape[1] // WIDE, width // WIDE
    repeat = q_heads // k_heads
    rows = block_rows(keys)
    blocks = half // rows
    scale = HD ** (-0.5)

    def span(first, size):
        return pl.ds(pl.multiple_of(first, 32), size)

    neighbours = [
        (t > 0, {"tensor": jnp.maximum(t - 1, 0)}, 1),
        (t < 3, {"tensor": jnp.minimum(t + 1, 3)}, 0),
    ]
    for k in range(levels):
        neighbours.append((t >= 0, dp_partner(k)[0], 2 + k))

    for _, where, _ in neighbours[2:]:
        greet(where)
    Line.greet()
    greet({"section": 1 - section})

    ends = [0]
    for item in far_weights[:3]:
        ends.append(ends[-1] + item.shape[1])
    parts = [wqkv.at[:, a:b] for a, b in zip(ends, ends[1:])]
    copies = load_all(list(zip(far_weights, parts + list(near_weights[1:]))), w_sem)
    loads = [copies[:3], *[[item] for item in copies[3:]]]

    place = span(lax.axis_index("dp") * spare, spare)
    fetch_first = pltpu.make_async_copy(extra_first, spares, io_sem.at[2])
    fetch_extra = pltpu.make_async_copy(extra_second, spares.at[place], io_sem.at[2])
    fetch_first.start()
    for which, target in enumerate((xs, dys)):

        @pl.when(section == which)
        def _():
            pltpu.make_async_copy(own_rows, target, io_sem.at[0]).start()

    pl.semaphore_wait(pltpu.get_barrier_semaphore(), jnp.where(jnp.logical_or(t == 1, t == 2), 2, 1) + levels + 1)
    announce(meet_sem, neighbours)
    gsum_one[...] = jnp.zeros_like(gsum_one)
    gsum_two[...] = jnp.zeros_like(gsum_two)
    fetch_first.wait()
    brought_first = times(chosen[:count], spares[...])
    for which, target in enumerate((xs, dys)):

        @pl.when(section == which)
        def _():
            pltpu.make_async_copy(own_rows, target, io_sem.at[0]).wait()
            target[:count] = (target[:count].astype(F32) + brought_first).astype(BF16)

    fetch_extra.start()
    fetch_extra.wait()

    def keep(index, slot):
        near, there = near_state[index], far_state[index]
        part = near.shape[0] // 2
        here = span(slot * part, part)
        return pltpu.make_async_copy(near.at[here], there.at[here], state_sem.at[index, slot])

    def projected(target, left, right, first, left_at, each=None):
        here, there = span(first, half), span(first + left_at, half)

        def one(i, c):
            target[here, lanes(i, WIDE)] = times(left[there], right[:, lanes(i, WIDE)]).astype(BF16)
            if each:
                each(i)
            return c

        lax.fori_loop(0, wide, one, 0)

    def give_back(slot, now, line):
        @pl.when(now)
        def _():
            spares[...] = times(holder[span(slot * groups * spare, groups * spare)], y[...]).astype(BF16)
            give.start()

        def one(i, c):
            line.step(i)

            @pl.when(now)
            def _():
                give.step(i, give_lag)

            return c

        lax.fori_loop(0, line.steps, one, 0)

    def give_rest(now, line, begun):
        def one(i, c):
            line.step(i)

            @pl.when(now)
            def _():
                give.step(i - begun + give_lag, give_lag)

            return c

        lax.fori_loop(begun, max(line.steps, begun + give.steps(give_lag) - give_lag), one, 0)

    def given(place, now):
        @pl.when(now)
        def _():
            give.finish()
            pltpu.make_async_copy(returned, back_out.at[span(place * spare, spare)], io_sem.at[1]).start()
            pltpu.make_async_copy(returned, back_out.at[span(place * spare, spare)], io_sem.at[1]).wait()

    def ffn_back(slot, first, each=None):
        here, there = span(first, half), span(slot * count + first, half)

        def one(i, c):
            columns = lanes(i, WIDE)
            d_act = with_transpose(dys[there], wdown[columns, :])
            gate_pre, up_pre = gate[there, columns].astype(F32), up[there, columns].astype(F32)
            sigma = jax.nn.sigmoid(gate_pre)
            d_silu = d_act * sigma
            dup[there, columns] = (d_silu * gate_pre).astype(BF16)
            dgate[there, columns] = (d_silu * up_pre * (1.0 + gate_pre * (1.0 - sigma))).astype(BF16)
            if each:
                each(i)
            return c

        lax.fori_loop(0, tiles, one, 0)

        def two(i, c):
            columns = lanes(i, WIDE)
            total = with_transpose(dgate[there], wgate[columns, :]) + with_transpose(dup[there], wup[columns, :])
            part_one[here, columns] = total.astype(BF16)
            if each:
                each(tiles + i)
            return c

        lax.fori_loop(0, wide, two, 0)

    def back_lines(slot):
        base = slot * count
        made = []
        for k in range(4):
            first = (k % 2) * half
            scratch = list(line_scratch[k])
            if k < 2:
                norm = (resid, gain_two, gsum_two, base)
                made.append(Line(first, quarter, pieces, part_one, dys, dresid, scratch, norm=norm, at=(base, base, 0)))
            else:
                scratch += [back_s.at[k - 2], back_r.at[2 * slot + k - 2]]
                norm = (xs, gain_one, gsum_one, base)
                made.append(
                    Line(
                        first, quarter, pieces, part_two, dresid, y, scratch, norm=norm, moved=(dys, -1), at=(base, 0, base)
                    )
                )
        return made

    def forward_lines(slot):
        base = slot * count
        made = []
        for k in range(4):
            first = (k % 2) * half
            scratch = list(line_scratch[k])
            if k < 2:
                made.append(Line(first, quarter, pieces, part_one, xs, resid, scratch, at=(base, base, 0)))
            else:
                scratch += [forth_s.at[k - 2], forth_r.at[2 * slot + k - 2]]
                made.append(
                    Line(first, quarter, pieces, part_two, resid, y, scratch, moved=(xs, 1), at=(base, 0, base))
                )
        return made

    def gathers_of(slot):
        place = kv.at[span(slot * keys, keys)]
        return [Gather(groups, count, place, *gather_sems[h], h * half, half) for h in range(2)]

    def keep_normed(slot):
        return pltpu.make_async_copy(normed, normed_one.at[span(slot * count, count)], io_sem.at[1])

    def begin(slot, sync):
        base = slot * count
        middle = (q_heads + k_heads) * LANES
        for h, (line, gather) in enumerate(zip(forward_lines(slot)[2:], gathers_of(slot))):
            line.receive()
            normalize_into(normed, xs, gain_one, h * half, half, source_at=base)
            if h == 0:

                @pl.when(slot == 0)
                def _():
                    for item in loads[0]:
                        item.wait()

            here, there = span(h * half, half), span(base + h * half, half)
            mine = span(slot * keys + lax.axis_index("dp") * count + h * half, half)
            value = times(normed[here], wqkv[:, q_heads * LANES : middle])
            for g in range(k_heads):
                columns = slice(g * LANES, (g + 1) * LANES)
                kv[mine, columns] = rolled(value[:, columns], cosine[there], sine[there]).astype(BF16)
            kv[mine, k_heads * LANES :] = times(normed[here], wqkv[:, middle:]).astype(BF16)
            if h == 0 and sync:
                heard(meet_sem, neighbours)
            gather.start(levels - 1)
        keep_normed(slot).start()
        whole = span(base, count)
        for first in range(0, q_heads, 2):
            value = times(normed[...], wqkv[:, first * LANES : (first + 2) * LANES])
            for h in range(2):
                columns = slice((first + h) * LANES, (first + h + 1) * LANES)
                q[whole, columns] = rolled(
                    value[:, h * LANES : (h + 1) * LANES], cosine[whole], sine[whole]
                ).astype(BF16)

    def forward(slot):
        base = slot * count
        whole = span(base, count)
        pending = jnp.logical_and(section == 1, slot == 1)
        left_a, left_b = back_lines(0)[2:]
        one_a, one_b, two_a, two_b = forward_lines(slot)
        gathers = gathers_of(slot)
        keep_one = keep_normed(slot)
        keep_two = pltpu.make_async_copy(normed, normed_two.at[whole], io_sem.at[2])

        @pl.when(jnp.logical_not(pending))
        def _():
            begin(slot, True)

        for level in range(levels - 1, 0, -1):
            for gather in gathers:
                gather.arrive(level)
                gather.start(level - 1)

        @pl.when(pending)
        def _():
            run_steps(0, left_a.steps, (left_a.step, 0))

        for gather in gathers:
            gather.arrive(0)

        @pl.when(slot == 0)
        def _():
            second.start(levels - 1)

        def attend(first, each=None):
            def one(i, c):
                h, b = i // blocks, lax.rem(i, blocks)
                g = h // repeat
                here = span(base + first + b * rows, rows)
                scores = with_transpose(q[here, lanes(h)], kv[span(slot * keys, keys), lanes(g)]) * scale
                code = kcode[slot]
                allowed = jnp.logical_and(code <= qcode[here][:, :1], code >= qstart[here][:, :1])
                scores = jnp.where(allowed, scores, negative)
                row_max = jnp.max(scores, axis=-1, keepdims=True)
                expo = jnp.exp(scores - row_max)
                row_total = jnp.sum(expo, axis=-1, keepdims=True)
                prob = (expo * (1.0 / row_total)).astype(BF16)
                mixed[here, lanes(h)] = times(prob, kv[span(slot * keys, keys), lanes(k_heads + g)]).astype(BF16)
                lse[span((slot * q_heads + h) * count + first + b * rows, rows)] = jnp.broadcast_to(
                    row_max + jnp.log(row_total), (rows, LANES)
                )
                if each:
                    each(i)
                return c

            lax.fori_loop(0, q_heads * blocks, one, 0)

        attend(0)

        @pl.when(slot == 0)
        def _():
            loads[1][0].wait()

        projected(part_one, mixed, wout, 0, base)

        @pl.when(pending)
        def _():
            heard(meet_sem, neighbours)

        one_a.start()

        @pl.when(pending)
        def _():
            run_steps(0, left_b.steps, (left_b.step, 0))
            left_out = pltpu.make_async_copy(y, dx_out.at[:count], io_sem.at[0])
            left_out.start()
            left_a.finish()
            left_b.finish()
            left_out.wait()

        attend(half)
        projected(part_one, mixed, wout, half, base)
        one_b.start()
        run_steps(0, one_a.steps, (one_a.step, 0))

        @pl.when(slot == 0)
        def _():
            for (item,) in loads[2:]:
                item.wait()
            for level in range(levels - 1, 0, -1):
                second.arrive(level)
                second.start(level - 1)

        def hidden(first, each):
            here, there = span(first, half), span(base + first, half)
            normalize_into(normed, resid, gain_two, first, half, source_at=base)

            def one(i, c):
                columns = lanes(i, WIDE)
                gate_pre = times(normed[here], wgate[:, columns])
                up_pre = times(normed[here], wup[:, columns])
                gate[there, columns] = gate_pre.astype(BF16)
                up[there, columns] = up_pre.astype(BF16)
                act[there, columns] = (gate_pre * jax.nn.sigmoid(gate_pre) * up_pre).astype(BF16)
                each(i)
                return c

            lax.fori_loop(0, tiles, one, 0)

        keep_one.wait()
        hidden(0, one_b.step)

        @pl.when(section == 0)
        def _():
            projected(part_two, act, wdown, 0, base)
            two_a.start()

        @pl.when(slot == 0)
        def _():
            second.arrive(0)
            brought = times(chosen[count:], spares[...])
            for which, target in enumerate((xs, dys)):

                @pl.when(section == which)
                def _():
                    target[count:] = (target[count:].astype(F32) + brought).astype(BF16)

        @pl.when(section == 1)
        def _():
            one_a.finish()
            ffn_back(slot, 0, lambda i: one_b.step(tiles + i))
            run_steps(2 * tiles + wide, one_b.steps, (one_b.step, 0))

        @pl.when(section == 0)
        def _():
            run_steps(tiles, one_b.steps, (one_b.step, 0))

        @pl.when(section == 1)
        def _():
            one_b.finish()
            for gather in gathers:
                gather.finish()
            announce(meet_sem, neighbours)

        def early(i):
            @pl.when(section == 0)
            def _():
                two_a.step(i)

        hidden(half, early)
        keep_two.start()
        out = pltpu.make_async_copy(y, y_out.at[whole], io_sem.at[0])

        @pl.when(section == 0)
        def _():
            projected(part_two, act, wdown, half, base)
            two_b.start()
            run_steps(tiles, two_a.steps, (two_a.step, 0))
            run_steps(0, two_b.steps, (two_b.step, 0))
            out.start()
            two_a.finish()
            two_b.finish()
            for gather in gathers:
                gather.finish()
            one_a.finish()
            one_b.finish()

        keep_two.wait()

        @pl.when(slot == 0)
        def _():
            second.finish()

        for index in range(9):
            keep(index, slot).start()

        @pl.when(section == 0)
        def _():
            out.wait()
            announce(meet_sem, neighbours)

    def backward(slot):
        giving = jnp.logical_and(section == 1, slot == 1)
        later = jnp.logical_and(section == 1, slot == 0)
        base = slot * count
        whole = span(base, count)
        lines = back_lines(slot)
        one_a, one_b, two_a, two_b = lines
        two_a.receive()
        two_b.receive()
        dkv[...] = jnp.zeros_like(dkv)
        heard(meet_sem, neighbours)

        @pl.when(section == 0)
        def _():
            ffn_back(slot, 0)

        one_a.start()
        ffn_back(slot, half)
        one_b.start()
        give_back(0, giving, one_a)

        def attend(first, g, each=None):
            def one(i, c):
                h, n = g * repeat + i // blocks, lax.rem(i, blocks)
                here = span(base + first + n * rows, rows)
                near = span(first + n * rows, rows)
                k_rows = kv[span(slot * keys, keys), lanes(g)]
                scores = with_transpose(q[here, lanes(h)], k_rows) * scale
                code = kcode[slot]
                allowed = jnp.logical_and(code <= qcode[here][:, :1], code >= qstart[here][:, :1])
                known = lse[span((slot * q_heads + h) * count + first + n * rows, rows)][:, :1]
                prob = jnp.where(allowed, jnp.exp(scores - known), 0.0)
                dm = dmixed[near, lanes(h)]
                d_prob = with_transpose(dm, kv[span(slot * keys, keys), lanes(k_heads + g)])
                row_dot = jnp.sum(prob * d_prob, axis=-1, keepdims=True)
                d_scores = (prob * (d_prob - row_dot)).astype(BF16)
                d_query = times(d_scores, k_rows) * scale
                dqkv[here, lanes(h)] = rolled(d_query, cosine[here], -sine[here]).astype(BF16)
                dkv[lanes(g), :] += rows_contract(q[here, lanes(h)], d_scores) * scale
                dkv[lanes(k_heads + g), :] += rows_contract(dm, prob.astype(BF16))
                if each:
                    each(i)
                return c

            lax.fori_loop(0, repeat * blocks, one, 0)

        def mix(first):
            here, there = span(first, half), span(base + first, half)

            def one(h, c):
                dmixed[here, lanes(h)] = with_transpose(dresid[there], wout[lanes(h), :]).astype(BF16)
                return c

            lax.fori_loop(0, q_heads, one, 0)

        mix(0)
        turns = repeat * blocks
        for g in range(k_heads):
            attend(0, g, lambda i: one_b.step(g * turns + i))
        give_rest(giving, one_b, k_heads * turns)
        mix(half)
        for g in range(k_heads):
            attend(half, g)

            shares[g][:, :LANES] = jnp.transpose(dkv[lanes(g), :]).astype(BF16)
            shares[g][:, LANES:] = jnp.transpose(dkv[lanes(k_heads + g), :]).astype(BF16)
            scatters[g].start()
        far = give_lag
        everyone = [(functools.partial(lambda s, i: s.step(i, far), s), 0) for s in scatters]
        run_steps(0, scatters[0].chunks, *everyone)

        @pl.when(later)
        def _():
            begin(1, False)

        run_steps(far, far + scatters[0].chunks, *everyone)
        for g in range(k_heads):
            dqkv[whole, lanes(q_heads + g)] = rolled(owns[g][:, :LANES], cosine[whole], -sine[whole]).astype(BF16)
            dqkv[whole, lanes(q_heads + k_heads + g)] = owns[g][:, LANES:].astype(BF16)

        def back(first, each=None):
            here, there = span(first, half), span(base + first, half)

            def one(i, c):
                columns = lanes(i, WIDE)
                part_two[here, columns] = with_transpose(dqkv[there], wqkv[columns, :]).astype(BF16)
                if each:
                    each(i)
                return c

            lax.fori_loop(0, wide, one, 0)

        back(0)
        two_a.start()
        back(half)
        two_b.start()

        @pl.when(jnp.logical_not(later))
        def _():
            run_steps(0, two_a.steps, (two_a.step, 0))
            run_steps(0, two_b.steps, (two_b.step, 0))
            out = pltpu.make_async_copy(y, dx_out.at[whole], io_sem.at[0])
            out.start()
            two_a.finish()
            two_b.finish()
            out.wait()

        one_a.finish()
        one_b.finish()
        for item in scatters:
            item.finish()
        given(2, giving)
        for index in range(9, 14):
            keep(index, slot).start()
        announce(meet_sem, neighbours)

    def give_alone(slot, place):
        heard(meet_sem, neighbours)
        spares[...] = times(holder[slot * groups * spare : (slot + 1) * groups * spare], y[...]).astype(BF16)
        give.start()
        run_steps(0, give.steps(give_lag), (lambda i: give.step(i, give_lag), 0))
        given(place, section == 0)
        announce(meet_sem, neighbours)

    def turn(k, carry):
        @pl.when(jnp.where(section == 0, k < 2, lax.rem(k, 2) == 0))
        def _():
            forward(jnp.where(section == 0, jnp.minimum(k, 1), k // 2))

        @pl.when(jnp.logical_and(section == 0, k == 2))
        def _():
            give_alone(1, 1)
            again = pltpu.make_async_copy(y_out.at[:count], y, io_sem.at[0])
            again.start()
            again.wait()
            give_alone(0, 0)

        @pl.when(jnp.where(section == 0, k == 2, lax.rem(k, 2) == 1))
        def _():
            backward(jnp.where(section == 0, 0, k // 2))

        return carry

    lax.fori_loop(0, 3 + section, turn, 0)

    @pl.when(section == 0)
    def _():
        give_alone(0, 2)

    heard(meet_sem, neighbours)
    for k in range(2):
        Line(
            k * half,
            quarter,
            pieces,
            part_two,
            dresid,
            y,
            list(line_scratch[2 + k]) + [back_s.at[k], back_r.at[2 + k]],
            moved=(dys, -1),
            at=(0, 0, count),
        ).receive()
    for index in range(14):
        keep(index, 0).wait()
        if index < 9:
            keep(index, 1).wait()

    @pl.when(section > 0)
    def _():
        for index in range(9, 14):
            keep(index, 1).wait()

    @pl.when(section == 0)
    def _():
        keep(9, 1).start()
        keep(9, 1).wait()


def main_ticks(rows, spots, holder, weights, qkv, groups, q_heads, k_heads, cid):
    norm_one, wqkv, wout, norm_two, wgate, wup, wdown = weights
    own_rows, extra_first, extra_second, chosen = rows
    count, width = own_rows.shape[0] // 2, own_rows.shape[1]
    hidden, keys = wgate.shape[1], groups * count
    pieces = 5
    vmem = pl.BlockSpec(memory_space=pltpu.VMEM)
    far = pl.BlockSpec(memory_space=pl.ANY)
    dma = pltpu.SemaphoreType.DMA

    def shape(columns, rows=2 * count, dtype=BF16):
        return jax.ShapeDtypeStruct((rows, columns), dtype)

    heads, both = q_heads * LANES, (q_heads + 2 * k_heads) * LANES
    spare = holder.shape[0] // (2 * groups)
    outs = [
        shape(width),
        shape(width),
        shape(width, 3 * spare),
        shape(width),
        shape(width),
    ]
    state = [
        shape(width),
        shape(heads),
        shape(2 * k_heads * LANES, 2 * keys),
        shape(LANES, 2 * q_heads * count, F32),
        shape(heads),
        shape(width),
        shape(hidden),
        shape(hidden),
        shape(hidden),
        shape(width),
        shape(width),
        shape(hidden),
        shape(hidden),
        shape(both),
    ]
    outs += state + [shape(width, 1, F32)] * 2
    near_weights = [wqkv, wout, wgate, wup, wdown]
    far_weights = [*qkv, wout, wgate, wup, wdown]
    scratch = [pltpu.VMEM(item.shape, item.dtype) for item in state] + [dma((14, 2))]
    scratch += [pltpu.VMEM(item.shape, BF16) for item in near_weights]
    scratch += [pltpu.VMEM((count, width), BF16)] * 4 + [
        pltpu.VMEM((count, heads), BF16),
        pltpu.VMEM((2 * k_heads * LANES, keys), F32),
        dma((7,)),
        dma((3,)),
        pltpu.SemaphoreType.REGULAR((2 + dp_bits(groups),)),
    ]
    scratch += Gather.scratch(groups) * 2
    for k in range(4):
        scratch += Line.scratch(quarter_rows(count), pieces, width, False)
    scratch += [dma((2, 2, pieces)), dma((4, 2, pieces))] * 2
    scratch += [pltpu.VMEM((groups * spare, width), BF16), pltpu.VMEM((spare, width), BF16)]
    scratch += OwnScatter.scratch(groups, spare, width, spare // 32, BF16)
    scratch += Gather.scratch(groups)
    for _ in range(k_heads):
        scratch += [pltpu.VMEM((keys, 2 * LANES), BF16), pltpu.VMEM((count, 2 * LANES), F32)]
        scratch += Scatter.scratch(groups, count, 2 * LANES, 5, BF16)
    return pl.pallas_call(
        functools.partial(main_kernel, groups, q_heads, k_heads, pieces),
        out_shape=outs,
        in_specs=[vmem] * 9 + [far] * 10,
        out_specs=[far] * (len(outs) - 2) + [vmem] * 2,
        scratch_shapes=scratch,
        compiler_params=pltpu.CompilerParams(
            collective_id=cid, has_side_effects=True, vmem_limit_bytes=VMEM_LIMIT
        ),
        name="main_ticks",
    )(*spots, norm_one[None], norm_two[None], holder, chosen, own_rows, extra_first, extra_second, *far_weights)


def quarter_rows(count):
    return count // 4


def weight_job(target, left, right, i, block=256):
    here = lanes(i, block)
    target[here, :] = rows_contract(left[:, here], right[...]).astype(BF16)


def last_ffn_kernel(groups, pieces, chunks, *refs):
    refs = list(refs)

    def take(count):
        taken = refs[:count]
        del refs[:count]
        return taken

    gain, holder = take(2)
    sources = take(15)
    last_dresid, gsum, g_up, down_sum, gate_sum, y, returned, returned_dx = take(8)
    wdown, wgate, wup, dys, act, gate, up, dgate, dup, resid = kept = take(10)
    n2, part, g_down, g_gate, spares, spares_dx, dx, w_sem = take(8)
    line_scratch = [take(12) for _ in range(4)]
    count, width = last_dresid.shape
    half = count // 2
    line_a, line_b = [
        Line(
            k * half,
            half // 2,
            pieces,
            part,
            dys,
            last_dresid,
            line_scratch[k],
            norm=(resid, gain, gsum, count),
            at=(count, 0, 0),
        )
        for k in range(2)
    ]
    results = [Line(k * half, half // 2, pieces, part, resid, y, line_scratch[k]) for k in range(4)]
    down = OwnScatter(groups, width // groups, chunks, [g_down, down_sum] + take(OwnScatter.refs(groups)))
    gated = OwnScatter(groups, width // groups, chunks, [g_gate, gate_sum] + take(OwnScatter.refs(groups)))
    spare = returned.shape[0]
    give = OwnScatter(groups, spare, spare // 32, [spares, returned] + take(OwnScatter.refs(groups)))
    give_dx = OwnScatter(groups, spare, spare // 32, [spares_dx, returned_dx] + take(OwnScatter.refs(groups)))
    load_dx = pltpu.make_async_copy(sources[14].at[count:], dx, w_sem.at[16])
    section = lax.axis_index("section")
    mine = section == 0
    tiles, wide, blocks = act.shape[1] // WIDE, width // WIDE, width // TILE

    def load(k):
        if k in (7, 8):
            return pltpu.make_async_copy(sources[k].at[:count], kept[k].at[:count], w_sem.at[k])
        return pltpu.make_async_copy(sources[k], kept[k], w_sem.at[k])

    lacks = [
        pltpu.make_async_copy(sources[7].at[count:], kept[7].at[count:], w_sem.at[10]),
        pltpu.make_async_copy(sources[8].at[count:], kept[8].at[count:], w_sem.at[11]),
        pltpu.make_async_copy(sources[10].at[count:], last_dresid, w_sem.at[12]),
    ]
    known = [
        pltpu.make_async_copy(sources[11], y, w_sem.at[13]),
        pltpu.make_async_copy(sources[12].at[:spare], returned, w_sem.at[14]),
    ]
    loads = [load(k) for k in range(10)] + [pltpu.make_async_copy(sources[13], n2, w_sem.at[15])]
    @pl.when(section > 0)
    def _():
        load_dx.start()

    for k in (3, 0, 5, 6, 1, 2, 4, 9, 10, 7, 8):
        loads[k].start()

    @pl.when(section > 0)
    def _():
        for item in lacks:
            item.start()

    @pl.when(mine)
    def _():
        for item in known:
            item.start()

    Line.greet()
    for where, _ in down.links:
        greet(where)
    gsum[...] = jnp.zeros_like(gsum)
    line_a.enter(down.levels)
    for k in (3, 0, 5, 6):
        loads[k].wait()

    def hidden(first):
        here = pl.ds(count + first, half)

        def one(i, c):
            columns = lanes(i, WIDE)
            d_act = with_transpose(dys[here], wdown[columns, :])
            gate_pre, up_pre = gate[here, columns].astype(F32), up[here, columns].astype(F32)
            sigma = jax.nn.sigmoid(gate_pre)
            d_silu = d_act * sigma
            dup[here, columns] = (d_silu * gate_pre).astype(BF16)
            dgate[here, columns] = (d_silu * up_pre * (1.0 + gate_pre * (1.0 - sigma))).astype(BF16)
            return c

        lax.fori_loop(0, tiles, one, 0)

    def back(first):
        here, there = pl.ds(first, half), pl.ds(count + first, half)

        def one(i, c):
            columns = lanes(i, WIDE)
            total = with_transpose(dgate[there], wgate[columns, :]) + with_transpose(dup[there], wup[columns, :])
            part[here, columns] = total.astype(BF16)
            return c

        lax.fori_loop(0, wide, one, 0)

    @pl.when(mine)
    def _():
        hidden(0)

    loads[1].wait()
    loads[2].wait()

    @pl.when(mine)
    def _():
        back(0)
        line_a.start()

    loads[4].wait()

    late = 100

    def begin_results(which):
        for k in which:
            here = pl.ds(k * half, half)

            def one(i, c):
                part[here, lanes(i, WIDE)] = times(act[here], wdown[:, lanes(i, WIDE)]).astype(BF16)
                return c

            lax.fori_loop(0, wide, one, 0)
            results[k].start()

    @pl.when(section > 0)
    def _():
        load_dx.wait()
        spares_dx[...] = times(holder[groups * spare :], dx[...]).astype(BF16)
        give_dx.start()
        begin_results((0, 1))
        run_steps(0, give_dx.chunks, (lambda i: give_dx.step(i, late), 0))

    def down_job(i, c):
        weight_job(g_down, dys, act, i)
        return c

    lax.fori_loop(0, blocks, down_job, 0)
    down.start()

    @pl.when(section > 0)
    def _():
        begin_results((2, 3))
        loads[9].wait()

    @pl.when(mine)
    def _():
        hidden(half)
        back(half)
        line_b.start()

    @pl.when(mine)
    def _():
        loads[9].wait()

    for k in (10, 7, 8):
        loads[k].wait()

    @pl.when(section > 0)
    def _():
        lacks[0].wait()
        lacks[1].wait()

    spans = 0

    first_done = line_a.steps + pieces

    def step(i, c):
        @pl.when(mine)
        def _():
            line_a.step(i)
            line_b.step(i - line_a.steps)

        @pl.when(section > 0)
        def _():
            for k, item in enumerate(results):
                item.step(i - k * pieces)

            @pl.when(i == first_done)
            def _():
                spares[...] = times(holder[: groups * spare], y[:count]).astype(BF16)
                give.start()

            give.step(i - first_done, late)

        @pl.when(i < late)
        def _():
            down.step(i, late)
            gated.step(i - spans - blocks, late)

        @pl.when(jnp.logical_and(i >= spans, i < spans + blocks))
        def _():
            weight_job(g_gate, n2, dgate, i - spans)

        @pl.when(i == spans + blocks - 1)
        def _():
            gated.start()

        @pl.when(jnp.logical_and(i >= spans + blocks, i < spans + 2 * blocks))
        def _():
            weight_job(g_up, n2, dup, i - spans - blocks)

        return c

    enough = max(line_a.steps + line_b.steps, spans + 2 * blocks, spans + blocks + chunks)
    lax.fori_loop(0, jnp.where(mine, enough, max(enough, line_a.steps + 3 * pieces, first_done + give.chunks)), step, 0)
    run_steps(late, late + chunks, (lambda i: down.step(i, late), 0), (lambda i: gated.step(i, late), 0))

    @pl.when(mine)
    def _():
        line_a.finish()
        line_b.finish()

        for item in known:
            item.wait()

    @pl.when(section > 0)
    def _():
        lacks[2].wait()
        run_steps(late, late + give.chunks, (lambda i: give_dx.step(i, late), 0))
        run_steps(late, late + give.chunks, (lambda i: give.step(i, late), 0))
        give.finish()
        give_dx.finish()
        for item in results:
            item.finish()

    down.finish()
    gated.finish()


def last_ffn(known, holder, weights, groups, cid):
    norm_one, wqkv, wout, norm_two, wgate, wup, wdown = weights
    dys, act, gate, up, dgate, dup, resid, dresid, y, y_back, normed_two, dx = known
    spare = holder.shape[0] // (2 * groups)
    count, width = dys.shape[0] // 2, dys.shape[1]
    hidden = act.shape[1]
    pieces, chunks = 5, 8
    vmem = pl.BlockSpec(memory_space=pltpu.VMEM)
    far = pl.BlockSpec(memory_space=pl.ANY)
    sources = [wdown, wgate, wup, dys, act, gate, up, dgate, dup, resid]
    scratch = [pltpu.VMEM(item.shape, BF16) for item in sources]
    scratch += [
        pltpu.VMEM((2 * count, width), BF16),
        pltpu.VMEM((2 * count, width), BF16),
        pltpu.VMEM((width, hidden), BF16),
        pltpu.VMEM((width, hidden), BF16),
        pltpu.VMEM((groups * spare, width), BF16),
        pltpu.VMEM((groups * spare, width), BF16),
        pltpu.VMEM((count, width), BF16),
        pltpu.SemaphoreType.DMA((17,)),
    ]
    scratch += Line.scratch(count // 4, pieces, width, False) * 4
    scratch += OwnScatter.scratch(groups, width // groups, hidden, chunks, BF16) * 2
    scratch += OwnScatter.scratch(groups, spare, width, spare // 32, BF16) * 2
    return pl.pallas_call(
        functools.partial(last_ffn_kernel, groups, pieces, chunks),
        out_shape=[
            jax.ShapeDtypeStruct((count, width), BF16),
            jax.ShapeDtypeStruct((1, width), F32),
            jax.ShapeDtypeStruct((width, hidden), BF16),
            jax.ShapeDtypeStruct((width // groups, hidden), BF16),
            jax.ShapeDtypeStruct((width // groups, hidden), BF16),
            jax.ShapeDtypeStruct((2 * count, width), BF16),
            jax.ShapeDtypeStruct((spare, width), BF16),
            jax.ShapeDtypeStruct((spare, width), BF16),
        ],
        in_specs=[vmem] * 2 + [far] * 15,
        out_specs=[vmem] * 8,
        scratch_shapes=scratch,
        compiler_params=pltpu.CompilerParams(
            collective_id=cid, has_side_effects=True, vmem_limit_bytes=VMEM_LIMIT
        ),
        name="last_ffn",
    )(norm_two[None], holder, *sources, dresid, y, y_back, normed_two, dx)


def last_attn_kernel(groups, q_heads, k_heads, pieces, chunks, spare_chunks, *refs):
    refs = list(refs)

    def take(count):
        taken = refs[:count]
        del refs[:count]
        return taken

    cosine, sine, qcode, qstart, kcode, gain, dresid, holder, gain_one, gain_two, gain_last, spread_q, spread_k, spread_v, spread_o = take(15)
    sources = take(10)
    dx_known, y, y_back, normed_one, back_known = take(5)
    dx, returned, returned_y, gains_out, up_sum, attn_sum = take(6)
    wout, wqkv, x, q, kv, lse, mixed, dqkv, other_dresid, g_up = kept = take(10)
    plain, plain_mixed = take(2)
    part, dmixed, dkv, n1, g_attn, spares, spares_y, gsum, gains_own, gains_all, gains_sum, w_sem, g_s, g_r = take(14)
    levels = dp_bits(groups)
    count, width = part.shape
    half = count // 2
    keys = kv.shape[0]
    shares, owns, scatters = [], [], []
    for g in range(k_heads):
        share, own = take(2)
        shares.append(share)
        owns.append(own)
        scatters.append(OwnScatter(groups, count, 5, [share, own] + take(OwnScatter.refs(groups))))
    block = width // groups
    up_task, attn_task = [
        OwnScatter(groups, block, chunks, [value, total] + take(OwnScatter.refs(groups)))
        for value, total in ((g_up, up_sum), (g_attn, attn_sum))
    ]
    spare = spares.shape[0] // groups
    back_task = OwnScatter(groups, spare, spare_chunks, [spares, returned] + take(OwnScatter.refs(groups)))
    give_y = OwnScatter(groups, spare, spare_chunks, [spares_y, returned_y] + take(OwnScatter.refs(groups)))
    small = OwnScatter(groups, 8, 1, [gains_sum, gains_out] + take(OwnScatter.refs(groups)))
    line_a, line_b = [
        Line(k * half, half // 2, pieces, part, dresid, dx, take(12), norm=(x, gain, gsum, count)) for k in range(2)
    ]
    section, t = lax.axis_index("section"), lax.axis_index("tensor")
    mine = section == 0
    order = [9, 0, 3, 4, 5, 1, 2, 6, 7, 8]

    def load(k):
        here, there = sources[k].at[sources[k].shape[0] - kept[k].shape[0] :], kept[k]
        if k in (7, 8):
            here, there = sources[k].at[:count], kept[k].at[:count]
        return pltpu.make_async_copy(here, there, w_sem.at[k])

    lack = pltpu.make_async_copy(sources[7].at[count:], dqkv.at[count:], w_sem.at[13])
    loads = [load(k) for k in range(10)]
    for k in order:
        loads[k].start()
    known = pltpu.make_async_copy(dx_known.at[count:], dx, w_sem.at[11])
    known_back = pltpu.make_async_copy(back_known, returned, w_sem.at[14])
    load_n1 = pltpu.make_async_copy(normed_one, n1, w_sem.at[10])
    load_n1.start()
    known_y = pltpu.make_async_copy(y_back.at[spare : 2 * spare], returned_y, w_sem.at[12])
    load_y = pltpu.make_async_copy(y.at[count:], part, w_sem.at[12])

    @pl.when(mine)
    def _():
        known_y.start()

    @pl.when(section > 0)
    def _():
        known.start()
        lack.start()
        known_back.start()

    for k in range(1, 4):
        greet({"tensor": lax.rem(t + k, 4)})
    for where, _ in up_task.links:
        greet(where)
    gsum[...] = jnp.zeros_like(gsum)
    dkv[...] = jnp.zeros_like(dkv)
    pl.semaphore_wait(pltpu.get_barrier_semaphore(), 3 + levels)
    loads[9].wait()
    up_task.start()
    for k in (0, 3, 4, 5):
        loads[k].wait()

    wide, jobs = width // WIDE, width // TILE
    repeat = q_heads // k_heads
    rows = block_rows(keys)
    blocks = half // rows
    turns = repeat * blocks
    scale = HD ** (-0.5)
    late = 100
    begun = 2 * k_heads * turns

    def early(i):
        @pl.when(lax.rem(i, 2) == 1)
        def _():
            up_task.step(i // 2, late)

    def mix(first):
        here = pl.ds(first, half)

        def one(h, c):
            dmixed[here, lanes(h)] = with_transpose(dresid[here], wout[lanes(h), :]).astype(BF16)
            return c

        lax.fori_loop(0, q_heads, one, 0)

    def attend(first, g, each):
        heads = [g * repeat + r for r in range(repeat)]

        def one(n, c):
            here = pl.ds(pl.multiple_of(first + n * rows, rows), rows)
            there = pl.ds(pl.multiple_of(count + first + n * rows, rows), rows)
            stacked = jnp.concatenate([q[here, lanes(h)] for h in heads], axis=0)
            scores = with_transpose(stacked, kv[:, lanes(g)]) * scale
            code = kcode[...]
            upper = jnp.concatenate([qcode[here][:, :1]] * repeat, axis=0)
            lower = jnp.concatenate([qstart[here][:, :1]] * repeat, axis=0)
            allowed = jnp.logical_and(code <= upper, code >= lower)
            known = jnp.concatenate(
                [lse[pl.ds(pl.multiple_of(h * count + first + n * rows, rows), rows)][:, :1] for h in heads], axis=0
            )
            prob = jnp.where(allowed, jnp.exp(scores - known), 0.0)
            dm = jnp.concatenate([dmixed[here, lanes(h)] for h in heads], axis=0)
            d_prob = with_transpose(dm, kv[:, lanes(k_heads + g)])
            row_dot = jnp.sum(prob * d_prob, axis=-1, keepdims=True)
            d_scores = (prob * (d_prob - row_dot)).astype(BF16)
            d_query = times(d_scores, kv[:, lanes(g)]) * scale
            for r, h in enumerate(heads):
                turned = rolled(d_query[r * rows : (r + 1) * rows], cosine[here], -sine[here])
                dqkv[there, lanes(h)] = turned.astype(BF16)
            dkv[lanes(g), :] += rows_contract(stacked, d_scores) * scale
            dkv[lanes(k_heads + g), :] += rows_contract(dm, prob.astype(BF16))
            for r in range(repeat):
                each(n * repeat + r)
            return c

        lax.fori_loop(0, blocks, one, 0)

    def back(first):
        here, there = pl.ds(first, half), pl.ds(count + first, half)

        def one(i, c):
            columns = lanes(i, WIDE)
            part[here, columns] = with_transpose(dqkv[there], wqkv[columns, :]).astype(BF16)
            return c

        lax.fori_loop(0, wide, one, 0)

    @pl.when(mine)
    def _():
        mix(0)
        mix(half)
        for g in range(k_heads):
            for first in (0, half):
                at = 2 * g * turns + (turns if first else 0)
                attend(first, g, lambda i: early(at + i))

            shares[g][:, :LANES] = jnp.transpose(dkv[lanes(g), :]).astype(BF16)
            shares[g][:, LANES:] = jnp.transpose(dkv[lanes(k_heads + g), :]).astype(BF16)
            scatters[g].start()
        run_steps(0, scatters[0].chunks, *[(functools.partial(lambda s, i: s.step(i, late), s), 0) for s in scatters])

    @pl.when(section > 0)
    def _():
        run_steps(0, begun, (early, 0))
        known.wait()
        lack.wait()

    ends = [0]
    for item in (spread_q, spread_k, spread_v, spread_o):
        ends.append(ends[-1] + item.shape[0])
    starts = [0, q_heads, q_heads + k_heads, q_heads + 2 * k_heads]

    @pl.when(section > 0)
    def _():
        load_y.start()
        load_y.wait()
        spares_y[...] = times(holder[...], part[...]).astype(BF16)
        give_y.start()

    for k in (1, 2, 6, 7, 8):
        loads[k].wait()
    load_n1.wait()
    plain_mixed[...] = with_transpose(mixed[...], spread_o[...]).astype(BF16)
    other_dresid[count:] = dresid[...]

    def out_job(i, c):
        here = lanes(i, TILE)
        g_attn[here, ends[3] :] = rows_contract(other_dresid[:, here], plain_mixed[...]).astype(BF16)
        return c

    lax.fori_loop(0, jobs, out_job, 0)

    @pl.when(mine)
    def _():
        ending = late + scatters[0].chunks
        run_steps(late, ending, *[(functools.partial(lambda s, i: s.step(i, late), s), 0) for s in scatters])
        for g in range(k_heads):
            dqkv[count:, lanes(q_heads + g)] = rolled(owns[g][:, :LANES], cosine[...], -sine[...]).astype(BF16)
            dqkv[count:, lanes(q_heads + k_heads + g)] = owns[g][:, LANES:].astype(BF16)
        back(0)
        line_a.start()
        back(half)
        line_b.start()

    def spread(k):
        return remote(gains_own, gains_all.at[k - 1], g_s.at[k - 1], g_r.at[k - 1], {"tensor": lax.rem(t + k, 4)})

    first_job = begun // 2

    def step(i, c):
        @pl.when(mine)
        def _():
            line_a.step(i)
            line_b.step(i - line_a.steps)

        up_task.step(i + first_job, late)

        @pl.when(i == 0)
        def _():
            for a, b, n, item in zip(starts, starts[1:], ends, (spread_q, spread_k, spread_v)):
                plain[:, n : n + item.shape[0]] = with_transpose(
                    dqkv[:, a * LANES : b * LANES], item[...]
                ).astype(BF16)

        @pl.when(jnp.logical_and(i >= 1, i <= jobs))
        def _():
            here = lanes(jnp.clip(i - 1, 0, jobs - 1), TILE)
            g_attn[here, : ends[3]] = rows_contract(n1[:, here], plain[...]).astype(BF16)

        @pl.when(i == jobs)
        def _():
            attn_task.start()

        attn_task.step(i - jobs - 1, late)

        @pl.when(section > 0)
        def _():
            give_y.step(i - first_job, late)

        return c

    lax.fori_loop(0, max(line_a.steps + line_b.steps, jobs + 1 + chunks), step, 0)
    @pl.when(mine)
    def _():
        spares[...] = times(holder[...], dx[...]).astype(BF16)
        back_task.start()

    gains_own[...] = jnp.zeros_like(gains_own)
    gains_own[:1] = gain_one[...] + jnp.where(mine, gsum[...], 0.0)
    gains_own[1:2] = gain_two[...] + jnp.where(mine, gain_last[...], 0.0)
    for k in range(1, 4):
        spread(k).start()

    @pl.when(mine)
    def _():
        run_steps(0, spare_chunks, (lambda i: back_task.step(i, late), 0))

    for k in range(1, 4):
        spread(k).wait()
    total = gains_own[...] + gains_all[0] + gains_all[1] + gains_all[2]
    part_width = width // groups
    for d in range(groups):
        gains_sum[8 * d : 8 * d + 8, :] = total[:, d * part_width : (d + 1) * part_width]
    small.start()

    def close(i, c):
        up_task.step(late + i, late)
        attn_task.step(late + i, late)

        @pl.when(section > 0)
        def _():
            give_y.step(late + i, late)

        small.step(i, 4)
        return c

    lax.fori_loop(0, max(chunks, spare_chunks, small.steps(4)), close, 0)

    @pl.when(mine)
    def _():
        run_steps(late, late + spare_chunks, (lambda i: back_task.step(i, late), 0))
        back_task.finish()

    @pl.when(section > 0)
    def _():
        known_back.wait()


    @pl.when(mine)
    def _():
        line_a.finish()
        line_b.finish()
        for item in scatters:
            item.finish()
        known_y.wait()

    @pl.when(section > 0)
    def _():
        give_y.finish()

    for item in (up_task, attn_task, small):
        item.finish()


def last_attn(known, spots, dresid, dx, y, y_back, normed_one, back_known, holder, gains, spreads, grads, weights, groups, q_heads, k_heads, cid):
    norm_one, wqkv, wout, norm_two, wgate, wup, wdown = weights
    x, q, kv, lse, mixed, dqkv, other_dresid = known
    count, width = dresid.shape
    keys = groups * count
    spare = holder.shape[0] // groups
    pieces, chunks, spare_chunks = 5, 8, spare // 32
    vmem = pl.BlockSpec(memory_space=pltpu.VMEM)
    far = pl.BlockSpec(memory_space=pl.ANY)
    dma = pltpu.SemaphoreType.DMA
    sources = [wout, wqkv, x, q, kv, lse, mixed, dqkv, other_dresid, *grads]
    attn_width = sum(item.shape[0] for item in spreads)
    block = width // groups
    first_only = {3: count, 4: keys, 5: q_heads * count}
    scratch = [
        pltpu.VMEM((first_only.get(k, item.shape[0]),) + item.shape[1:], item.dtype) for k, item in enumerate(sources)
    ]
    scratch += [
        pltpu.VMEM((2 * count, attn_width - spreads[3].shape[0]), BF16),
        pltpu.VMEM((2 * count, spreads[3].shape[0]), BF16),
        pltpu.VMEM((count, width), BF16),
        pltpu.VMEM((count, q.shape[1]), BF16),
        pltpu.VMEM((kv.shape[1], keys), F32),
        pltpu.VMEM((2 * count, width), BF16),
        pltpu.VMEM((width, attn_width), BF16),
        pltpu.VMEM((groups * spare, width), BF16),
        pltpu.VMEM((groups * spare, width), BF16),
        pltpu.VMEM((1, width), F32),
        pltpu.VMEM((8, width), F32),
        pltpu.VMEM((3, 8, width), F32),
        pltpu.VMEM((groups * 8, block), F32),
        dma((15,)),
        dma((3,)),
        dma((3,)),
    ]
    for _ in range(k_heads):
        scratch += [pltpu.VMEM((keys, 2 * LANES), BF16), pltpu.VMEM((count, 2 * LANES), F32)]
        scratch += OwnScatter.scratch(groups, count, 2 * LANES, 5, BF16)
    for columns in (grads[0].shape[1], attn_width):
        scratch += OwnScatter.scratch(groups, block, columns, chunks, BF16)
    scratch += OwnScatter.scratch(groups, spare, width, spare_chunks, BF16) * 2
    scratch += OwnScatter.scratch(groups, 8, block, 1, F32)
    scratch += Line.scratch(count // 4, pieces, width, False) * 2
    return pl.pallas_call(
        functools.partial(last_attn_kernel, groups, q_heads, k_heads, pieces, chunks, spare_chunks),
        out_shape=[
            jax.ShapeDtypeStruct((count, width), BF16),
            jax.ShapeDtypeStruct((spare, width), BF16),
            jax.ShapeDtypeStruct((spare, width), BF16),
            jax.ShapeDtypeStruct((8, block), F32),
            jax.ShapeDtypeStruct((block, grads[0].shape[1]), BF16),
            jax.ShapeDtypeStruct((block, attn_width), BF16),
        ],
        in_specs=[vmem] * 15 + [far] * 15,
        out_specs=[vmem] * 6,
        scratch_shapes=scratch,
        compiler_params=pltpu.CompilerParams(
            collective_id=cid, has_side_effects=True, vmem_limit_bytes=VMEM_LIMIT
        ),
        name="last_attn",
    )(*spots, norm_one[None], dresid, holder, *gains, *spreads, *sources, dx, y, y_back, normed_one, back_known)


def finish_kernel(groups, parts, *refs):
    refs = list(refs)

    def take(count):
        taken = refs[:count]
        del refs[:count]
        return taken

    live, gains = take(2)
    through, y, y_first, y_second, cot, dx_first, dx_second, back_first, back_second = take(9)
    gate, up, down, attn = take(4)
    acts, backs = take(2)
    outs = take(7)
    gain_one_out, gain_two_out = take(2)
    tiles = take(4)
    rows = take(4)
    backs_near = take(4)
    down_near, down_turned, attn_near, *attn_parts = take(7)
    plain_near, plain_wide = take(2), take(2)
    sems, out_sems = take(2)
    count, spare = rows[0].shape[0], backs_near[0].shape[0]
    seq = count + spare
    whole = [
        (through.at[0, 0], y.at[:count], y_first, acts.at[0, 0, 0]),
        (through.at[1, 0], y.at[count:], y_second, acts.at[0, 1, 0]),
        (cot.at[0, 0], dx_first.at[:count], back_first.at[2 * spare :], backs.at[0, 0, 0]),
        (cot.at[1, 0], dx_second, back_second, backs.at[0, 1, 0]),
    ]
    query_out, key_out, value_out, out_out, gate_out, up_out, down_out = outs
    plain_in = [pltpu.make_async_copy(a, b, sems.at[14 + k]) for k, (a, b) in enumerate(zip((gate, up), plain_near))]
    plain = [pltpu.make_async_copy(a, b, out_sems.at[k]) for k, (a, b) in enumerate(zip(plain_wide, (gate_out.at[0], up_out.at[0])))]
    load_down = pltpu.make_async_copy(down, down_near, sems.at[12])
    load_attn = pltpu.make_async_copy(attn, attn_near, sems.at[13])
    loads = []
    for k, (a, b, c, _) in enumerate(whole):
        loads.append(
            [
                pltpu.make_async_copy(src, dst, sems.at[3 * k + n])
                for n, (src, dst) in enumerate(((a, tiles[k]), (b, rows[k]), (c, backs_near[k])))
            ]
        )
    load_attn.start()
    load_down.start()
    for item in plain_in:
        item.start()
    for group in loads:
        for item in group:
            item.start()
    stores = []
    load_attn.wait()
    at = 0
    for k, (size, near, there) in enumerate(zip(parts, attn_parts, (query_out, key_out, value_out, out_out))):
        value = attn_near[:, at : at + size].astype(F32)
        near[...] = value if k == 0 else jnp.transpose(value)
        at += size
        stores.append(pltpu.make_async_copy(near, there.at[0], out_sems.at[2 + k]))
        stores[-1].start()
    gain_one_out[...] = gains[:1]
    gain_two_out[...] = gains[1:2]
    for before, near, wide, item in zip(plain_in, plain_near, plain_wide, plain):
        before.wait()
        wide[...] = near[...].astype(F32)
        item.start()
    load_down.wait()
    down_turned[...] = jnp.transpose(down_near[...].astype(F32))
    stores.append(pltpu.make_async_copy(down_turned, down_out.at[0], out_sems.at[6]))
    stores[-1].start()
    for k, group in enumerate(loads):
        for item in group:
            item.wait()
        first = (k % 2) * seq

        def one(i, c):
            here = pl.ds(pl.multiple_of(i * 64, 64), 64)
            alive = live[pl.ds(pl.multiple_of(first + i * 64, 64), 64)] > 0
            tiles[k][here] = jnp.where(alive, rows[k][here], tiles[k][here])
            return c

        lax.fori_loop(0, count // 64, one, 0)

        def two(i, c):
            near = pl.ds(pl.multiple_of(i * 64, 64), 64)
            here = pl.ds(pl.multiple_of(count + i * 64, 64), 64)
            alive = live[pl.ds(pl.multiple_of(first + count + i * 64, 64), 64)] > 0
            tiles[k][here] = jnp.where(alive, backs_near[k][near], tiles[k][here])
            return c

        lax.fori_loop(0, spare // 64, two, 0)
        stores.append(pltpu.make_async_copy(tiles[k], whole[k][3], out_sems.at[7 + k]))
        stores[-1].start()
    for item in stores + plain:
        item.wait()


def finish(live, gains, through, y, y_backs, cot, dx_first, dx_second, back_first, back_second, grads, parts, groups):
    count, width = dx_second.shape
    spare = back_second.shape[0]
    gate, up, down, attn = grads
    block, hidden = down.shape
    vmem = pl.BlockSpec(memory_space=pltpu.VMEM)
    far = pl.BlockSpec(memory_space=pl.ANY)
    shapes = [(block, parts[0])] + [(size, block) for size in parts[1:]]
    outs = [jax.ShapeDtypeStruct((1, 2, 1, count + spare, width), BF16)] * 2
    outs += [jax.ShapeDtypeStruct((1,) + item, F32) for item in shapes + [gate.shape, up.shape, (hidden, block)]]
    outs += [jax.ShapeDtypeStruct((1, block), F32)] * 2
    scratch = [pltpu.VMEM((count + spare, width), BF16)] * 4
    scratch += [pltpu.VMEM((count, width), BF16)] * 4 + [pltpu.VMEM((spare, width), BF16)] * 4
    scratch += [pltpu.VMEM(down.shape, BF16), pltpu.VMEM((hidden, block), F32), pltpu.VMEM(attn.shape, BF16)]
    scratch += [pltpu.VMEM(item, F32) for item in shapes]
    scratch += [pltpu.VMEM(gate.shape, BF16)] * 2 + [pltpu.VMEM(gate.shape, F32)] * 2
    scratch += [pltpu.SemaphoreType.DMA((16,)), pltpu.SemaphoreType.DMA((11,))]
    return pl.pallas_call(
        functools.partial(finish_kernel, groups, parts),
        out_shape=outs,
        in_specs=[vmem] * 2 + [far] * 13,
        out_specs=[far] * 9 + [vmem] * 2,
        scratch_shapes=scratch,
        compiler_params=pltpu.CompilerParams(vmem_limit_bytes=VMEM_LIMIT),
        name="finish",
    )(live, gains, through, y, *y_backs, cot, dx_first, dx_second, back_first, back_second, gate, up, down, attn)


def rope_tables(seq_len):
    half_width = HD // 2
    inverse = np.float32(rope_base) ** (-(np.arange(half_width, dtype=np.float32) * np.float32(2.0) / np.float32(HD)))
    angle = np.arange(seq_len, dtype=np.float32)[:, None] * inverse[None, :].astype(np.float32)
    cosine, sine = np.cos(angle), np.sin(angle)
    table = np.zeros((seq_len, 4, LANES // 2), np.float32)
    table[:, 0, :half_width] = cosine
    table[:, 1, :half_width] = cosine
    table[:, 2, :half_width] = -sine
    table[:, 3, :half_width] = sine
    return table.reshape(seq_len, 2 * LANES)


def spreader(heads, turned):
    feature = jnp.arange(HD)
    place = jnp.where(feature < HD // 2, feature, feature - HD // 2 + LANES // 2) if turned else feature
    lane = (jnp.arange(heads)[:, None] * LANES + place[None, :]).reshape(-1)
    return (lane[:, None] == jnp.arange(heads * LANES)[None, :]).astype(BF16)


def slots_of(lens, count):
    groups = lens.shape[0]
    kept = jnp.minimum(lens, count)
    free, extra = count - kept, lens - kept
    free_off = jnp.cumsum(free) - free
    extra_end = jnp.cumsum(extra)
    slot = jnp.arange(count)
    own = slot[None, :] < kept[:, None]
    index = free_off[:, None] + slot[None, :] - kept[:, None]
    source = jnp.sum(index[:, :, None] >= extra_end[None, None, :], axis=-1)
    begins = jnp.sum(jnp.where(index[:, :, None] >= extra_end[None, None, :], extra[None, None, :], 0), axis=-1)
    seq = jnp.where(own, jnp.arange(groups)[:, None], source)
    pos = jnp.where(own, slot[None, :], count + index - begins)
    return seq, pos, own


def on_device(
    inputs,
    cotangent,
    lengths,
    norm_attn,
    w_query,
    w_key,
    w_value,
    w_out,
    norm_ffn,
    w_gate,
    w_up,
    w_down,
):
    first = lax.axis_index("section") == 0
    me = lax.axis_index("dp")
    groups = lax.axis_size("dp")
    micro, seq_len, width = inputs.shape[0], inputs.shape[2], inputs.shape[3]
    count = seq_len * 5 // 8
    spare = seq_len - count
    q_heads, k_heads = w_query.shape[2] // HD, w_key.shape[2] // HD
    spread_q, spread_k = spreader(q_heads, True), spreader(k_heads, True)
    spread_v, spread_o = spreader(k_heads, False), spreader(q_heads, False)
    qkv = [
        times(item[0], spread).astype(BF16)
        for item, spread in ((w_query, spread_q), (w_key, spread_k), (w_value, spread_v))
    ]
    wqkv = jnp.concatenate(qkv, axis=1)
    wout = rows_contract(spread_o, w_out[0]).astype(BF16)
    weights = (norm_attn[0], wqkv, wout, norm_ffn[0], w_gate[0], w_up[0], w_down[0])

    all_in_one = micro == 2 and groups == 4

    extras = [jnp.where(first, inputs[b, 0, count:], cotangent[b, 0, count:]) for b in range(micro)]
    first_extra = lax.all_gather(extras[0], "dp", axis=0, tiled=True)
    length_rows = jnp.broadcast_to(lengths[:, 0].astype(F32)[:, None], (micro, LANES))
    length_rows = jnp.concatenate([length_rows, jnp.zeros((8 - micro, LANES), F32)], axis=0)
    (length_all,) = gather_rows([length_rows], groups, 4)
    lens = length_all.reshape(groups, 8, LANES)[:, :micro, 0].T.astype(jnp.int32)
    packed, slots, spots, chosen, kept_own = [], [], [], [], []
    for b in range(micro):
        seq, pos, own = slots_of(lens[b], count)
        slots.append((seq, pos))
        my_seq, my_pos, own = seq[me][:, None], pos[me][:, None], own[me][:, None]
        here = (jnp.arange(seq_len)[None, :] == my_pos).astype(F32)
        turned = jnp.dot(here, rope_tables(seq_len), precision=lax.Precision.HIGHEST)
        code = (seq * seq_len + pos).reshape(1, -1)
        spots.append((turned[:, :LANES], turned[:, LANES:], my_seq * seq_len + my_pos, my_seq * seq_len, code))
        wanted = jnp.where(own, -1, my_seq * spare + my_pos - count)
        chosen.append((jnp.arange(groups * spare)[None, :] == wanted).astype(BF16))
        kept = jnp.where(first, inputs[b, 0, :count], cotangent[b, 0, :count])
        kept_own.append(jnp.where(own, kept, jnp.zeros((), BF16)))
    for b in range(0 if all_in_one else micro):
        extra = first_extra if b == 0 else lax.all_gather(extras[b], "dp", axis=0, tiled=True)
        packed.append((kept_own[b].astype(F32) + times(chosen[b], extra)).astype(BF16))

    def holder(b):
        seq, pos = slots[b]
        row = jnp.arange(groups * spare)[:, None]
        return jnp.logical_and(row == seq[me][None, :] * spare + pos[me][None, :] - count, pos[me][None, :] >= count)

    def spread(rows, b):
        return jnp.dot(holder(b).astype(BF16), rows, preferred_element_type=F32).astype(BF16)

    def unpack(rows, back, b, through):
        live = (jnp.arange(seq_len) < lens[b, me])[:, None]
        return jnp.where(live, jnp.concatenate([rows, back], axis=0), through)

    def come_back(rows, b):
        return lax.psum_scatter(spread(rows, b), "dp", scatter_dimension=0, tiled=True)

    norm_one, norm_two = weights[0], weights[3]
    empty = jnp.zeros((count, width), BF16)

    def spots_at(tick):
        early, late = spots[min(tick, micro - 1)], spots[max(tick - 1, 0)]
        return tuple(jnp.where(first, a, b) for a, b in zip(early, late))

    grads_in, before, gain_sums = [], [], []
    if all_in_one:
        joined = [jnp.concatenate(items, axis=0) for items in zip(*spots)]
        joined[4] = joined[4][:, None]
        held = jnp.concatenate([holder(b) for b in range(micro)], axis=0).astype(BF16)
        y, dx, y_back, normed_one, normed_two, x, q, kv, lse, mixed, resid, gate, up, act, dy, d_resid, d_gate, d_up, d_qkv, gain_one, gain_two = main_ticks(
            (jnp.concatenate(kept_own, axis=0), first_extra, extras[1], jnp.concatenate(chosen, axis=0)),
            joined,
            held,
            weights,
            qkv,
            groups,
            q_heads,
            k_heads,
            0,
        )
        last_dresid, gain_last, grad_up, grad_down, grad_gate, y, y_first, back_known = last_ffn(
            (dy, act, gate, up, d_gate, d_up, resid, d_resid, y, y_back, normed_two, dx), held, weights, groups, 1
        )
        last_dx, back_second, y_second, gains, grad_up, grad_attn = last_attn(
            (x, q, kv, lse, mixed, d_qkv, d_resid),
            spots[1],
            last_dresid,
            dx,
            y,
            y_back,
            normed_one,
            back_known,
            held[groups * spare :],
            (gain_one, gain_two, gain_last),
            (spread_q, spread_k, spread_v, spread_o),
            (grad_up,),
            weights,
            groups,
            q_heads,
            k_heads,
            2,
        )
        live = (jnp.arange(seq_len)[None, :] < lens[:, me][:, None]).astype(jnp.int32).reshape(-1, 1)
        acts, backs, *grads = finish(
            live,
            gains,
            inputs,
            y,
            (y_first, y_second),
            cotangent,
            dx,
            last_dx,
            y_back,
            back_second,
            (grad_gate, grad_up, grad_down, grad_attn),
            [w_query.shape[2], w_key.shape[2], w_value.shape[2], w_query.shape[2]],
            groups,
        )
        grads[1:3] = [jnp.swapaxes(item, 1, 2) for item in grads[1:3]]
        return (acts, backs, grads[7], *grads[:4], grads[8], *grads[4:7])

    else:
        arriving = empty
        results, saved = [], []
        for tick in range(micro + 1):
            stream = jnp.where(first, packed[tick] if tick < micro else empty, arriving)
            result, arriving, kept = forward_tick(stream, spots_at(tick), weights, groups, q_heads, k_heads, 0)
            results.append(result)
            saved.append(kept)
        results = [jnp.where(first, results[b], results[b + 1]) for b in range(micro)]
        arriving = empty
        for tick in range(micro):
            kept = saved[micro - tick]
            incoming = jnp.where(first, arriving, packed[micro - 1 - tick])
            d_resid, gain_two, d_gate, d_up = back_ffn(incoming, kept, weights, 1)
            d_stream, gain_one, d_qkv, arriving = back_attn(
                d_resid, kept, spots_at(micro - tick), weights, groups, q_heads, k_heads, 2, -1
            )
            before.append((kept[5], d_gate, d_up, incoming, kept[8], kept[0], d_qkv, d_resid, kept[4]))
            grads_in.append(d_stream)
            gain_sums.append(jnp.concatenate([gain_one, gain_two], axis=0))
        kept_last = saved[0]
        last_in, last_spots = jnp.where(first, arriving, empty), spots_at(0)
        grads_at = [grads_in[micro - 1 - b] if b == 0 else jnp.where(first, grads_in[micro - b], grads_in[micro - 1 - b]) for b in range(micro)]

        def all_rows(now, index):
            old = [item[index] for item in before]
            return jnp.concatenate([jnp.where(first, now, old[0])] + old[1:], axis=0)

        x, mixed, resid, act = kept_last[0], kept_last[4], kept_last[5], kept_last[8]
        d_resid, gain_two, d_gate, d_up = back_ffn(last_in, kept_last, weights, 1)
        n2 = normalize(all_rows(resid, 0), norm_two)
        grad_gate = rows_contract(n2, all_rows(d_gate, 1)).astype(BF16)
        grad_up = rows_contract(n2, all_rows(d_up, 2)).astype(BF16)
        grad_down = rows_contract(all_rows(last_in, 3), all_rows(act, 4)).astype(BF16)
        ffn_grads = (grad_gate, grad_up, grad_down)
        beside = len(ffn_grads) if groups * count <= 2048 else 1
        d_stream, gain_one, d_qkv, *ffn_sums = back_attn(
            d_resid, kept_last, last_spots, weights, groups, q_heads, k_heads, 3, 0, sums=ffn_grads[:beside]
        )
        n1 = normalize(all_rows(x, 5), norm_one)
        back_spread = [(spread_q, 0, q_heads), (spread_k, q_heads, k_heads), (spread_v, q_heads + k_heads, k_heads)]
        dqkv = all_rows(d_qkv, 6)
        dqkv = jnp.concatenate(
            [with_transpose(dqkv[:, i * LANES : (i + n) * LANES], item) for item, i, n in back_spread], axis=1
        ).astype(BF16)
        mix = with_transpose(all_rows(mixed, 8), spread_o).astype(BF16)
        grad_attn = jnp.concatenate(
            [rows_contract(n1, dqkv).astype(BF16), rows_contract(all_rows(d_resid, 7), mix).astype(BF16)], axis=1
        )
        grads_at[0] = jnp.where(first, d_stream, grads_at[0])
        last_gains = jnp.concatenate([gain_one, gain_two], axis=0)
        gain_sums.append(jnp.where(first, last_gains, jnp.zeros_like(last_gains)))

        gains = sum(gain_sums[1:], gain_sums[0])
        gains = jnp.concatenate([gains, jnp.zeros((6, width), F32)], axis=0)
        gains = gains.reshape(8, groups, -1).transpose(1, 0, 2).reshape(groups * 8, -1)

    acts = []
    for b in range(micro):
        rows = results[b]
        acts.append(unpack(rows, come_back(rows, b), b, inputs[b, 0]))
    backs = []
    for b in range(micro):
        rows = grads_at[b]
        if b == 0:
            back, gains, grad_attn, *rest = return_rows(
                spread(rows, b), gains, (grad_attn,) + ffn_grads[beside:], groups, 5, spare // 16
            )
            grad_gate, grad_up, grad_down = ffn_sums + rest
        else:
            back = come_back(rows, b)
        backs.append(unpack(rows, back, b, cotangent[b, 0]))
    acts, backs = jnp.stack(acts), jnp.stack(backs)
    ends = [0]
    for item in (w_query, w_key, w_value, w_query):
        ends.append(ends[-1] + item.shape[2])
    grad_query, grad_key, grad_value, grad_out = (grad_attn[:, a:b] for a, b in zip(ends, ends[1:]))
    final = (
        gains[0],
        grad_query,
        grad_key,
        grad_value,
        grad_out.T,
        gains[1],
        grad_gate,
        grad_up,
        grad_down.T,
    )
    return (acts[None, :, None], backs[None, :, None]) + tuple(item[None] for item in final)


def solution(mesh):
    placed = (
        P(None, "dp", None, None),
        P(None, "dp", None, None),
        P(None, "dp"),
        P("section", None),
        P("section", None, "tensor"),
        P("section", None, "tensor"),
        P("section", None, "tensor"),
        P("section", "tensor", None),
        P("section", None),
        P("section", None, "tensor"),
        P("section", None, "tensor"),
        P("section", "tensor", None),
    )
    return jax.shard_map(
        on_device,
        mesh=mesh,
        in_specs=placed,
        out_specs=(
            P("section", None, "dp", None, None),
            P("section", None, "dp", None, None),
            P("section", "dp"),
            P("section", "dp", "tensor"),
            P("section", "dp", "tensor"),
            P("section", "dp", "tensor"),
            P("section", "tensor", "dp"),
            P("section", "dp"),
            P("section", "dp", "tensor"),
            P("section", "dp", "tensor"),
            P("section", "tensor", "dp"),
        ),
        check_vma=False,
    )
```

```python
import functools

import jax
import jax.numpy as jnp
import numpy as np
from jax import lax
from jax.experimental import pallas as pl
from jax.experimental.pallas import tpu as pltpu
from jax.sharding import PartitionSpec as P

HD = 96

epsilon = 1e-05
rope_base = 100000.0
negative = -1e30
MESH = pl.DeviceIdType.MESH
F32 = jnp.float32
BF16 = jnp.bfloat16


def remote(src, dst, s_sem, r_sem, where):
    return pltpu.make_async_remote_copy(
        src_ref=src, dst_ref=dst, send_sem=s_sem, recv_sem=r_sem, device_id=where, device_id_type=MESH
    )


def greet(where):
    pl.semaphore_signal(pltpu.get_barrier_semaphore(), inc=1, device_id=where, device_id_type=MESH)


def dp_bits(groups):
    return groups.bit_length() - 1


def dp_partner(level):
    me = lax.axis_index("dp")
    bit = lax.rem(me // (1 << level), 2)
    return {"dp": me + (1 - 2 * bit) * (1 << level)}, bit


class Scatter:
    def __init__(self, groups, rows, chunks, refs):
        self.levels = dp_bits(groups)
        self.groups, self.rows, self.chunks, self.size = groups, rows, chunks, rows // chunks
        self.value, self.out = refs[0], refs[1]
        m = self.levels
        self.arrive = refs[2 : 2 + m]
        self.held = refs[2 + m : 1 + 2 * m]
        self.s_sem = refs[1 + 2 * m : 1 + 3 * m]
        self.r_sem = refs[1 + 3 * m : 1 + 4 * m]
        self.links = [dp_partner(k) for k in range(m)]

    @staticmethod
    def scratch(groups, rows, width, chunks, dtype):
        m = dp_bits(groups)
        sizes = [groups >> (k + 1) for k in range(m)]
        return (
            [pltpu.VMEM((size * rows, width), dtype) for size in sizes]
            + [pltpu.VMEM((size * rows, width), dtype) for size in sizes[:-1]]
            + [pltpu.SemaphoreType.DMA((size, chunks)) for size in sizes] * 2
        )

    def at(self, block, c):
        return pl.ds(pl.multiple_of(block * self.rows + c * self.size, self.size), self.size)

    def copy(self, level, slot, c):
        where, bit = self.links[level]
        source = self.value if level == 0 else self.held[level - 1]
        return remote(
            source.at[self.at(2 * slot + 1 - bit, c)],
            self.arrive[level].at[self.at(slot, c)],
            self.s_sem[level].at[slot, c],
            self.r_sem[level].at[slot, c],
            where,
        )

    def order(self, level):
        count = self.groups >> (level + 1)
        if count == 1:
            return [(0, False)]
        bit = self.links[level + 1][1]
        return [(2 * i + 1 - bit, True) for i in range(count // 2)] + [(2 * i + bit, False) for i in range(count // 2)]

    def start(self):
        def one(c, carry):
            for slot, _ in self.order(0):
                self.copy(0, slot, c).start()
            return carry

        lax.fori_loop(0, self.chunks, one, 0)

    def step(self, i, lag):
        for level in range(self.levels):
            c = i - level * lag

            @pl.when(jnp.logical_and(c >= 0, c < self.chunks))
            def _():
                bit = self.links[level][1]
                source = self.value if level == 0 else self.held[level - 1]
                for slot, goes in self.order(level):
                    self.copy(level, slot, c).wait_recv()
                    here = self.at(slot, c)
                    total = source[self.at(2 * slot + bit, c)].astype(F32) + self.arrive[level][here].astype(F32)
                    if level == self.levels - 1:
                        self.out[here] = total.astype(self.out.dtype)
                    else:
                        self.held[level][here] = total.astype(self.held[level].dtype)
                        if goes:
                            self.copy(level + 1, slot // 2, c).start()

    def steps(self, lag):
        return self.chunks + (self.levels - 1) * lag

    def finish(self):
        def one(c, carry):
            for level in range(self.levels):
                for slot in range(self.groups >> (level + 1)):
                    self.copy(level, slot, c).wait_send()
            return carry

        lax.fori_loop(0, self.chunks, one, 0)


def return_kernel(groups, rows, chunks, plans, *refs):
    refs = list(refs)

    def take(count):
        taken = refs[:count]
        del refs[:count]
        return taken

    m = dp_bits(groups)
    count = 4 * m - 1
    value, gains = take(2)
    grads = take(len(plans))
    out, gains_out = take(2)
    totals = take(len(plans))
    gains_all, gains_sum, g_s, g_r = take(4)
    task = Scatter(groups, rows, chunks, [value, out] + take(count))
    small = Scatter(groups, 8, 1, [gains_sum, gains_out] + take(count))
    large = [
        Scatter(groups, block, parts, [grad, total] + take(count))
        for (block, parts), grad, total in zip(plans, grads, totals)
    ]
    t = lax.axis_index("tensor")
    for where, _ in task.links:
        greet(where)
    for k in range(1, 4):
        greet({"tensor": lax.rem(t + k, 4)})
    pl.semaphore_wait(pltpu.get_barrier_semaphore(), m + 3)

    def spread(k):
        return remote(gains, gains_all.at[k - 1], g_s.at[k - 1], g_r.at[k - 1], {"tensor": lax.rem(t + k, 4)})

    for k in range(1, 4):
        spread(k).start()
    task.start()
    for item in large:
        item.start()
    for k in range(1, 4):
        spread(k).wait()
    gains_sum[...] = gains[...] + gains_all[0] + gains_all[1] + gains_all[2]
    small.start()

    def body(i, c):
        small.step(i, 1)
        task.step(i, 2)
        for item in large:
            item.step(i, 4)
        return c

    lax.fori_loop(0, max([task.steps(2), small.steps(1)] + [item.steps(4) for item in large]), body, 0)
    small.finish()
    task.finish()
    for item in large:
        item.finish()


def return_rows(value, gains, grads, groups, cid, chunks):
    rows, width = value.shape[0] // groups, value.shape[1]
    vmem = pl.BlockSpec(memory_space=pltpu.VMEM)
    part = gains.shape[1]
    plans, outs = [], [jax.ShapeDtypeStruct((rows, width), BF16), jax.ShapeDtypeStruct((8, part), F32)]
    scratch = [
        pltpu.VMEM((3,) + gains.shape, F32),
        pltpu.VMEM(gains.shape, F32),
        pltpu.SemaphoreType.DMA((3,)),
        pltpu.SemaphoreType.DMA((3,)),
    ]
    scratch += Scatter.scratch(groups, rows, width, chunks, BF16) + Scatter.scratch(groups, 8, part, 1, F32)
    for grad in grads:
        block = grad.shape[0] // groups
        plans.append((block, max(1, block // 48)))
        outs.append(jax.ShapeDtypeStruct((block, grad.shape[1]), F32))
        scratch += Scatter.scratch(groups, block, grad.shape[1], plans[-1][1], BF16)
    return pl.pallas_call(
        functools.partial(return_kernel, groups, rows, chunks, plans),
        out_shape=outs,
        in_specs=[vmem] * (2 + len(grads)),
        out_specs=[vmem] * len(outs),
        scratch_shapes=scratch,
        compiler_params=pltpu.CompilerParams(
            collective_id=cid, has_side_effects=True, vmem_limit_bytes=VMEM_LIMIT
        ),
        name="return_%d" % cid,
    )(value, gains, *grads)


def gather_kernel(groups, count, *refs):
    values, outs = refs[:count], refs[count : 2 * count]
    s_sem, r_sem, own = refs[2 * count :]
    m = dp_bits(groups)
    me = lax.axis_index("dp")
    links = [dp_partner(k) for k in range(m)]
    for where, _ in links:
        greet(where)
    pl.semaphore_wait(pltpu.get_barrier_semaphore(), m)

    def place(a, block):
        rows = values[a].shape[0]
        return outs[a].at[pl.ds(pl.multiple_of(block * rows, rows), rows)]

    def copy(a, level, i, mine):
        where, bit = links[level]
        low = lax.rem(me, 1 << (level + 1))
        if not mine:
            low = low + (1 - 2 * bit) * (1 << level)
        block = i * (1 << (level + 1)) + low
        return remote(place(a, block), place(a, block), s_sem.at[a, level, i], r_sem.at[a, level, i], where)

    locals_ = [pltpu.make_async_copy(values[a], place(a, me), own.at[a]) for a in range(count)]
    for item in locals_:
        item.start()
    for item in locals_:
        item.wait()
    for level in reversed(range(m)):
        for i in range(groups >> (level + 1)):
            for a in range(count):
                copy(a, level, i, True).start()
        for i in range(groups >> (level + 1)):
            for a in range(count):
                copy(a, level, i, False).wait_recv()
    for level in range(m):
        for i in range(groups >> (level + 1)):
            for a in range(count):
                copy(a, level, i, True).wait_send()


def gather_rows(values, groups, cid):
    vmem = pl.BlockSpec(memory_space=pltpu.VMEM)
    m, count = dp_bits(groups), len(values)
    dma = pltpu.SemaphoreType.DMA
    return pl.pallas_call(
        functools.partial(gather_kernel, groups, count),
        out_shape=[jax.ShapeDtypeStruct((groups * v.shape[0], v.shape[1]), v.dtype) for v in values],
        in_specs=[vmem] * count,
        out_specs=[vmem] * count,
        scratch_shapes=[dma((count, m, groups // 2)), dma((count, m, groups // 2)), dma((count,))],
        compiler_params=pltpu.CompilerParams(
            collective_id=cid, has_side_effects=True, vmem_limit_bytes=48 * 2**20
        ),
        name="gather_%d" % cid,
    )(*values)


class OwnScatter(Scatter):
    def __init__(self, groups, rows, chunks, refs):
        m = dp_bits(groups)
        super().__init__(groups, rows, chunks, list(refs[: 2 + m]) + [None] * (m - 1) + list(refs[2 + m :]))
        self.me = lax.axis_index("dp")

    @staticmethod
    def scratch(groups, rows, width, chunks, dtype):
        m = dp_bits(groups)
        kinds = Scatter.scratch(groups, rows, width, chunks, dtype)
        return kinds[:m] + kinds[2 * m - 1 :]

    @staticmethod
    def refs(groups):
        return 3 * dp_bits(groups)

    def whole(self, level, slot, c):
        return self.at(slot * (1 << level) + lax.rem(self.me, 1 << level), c)

    def copy(self, level, slot, c):
        where, bit = self.links[level]
        return remote(
            self.value.at[self.whole(level, 2 * slot + 1 - bit, c)],
            self.arrive[level].at[self.at(slot, c)],
            self.s_sem[level].at[slot, c],
            self.r_sem[level].at[slot, c],
            where,
        )

    def step(self, i, lag):
        for level in range(self.levels):
            c = i - level * lag

            @pl.when(jnp.logical_and(c >= 0, c < self.chunks))
            def _():
                bit = self.links[level][1]
                for slot, goes in self.order(level):
                    self.copy(level, slot, c).wait_recv()
                    here, there = self.whole(level, 2 * slot + bit, c), self.at(slot, c)
                    if level == self.levels - 1:
                        total = self.value[here].astype(F32) + self.arrive[level][there].astype(F32)
                        self.out[self.at(0, c)] = total.astype(self.out.dtype)
                    else:
                        self.value[here] = self.value[here] + self.arrive[level][there]
                        if goes:
                            self.copy(level + 1, slot // 2, c).start()


class Line:
    lag_b, lag_c, lag_o = 2, 4, 5

    def __init__(self, first, half, pieces, part, base, out, scratch, norm=None, moved=None, at=(0, 0, 0), turns=1):
        self.first, self.half, self.size = first, half, half // pieces
        self.each, self.pieces = pieces, pieces * turns
        self.base_at, self.out_at, self.moved_at = at
        self.part, self.base, self.out = part, base, out
        (self.rin, self.smid, self.rmid) = scratch[:3]
        (self.s_up, self.r_up, self.s_mid, self.r_mid, self.s_b1, self.s_b2, self.r_b, self.s_c, self.r_c) = scratch[3:12]
        self.norm, self.moved = norm, moved
        if moved:
            self.arrived, self.shift = moved
            self.s_s, self.r_s = scratch[12:14]
            section = lax.axis_index("section")
            self.sends = section == (0 if self.shift > 0 else 1)
            self.partner = {"section": 1 - section}
        t = lax.axis_index("tensor")
        self.mid = jnp.logical_or(t == 1, t == 2)
        self.outside = jnp.logical_not(self.mid)
        self.outer = {"tensor": jnp.where(t == 1, 0, 3)}
        self.other = {"tensor": jnp.where(t == 1, 2, 1)}
        self.nbr = {"tensor": jnp.where(t == 0, 1, 2)}
        self.near = jnp.where(t < 2, 0, half)
        self.far = half - self.near

    @staticmethod
    def scratch(half, pieces, width, moved, turns=1):
        dma = pltpu.SemaphoreType.DMA
        half, pieces = half * turns, pieces * turns
        kinds = [
            pltpu.VMEM((2 * half, width), BF16),
            pltpu.VMEM((half, width), BF16),
            pltpu.VMEM((half, width), BF16),
            dma((2, pieces)),
            dma((2, pieces)),
        ] + [dma((pieces,))] * 7
        return kinds + ([dma((2, pieces))] * 2 if moved else [])

    @staticmethod
    def greet():
        t = lax.axis_index("tensor")

        @pl.when(t > 0)
        def _():
            greet({"tensor": jnp.maximum(t - 1, 0)})

        @pl.when(t < 3)
        def _():
            greet({"tensor": jnp.minimum(t + 1, 3)})

    def greet_sender(self):
        if self.moved:

            @pl.when(jnp.logical_not(self.sends))
            def _():
                greet(self.partner)

    def enter(self, others):
        bar = pltpu.get_barrier_semaphore()
        count = jnp.where(self.mid, 2, 1) + others
        if self.moved:
            count = count + jnp.where(self.sends, 1, 0)
        pl.semaphore_wait(bar, count)

    def local(self, start, p):
        if self.each < self.pieces:
            start, p = start + (p // self.each) * (2 * self.half), lax.rem(p, self.each)
        return pl.ds(pl.multiple_of(start + p * self.size, self.size), self.size)

    def own(self, p):
        return pl.ds(pl.multiple_of(p * self.size, self.size), self.size)

    def rows(self, start, p, at=0):
        return self.local(self.first + at + start, p)

    def shifted(self, start, p):
        side = start // self.half
        here, there = self.rows(start, p, self.out_at), self.rows(start, p, self.moved_at)
        return remote(self.out.at[here], self.arrived.at[there], self.s_s.at[side, p], self.r_s.at[side, p], self.partner)

    def pass_on(self, start, p):
        if self.moved:

            @pl.when(self.sends)
            def _():
                self.shifted(start, p).start()

    def outcome(self, s_sem, r_sem, where, start, p):
        here = self.rows(start, p, self.out_at)
        return remote(self.out.at[here], self.out.at[here], s_sem.at[p], r_sem.at[p], where)

    def up(self, start, p, k, where):
        return remote(
            self.part.at[self.rows(start, p)], self.rin.at[self.local(start, p)], self.s_up.at[k, p], self.r_up.at[k, p], where
        )

    def cross(self, p):
        return remote(
            self.smid.at[self.own(p)], self.rmid.at[self.own(p)], self.s_mid.at[p], self.r_mid.at[p], self.other
        )

    def start(self, turn=0):
        @pl.when(self.outside)
        def _():
            def begin(p, c):
                self.up(self.far, p, 0, self.nbr).start()
                self.up(self.near, p, 1, self.nbr).start()
                return c

            lax.fori_loop(turn * self.each, (turn + 1) * self.each, begin, 0)

    def outer_step(self, i):
        p = i - self.lag_o

        @pl.when(jnp.logical_and(p >= 0, p < self.pieces))
        def _():
            self.outcome(self.s_b2, self.r_b, self.nbr, self.near, p).wait_recv()
            self.pass_on(self.near, p)
            self.outcome(self.s_c, self.r_c, self.nbr, self.far, p).wait_recv()
            self.pass_on(self.far, p)

    def mid_step(self, i):
        @pl.when(jnp.logical_and(i >= 0, i < self.pieces))
        def _():
            self.up(self.far, i, 0, self.outer).wait_recv()
            total = self.part[self.rows(self.far, i)].astype(F32) + self.rin[self.local(self.far, i)].astype(F32)
            self.smid[self.own(i)] = total.astype(BF16)
            self.cross(i).start()

        j = i - self.lag_b

        @pl.when(jnp.logical_and(j >= 0, j < self.pieces))
        def _():
            self.up(self.near, j, 1, self.outer).wait_recv()
            self.cross(j).wait_recv()
            here = self.rows(self.near, j, self.base_at)
            total = self.part[self.rows(self.near, j)].astype(F32) + self.rin[self.local(self.near, j)].astype(F32)
            total = total + self.rmid[self.own(j)].astype(F32)
            if self.norm:
                xrow, gain, gsum, norm_at = self.norm
                x = xrow[self.rows(self.near, j, norm_at)].astype(F32)
                scale = lax.rsqrt(jnp.mean(x * x, axis=-1, keepdims=True) + epsilon)
                unit = x * scale
                gsum[...] += jnp.sum(total * unit, axis=0, keepdims=True)
                inner = total * gain[...]
                total = scale * (inner - unit * jnp.mean(inner * unit, axis=-1, keepdims=True))
            total = self.base[here].astype(F32) + total
            self.out[self.rows(self.near, j, self.out_at)] = total.astype(BF16)
            self.outcome(self.s_b1, self.r_b, self.other, self.near, j).start()
            self.outcome(self.s_b2, self.r_b, self.outer, self.near, j).start()
            self.pass_on(self.near, j)

        k = i - self.lag_c

        @pl.when(jnp.logical_and(k >= 0, k < self.pieces))
        def _():
            self.outcome(self.s_b1, self.r_b, self.other, self.far, k).wait_recv()
            self.outcome(self.s_c, self.r_c, self.outer, self.far, k).start()
            self.pass_on(self.far, k)

    @property
    def steps(self):
        return self.pieces + self.lag_o

    def step(self, i):
        @pl.when(self.mid)
        def _():
            self.mid_step(i)

        @pl.when(self.outside)
        def _():
            self.outer_step(i)

    def finish(self):
        @pl.when(self.mid)
        def _():
            def one(p, c):
                self.cross(p).wait_send()
                self.outcome(self.s_b1, self.r_b, self.other, self.near, p).wait_send()
                self.outcome(self.s_b2, self.r_b, self.outer, self.near, p).wait_send()
                self.outcome(self.s_c, self.r_c, self.outer, self.far, p).wait_send()
                return c

            lax.fori_loop(0, self.pieces, one, 0)

        @pl.when(self.outside)
        def _():
            def one(p, c):
                self.up(self.far, p, 0, self.nbr).wait_send()
                self.up(self.near, p, 1, self.nbr).wait_send()
                return c

            lax.fori_loop(0, self.pieces, one, 0)

        if self.moved:

            @pl.when(self.sends)
            def _():
                def close(p, c):
                    self.shifted(0, p).wait_send()
                    self.shifted(self.half, p).wait_send()
                    return c

                lax.fori_loop(0, self.pieces, close, 0)

    def receive(self):
        @pl.when(jnp.logical_not(self.sends))
        def _():
            def close(p, c):
                self.shifted(0, p).wait_recv()
                self.shifted(self.half, p).wait_recv()
                return c

            lax.fori_loop(0, self.pieces, close, 0)


def run_steps(begin, end, *planned):
    def body(i, c):
        for step, offset in planned:
            step(i - offset)
        return c

    lax.fori_loop(begin, end, body, 0)


class Gather:
    def __init__(self, groups, rows, out, s_sem, r_sem, first=0, size=None):
        self.first, self.size = first, size or rows
        self.groups, self.rows, self.out, self.s_sem, self.r_sem = groups, rows, out, s_sem, r_sem
        self.levels = dp_bits(groups)
        self.links = [dp_partner(k) for k in range(self.levels)]
        self.me = lax.axis_index("dp")

    @staticmethod
    def scratch(groups):
        return [pltpu.SemaphoreType.DMA((dp_bits(groups), groups // 2))] * 2

    def copy(self, level, i, mine):
        where, bit = self.links[level]
        low = lax.rem(self.me, 1 << (level + 1))
        if not mine:
            low = low + (1 - 2 * bit) * (1 << level)
        block = i * (1 << (level + 1)) + low
        place = self.out.at[pl.ds(pl.multiple_of(block * self.rows + self.first, self.size), self.size)]
        return remote(place, place, self.s_sem.at[level, i], self.r_sem.at[level, i], where)

    def start(self, level):
        for i in range(self.groups >> (level + 1)):
            self.copy(level, i, True).start()

    def arrive(self, level):
        for i in range(self.groups >> (level + 1)):
            self.copy(level, i, False).wait_recv()

    def finish(self):
        for level in range(self.levels):
            for i in range(self.groups >> (level + 1)):
                self.copy(level, i, True).wait_send()


def with_transpose(left, right):
    return lax.dot_general(left, right, (((1,), (1,)), ((), ())), preferred_element_type=F32)


def rows_contract(left, right):
    return lax.dot_general(left, right, (((0,), (0,)), ((), ())), preferred_element_type=F32)


def times(left, right):
    return jnp.dot(left, right, preferred_element_type=F32)


LANES = 128
TILE = 256
WIDE = 512


def lanes(i, size=LANES):
    return pl.ds(pl.multiple_of(i * size, size), size)


def normalize(rows, gain):
    rows = rows.astype(F32)
    scale = lax.rsqrt(jnp.mean(rows * rows, axis=-1, keepdims=True) + epsilon)
    return (rows * scale * gain).astype(BF16)


def normalize_into(target, source, gain, first, count, block=32, source_at=0):
    def one(i, c):
        here = pl.ds(pl.multiple_of(first + i * block, block), block)
        there = pl.ds(pl.multiple_of(source_at + first + i * block, block), block)
        target[here] = normalize(source[there], gain[...])
        return c

    lax.fori_loop(0, count // block, one, 0)


def rolled(value, cosine, sine):
    return value * cosine + pltpu.roll(value, LANES // 2, 1) * sine


def block_rows(keys):
    for rows in (160, 80, 32):
        if rows * keys <= 160 * 1280:
            return rows
    return 16


def score_rows(q, kv, h, g, here, qcode, qstart, kcode):
    scores = with_transpose(q[here, lanes(h)], kv[:, lanes(g)]) * HD ** (-0.5)
    code = kcode[...]
    return scores, jnp.logical_and(code <= qcode[here][:, :1], code >= qstart[here][:, :1])


def load_all(pairs, sems):
    copies = [pltpu.make_async_copy(src, dst, sems.at[i]) for i, (src, dst) in enumerate(pairs)]
    for item in copies:
        item.start()
    return copies


def forward_kernel(groups, q_heads, k_heads, pieces, *refs):
    refs = list(refs)

    def take(count):
        taken = refs[:count]
        del refs[:count]
        return taken

    x, cosine, sine, qcode, qstart, kcode, gain_one, gain_two = take(8)
    far_weights = take(5)
    q, kv, lse, mixed, resid, gate, up, act, y, arrived = take(10)
    near_weights = take(5)
    wqkv, wout, wgate, wup, wdown = near_weights
    part_one, part_two, n1, n2, w_sem = take(5)
    gather = Gather(groups, x.shape[0], kv, *take(2))
    count, width = x.shape
    quarter = count // 4
    lines = []
    for k in range(4):
        first = (k % 2) * 2 * quarter
        source = (part_one, x, resid) if k < 2 else (part_two, resid, y)
        lines.append(
            Line(first, quarter, pieces, *source, take(12 if k < 2 else 14), moved=None if k < 2 else (arrived, 1))
        )
    one_a, one_b, two_a, two_b = lines

    loads = load_all(list(zip(far_weights, near_weights)), w_sem)
    Line.greet()
    two_a.greet_sender()
    for where, _ in gather.links:
        greet(where)
    normalize_into(n1, x, gain_one, 0, count)
    loads[0].wait()

    mine = pl.ds(pl.multiple_of(lax.axis_index("dp") * count, count), count)
    for g in range(k_heads):
        column = (q_heads + g) * LANES
        value = times(n1[...], wqkv[:, column : column + LANES])
        kv[mine, g * LANES : (g + 1) * LANES] = rolled(value, cosine[...], sine[...]).astype(BF16)
        column += k_heads * LANES
        kv[mine, (k_heads + g) * LANES : (k_heads + g + 1) * LANES] = times(
            n1[...], wqkv[:, column : column + LANES]
        ).astype(BF16)

    two_a.enter(gather.levels)

    top = gather.levels - 1
    gather.start(top)

    def queries(h, c):
        value = times(n1[...], wqkv[:, lanes(h)])
        q[:, lanes(h)] = rolled(value, cosine[...], sine[...]).astype(BF16)
        return c

    lax.fori_loop(0, q_heads, queries, 0)
    for level in range(top, -1, -1):
        gather.arrive(level)
        if level:
            gather.start(level - 1)

    rows = block_rows(kv.shape[0])
    blocks = count // rows

    def attend(i, c):
        h, b = i // blocks, lax.rem(i, blocks)
        g = h // (q_heads // k_heads)
        here = pl.ds(pl.multiple_of(b * rows, rows), rows)
        scores, allowed = score_rows(q, kv, h, g, here, qcode, qstart, kcode)
        scores = jnp.where(allowed, scores, negative)
        row_max = jnp.max(scores, axis=-1, keepdims=True)
        expo = jnp.exp(scores - row_max)
        row_total = jnp.sum(expo, axis=-1, keepdims=True)
        prob = (expo * (1.0 / row_total)).astype(BF16)
        mixed[here, lanes(h)] = times(prob, kv[:, lanes(k_heads + g)]).astype(BF16)
        there = pl.ds(pl.multiple_of(h * count + b * rows, rows), rows)
        lse[there] = jnp.broadcast_to(row_max + jnp.log(row_total), (rows, LANES))
        return c

    lax.fori_loop(0, q_heads * blocks, attend, 0)
    loads[1].wait()

    def projected(target, left, right, first, each=None):
        here = pl.ds(first, 2 * quarter)

        def one(i, c):
            target[here, lanes(i, TILE)] = times(left[here], right[:, lanes(i, TILE)]).astype(BF16)
            if each:
                each(i)
            return c

        lax.fori_loop(0, width // TILE, one, 0)

    projected(part_one, mixed, wout, 0)
    one_a.start()
    projected(part_one, mixed, wout, 2 * quarter)
    one_b.start()
    run_steps(0, one_a.steps, (one_a.step, 0), (one_b.step, pieces))
    loads[2].wait()
    loads[3].wait()
    loads[4].wait()

    def hidden(first, each):
        here = pl.ds(first, 2 * quarter)
        normalize_into(n2, resid, gain_two, first, 2 * quarter)

        def one(i, c):
            columns = lanes(i, TILE)
            gate_pre = times(n2[here], wgate[:, columns])
            up_pre = times(n2[here], wup[:, columns])
            gate[here, columns] = gate_pre.astype(BF16)
            up[here, columns] = up_pre.astype(BF16)
            act[here, columns] = (gate_pre * jax.nn.sigmoid(gate_pre) * up_pre).astype(BF16)
            each(i)
            return c

        lax.fori_loop(0, gate.shape[1] // TILE, one, 0)

    tiles = gate.shape[1] // TILE
    done = one_a.steps - pieces
    hidden(0, lambda i: one_b.step(done + i))
    projected(part_two, act, wdown, 0)
    two_a.start()
    run_steps(done + tiles, one_b.steps, (one_b.step, 0))
    hidden(2 * quarter, lambda i: two_a.step(i))
    projected(part_two, act, wdown, 2 * quarter)
    two_b.start()
    run_steps(tiles, two_b.steps + tiles, (two_a.step, 0), (two_b.step, tiles))
    gather.finish()
    for line in lines:
        line.finish()
    two_a.receive()
    two_b.receive()


VMEM_LIMIT = 60 * 2**20


def forward_tick(x, spots, weights, groups, q_heads, k_heads, cid):
    norm_one, wqkv, wout, norm_two, wgate, wup, wdown = weights
    count, width = x.shape
    hidden = wgate.shape[1]
    pieces = 5
    vmem = pl.BlockSpec(memory_space=pltpu.VMEM)
    far = pl.BlockSpec(memory_space=pl.ANY)

    def shape(*dims, dtype=BF16):
        return jax.ShapeDtypeStruct(dims, dtype)

    outs = [
        shape(count, q_heads * LANES),
        shape(groups * count, 2 * k_heads * LANES),
        shape(q_heads * count, LANES, dtype=F32),
        shape(count, q_heads * LANES),
        shape(count, width),
        shape(count, hidden),
        shape(count, hidden),
        shape(count, hidden),
        shape(count, width),
        shape(count, width),
    ]
    far_weights = [wqkv, wout, wgate, wup, wdown]
    scratch = [pltpu.VMEM(item.shape, BF16) for item in far_weights]
    scratch += [pltpu.VMEM((count, width), BF16)] * 4 + [pltpu.SemaphoreType.DMA((5,))]
    scratch += Gather.scratch(groups)
    for k in range(4):
        scratch += Line.scratch(count // 4, pieces, width, k >= 2)
    q, kv, lse, mixed, resid, gate, up, act, y, arrived = pl.pallas_call(
        functools.partial(forward_kernel, groups, q_heads, k_heads, pieces),
        out_shape=outs,
        in_specs=[vmem] * 8 + [far] * 5,
        out_specs=[vmem] * len(outs),
        scratch_shapes=scratch,
        compiler_params=pltpu.CompilerParams(
            collective_id=cid, has_side_effects=True, vmem_limit_bytes=VMEM_LIMIT
        ),
        name="forward_tick",
    )(x, *spots, norm_one[None], norm_two[None], *far_weights)
    return y, arrived, (x, q, kv, lse, mixed, resid, gate, up, act)


def back_ffn_kernel(pieces, *refs):
    dy, gate, up, resid, gain = refs[:5]
    far_weights = refs[5:8]
    dresid, gsum, dgate, dup = refs[8:12]
    wdown, wgate, wup = near_weights = refs[12:15]
    part, w_sem = refs[15:17]
    count, width = dy.shape
    quarter = count // 4
    a, b = [
        Line(k * 2 * quarter, quarter, pieces, part, dy, dresid, refs[17 + 12 * k : 29 + 12 * k], norm=(resid, gain, gsum, 0))
        for k in range(2)
    ]
    loads = load_all(list(zip(far_weights, near_weights)), w_sem)
    Line.greet()
    gsum[...] = jnp.zeros_like(gsum)

    def hidden(first, each=None):
        here = pl.ds(first, 2 * quarter)

        def one(i, c):
            columns = lanes(i, TILE)
            d_act = with_transpose(dy[here], wdown[columns, :])
            gate_pre, up_pre = gate[here, columns].astype(F32), up[here, columns].astype(F32)
            sigma = jax.nn.sigmoid(gate_pre)
            d_silu = d_act * sigma
            dup[here, columns] = (d_silu * gate_pre).astype(BF16)
            dgate[here, columns] = (d_silu * up_pre * (1.0 + gate_pre * (1.0 - sigma))).astype(BF16)
            if each:
                each(i)
            return c

        lax.fori_loop(0, gate.shape[1] // TILE, one, 0)

    def back(first):
        here = pl.ds(first, 2 * quarter)

        def one(i, c):
            columns = lanes(i, TILE)
            total = with_transpose(dgate[here], wgate[columns, :]) + with_transpose(dup[here], wup[columns, :])
            part[here, columns] = total.astype(BF16)
            return c

        lax.fori_loop(0, width // TILE, one, 0)

    loads[0].wait()
    hidden(0)
    loads[1].wait()
    loads[2].wait()
    back(0)
    a.enter(0)
    a.start()
    tiles = gate.shape[1] // TILE
    hidden(2 * quarter, lambda i: a.step(i))
    back(2 * quarter)
    b.start()
    run_steps(tiles, b.steps + tiles, (a.step, 0), (b.step, tiles))
    a.finish()
    b.finish()


def back_ffn(dy, kept, weights, cid):
    norm_one, wqkv, wout, norm_two, wgate, wup, wdown = weights
    x, q, kv, lse, mixed, resid, gate, up, act = kept
    count, width = dy.shape
    pieces = 5
    vmem = pl.BlockSpec(memory_space=pltpu.VMEM)
    far = pl.BlockSpec(memory_space=pl.ANY)
    far_weights = [wdown, wgate, wup]
    scratch = [pltpu.VMEM(item.shape, BF16) for item in far_weights]
    scratch += [pltpu.VMEM((count, width), BF16), pltpu.SemaphoreType.DMA((3,))]
    scratch += Line.scratch(count // 4, pieces, width, False) * 2
    return pl.pallas_call(
        functools.partial(back_ffn_kernel, pieces),
        out_shape=[
            jax.ShapeDtypeStruct((count, width), BF16),
            jax.ShapeDtypeStruct((1, width), F32),
            jax.ShapeDtypeStruct(gate.shape, BF16),
            jax.ShapeDtypeStruct(gate.shape, BF16),
        ],
        in_specs=[vmem] * 5 + [far] * 3,
        out_specs=[vmem] * 4,
        scratch_shapes=scratch,
        compiler_params=pltpu.CompilerParams(
            collective_id=cid, has_side_effects=True, vmem_limit_bytes=VMEM_LIMIT
        ),
        name="back_ffn",
    )(dy, gate, up, resid, norm_two[None], *far_weights)


def back_attn_kernel(groups, q_heads, k_heads, pieces, shift, plans, *refs):
    refs = list(refs)

    def take(count):
        taken = refs[:count]
        del refs[:count]
        return taken

    dresid, x, q, kv, lse, cosine, sine, qcode, qstart, kcode, gain = take(11)
    far_weights = take(2)
    values = take(len(plans))
    dx, gsum, dqkv = take(3)
    (arrived,) = take(1) if shift else (None,)
    totals = take(len(plans))
    wout, wqkv = near_weights = take(2)
    part, dmixed, dkv, w_sem = take(4)
    levels = dp_bits(groups)
    count, width = x.shape
    quarter = count // 4
    keys = kv.shape[0]
    shares, owns, scatters = [], [], []
    for g in range(k_heads):
        share, own = take(2)
        shares.append(share)
        owns.append(own)
        scatters.append(Scatter(groups, count, 2, [share, own] + take(4 * levels - 1)))
    tasks = [
        Scatter(groups, rows, chunks, [value, total] + take(4 * levels - 1))
        for (rows, chunks), value, total in zip(plans, values, totals)
    ]
    moved = (arrived, shift) if shift else None
    a, b = [
        Line(
            k * 2 * quarter,
            quarter,
            pieces,
            part,
            dresid,
            dx,
            take(14 if shift else 12),
            norm=(x, gain, gsum, 0),
            moved=moved,
        )
        for k in range(2)
    ]
    loads = load_all(list(zip(far_weights, near_weights)), w_sem)
    Line.greet()
    for where, _ in scatters[0].links:
        greet(where)
    a.greet_sender()
    gsum[...] = jnp.zeros_like(gsum)
    dkv[...] = jnp.zeros_like(dkv)
    a.enter(levels)
    for task in tasks:
        task.start()
    loads[0].wait()

    def mix(h, c):
        dmixed[:, lanes(h)] = with_transpose(dresid[...], wout[lanes(h), :]).astype(BF16)
        return c

    lax.fori_loop(0, q_heads, mix, 0)
    rows = block_rows(keys)
    blocks = count // rows
    repeat = q_heads // k_heads
    lag = 4
    scale = HD ** (-0.5)

    for g in range(k_heads):

        def one(i, c):
            h, n = g * repeat + i // blocks, lax.rem(i, blocks)
            here = pl.ds(pl.multiple_of(n * rows, rows), rows)
            there = pl.ds(pl.multiple_of(h * count + n * rows, rows), rows)
            scores, allowed = score_rows(q, kv, h, g, here, qcode, qstart, kcode)
            prob = jnp.where(allowed, jnp.exp(scores - lse[there][:, :1]), 0.0)
            dm = dmixed[here, lanes(h)]
            d_prob = with_transpose(dm, kv[:, lanes(k_heads + g)])
            row_dot = jnp.sum(prob * d_prob, axis=-1, keepdims=True)
            d_scores = (prob * (d_prob - row_dot)).astype(BF16)
            d_query = times(d_scores, kv[:, lanes(g)]) * scale
            dqkv[here, lanes(h)] = rolled(d_query, cosine[here], -sine[here]).astype(BF16)
            dkv[:, lanes(g)] += rows_contract(d_scores, q[here, lanes(h)]) * scale
            dkv[:, lanes(k_heads + g)] += rows_contract(prob.astype(BF16), dm)
            for task in tasks:
                task.step(g * repeat * blocks + i, lag)
            return c

        lax.fori_loop(0, repeat * blocks, one, 0)

        def narrow(i, c):
            here = pl.ds(pl.multiple_of(i * LANES, LANES), LANES)
            shares[g][here, :LANES] = dkv[here, lanes(g)].astype(BF16)
            shares[g][here, LANES:] = dkv[here, lanes(k_heads + g)].astype(BF16)
            return c

        lax.fori_loop(0, keys // LANES, narrow, 0)
        scatters[g].start()
    run_steps(0, scatters[0].steps(1), *[(functools.partial(lambda s, i: s.step(i, 1), s), 0) for s in scatters])
    for g in range(k_heads):
        dqkv[:, lanes(q_heads + g)] = rolled(owns[g][:, :LANES], cosine[...], -sine[...]).astype(BF16)
        dqkv[:, lanes(q_heads + k_heads + g)] = owns[g][:, LANES:].astype(BF16)
    loads[1].wait()

    def back(first, each=None):
        here = pl.ds(first, 2 * quarter)

        def one(i, c):
            columns = lanes(i, TILE)
            part[here, columns] = with_transpose(dqkv[here], wqkv[columns, :]).astype(BF16)
            if each:
                each(i)
            return c

        lax.fori_loop(0, width // TILE, one, 0)

    back(0)
    a.start()
    back(2 * quarter)
    b.start()
    begun = q_heads * blocks
    more = [(functools.partial(lambda s, i: s.step(i + begun, lag), s), 0) for s in tasks]
    last = max([b.steps + pieces] + [s.steps(lag) - begun for s in tasks])
    run_steps(0, last, (a.step, 0), (b.step, pieces), *more)
    a.finish()
    b.finish()
    if shift:
        a.receive()
        b.receive()
    for item in scatters + tasks:
        item.finish()


def back_attn(dresid, kept, spots, weights, groups, q_heads, k_heads, cid, shift, sums=()):
    norm_one, wqkv, wout, norm_two, wgate, wup, wdown = weights
    x, q, kv, lse, mixed, resid, gate, up, act = kept
    count, width = x.shape
    keys = kv.shape[0]
    pieces = 5
    vmem = pl.BlockSpec(memory_space=pltpu.VMEM)
    far = pl.BlockSpec(memory_space=pl.ANY)
    outs = [
        jax.ShapeDtypeStruct((count, width), BF16),
        jax.ShapeDtypeStruct((1, width), F32),
        jax.ShapeDtypeStruct((count, wqkv.shape[1]), BF16),
    ]
    if shift:
        outs.append(jax.ShapeDtypeStruct((count, width), BF16))
    scratch = [
        pltpu.VMEM(wout.shape, BF16),
        pltpu.VMEM(wqkv.shape, BF16),
        pltpu.VMEM((count, width), BF16),
        pltpu.VMEM(q.shape, BF16),
        pltpu.VMEM(kv.shape, F32),
        pltpu.SemaphoreType.DMA((2,)),
    ]
    for _ in range(k_heads):
        scratch += [pltpu.VMEM((keys, 2 * LANES), BF16), pltpu.VMEM((count, 2 * LANES), F32)]
        scratch += Scatter.scratch(groups, count, 2 * LANES, 2, BF16)
    plans = []
    for value in sums:
        rows = value.shape[0] // groups
        parts = max(1, min(8, rows // 16))
        while rows % (parts * 16):
            parts -= 1
        plans.append((rows, parts))
        outs.append(jax.ShapeDtypeStruct((rows, value.shape[1]), F32))
        scratch += Scatter.scratch(groups, rows, value.shape[1], parts, BF16)
    scratch += Line.scratch(count // 4, pieces, width, bool(shift)) * 2
    return pl.pallas_call(
        functools.partial(back_attn_kernel, groups, q_heads, k_heads, pieces, shift, plans),
        out_shape=outs,
        in_specs=[vmem] * 11 + [far] * 2 + [vmem] * len(sums),
        out_specs=[vmem] * len(outs),
        scratch_shapes=scratch,
        compiler_params=pltpu.CompilerParams(
            collective_id=cid, has_side_effects=True, vmem_limit_bytes=VMEM_LIMIT
        ),
        name="back_attn_%d" % cid,
    )(dresid, x, q, kv, lse, *spots, norm_one[None], wout, wqkv, *sums)


def announce(sems, neighbours):
    for here, where, k in neighbours:

        @pl.when(here)
        def _():
            pl.semaphore_signal(sems.at[k], inc=1, device_id=where, device_id_type=MESH)


def heard(sems, neighbours):
    for k, (here, _, _) in enumerate(neighbours):

        @pl.when(here)
        def _():
            pl.semaphore_wait(sems.at[k], 1)


def main_kernel(groups, q_heads, k_heads, pieces, *refs):
    refs = list(refs)

    def take(count):
        taken = refs[:count]
        del refs[:count]
        return taken

    cosine, sine, qcode, qstart, kcode, gain_one, gain_two, holder, chosen = take(9)
    own_rows, extra_first, extra_second = take(3)
    far_weights = take(7)
    y_out, dx_out, back_out, normed_one, normed_two = take(5)
    far_state = take(14)
    gsum_one, gsum_two = take(2)
    near_state = xs, q, kv, lse, mixed, resid, gate, up, act, dys, dresid, dgate, dup, dqkv = take(14)
    state_sem = take(1)[0]
    wqkv, wout, wgate, wup, wdown = near_weights = take(5)
    part_one, part_two, normed, y, dmixed, dkv, w_sem, io_sem, meet_sem = take(9)
    levels = dp_bits(groups)
    gather_sems = [take(2) for _ in range(2)]
    line_scratch = [take(12) for _ in range(4)]
    forth_s, forth_r, back_s, back_r = take(4)
    spares, returned = take(2)
    spare = returned.shape[0]
    give_lag = Line.lag_o + pieces
    give = OwnScatter(groups, spare, spare // 32, [spares, returned] + take(OwnScatter.refs(groups)))
    second = Gather(groups, spare, spares, *take(2))
    count, width = part_one.shape
    keys = groups * count
    quarter = count // 4
    half = 2 * quarter
    shares, owns, scatters = [], [], []
    for g in range(k_heads):
        share, own = take(2)
        shares.append(share)
        owns.append(own)
        scatters.append(Scatter(groups, count, 2, [share, own] + take(4 * levels - 1)))
    section = lax.axis_index("section")
    t = lax.axis_index("tensor")
    tiles, wide = gate.shape[1] // WIDE, width // WIDE
    repeat = q_heads // k_heads
    rows = block_rows(keys)
    blocks = half // rows
    scale = HD ** (-0.5)

    def span(first, size):
        return pl.ds(pl.multiple_of(first, 32), size)

    neighbours = [
        (t > 0, {"tensor": jnp.maximum(t - 1, 0)}, 1),
        (t < 3, {"tensor": jnp.minimum(t + 1, 3)}, 0),
    ]
    for k in range(levels):
        neighbours.append((t >= 0, dp_partner(k)[0], 2 + k))

    for _, where, _ in neighbours[2:]:
        greet(where)
    Line.greet()
    greet({"section": 1 - section})

    ends = [0]
    for item in far_weights[:3]:
        ends.append(ends[-1] + item.shape[1])
    parts = [wqkv.at[:, a:b] for a, b in zip(ends, ends[1:])]
    copies = load_all(list(zip(far_weights, parts + list(near_weights[1:]))), w_sem)
    loads = [copies[:3], *[[item] for item in copies[3:]]]

    place = span(lax.axis_index("dp") * spare, spare)
    fetch_first = pltpu.make_async_copy(extra_first, spares, io_sem.at[2])
    fetch_extra = pltpu.make_async_copy(extra_second, spares.at[place], io_sem.at[2])
    fetch_first.start()
    for which, target in enumerate((xs, dys)):

        @pl.when(section == which)
        def _():
            pltpu.make_async_copy(own_rows, target, io_sem.at[0]).start()

    pl.semaphore_wait(pltpu.get_barrier_semaphore(), jnp.where(jnp.logical_or(t == 1, t == 2), 2, 1) + levels + 1)
    announce(meet_sem, neighbours)
    gsum_one[...] = jnp.zeros_like(gsum_one)
    gsum_two[...] = jnp.zeros_like(gsum_two)
    fetch_first.wait()
    brought_first = times(chosen[:count], spares[...])
    for which, target in enumerate((xs, dys)):

        @pl.when(section == which)
        def _():
            pltpu.make_async_copy(own_rows, target, io_sem.at[0]).wait()
            target[:count] = (target[:count].astype(F32) + brought_first).astype(BF16)

    fetch_extra.start()
    fetch_extra.wait()

    def keep(index, slot):
        near, there = near_state[index], far_state[index]
        part = near.shape[0] // 2
        here = span(slot * part, part)
        return pltpu.make_async_copy(near.at[here], there.at[here], state_sem.at[index, slot])

    def projected(target, left, right, first, left_at, each=None):
        here, there = span(first, half), span(first + left_at, half)

        def one(i, c):
            target[here, lanes(i, WIDE)] = times(left[there], right[:, lanes(i, WIDE)]).astype(BF16)
            if each:
                each(i)
            return c

        lax.fori_loop(0, wide, one, 0)

    def give_back(slot, now, line):
        @pl.when(now)
        def _():
            spares[...] = times(holder[span(slot * groups * spare, groups * spare)], y[...]).astype(BF16)
            give.start()

        def one(i, c):
            line.step(i)

            @pl.when(now)
            def _():
                give.step(i, give_lag)

            return c

        lax.fori_loop(0, line.steps, one, 0)

    def give_rest(now, line, begun):
        def one(i, c):
            line.step(i)

            @pl.when(now)
            def _():
                give.step(i - begun + give_lag, give_lag)

            return c

        lax.fori_loop(begun, max(line.steps, begun + give.steps(give_lag) - give_lag), one, 0)

    def given(place, now):
        @pl.when(now)
        def _():
            give.finish()
            pltpu.make_async_copy(returned, back_out.at[span(place * spare, spare)], io_sem.at[1]).start()
            pltpu.make_async_copy(returned, back_out.at[span(place * spare, spare)], io_sem.at[1]).wait()

    def ffn_back(slot, first, each=None):
        here, there = span(first, half), span(slot * count + first, half)

        def one(i, c):
            columns = lanes(i, WIDE)
            d_act = with_transpose(dys[there], wdown[columns, :])
            gate_pre, up_pre = gate[there, columns].astype(F32), up[there, columns].astype(F32)
            sigma = jax.nn.sigmoid(gate_pre)
            d_silu = d_act * sigma
            dup[there, columns] = (d_silu * gate_pre).astype(BF16)
            dgate[there, columns] = (d_silu * up_pre * (1.0 + gate_pre * (1.0 - sigma))).astype(BF16)
            if each:
                each(i)
            return c

        lax.fori_loop(0, tiles, one, 0)

        def two(i, c):
            columns = lanes(i, WIDE)
            total = with_transpose(dgate[there], wgate[columns, :]) + with_transpose(dup[there], wup[columns, :])
            part_one[here, columns] = total.astype(BF16)
            if each:
                each(tiles + i)
            return c

        lax.fori_loop(0, wide, two, 0)

    def back_lines(slot):
        base = slot * count
        made = []
        for k in range(4):
            first = (k % 2) * half
            scratch = list(line_scratch[k])
            if k < 2:
                norm = (resid, gain_two, gsum_two, base)
                made.append(Line(first, quarter, pieces, part_one, dys, dresid, scratch, norm=norm, at=(base, base, 0)))
            else:
                scratch += [back_s.at[k - 2], back_r.at[2 * slot + k - 2]]
                norm = (xs, gain_one, gsum_one, base)
                made.append(
                    Line(
                        first, quarter, pieces, part_two, dresid, y, scratch, norm=norm, moved=(dys, -1), at=(base, 0, base)
                    )
                )
        return made

    def forward_lines(slot):
        base = slot * count
        made = []
        for k in range(4):
            first = (k % 2) * half
            scratch = list(line_scratch[k])
            if k < 2:
                made.append(Line(first, quarter, pieces, part_one, xs, resid, scratch, at=(base, base, 0)))
            else:
                scratch += [forth_s.at[k - 2], forth_r.at[2 * slot + k - 2]]
                made.append(
                    Line(first, quarter, pieces, part_two, resid, y, scratch, moved=(xs, 1), at=(base, 0, base))
                )
        return made

    def gathers_of(slot):
        place = kv.at[span(slot * keys, keys)]
        return [Gather(groups, count, place, *gather_sems[h], h * half, half) for h in range(2)]

    def keep_normed(slot):
        return pltpu.make_async_copy(normed, normed_one.at[span(slot * count, count)], io_sem.at[1])

    def begin(slot, sync):
        base = slot * count
        middle = (q_heads + k_heads) * LANES
        for h, (line, gather) in enumerate(zip(forward_lines(slot)[2:], gathers_of(slot))):
            line.receive()
            normalize_into(normed, xs, gain_one, h * half, half, source_at=base)
            if h == 0:

                @pl.when(slot == 0)
                def _():
                    for item in loads[0]:
                        item.wait()

            here, there = span(h * half, half), span(base + h * half, half)
            mine = span(slot * keys + lax.axis_index("dp") * count + h * half, half)
            value = times(normed[here], wqkv[:, q_heads * LANES : middle])
            for g in range(k_heads):
                columns = slice(g * LANES, (g + 1) * LANES)
                kv[mine, columns] = rolled(value[:, columns], cosine[there], sine[there]).astype(BF16)
            kv[mine, k_heads * LANES :] = times(normed[here], wqkv[:, middle:]).astype(BF16)
            if h == 0 and sync:
                heard(meet_sem, neighbours)
            gather.start(levels - 1)
        keep_normed(slot).start()
        whole = span(base, count)
        for first in range(0, q_heads, 2):
            value = times(normed[...], wqkv[:, first * LANES : (first + 2) * LANES])
            for h in range(2):
                columns = slice((first + h) * LANES, (first + h + 1) * LANES)
                q[whole, columns] = rolled(
                    value[:, h * LANES : (h + 1) * LANES], cosine[whole], sine[whole]
                ).astype(BF16)

    def forward(slot):
        base = slot * count
        whole = span(base, count)
        pending = jnp.logical_and(section == 1, slot == 1)
        left_a, left_b = back_lines(0)[2:]
        one_a, one_b, two_a, two_b = forward_lines(slot)
        gathers = gathers_of(slot)
        keep_one = keep_normed(slot)
        keep_two = pltpu.make_async_copy(normed, normed_two.at[whole], io_sem.at[2])

        @pl.when(jnp.logical_not(pending))
        def _():
            begin(slot, True)

        for level in range(levels - 1, 0, -1):
            for gather in gathers:
                gather.arrive(level)
                gather.start(level - 1)

        @pl.when(pending)
        def _():
            run_steps(0, left_a.steps, (left_a.step, 0))

        for gather in gathers:
            gather.arrive(0)

        @pl.when(slot == 0)
        def _():
            second.start(levels - 1)

        def attend(first, each=None):
            def one(i, c):
                h, b = i // blocks, lax.rem(i, blocks)
                g = h // repeat
                here = span(base + first + b * rows, rows)
                scores = with_transpose(q[here, lanes(h)], kv[span(slot * keys, keys), lanes(g)]) * scale
                code = kcode[slot]
                allowed = jnp.logical_and(code <= qcode[here][:, :1], code >= qstart[here][:, :1])
                scores = jnp.where(allowed, scores, negative)
                row_max = jnp.max(scores, axis=-1, keepdims=True)
                expo = jnp.exp(scores - row_max)
                row_total = jnp.sum(expo, axis=-1, keepdims=True)
                prob = (expo * (1.0 / row_total)).astype(BF16)
                mixed[here, lanes(h)] = times(prob, kv[span(slot * keys, keys), lanes(k_heads + g)]).astype(BF16)
                lse[span((slot * q_heads + h) * count + first + b * rows, rows)] = jnp.broadcast_to(
                    row_max + jnp.log(row_total), (rows, LANES)
                )
                if each:
                    each(i)
                return c

            lax.fori_loop(0, q_heads * blocks, one, 0)

        attend(0)

        @pl.when(slot == 0)
        def _():
            loads[1][0].wait()

        projected(part_one, mixed, wout, 0, base)

        @pl.when(pending)
        def _():
            heard(meet_sem, neighbours)

        one_a.start()

        @pl.when(pending)
        def _():
            run_steps(0, left_b.steps, (left_b.step, 0))
            left_out = pltpu.make_async_copy(y, dx_out.at[:count], io_sem.at[0])
            left_out.start()
            left_a.finish()
            left_b.finish()
            left_out.wait()

        attend(half)
        projected(part_one, mixed, wout, half, base)
        one_b.start()
        run_steps(0, one_a.steps, (one_a.step, 0))

        @pl.when(slot == 0)
        def _():
            for (item,) in loads[2:]:
                item.wait()
            for level in range(levels - 1, 0, -1):
                second.arrive(level)
                second.start(level - 1)

        def hidden(first, each):
            here, there = span(first, half), span(base + first, half)
            normalize_into(normed, resid, gain_two, first, half, source_at=base)

            def one(i, c):
                columns = lanes(i, WIDE)
                gate_pre = times(normed[here], wgate[:, columns])
                up_pre = times(normed[here], wup[:, columns])
                gate[there, columns] = gate_pre.astype(BF16)
                up[there, columns] = up_pre.astype(BF16)
                act[there, columns] = (gate_pre * jax.nn.sigmoid(gate_pre) * up_pre).astype(BF16)
                each(i)
                return c

            lax.fori_loop(0, tiles, one, 0)

        keep_one.wait()
        hidden(0, one_b.step)

        @pl.when(section == 0)
        def _():
            projected(part_two, act, wdown, 0, base)
            two_a.start()

        @pl.when(slot == 0)
        def _():
            second.arrive(0)
            brought = times(chosen[count:], spares[...])
            for which, target in enumerate((xs, dys)):

                @pl.when(section == which)
                def _():
                    target[count:] = (target[count:].astype(F32) + brought).astype(BF16)

        @pl.when(section == 1)
        def _():
            one_a.finish()
            ffn_back(slot, 0, lambda i: one_b.step(tiles + i))
            run_steps(2 * tiles + wide, one_b.steps, (one_b.step, 0))

        @pl.when(section == 0)
        def _():
            run_steps(tiles, one_b.steps, (one_b.step, 0))

        @pl.when(section == 1)
        def _():
            one_b.finish()
            for gather in gathers:
                gather.finish()
            announce(meet_sem, neighbours)

        def early(i):
            @pl.when(section == 0)
            def _():
                two_a.step(i)

        hidden(half, early)
        keep_two.start()
        out = pltpu.make_async_copy(y, y_out.at[whole], io_sem.at[0])

        @pl.when(section == 0)
        def _():
            projected(part_two, act, wdown, half, base)
            two_b.start()
            run_steps(tiles, two_a.steps, (two_a.step, 0))
            run_steps(0, two_b.steps, (two_b.step, 0))
            out.start()
            two_a.finish()
            two_b.finish()
            for gather in gathers:
                gather.finish()
            one_a.finish()
            one_b.finish()

        keep_two.wait()

        @pl.when(slot == 0)
        def _():
            second.finish()

        for index in range(9):
            keep(index, slot).start()

        @pl.when(section == 0)
        def _():
            out.wait()
            announce(meet_sem, neighbours)

    def backward(slot):
        giving = jnp.logical_and(section == 1, slot == 1)
        later = jnp.logical_and(section == 1, slot == 0)
        base = slot * count
        whole = span(base, count)
        lines = back_lines(slot)
        one_a, one_b, two_a, two_b = lines
        two_a.receive()
        two_b.receive()
        dkv[...] = jnp.zeros_like(dkv)
        heard(meet_sem, neighbours)

        @pl.when(section == 0)
        def _():
            ffn_back(slot, 0)

        one_a.start()
        ffn_back(slot, half)
        one_b.start()
        give_back(0, giving, one_a)

        def attend(first, g, each=None):
            def one(i, c):
                h, n = g * repeat + i // blocks, lax.rem(i, blocks)
                here = span(base + first + n * rows, rows)
                near = span(first + n * rows, rows)
                k_rows = kv[span(slot * keys, keys), lanes(g)]
                scores = with_transpose(q[here, lanes(h)], k_rows) * scale
                code = kcode[slot]
                allowed = jnp.logical_and(code <= qcode[here][:, :1], code >= qstart[here][:, :1])
                known = lse[span((slot * q_heads + h) * count + first + n * rows, rows)][:, :1]
                prob = jnp.where(allowed, jnp.exp(scores - known), 0.0)
                dm = dmixed[near, lanes(h)]
                d_prob = with_transpose(dm, kv[span(slot * keys, keys), lanes(k_heads + g)])
                row_dot = jnp.sum(prob * d_prob, axis=-1, keepdims=True)
                d_scores = (prob * (d_prob - row_dot)).astype(BF16)
                d_query = times(d_scores, k_rows) * scale
                dqkv[here, lanes(h)] = rolled(d_query, cosine[here], -sine[here]).astype(BF16)
                dkv[lanes(g), :] += rows_contract(q[here, lanes(h)], d_scores) * scale
                dkv[lanes(k_heads + g), :] += rows_contract(dm, prob.astype(BF16))
                if each:
                    each(i)
                return c

            lax.fori_loop(0, repeat * blocks, one, 0)

        def mix(first):
            here, there = span(first, half), span(base + first, half)

            def one(h, c):
                dmixed[here, lanes(h)] = with_transpose(dresid[there], wout[lanes(h), :]).astype(BF16)
                return c

            lax.fori_loop(0, q_heads, one, 0)

        mix(0)
        turns = repeat * blocks
        for g in range(k_heads):
            attend(0, g, lambda i: one_b.step(g * turns + i))
        give_rest(giving, one_b, k_heads * turns)
        mix(half)
        for g in range(k_heads):
            attend(half, g)

            shares[g][:, :LANES] = jnp.transpose(dkv[lanes(g), :]).astype(BF16)
            shares[g][:, LANES:] = jnp.transpose(dkv[lanes(k_heads + g), :]).astype(BF16)
            scatters[g].start()
        far = give_lag
        everyone = [(functools.partial(lambda s, i: s.step(i, far), s), 0) for s in scatters]
        run_steps(0, scatters[0].chunks, *everyone)

        @pl.when(later)
        def _():
            begin(1, False)

        run_steps(far, far + scatters[0].chunks, *everyone)
        for g in range(k_heads):
            dqkv[whole, lanes(q_heads + g)] = rolled(owns[g][:, :LANES], cosine[whole], -sine[whole]).astype(BF16)
            dqkv[whole, lanes(q_heads + k_heads + g)] = owns[g][:, LANES:].astype(BF16)

        def back(first, each=None):
            here, there = span(first, half), span(base + first, half)

            def one(i, c):
                columns = lanes(i, WIDE)
                part_two[here, columns] = with_transpose(dqkv[there], wqkv[columns, :]).astype(BF16)
                if each:
                    each(i)
                return c

            lax.fori_loop(0, wide, one, 0)

        back(0)
        two_a.start()
        back(half)
        two_b.start()

        @pl.when(jnp.logical_not(later))
        def _():
            run_steps(0, two_a.steps, (two_a.step, 0))
            run_steps(0, two_b.steps, (two_b.step, 0))
            out = pltpu.make_async_copy(y, dx_out.at[whole], io_sem.at[0])
            out.start()
            two_a.finish()
            two_b.finish()
            out.wait()

        one_a.finish()
        one_b.finish()
        for item in scatters:
            item.finish()
        given(2, giving)
        for index in range(9, 14):
            keep(index, slot).start()
        announce(meet_sem, neighbours)

    def give_alone(slot, place):
        heard(meet_sem, neighbours)
        spares[...] = times(holder[slot * groups * spare : (slot + 1) * groups * spare], y[...]).astype(BF16)
        give.start()
        run_steps(0, give.steps(give_lag), (lambda i: give.step(i, give_lag), 0))
        given(place, section == 0)
        announce(meet_sem, neighbours)

    def turn(k, carry):
        @pl.when(jnp.where(section == 0, k < 2, lax.rem(k, 2) == 0))
        def _():
            forward(jnp.where(section == 0, jnp.minimum(k, 1), k // 2))

        @pl.when(jnp.logical_and(section == 0, k == 2))
        def _():
            give_alone(1, 1)
            again = pltpu.make_async_copy(y_out.at[:count], y, io_sem.at[0])
            again.start()
            again.wait()
            give_alone(0, 0)

        @pl.when(jnp.where(section == 0, k == 2, lax.rem(k, 2) == 1))
        def _():
            backward(jnp.where(section == 0, 0, k // 2))

        return carry

    lax.fori_loop(0, 3 + section, turn, 0)

    @pl.when(section == 0)
    def _():
        give_alone(0, 2)

    heard(meet_sem, neighbours)
    for k in range(2):
        Line(
            k * half,
            quarter,
            pieces,
            part_two,
            dresid,
            y,
            list(line_scratch[2 + k]) + [back_s.at[k], back_r.at[2 + k]],
            moved=(dys, -1),
            at=(0, 0, count),
        ).receive()
    for index in range(14):
        keep(index, 0).wait()
        if index < 9:
            keep(index, 1).wait()

    @pl.when(section > 0)
    def _():
        for index in range(9, 14):
            keep(index, 1).wait()

    @pl.when(section == 0)
    def _():
        keep(9, 1).start()
        keep(9, 1).wait()


def main_ticks(rows, spots, holder, weights, qkv, groups, q_heads, k_heads, cid):
    norm_one, wqkv, wout, norm_two, wgate, wup, wdown = weights
    own_rows, extra_first, extra_second, chosen = rows
    count, width = own_rows.shape[0] // 2, own_rows.shape[1]
    hidden, keys = wgate.shape[1], groups * count
    pieces = 5
    vmem = pl.BlockSpec(memory_space=pltpu.VMEM)
    far = pl.BlockSpec(memory_space=pl.ANY)
    dma = pltpu.SemaphoreType.DMA

    def shape(columns, rows=2 * count, dtype=BF16):
        return jax.ShapeDtypeStruct((rows, columns), dtype)

    heads, both = q_heads * LANES, (q_heads + 2 * k_heads) * LANES
    spare = holder.shape[0] // (2 * groups)
    outs = [
        shape(width),
        shape(width),
        shape(width, 3 * spare),
        shape(width),
        shape(width),
    ]
    state = [
        shape(width),
        shape(heads),
        shape(2 * k_heads * LANES, 2 * keys),
        shape(LANES, 2 * q_heads * count, F32),
        shape(heads),
        shape(width),
        shape(hidden),
        shape(hidden),
        shape(hidden),
        shape(width),
        shape(width),
        shape(hidden),
        shape(hidden),
        shape(both),
    ]
    outs += state + [shape(width, 1, F32)] * 2
    near_weights = [wqkv, wout, wgate, wup, wdown]
    far_weights = [*qkv, wout, wgate, wup, wdown]
    scratch = [pltpu.VMEM(item.shape, item.dtype) for item in state] + [dma((14, 2))]
    scratch += [pltpu.VMEM(item.shape, BF16) for item in near_weights]
    scratch += [pltpu.VMEM((count, width), BF16)] * 4 + [
        pltpu.VMEM((count, heads), BF16),
        pltpu.VMEM((2 * k_heads * LANES, keys), F32),
        dma((7,)),
        dma((3,)),
        pltpu.SemaphoreType.REGULAR((2 + dp_bits(groups),)),
    ]
    scratch += Gather.scratch(groups) * 2
    for k in range(4):
        scratch += Line.scratch(quarter_rows(count), pieces, width, False)
    scratch += [dma((2, 2, pieces)), dma((4, 2, pieces))] * 2
    scratch += [pltpu.VMEM((groups * spare, width), BF16), pltpu.VMEM((spare, width), BF16)]
    scratch += OwnScatter.scratch(groups, spare, width, spare // 32, BF16)
    scratch += Gather.scratch(groups)
    for _ in range(k_heads):
        scratch += [pltpu.VMEM((keys, 2 * LANES), BF16), pltpu.VMEM((count, 2 * LANES), F32)]
        scratch += Scatter.scratch(groups, count, 2 * LANES, 2, BF16)
    return pl.pallas_call(
        functools.partial(main_kernel, groups, q_heads, k_heads, pieces),
        out_shape=outs,
        in_specs=[vmem] * 9 + [far] * 10,
        out_specs=[far] * (len(outs) - 2) + [vmem] * 2,
        scratch_shapes=scratch,
        compiler_params=pltpu.CompilerParams(
            collective_id=cid, has_side_effects=True, vmem_limit_bytes=VMEM_LIMIT
        ),
        name="main_ticks",
    )(*spots, norm_one[None], norm_two[None], holder, chosen, own_rows, extra_first, extra_second, *far_weights)


def quarter_rows(count):
    return count // 4


def weight_job(target, left, right, i, block=256):
    here = lanes(i, block)
    target[here, :] = rows_contract(left[:, here], right[...]).astype(BF16)


def last_ffn_kernel(groups, pieces, chunks, *refs):
    refs = list(refs)

    def take(count):
        taken = refs[:count]
        del refs[:count]
        return taken

    gain, holder = take(2)
    sources = take(15)
    last_dresid, gsum, g_up, down_sum, gate_sum, y, returned, returned_dx = take(8)
    wdown, wgate, wup, dys, act, gate, up, dgate, dup, resid = kept = take(10)
    n2, part, g_down, g_gate, spares, spares_dx, dx, w_sem = take(8)
    line_scratch = [take(12) for _ in range(4)]
    count, width = last_dresid.shape
    half = count // 2
    line_a, line_b = [
        Line(
            k * half,
            half // 2,
            pieces,
            part,
            dys,
            last_dresid,
            line_scratch[k],
            norm=(resid, gain, gsum, count),
            at=(count, 0, 0),
        )
        for k in range(2)
    ]
    results = [Line(k * half, half // 2, pieces, part, resid, y, line_scratch[k]) for k in range(4)]
    down = OwnScatter(groups, width // groups, chunks, [g_down, down_sum] + take(OwnScatter.refs(groups)))
    gated = OwnScatter(groups, width // groups, chunks, [g_gate, gate_sum] + take(OwnScatter.refs(groups)))
    spare = returned.shape[0]
    give = OwnScatter(groups, spare, spare // 32, [spares, returned] + take(OwnScatter.refs(groups)))
    give_dx = OwnScatter(groups, spare, spare // 32, [spares_dx, returned_dx] + take(OwnScatter.refs(groups)))
    load_dx = pltpu.make_async_copy(sources[14].at[count:], dx, w_sem.at[16])
    section = lax.axis_index("section")
    mine = section == 0
    tiles, wide, blocks = act.shape[1] // WIDE, width // WIDE, width // TILE

    def load(k):
        if k in (7, 8):
            return pltpu.make_async_copy(sources[k].at[:count], kept[k].at[:count], w_sem.at[k])
        return pltpu.make_async_copy(sources[k], kept[k], w_sem.at[k])

    lacks = [
        pltpu.make_async_copy(sources[7].at[count:], kept[7].at[count:], w_sem.at[10]),
        pltpu.make_async_copy(sources[8].at[count:], kept[8].at[count:], w_sem.at[11]),
        pltpu.make_async_copy(sources[10].at[count:], last_dresid, w_sem.at[12]),
    ]
    known = [
        pltpu.make_async_copy(sources[11], y, w_sem.at[13]),
        pltpu.make_async_copy(sources[12].at[:spare], returned, w_sem.at[14]),
    ]
    loads = [load(k) for k in range(10)] + [pltpu.make_async_copy(sources[13], n2, w_sem.at[15])]
    @pl.when(section > 0)
    def _():
        load_dx.start()

    for k in (3, 0, 5, 6, 1, 2, 4, 9, 10, 7, 8):
        loads[k].start()

    @pl.when(section > 0)
    def _():
        for item in lacks:
            item.start()

    @pl.when(mine)
    def _():
        for item in known:
            item.start()

    Line.greet()
    for where, _ in down.links:
        greet(where)
    gsum[...] = jnp.zeros_like(gsum)
    line_a.enter(down.levels)
    for k in (3, 0, 5, 6):
        loads[k].wait()

    def hidden(first):
        here = pl.ds(count + first, half)

        def one(i, c):
            columns = lanes(i, WIDE)
            d_act = with_transpose(dys[here], wdown[columns, :])
            gate_pre, up_pre = gate[here, columns].astype(F32), up[here, columns].astype(F32)
            sigma = jax.nn.sigmoid(gate_pre)
            d_silu = d_act * sigma
            dup[here, columns] = (d_silu * gate_pre).astype(BF16)
            dgate[here, columns] = (d_silu * up_pre * (1.0 + gate_pre * (1.0 - sigma))).astype(BF16)
            return c

        lax.fori_loop(0, tiles, one, 0)

    def back(first):
        here, there = pl.ds(first, half), pl.ds(count + first, half)

        def one(i, c):
            columns = lanes(i, WIDE)
            total = with_transpose(dgate[there], wgate[columns, :]) + with_transpose(dup[there], wup[columns, :])
            part[here, columns] = total.astype(BF16)
            return c

        lax.fori_loop(0, wide, one, 0)

    @pl.when(mine)
    def _():
        hidden(0)

    loads[1].wait()
    loads[2].wait()

    @pl.when(mine)
    def _():
        back(0)
        line_a.start()

    loads[4].wait()

    late = 100

    def begin_results(which):
        for k in which:
            here = pl.ds(k * half, half)

            def one(i, c):
                part[here, lanes(i, WIDE)] = times(act[here], wdown[:, lanes(i, WIDE)]).astype(BF16)
                return c

            lax.fori_loop(0, wide, one, 0)
            results[k].start()

    @pl.when(section > 0)
    def _():
        load_dx.wait()
        spares_dx[...] = times(holder[groups * spare :], dx[...]).astype(BF16)
        give_dx.start()
        begin_results((0, 1))
        run_steps(0, give_dx.chunks, (lambda i: give_dx.step(i, late), 0))

    def down_job(i, c):
        weight_job(g_down, dys, act, i)
        return c

    lax.fori_loop(0, blocks, down_job, 0)
    down.start()

    @pl.when(section > 0)
    def _():
        begin_results((2, 3))
        loads[9].wait()

    @pl.when(mine)
    def _():
        hidden(half)
        back(half)
        line_b.start()

    @pl.when(mine)
    def _():
        loads[9].wait()

    for k in (10, 7, 8):
        loads[k].wait()

    @pl.when(section > 0)
    def _():
        lacks[0].wait()
        lacks[1].wait()

    spans = 0

    first_done = line_a.steps + pieces

    def step(i, c):
        @pl.when(mine)
        def _():
            line_a.step(i)
            line_b.step(i - line_a.steps)

        @pl.when(section > 0)
        def _():
            for k, item in enumerate(results):
                item.step(i - k * pieces)

            @pl.when(i == first_done)
            def _():
                spares[...] = times(holder[: groups * spare], y[:count]).astype(BF16)
                give.start()

            give.step(i - first_done, late)

        @pl.when(i < late)
        def _():
            down.step(i, late)
            gated.step(i - spans - blocks, late)

        @pl.when(jnp.logical_and(i >= spans, i < spans + blocks))
        def _():
            weight_job(g_gate, n2, dgate, i - spans)

        @pl.when(i == spans + blocks - 1)
        def _():
            gated.start()

        @pl.when(jnp.logical_and(i >= spans + blocks, i < spans + 2 * blocks))
        def _():
            weight_job(g_up, n2, dup, i - spans - blocks)

        return c

    enough = max(line_a.steps + line_b.steps, spans + 2 * blocks, spans + blocks + chunks)
    lax.fori_loop(0, jnp.where(mine, enough, max(enough, line_a.steps + 3 * pieces, first_done + give.chunks)), step, 0)
    run_steps(late, late + chunks, (lambda i: down.step(i, late), 0), (lambda i: gated.step(i, late), 0))

    @pl.when(mine)
    def _():
        line_a.finish()
        line_b.finish()

        for item in known:
            item.wait()

    @pl.when(section > 0)
    def _():
        lacks[2].wait()
        run_steps(late, late + give.chunks, (lambda i: give_dx.step(i, late), 0))
        run_steps(late, late + give.chunks, (lambda i: give.step(i, late), 0))
        give.finish()
        give_dx.finish()
        for item in results:
            item.finish()

    down.finish()
    gated.finish()


def last_ffn(known, holder, weights, groups, cid):
    norm_one, wqkv, wout, norm_two, wgate, wup, wdown = weights
    dys, act, gate, up, dgate, dup, resid, dresid, y, y_back, normed_two, dx = known
    spare = holder.shape[0] // (2 * groups)
    count, width = dys.shape[0] // 2, dys.shape[1]
    hidden = act.shape[1]
    pieces, chunks = 5, 8
    vmem = pl.BlockSpec(memory_space=pltpu.VMEM)
    far = pl.BlockSpec(memory_space=pl.ANY)
    sources = [wdown, wgate, wup, dys, act, gate, up, dgate, dup, resid]
    scratch = [pltpu.VMEM(item.shape, BF16) for item in sources]
    scratch += [
        pltpu.VMEM((2 * count, width), BF16),
        pltpu.VMEM((2 * count, width), BF16),
        pltpu.VMEM((width, hidden), BF16),
        pltpu.VMEM((width, hidden), BF16),
        pltpu.VMEM((groups * spare, width), BF16),
        pltpu.VMEM((groups * spare, width), BF16),
        pltpu.VMEM((count, width), BF16),
        pltpu.SemaphoreType.DMA((17,)),
    ]
    scratch += Line.scratch(count // 4, pieces, width, False) * 4
    scratch += OwnScatter.scratch(groups, width // groups, hidden, chunks, BF16) * 2
    scratch += OwnScatter.scratch(groups, spare, width, spare // 32, BF16) * 2
    return pl.pallas_call(
        functools.partial(last_ffn_kernel, groups, pieces, chunks),
        out_shape=[
            jax.ShapeDtypeStruct((count, width), BF16),
            jax.ShapeDtypeStruct((1, width), F32),
            jax.ShapeDtypeStruct((width, hidden), BF16),
            jax.ShapeDtypeStruct((width // groups, hidden), BF16),
            jax.ShapeDtypeStruct((width // groups, hidden), BF16),
            jax.ShapeDtypeStruct((2 * count, width), BF16),
            jax.ShapeDtypeStruct((spare, width), BF16),
            jax.ShapeDtypeStruct((spare, width), BF16),
        ],
        in_specs=[vmem] * 2 + [far] * 15,
        out_specs=[vmem] * 8,
        scratch_shapes=scratch,
        compiler_params=pltpu.CompilerParams(
            collective_id=cid, has_side_effects=True, vmem_limit_bytes=VMEM_LIMIT
        ),
        name="last_ffn",
    )(norm_two[None], holder, *sources, dresid, y, y_back, normed_two, dx)


def last_attn_kernel(groups, q_heads, k_heads, pieces, chunks, spare_chunks, *refs):
    refs = list(refs)

    def take(count):
        taken = refs[:count]
        del refs[:count]
        return taken

    cosine, sine, qcode, qstart, kcode, gain, dresid, holder, gain_one, gain_two, gain_last, spread_q, spread_k, spread_v, spread_o = take(15)
    sources = take(10)
    dx_known, y, y_back, normed_one, back_known = take(5)
    dx, returned, returned_y, gains_out, up_sum, attn_sum = take(6)
    wout, wqkv, x, q, kv, lse, mixed, dqkv, other_dresid, g_up = kept = take(10)
    plain, plain_mixed = take(2)
    part, dmixed, dkv, n1, g_attn, spares, spares_y, gsum, gains_own, gains_all, gains_sum, w_sem, g_s, g_r = take(14)
    levels = dp_bits(groups)
    count, width = part.shape
    half = count // 2
    keys = kv.shape[0]
    shares, owns, scatters = [], [], []
    for g in range(k_heads):
        share, own = take(2)
        shares.append(share)
        owns.append(own)
        scatters.append(OwnScatter(groups, count, 5, [share, own] + take(OwnScatter.refs(groups))))
    block = width // groups
    up_task, attn_task = [
        OwnScatter(groups, block, chunks, [value, total] + take(OwnScatter.refs(groups)))
        for value, total in ((g_up, up_sum), (g_attn, attn_sum))
    ]
    spare = spares.shape[0] // groups
    back_task = OwnScatter(groups, spare, spare_chunks, [spares, returned] + take(OwnScatter.refs(groups)))
    give_y = OwnScatter(groups, spare, spare_chunks, [spares_y, returned_y] + take(OwnScatter.refs(groups)))
    small = OwnScatter(groups, 8, 1, [gains_sum, gains_out] + take(OwnScatter.refs(groups)))
    line_a, line_b = [
        Line(k * half, half // 2, pieces, part, dresid, dx, take(12), norm=(x, gain, gsum, count)) for k in range(2)
    ]
    section, t = lax.axis_index("section"), lax.axis_index("tensor")
    mine = section == 0
    order = [9, 0, 3, 4, 5, 1, 2, 6, 7, 8]

    def load(k):
        here, there = sources[k].at[sources[k].shape[0] - kept[k].shape[0] :], kept[k]
        if k in (7, 8):
            here, there = sources[k].at[:count], kept[k].at[:count]
        return pltpu.make_async_copy(here, there, w_sem.at[k])

    lack = pltpu.make_async_copy(sources[7].at[count:], dqkv.at[count:], w_sem.at[13])
    loads = [load(k) for k in range(10)]
    for k in order:
        loads[k].start()
    known = pltpu.make_async_copy(dx_known.at[count:], dx, w_sem.at[11])
    known_back = pltpu.make_async_copy(back_known, returned, w_sem.at[14])
    load_n1 = pltpu.make_async_copy(normed_one, n1, w_sem.at[10])
    load_n1.start()
    known_y = pltpu.make_async_copy(y_back.at[spare : 2 * spare], returned_y, w_sem.at[12])
    load_y = pltpu.make_async_copy(y.at[count:], part, w_sem.at[12])

    @pl.when(mine)
    def _():
        known_y.start()

    @pl.when(section > 0)
    def _():
        known.start()
        lack.start()
        known_back.start()

    for k in range(1, 4):
        greet({"tensor": lax.rem(t + k, 4)})
    for where, _ in up_task.links:
        greet(where)
    gsum[...] = jnp.zeros_like(gsum)
    dkv[...] = jnp.zeros_like(dkv)
    pl.semaphore_wait(pltpu.get_barrier_semaphore(), 3 + levels)
    loads[9].wait()
    up_task.start()
    for k in (0, 3, 4, 5):
        loads[k].wait()

    wide, jobs = width // WIDE, width // TILE
    repeat = q_heads // k_heads
    rows = block_rows(keys)
    blocks = half // rows
    turns = repeat * blocks
    scale = HD ** (-0.5)
    late = 100
    begun = 2 * k_heads * turns

    def early(i):
        @pl.when(lax.rem(i, 2) == 1)
        def _():
            up_task.step(i // 2, late)

    def mix(first):
        here = pl.ds(first, half)

        def one(h, c):
            dmixed[here, lanes(h)] = with_transpose(dresid[here], wout[lanes(h), :]).astype(BF16)
            return c

        lax.fori_loop(0, q_heads, one, 0)

    def attend(first, g, each):
        heads = [g * repeat + r for r in range(repeat)]

        def one(n, c):
            here = pl.ds(pl.multiple_of(first + n * rows, rows), rows)
            there = pl.ds(pl.multiple_of(count + first + n * rows, rows), rows)
            stacked = jnp.concatenate([q[here, lanes(h)] for h in heads], axis=0)
            scores = with_transpose(stacked, kv[:, lanes(g)]) * scale
            code = kcode[...]
            upper = jnp.concatenate([qcode[here][:, :1]] * repeat, axis=0)
            lower = jnp.concatenate([qstart[here][:, :1]] * repeat, axis=0)
            allowed = jnp.logical_and(code <= upper, code >= lower)
            known = jnp.concatenate(
                [lse[pl.ds(pl.multiple_of(h * count + first + n * rows, rows), rows)][:, :1] for h in heads], axis=0
            )
            prob = jnp.where(allowed, jnp.exp(scores - known), 0.0)
            dm = jnp.concatenate([dmixed[here, lanes(h)] for h in heads], axis=0)
            d_prob = with_transpose(dm, kv[:, lanes(k_heads + g)])
            row_dot = jnp.sum(prob * d_prob, axis=-1, keepdims=True)
            d_scores = (prob * (d_prob - row_dot)).astype(BF16)
            d_query = times(d_scores, kv[:, lanes(g)]) * scale
            for r, h in enumerate(heads):
                turned = rolled(d_query[r * rows : (r + 1) * rows], cosine[here], -sine[here])
                dqkv[there, lanes(h)] = turned.astype(BF16)
            dkv[lanes(g), :] += rows_contract(stacked, d_scores) * scale
            dkv[lanes(k_heads + g), :] += rows_contract(dm, prob.astype(BF16))
            for r in range(repeat):
                each(n * repeat + r)
            return c

        lax.fori_loop(0, blocks, one, 0)

    def back(first):
        here, there = pl.ds(first, half), pl.ds(count + first, half)

        def one(i, c):
            columns = lanes(i, WIDE)
            part[here, columns] = with_transpose(dqkv[there], wqkv[columns, :]).astype(BF16)
            return c

        lax.fori_loop(0, wide, one, 0)

    @pl.when(mine)
    def _():
        mix(0)
        mix(half)
        for g in range(k_heads):
            for first in (0, half):
                at = 2 * g * turns + (turns if first else 0)
                attend(first, g, lambda i: early(at + i))

            shares[g][:, :LANES] = jnp.transpose(dkv[lanes(g), :]).astype(BF16)
            shares[g][:, LANES:] = jnp.transpose(dkv[lanes(k_heads + g), :]).astype(BF16)
            scatters[g].start()
        run_steps(0, scatters[0].chunks, *[(functools.partial(lambda s, i: s.step(i, late), s), 0) for s in scatters])

    @pl.when(section > 0)
    def _():
        run_steps(0, begun, (early, 0))
        known.wait()
        lack.wait()

    ends = [0]
    for item in (spread_q, spread_k, spread_v, spread_o):
        ends.append(ends[-1] + item.shape[0])
    starts = [0, q_heads, q_heads + k_heads, q_heads + 2 * k_heads]

    @pl.when(section > 0)
    def _():
        load_y.start()
        load_y.wait()
        spares_y[...] = times(holder[...], part[...]).astype(BF16)
        give_y.start()

    for k in (1, 2, 6, 7, 8):
        loads[k].wait()
    load_n1.wait()
    plain_mixed[...] = with_transpose(mixed[...], spread_o[...]).astype(BF16)
    other_dresid[count:] = dresid[...]

    def out_job(i, c):
        here = lanes(i, TILE)
        g_attn[here, ends[3] :] = rows_contract(other_dresid[:, here], plain_mixed[...]).astype(BF16)
        return c

    lax.fori_loop(0, jobs, out_job, 0)

    @pl.when(mine)
    def _():
        ending = late + scatters[0].chunks
        run_steps(late, ending, *[(functools.partial(lambda s, i: s.step(i, late), s), 0) for s in scatters])
        for g in range(k_heads):
            dqkv[count:, lanes(q_heads + g)] = rolled(owns[g][:, :LANES], cosine[...], -sine[...]).astype(BF16)
            dqkv[count:, lanes(q_heads + k_heads + g)] = owns[g][:, LANES:].astype(BF16)
        back(0)
        line_a.start()
        back(half)
        line_b.start()

    def spread(k):
        return remote(gains_own, gains_all.at[k - 1], g_s.at[k - 1], g_r.at[k - 1], {"tensor": lax.rem(t + k, 4)})

    first_job = begun // 2

    def step(i, c):
        @pl.when(mine)
        def _():
            line_a.step(i)
            line_b.step(i - line_a.steps)

        up_task.step(i + first_job, late)

        @pl.when(i == 0)
        def _():
            for a, b, n, item in zip(starts, starts[1:], ends, (spread_q, spread_k, spread_v)):
                plain[:, n : n + item.shape[0]] = with_transpose(
                    dqkv[:, a * LANES : b * LANES], item[...]
                ).astype(BF16)

        @pl.when(jnp.logical_and(i >= 1, i <= jobs))
        def _():
            here = lanes(jnp.clip(i - 1, 0, jobs - 1), TILE)
            g_attn[here, : ends[3]] = rows_contract(n1[:, here], plain[...]).astype(BF16)

        @pl.when(i == jobs)
        def _():
            attn_task.start()

        attn_task.step(i - jobs - 1, late)

        @pl.when(section > 0)
        def _():
            give_y.step(i - first_job, late)

        return c

    lax.fori_loop(0, max(line_a.steps + line_b.steps, jobs + 1 + chunks), step, 0)
    @pl.when(mine)
    def _():
        spares[...] = times(holder[...], dx[...]).astype(BF16)
        back_task.start()

    gains_own[...] = jnp.zeros_like(gains_own)
    gains_own[:1] = gain_one[...] + jnp.where(mine, gsum[...], 0.0)
    gains_own[1:2] = gain_two[...] + jnp.where(mine, gain_last[...], 0.0)
    for k in range(1, 4):
        spread(k).start()

    @pl.when(mine)
    def _():
        run_steps(0, spare_chunks, (lambda i: back_task.step(i, late), 0))

    for k in range(1, 4):
        spread(k).wait()
    total = gains_own[...] + gains_all[0] + gains_all[1] + gains_all[2]
    part_width = width // groups
    for d in range(groups):
        gains_sum[8 * d : 8 * d + 8, :] = total[:, d * part_width : (d + 1) * part_width]
    small.start()

    def close(i, c):
        up_task.step(late + i, late)
        attn_task.step(late + i, late)

        @pl.when(section > 0)
        def _():
            give_y.step(late + i, late)

        small.step(i, 4)
        return c

    lax.fori_loop(0, max(chunks, spare_chunks, small.steps(4)), close, 0)

    @pl.when(mine)
    def _():
        run_steps(late, late + spare_chunks, (lambda i: back_task.step(i, late), 0))
        back_task.finish()

    @pl.when(section > 0)
    def _():
        known_back.wait()


    @pl.when(mine)
    def _():
        line_a.finish()
        line_b.finish()
        for item in scatters:
            item.finish()
        known_y.wait()

    @pl.when(section > 0)
    def _():
        give_y.finish()

    for item in (up_task, attn_task, small):
        item.finish()


def last_attn(known, spots, dresid, dx, y, y_back, normed_one, back_known, holder, gains, spreads, grads, weights, groups, q_heads, k_heads, cid):
    norm_one, wqkv, wout, norm_two, wgate, wup, wdown = weights
    x, q, kv, lse, mixed, dqkv, other_dresid = known
    count, width = dresid.shape
    keys = groups * count
    spare = holder.shape[0] // groups
    pieces, chunks, spare_chunks = 5, 8, spare // 32
    vmem = pl.BlockSpec(memory_space=pltpu.VMEM)
    far = pl.BlockSpec(memory_space=pl.ANY)
    dma = pltpu.SemaphoreType.DMA
    sources = [wout, wqkv, x, q, kv, lse, mixed, dqkv, other_dresid, *grads]
    attn_width = sum(item.shape[0] for item in spreads)
    block = width // groups
    first_only = {3: count, 4: keys, 5: q_heads * count}
    scratch = [
        pltpu.VMEM((first_only.get(k, item.shape[0]),) + item.shape[1:], item.dtype) for k, item in enumerate(sources)
    ]
    scratch += [
        pltpu.VMEM((2 * count, attn_width - spreads[3].shape[0]), BF16),
        pltpu.VMEM((2 * count, spreads[3].shape[0]), BF16),
        pltpu.VMEM((count, width), BF16),
        pltpu.VMEM((count, q.shape[1]), BF16),
        pltpu.VMEM((kv.shape[1], keys), F32),
        pltpu.VMEM((2 * count, width), BF16),
        pltpu.VMEM((width, attn_width), BF16),
        pltpu.VMEM((groups * spare, width), BF16),
        pltpu.VMEM((groups * spare, width), BF16),
        pltpu.VMEM((1, width), F32),
        pltpu.VMEM((8, width), F32),
        pltpu.VMEM((3, 8, width), F32),
        pltpu.VMEM((groups * 8, block), F32),
        dma((15,)),
        dma((3,)),
        dma((3,)),
    ]
    for _ in range(k_heads):
        scratch += [pltpu.VMEM((keys, 2 * LANES), BF16), pltpu.VMEM((count, 2 * LANES), F32)]
        scratch += OwnScatter.scratch(groups, count, 2 * LANES, 5, BF16)
    for columns in (grads[0].shape[1], attn_width):
        scratch += OwnScatter.scratch(groups, block, columns, chunks, BF16)
    scratch += OwnScatter.scratch(groups, spare, width, spare_chunks, BF16) * 2
    scratch += OwnScatter.scratch(groups, 8, block, 1, F32)
    scratch += Line.scratch(count // 4, pieces, width, False) * 2
    return pl.pallas_call(
        functools.partial(last_attn_kernel, groups, q_heads, k_heads, pieces, chunks, spare_chunks),
        out_shape=[
            jax.ShapeDtypeStruct((count, width), BF16),
            jax.ShapeDtypeStruct((spare, width), BF16),
            jax.ShapeDtypeStruct((spare, width), BF16),
            jax.ShapeDtypeStruct((8, block), F32),
            jax.ShapeDtypeStruct((block, grads[0].shape[1]), BF16),
            jax.ShapeDtypeStruct((block, attn_width), BF16),
        ],
        in_specs=[vmem] * 15 + [far] * 15,
        out_specs=[vmem] * 6,
        scratch_shapes=scratch,
        compiler_params=pltpu.CompilerParams(
            collective_id=cid, has_side_effects=True, vmem_limit_bytes=VMEM_LIMIT
        ),
        name="last_attn",
    )(*spots, norm_one[None], dresid, holder, *gains, *spreads, *sources, dx, y, y_back, normed_one, back_known)


def finish_kernel(groups, parts, *refs):
    refs = list(refs)

    def take(count):
        taken = refs[:count]
        del refs[:count]
        return taken

    live, gains = take(2)
    through, y, y_first, y_second, cot, dx_first, dx_second, back_first, back_second = take(9)
    gate, up, down, attn = take(4)
    acts, backs = take(2)
    outs = take(7)
    gain_one_out, gain_two_out = take(2)
    tiles = take(4)
    rows = take(4)
    backs_near = take(4)
    down_near, down_turned, attn_near, *attn_parts = take(7)
    plain_near, plain_wide = take(2), take(2)
    sems, out_sems = take(2)
    count, spare = rows[0].shape[0], backs_near[0].shape[0]
    seq = count + spare
    whole = [
        (through.at[0, 0], y.at[:count], y_first, acts.at[0, 0, 0]),
        (through.at[1, 0], y.at[count:], y_second, acts.at[0, 1, 0]),
        (cot.at[0, 0], dx_first.at[:count], back_first.at[2 * spare :], backs.at[0, 0, 0]),
        (cot.at[1, 0], dx_second, back_second, backs.at[0, 1, 0]),
    ]
    query_out, key_out, value_out, out_out, gate_out, up_out, down_out = outs
    plain_in = [pltpu.make_async_copy(a, b, sems.at[14 + k]) for k, (a, b) in enumerate(zip((gate, up), plain_near))]
    plain = [pltpu.make_async_copy(a, b, out_sems.at[k]) for k, (a, b) in enumerate(zip(plain_wide, (gate_out.at[0], up_out.at[0])))]
    load_down = pltpu.make_async_copy(down, down_near, sems.at[12])
    load_attn = pltpu.make_async_copy(attn, attn_near, sems.at[13])
    loads = []
    for k, (a, b, c, _) in enumerate(whole):
        loads.append(
            [
                pltpu.make_async_copy(src, dst, sems.at[3 * k + n])
                for n, (src, dst) in enumerate(((a, tiles[k]), (b, rows[k]), (c, backs_near[k])))
            ]
        )
    load_attn.start()
    load_down.start()
    for item in plain_in:
        item.start()
    for group in loads:
        for item in group:
            item.start()
    stores = []
    load_attn.wait()
    at = 0
    for k, (size, near, there) in enumerate(zip(parts, attn_parts, (query_out, key_out, value_out, out_out))):
        value = attn_near[:, at : at + size].astype(F32)
        near[...] = value if k == 0 else jnp.transpose(value)
        at += size
        stores.append(pltpu.make_async_copy(near, there.at[0], out_sems.at[2 + k]))
        stores[-1].start()
    gain_one_out[...] = gains[:1]
    gain_two_out[...] = gains[1:2]
    for before, near, wide, item in zip(plain_in, plain_near, plain_wide, plain):
        before.wait()
        wide[...] = near[...].astype(F32)
        item.start()
    load_down.wait()
    down_turned[...] = jnp.transpose(down_near[...].astype(F32))
    stores.append(pltpu.make_async_copy(down_turned, down_out.at[0], out_sems.at[6]))
    stores[-1].start()
    for k, group in enumerate(loads):
        for item in group:
            item.wait()
        first = (k % 2) * seq

        def one(i, c):
            here = pl.ds(pl.multiple_of(i * 64, 64), 64)
            alive = live[pl.ds(pl.multiple_of(first + i * 64, 64), 64)] > 0
            tiles[k][here] = jnp.where(alive, rows[k][here], tiles[k][here])
            return c

        lax.fori_loop(0, count // 64, one, 0)

        def two(i, c):
            near = pl.ds(pl.multiple_of(i * 64, 64), 64)
            here = pl.ds(pl.multiple_of(count + i * 64, 64), 64)
            alive = live[pl.ds(pl.multiple_of(first + count + i * 64, 64), 64)] > 0
            tiles[k][here] = jnp.where(alive, backs_near[k][near], tiles[k][here])
            return c

        lax.fori_loop(0, spare // 64, two, 0)
        stores.append(pltpu.make_async_copy(tiles[k], whole[k][3], out_sems.at[7 + k]))
        stores[-1].start()
    for item in stores + plain:
        item.wait()


def finish(live, gains, through, y, y_backs, cot, dx_first, dx_second, back_first, back_second, grads, parts, groups):
    count, width = dx_second.shape
    spare = back_second.shape[0]
    gate, up, down, attn = grads
    block, hidden = down.shape
    vmem = pl.BlockSpec(memory_space=pltpu.VMEM)
    far = pl.BlockSpec(memory_space=pl.ANY)
    shapes = [(block, parts[0])] + [(size, block) for size in parts[1:]]
    outs = [jax.ShapeDtypeStruct((1, 2, 1, count + spare, width), BF16)] * 2
    outs += [jax.ShapeDtypeStruct((1,) + item, F32) for item in shapes + [gate.shape, up.shape, (hidden, block)]]
    outs += [jax.ShapeDtypeStruct((1, block), F32)] * 2
    scratch = [pltpu.VMEM((count + spare, width), BF16)] * 4
    scratch += [pltpu.VMEM((count, width), BF16)] * 4 + [pltpu.VMEM((spare, width), BF16)] * 4
    scratch += [pltpu.VMEM(down.shape, BF16), pltpu.VMEM((hidden, block), F32), pltpu.VMEM(attn.shape, BF16)]
    scratch += [pltpu.VMEM(item, F32) for item in shapes]
    scratch += [pltpu.VMEM(gate.shape, BF16)] * 2 + [pltpu.VMEM(gate.shape, F32)] * 2
    scratch += [pltpu.SemaphoreType.DMA((16,)), pltpu.SemaphoreType.DMA((11,))]
    return pl.pallas_call(
        functools.partial(finish_kernel, groups, parts),
        out_shape=outs,
        in_specs=[vmem] * 2 + [far] * 13,
        out_specs=[far] * 9 + [vmem] * 2,
        scratch_shapes=scratch,
        compiler_params=pltpu.CompilerParams(vmem_limit_bytes=VMEM_LIMIT),
        name="finish",
    )(live, gains, through, y, *y_backs, cot, dx_first, dx_second, back_first, back_second, gate, up, down, attn)


def rope_tables(seq_len):
    half_width = HD // 2
    inverse = np.float32(rope_base) ** (-(np.arange(half_width, dtype=np.float32) * np.float32(2.0) / np.float32(HD)))
    angle = np.arange(seq_len, dtype=np.float32)[:, None] * inverse[None, :].astype(np.float32)
    cosine, sine = np.cos(angle), np.sin(angle)
    table = np.zeros((seq_len, 4, LANES // 2), np.float32)
    table[:, 0, :half_width] = cosine
    table[:, 1, :half_width] = cosine
    table[:, 2, :half_width] = -sine
    table[:, 3, :half_width] = sine
    return table.reshape(seq_len, 2 * LANES)


def spreader(heads, turned):
    feature = jnp.arange(HD)
    place = jnp.where(feature < HD // 2, feature, feature - HD // 2 + LANES // 2) if turned else feature
    lane = (jnp.arange(heads)[:, None] * LANES + place[None, :]).reshape(-1)
    return (lane[:, None] == jnp.arange(heads * LANES)[None, :]).astype(BF16)


def slots_of(lens, count):
    groups = lens.shape[0]
    kept = jnp.minimum(lens, count)
    free, extra = count - kept, lens - kept
    free_off = jnp.cumsum(free) - free
    extra_end = jnp.cumsum(extra)
    slot = jnp.arange(count)
    own = slot[None, :] < kept[:, None]
    index = free_off[:, None] + slot[None, :] - kept[:, None]
    source = jnp.sum(index[:, :, None] >= extra_end[None, None, :], axis=-1)
    begins = jnp.sum(jnp.where(index[:, :, None] >= extra_end[None, None, :], extra[None, None, :], 0), axis=-1)
    seq = jnp.where(own, jnp.arange(groups)[:, None], source)
    pos = jnp.where(own, slot[None, :], count + index - begins)
    return seq, pos, own


def on_device(
    inputs,
    cotangent,
    lengths,
    norm_attn,
    w_query,
    w_key,
    w_value,
    w_out,
    norm_ffn,
    w_gate,
    w_up,
    w_down,
):
    first = lax.axis_index("section") == 0
    me = lax.axis_index("dp")
    groups = lax.axis_size("dp")
    micro, seq_len, width = inputs.shape[0], inputs.shape[2], inputs.shape[3]
    count = seq_len * 5 // 8
    spare = seq_len - count
    q_heads, k_heads = w_query.shape[2] // HD, w_key.shape[2] // HD
    spread_q, spread_k = spreader(q_heads, True), spreader(k_heads, True)
    spread_v, spread_o = spreader(k_heads, False), spreader(q_heads, False)
    qkv = [
        times(item[0], spread).astype(BF16)
        for item, spread in ((w_query, spread_q), (w_key, spread_k), (w_value, spread_v))
    ]
    wqkv = jnp.concatenate(qkv, axis=1)
    wout = rows_contract(spread_o, w_out[0]).astype(BF16)
    weights = (norm_attn[0], wqkv, wout, norm_ffn[0], w_gate[0], w_up[0], w_down[0])

    all_in_one = micro == 2 and groups == 4

    extras = [jnp.where(first, inputs[b, 0, count:], cotangent[b, 0, count:]) for b in range(micro)]
    first_extra = lax.all_gather(extras[0], "dp", axis=0, tiled=True)
    length_rows = jnp.broadcast_to(lengths[:, 0].astype(F32)[:, None], (micro, LANES))
    length_rows = jnp.concatenate([length_rows, jnp.zeros((8 - micro, LANES), F32)], axis=0)
    (length_all,) = gather_rows([length_rows], groups, 4)
    lens = length_all.reshape(groups, 8, LANES)[:, :micro, 0].T.astype(jnp.int32)
    packed, slots, spots, chosen, kept_own = [], [], [], [], []
    for b in range(micro):
        seq, pos, own = slots_of(lens[b], count)
        slots.append((seq, pos))
        my_seq, my_pos, own = seq[me][:, None], pos[me][:, None], own[me][:, None]
        here = (jnp.arange(seq_len)[None, :] == my_pos).astype(F32)
        turned = jnp.dot(here, rope_tables(seq_len), precision=lax.Precision.HIGHEST)
        code = (seq * seq_len + pos).reshape(1, -1)
        spots.append((turned[:, :LANES], turned[:, LANES:], my_seq * seq_len + my_pos, my_seq * seq_len, code))
        wanted = jnp.where(own, -1, my_seq * spare + my_pos - count)
        chosen.append((jnp.arange(groups * spare)[None, :] == wanted).astype(BF16))
        kept = jnp.where(first, inputs[b, 0, :count], cotangent[b, 0, :count])
        kept_own.append(jnp.where(own, kept, jnp.zeros((), BF16)))
    for b in range(0 if all_in_one else micro):
        extra = first_extra if b == 0 else lax.all_gather(extras[b], "dp", axis=0, tiled=True)
        packed.append((kept_own[b].astype(F32) + times(chosen[b], extra)).astype(BF16))

    def holder(b):
        seq, pos = slots[b]
        row = jnp.arange(groups * spare)[:, None]
        return jnp.logical_and(row == seq[me][None, :] * spare + pos[me][None, :] - count, pos[me][None, :] >= count)

    def spread(rows, b):
        return jnp.dot(holder(b).astype(BF16), rows, preferred_element_type=F32).astype(BF16)

    def unpack(rows, back, b, through):
        live = (jnp.arange(seq_len) < lens[b, me])[:, None]
        return jnp.where(live, jnp.concatenate([rows, back], axis=0), through)

    def come_back(rows, b):
        return lax.psum_scatter(spread(rows, b), "dp", scatter_dimension=0, tiled=True)

    norm_one, norm_two = weights[0], weights[3]
    empty = jnp.zeros((count, width), BF16)

    def spots_at(tick):
        early, late = spots[min(tick, micro - 1)], spots[max(tick - 1, 0)]
        return tuple(jnp.where(first, a, b) for a, b in zip(early, late))

    grads_in, before, gain_sums = [], [], []
    if all_in_one:
        joined = [jnp.concatenate(items, axis=0) for items in zip(*spots)]
        joined[4] = joined[4][:, None]
        held = jnp.concatenate([holder(b) for b in range(micro)], axis=0).astype(BF16)
        y, dx, y_back, normed_one, normed_two, x, q, kv, lse, mixed, resid, gate, up, act, dy, d_resid, d_gate, d_up, d_qkv, gain_one, gain_two = main_ticks(
            (jnp.concatenate(kept_own, axis=0), first_extra, extras[1], jnp.concatenate(chosen, axis=0)),
            joined,
            held,
            weights,
            qkv,
            groups,
            q_heads,
            k_heads,
            0,
        )
        last_dresid, gain_last, grad_up, grad_down, grad_gate, y, y_first, back_known = last_ffn(
            (dy, act, gate, up, d_gate, d_up, resid, d_resid, y, y_back, normed_two, dx), held, weights, groups, 1
        )
        last_dx, back_second, y_second, gains, grad_up, grad_attn = last_attn(
            (x, q, kv, lse, mixed, d_qkv, d_resid),
            spots[1],
            last_dresid,
            dx,
            y,
            y_back,
            normed_one,
            back_known,
            held[groups * spare :],
            (gain_one, gain_two, gain_last),
            (spread_q, spread_k, spread_v, spread_o),
            (grad_up,),
            weights,
            groups,
            q_heads,
            k_heads,
            2,
        )
        live = (jnp.arange(seq_len)[None, :] < lens[:, me][:, None]).astype(jnp.int32).reshape(-1, 1)
        acts, backs, *grads = finish(
            live,
            gains,
            inputs,
            y,
            (y_first, y_second),
            cotangent,
            dx,
            last_dx,
            y_back,
            back_second,
            (grad_gate, grad_up, grad_down, grad_attn),
            [w_query.shape[2], w_key.shape[2], w_value.shape[2], w_query.shape[2]],
            groups,
        )
        grads[1:3] = [jnp.swapaxes(item, 1, 2) for item in grads[1:3]]
        return (acts, backs, grads[7], *grads[:4], grads[8], *grads[4:7])

    else:
        arriving = empty
        results, saved = [], []
        for tick in range(micro + 1):
            stream = jnp.where(first, packed[tick] if tick < micro else empty, arriving)
            result, arriving, kept = forward_tick(stream, spots_at(tick), weights, groups, q_heads, k_heads, 0)
            results.append(result)
            saved.append(kept)
        results = [jnp.where(first, results[b], results[b + 1]) for b in range(micro)]
        arriving = empty
        for tick in range(micro):
            kept = saved[micro - tick]
            incoming = jnp.where(first, arriving, packed[micro - 1 - tick])
            d_resid, gain_two, d_gate, d_up = back_ffn(incoming, kept, weights, 1)
            d_stream, gain_one, d_qkv, arriving = back_attn(
                d_resid, kept, spots_at(micro - tick), weights, groups, q_heads, k_heads, 2, -1
            )
            before.append((kept[5], d_gate, d_up, incoming, kept[8], kept[0], d_qkv, d_resid, kept[4]))
            grads_in.append(d_stream)
            gain_sums.append(jnp.concatenate([gain_one, gain_two], axis=0))
        kept_last = saved[0]
        last_in, last_spots = jnp.where(first, arriving, empty), spots_at(0)
        grads_at = [grads_in[micro - 1 - b] if b == 0 else jnp.where(first, grads_in[micro - b], grads_in[micro - 1 - b]) for b in range(micro)]

        def all_rows(now, index):
            old = [item[index] for item in before]
            return jnp.concatenate([jnp.where(first, now, old[0])] + old[1:], axis=0)

        x, mixed, resid, act = kept_last[0], kept_last[4], kept_last[5], kept_last[8]
        d_resid, gain_two, d_gate, d_up = back_ffn(last_in, kept_last, weights, 1)
        n2 = normalize(all_rows(resid, 0), norm_two)
        grad_gate = rows_contract(n2, all_rows(d_gate, 1)).astype(BF16)
        grad_up = rows_contract(n2, all_rows(d_up, 2)).astype(BF16)
        grad_down = rows_contract(all_rows(last_in, 3), all_rows(act, 4)).astype(BF16)
        ffn_grads = (grad_gate, grad_up, grad_down)
        beside = len(ffn_grads) if groups * count <= 2048 else 1
        d_stream, gain_one, d_qkv, *ffn_sums = back_attn(
            d_resid, kept_last, last_spots, weights, groups, q_heads, k_heads, 3, 0, sums=ffn_grads[:beside]
        )
        n1 = normalize(all_rows(x, 5), norm_one)
        back_spread = [(spread_q, 0, q_heads), (spread_k, q_heads, k_heads), (spread_v, q_heads + k_heads, k_heads)]
        dqkv = all_rows(d_qkv, 6)
        dqkv = jnp.concatenate(
            [with_transpose(dqkv[:, i * LANES : (i + n) * LANES], item) for item, i, n in back_spread], axis=1
        ).astype(BF16)
        mix = with_transpose(all_rows(mixed, 8), spread_o).astype(BF16)
        grad_attn = jnp.concatenate(
            [rows_contract(n1, dqkv).astype(BF16), rows_contract(all_rows(d_resid, 7), mix).astype(BF16)], axis=1
        )
        grads_at[0] = jnp.where(first, d_stream, grads_at[0])
        last_gains = jnp.concatenate([gain_one, gain_two], axis=0)
        gain_sums.append(jnp.where(first, last_gains, jnp.zeros_like(last_gains)))

        gains = sum(gain_sums[1:], gain_sums[0])
        gains = jnp.concatenate([gains, jnp.zeros((6, width), F32)], axis=0)
        gains = gains.reshape(8, groups, -1).transpose(1, 0, 2).reshape(groups * 8, -1)

    acts = []
    for b in range(micro):
        rows = results[b]
        acts.append(unpack(rows, come_back(rows, b), b, inputs[b, 0]))
    backs = []
    for b in range(micro):
        rows = grads_at[b]
        if b == 0:
            back, gains, grad_attn, *rest = return_rows(
                spread(rows, b), gains, (grad_attn,) + ffn_grads[beside:], groups, 5, spare // 16
            )
            grad_gate, grad_up, grad_down = ffn_sums + rest
        else:
            back = come_back(rows, b)
        backs.append(unpack(rows, back, b, cotangent[b, 0]))
    acts, backs = jnp.stack(acts), jnp.stack(backs)
    ends = [0]
    for item in (w_query, w_key, w_value, w_query):
        ends.append(ends[-1] + item.shape[2])
    grad_query, grad_key, grad_value, grad_out = (grad_attn[:, a:b] for a, b in zip(ends, ends[1:]))
    final = (
        gains[0],
        grad_query,
        grad_key,
        grad_value,
        grad_out.T,
        gains[1],
        grad_gate,
        grad_up,
        grad_down.T,
    )
    return (acts[None, :, None], backs[None, :, None]) + tuple(item[None] for item in final)


def solution(mesh):
    placed = (
        P(None, "dp", None, None),
        P(None, "dp", None, None),
        P(None, "dp"),
        P("section", None),
        P("section", None, "tensor"),
        P("section", None, "tensor"),
        P("section", None, "tensor"),
        P("section", "tensor", None),
        P("section", None),
        P("section", None, "tensor"),
        P("section", None, "tensor"),
        P("section", "tensor", None),
    )
    return jax.shard_map(
        on_device,
        mesh=mesh,
        in_specs=placed,
        out_specs=(
            P("section", None, "dp", None, None),
            P("section", None, "dp", None, None),
            P("section", "dp"),
            P("section", "dp", "tensor"),
            P("section", "dp", "tensor"),
            P("section", "dp", "tensor"),
            P("section", "tensor", "dp"),
            P("section", "dp"),
            P("section", "dp", "tensor"),
            P("section", "dp", "tensor"),
            P("section", "tensor", "dp"),
        ),
        check_vma=False,
    )
```
